32 devices in a mesh: dp: 4 (over z), ctx: 4 (over x, core), expert: 2 (over y).
Axes of the slice: x: 2, y: 2, z: 4, core: 2. Of those that a mesh axis runs over, the one named last changes fastest.
Arguments:
- hidden_in: bfloat16 [6144, 2048], P(('dp', 'ctx', 'expert')), may hold values from -6 to 6
- attn_gain: float32 [2048], replicated, may hold values from 0.5 to 1.5
- query_weight: bfloat16 [2048, 4096], P('expert'), may hold values from -0.125 to 0.125
- key_matrix: bfloat16 [2048, 512], P('expert'), may hold values from -0.125 to 0.125
- value_matrix: bfloat16 [2048, 512], P('expert'), may hold values from -0.125 to 0.125
- query_gain: float32 [128], replicated, may hold values from 0.5 to 1.5
- key_gain: float32 [128], replicated, may hold values from 0.5 to 1.5
- output_weight: bfloat16 [4096, 2048], P('expert'), may hold values from -1.5 to 1.5
- ffn_gain: float32 [2048], replicated, may hold values from 0.5 to 1.5
- router_weight: bfloat16 [2048, 16], replicated, may hold values from -0.0625 to 0.0625
- gate_up: bfloat16 [16, 2048, 1536], P(('ctx', 'expert')), may hold values from -0.125 to 0.125
- down_proj: bfloat16 [16, 768, 2048], P(('ctx', 'expert')), may hold values from -1.25 to 1.25
- routes: int32 [6144, 8], P(('dp', 'ctx', 'expert')), may hold values from 0 to 15, all different within a row; in each aligned block of 192 rows (0 to 191, 192 to 383, ...) at most 137 rows name the same one
- out_grad: bfloat16 [6144, 2048], P(('dp', 'ctx', 'expert')), may hold values from -6 to 6
Outputs:
- block_out: bfloat16 [6144, 2048], P(('dp', 'ctx', 'expert'))
- hidden_grad: float32 [6144, 2048], P(('dp', 'ctx', 'expert'))
- attn_gain_grad: float32 [2048], P(('dp', 'ctx', 'expert'))
- query_weight_grad: float32 [2048, 4096], P(('dp', 'ctx', 'expert'))
- key_weight_grad: float32 [2048, 512], P(('dp', 'ctx', 'expert'))
- value_weight_grad: float32 [2048, 512], P(('dp', 'ctx', 'expert'))
- query_gain_grad: float32 [128], P(('dp', 'ctx', 'expert'))
- key_gain_grad: float32 [128], P(('dp', 'ctx', 'expert'))
- output_weight_grad: float32 [4096, 2048], P(('dp', 'ctx', 'expert'))
- ffn_gain_grad: float32 [2048], P(('dp', 'ctx', 'expert'))
- router_grad: float32 [2048, 16], P(('dp', 'ctx', 'expert'))
- gate_up_grad: float32 [16, 2048, 1536], P(('ctx', 'expert'), 'dp')
- down_grad: float32 [16, 768, 2048], P(('ctx', 'expert'), 'dp')
The draws below stay inside these ranges and needn't reach their ends.
Inputs may be any that keep to these rules, and one draw needn't show every extreme that they name: `routes`: among the rows of one device no expert is named by more than 137 rows, a bound that some block reaches.
All inputs are finite; a program needn't handle non-finite values.
Results may differ from the reference program's by a relative error of at most 0.02.
Values may be sent and summed in bfloat16 or wider, within the bound.
A program may use at most 384 MiB of HBM per device.

```python
import math
import jax
import jax.numpy as jnp
import numpy as np
from jax import lax

MODEL_WIDTH = 2048
QUERY_HEADS = 32
KEY_VALUE_HEADS = 4
HEAD_SIZE = 128
FF = 768
TOP = 8
PROMPT_DEV = 128
TOK_DEV = 192
EXPERTS = 16
TOKENS = 6144
CAP = 137
N_DP = 4
N_CTX = 4
N_EXPERT = 2


def levels(own_key, dims, cuts, smallest, top_value):
    gain = 1.0
    for dim, shards_of in cuts:
        draws = jax.random.uniform(jax.random.fold_in(jax.random.fold_in(own_key, 6), dim), (shards_of,), jnp.float32, smallest / len(cuts), top_value / len(cuts))
        gain = gain * jnp.repeat(jnp.exp(draws), dims[dim] // shards_of).reshape((-1,) + (1,) * (len(dims) - 1 - dim))
    return gain


def assign_block(stream_key, own, number, rows, amount, top, reach, slope):
    sequence = jax.random.permutation(stream_key, amount)
    crowded, ordinary = load_shares(amount, rows * top, reach, slope, True), load_shares(amount, rows * top, reach, slope, False)
    places = jnp.arange(amount)

    def named(sizes, turn):
        used = int((sizes > 0).sum())
        fixed = max(1, used // 4)
        shifted = fixed + (places - fixed + turn * (used - fixed)) % max(1, amount - fixed)
        return jnp.zeros((amount,), jnp.int32).at[sequence[jnp.where(places < fixed, places, shifted)]].set(jnp.asarray(sizes, jnp.int32))

    sizes = jnp.where(number % 4 == 0, named(crowded, number // 4), named(ordinary, number - number // 4 - 1))
    mixed = jax.random.permutation(jax.random.fold_in(own, 3), amount)
    donor, receiver = mixed[0:amount // 2 * 2:2], mixed[1:amount // 2 * 2:2]
    margin = jnp.minimum(sizes[donor] - 1, reach - sizes[receiver]) // 2
    margin = jnp.where((donor == sequence[0]) | (receiver == sequence[0]) | (sizes[receiver] == 0), 0, jnp.maximum(margin, 0))
    shifted = jax.random.randint(jax.random.fold_in(own, 4), (amount // 2,), 0, 1 << 20) % (margin + 1)
    sizes = sizes.at[donor].add(-shifted).at[receiver].add(shifted)
    members = jnp.searchsorted(jnp.cumsum(sizes), jnp.arange(rows * top), side="right").astype(jnp.int32)
    table = members.reshape(top, rows).T
    table = table[jax.random.permutation(jax.random.fold_in(own, 1), rows)]
    turn = jax.random.randint(jax.random.fold_in(own, 2), (rows, 1), 0, top)
    return jnp.take_along_axis(table, (jnp.arange(top)[None, :] + turn) % top, axis=1)


def load_shares(number_of, total, limit, skew, full):
    weights = [(1 << 20) // math.isqrt(standing ** skew) + 1 for standing in range(1, number_of + 1)]
    largest = limit if full else min(limit, max(-(-total // number_of), total * weights[0] // sum(weights)))
    least = 1 if total - largest >= number_of - 1 else 0
    holding, rest = [largest] + [least] * (number_of - 1), total - largest - least * (number_of - 1)
    while rest > 0:
        candidates = [i for i in range(1, number_of) if holding[i] < largest] or [i for i in range(1, number_of) if holding[i] < limit]
        mass, left = sum([weights[i] for i in candidates]), rest
        for i in candidates:
            addition = min(limit - holding[i], max(1, left * weights[i] // mass), rest)
            holding[i] = holding[i] + addition
            rest = rest - addition
    return np.array(holding)


def normal_values(own_key, extent, width, most, cuts=(), kind=jnp.bfloat16):
    result = jax.random.normal(own_key, extent, jnp.float32) * width
    if len(cuts) > 0:
        result = levels(own_key, extent, cuts, -0.22, 0.18) * result
    return jnp.clip(result, min=-most, max=most).astype(kind)


def setup_inputs(seed: int = 0) -> dict:
    arg_keys = jax.random.split(jax.random.key(seed), 15)
    hidden_in = normal_values(arg_keys[0], (TOKENS, MODEL_WIDTH), 1.0, 6.0, ((0, 32),))
    attn_gain = jnp.clip(1.0 + 0.1 * jax.random.normal(arg_keys[1], (MODEL_WIDTH,), jnp.float32), 0.5, 1.5)
    query_weight = normal_values(arg_keys[2], (MODEL_WIDTH, QUERY_HEADS * HEAD_SIZE), MODEL_WIDTH ** -0.5, 0.125, ((0, 2),))
    key_matrix = normal_values(arg_keys[3], (MODEL_WIDTH, KEY_VALUE_HEADS * HEAD_SIZE), MODEL_WIDTH ** -0.5, 0.125, ((0, 2),))
    value_matrix = normal_values(arg_keys[4], (MODEL_WIDTH, KEY_VALUE_HEADS * HEAD_SIZE), MODEL_WIDTH ** -0.5, 0.125, ((0, 2),))
    query_gain = jnp.clip(1.0 + 0.1 * jax.random.normal(arg_keys[5], (HEAD_SIZE,), jnp.float32), 0.5, 1.5)
    key_gain = jnp.clip(1.0 + 0.1 * jax.random.normal(arg_keys[6], (HEAD_SIZE,), jnp.float32), 0.5, 1.5)
    output_weight = normal_values(arg_keys[7], (QUERY_HEADS * HEAD_SIZE, MODEL_WIDTH), (QUERY_HEADS * HEAD_SIZE // 256) ** -0.5, 1.5, ((0, 2),))
    ffn_gain = jnp.clip(1.0 + 0.1 * jax.random.normal(arg_keys[8], (MODEL_WIDTH,), jnp.float32), 0.5, 1.5)
    router_weight = normal_values(arg_keys[9], (MODEL_WIDTH, EXPERTS), (4 * MODEL_WIDTH) ** -0.5, 0.0625)
    gate_up = normal_values(arg_keys[10], (EXPERTS, MODEL_WIDTH, 2 * FF), MODEL_WIDTH ** -0.5, 0.125, ((0, 8),))
    down_proj = normal_values(arg_keys[11], (EXPERTS, FF, MODEL_WIDTH), (FF // 32) ** -0.5, 1.25, ((0, 8),))
    routes_keys = jax.random.split(jax.random.fold_in(arg_keys[12], 1), TOKENS // TOK_DEV)
    routes_turns = jax.random.permutation(jax.random.fold_in(arg_keys[12], 3), TOKENS // TOK_DEV)
    routes = jax.vmap(lambda own, number: assign_block(jax.random.fold_in(arg_keys[12], 2), own, number, TOK_DEV, EXPERTS, TOP, CAP, 2))(routes_keys, routes_turns).reshape((TOKENS, TOP))
    out_grad = normal_values(arg_keys[13], (TOKENS, MODEL_WIDTH), 1.0, 6.0, ((0, 32),))
    return dict(hidden_in=hidden_in, attn_gain=attn_gain, query_weight=query_weight, key_matrix=key_matrix, value_matrix=value_matrix, query_gain=query_gain, key_gain=key_gain, output_weight=output_weight, ffn_gain=ffn_gain, router_weight=router_weight, gate_up=gate_up, down_proj=down_proj, routes=routes, out_grad=out_grad)


highest = lax.Precision.HIGHEST
epsilon = 1e-06
rope_base = 1000000.0
masked = -1e+30

@jax.custom_vjp
def reduced_precision(v):
    return lax.optimization_barrier(v.astype(jnp.bfloat16)).astype(jnp.float32)

@jax.custom_vjp
def reduced_backward(v):
    return v

def low_keep(v):
    return (reduced_precision(v), None)

def low_pass(kept, grad):
    return (grad,)

def back_keep(v):
    return (v, None)

def back_low(kept, grad):
    return (reduced_precision(grad),)
reduced_precision.defvjp(low_keep, low_pass)
reduced_backward.defvjp(back_keep, back_low)

def matrix_product(left, right):
    return jnp.dot(left, right, precision=highest)

def rms_scale(value_rows):
    return lax.rsqrt(lax.optimization_barrier(jnp.mean(value_rows * value_rows, axis=-1, keepdims=True)) + epsilon)

def angles(position, head_width):
    freq_index = jnp.arange(head_width // 2, dtype=jnp.float32)
    inverse = jnp.exp(-(2.0 * freq_index / head_width) * math.log(rope_base))
    rope_angle = position.astype(jnp.float32)[:, None] * inverse[None, :]
    rope_angle = jnp.concatenate([rope_angle, rope_angle], axis=-1)
    return (jnp.cos(rope_angle), jnp.sin(rope_angle))

def rotate(value_rows, cosine, rope_sine):
    half_width = value_rows.shape[-1] // 2
    turned = jnp.concatenate([-value_rows[..., half_width:], value_rows[..., :half_width]], axis=-1)
    return value_rows * cosine + turned * rope_sine

def regroup(value_rows):
    trailing = tuple(value_rows.shape[1:])
    sectioned = value_rows.reshape((N_DP, N_CTX, N_EXPERT, TOK_DEV) + trailing)
    permuted = (0, 2, 1, 3) + tuple(range(4, 4 + len(trailing)))
    return sectioned.transpose(permuted).reshape((N_DP * N_EXPERT, N_CTX * TOK_DEV) + trailing)

def ungroup(value_rows):
    trailing = tuple(value_rows.shape[2:])
    sectioned = value_rows.reshape((N_DP, N_EXPERT, N_CTX, TOK_DEV) + trailing)
    permuted = (0, 2, 1, 3) + tuple(range(4, 4 + len(trailing)))
    return sectioned.transpose(permuted).reshape((N_DP * N_CTX * N_EXPERT * TOK_DEV,) + trailing)

def group_layout():
    group_rows = jnp.arange(N_CTX * TOK_DEV, dtype=jnp.int32)
    member = group_rows // TOK_DEV
    offset = group_rows % TOK_DEV
    in_prompt = offset < PROMPT_DEV
    position = jnp.where(in_prompt, member * PROMPT_DEV + offset, PROMPT_DEV * N_CTX + offset - PROMPT_DEV)
    seq_owner = jnp.where(in_prompt, -1, member)
    return (position, seq_owner)

def make_attend(position, seq_owner):
    visible = (position[None, :] <= position[:, None]) & ((seq_owner[None, :] < 0) | (seq_owner[None, :] == seq_owner[:, None]))
    heads_per_group = QUERY_HEADS // KEY_VALUE_HEADS
    score_scale = HEAD_SIZE ** (-0.5)

    def attend(operands):
        query_rows, keys, value_rows = operands
        count_of_rows = query_rows.shape[0]
        grouped_queries = query_rows.reshape(count_of_rows, KEY_VALUE_HEADS, heads_per_group, HEAD_SIZE)
        scores = reduced_backward(jnp.einsum('rkgd,skd->kgrs', grouped_queries, keys, precision=highest) * score_scale)
        scores = jnp.where(visible, scores, masked)
        row_max = lax.optimization_barrier(jnp.max(scores, axis=-1, keepdims=True))
        weights = jnp.exp(scores - row_max)
        attention = reduced_precision(weights / lax.optimization_barrier(jnp.sum(weights, axis=-1, keepdims=True)))
        mixed_values = jnp.einsum('kgrs,skd->rkgd', attention, value_rows, precision=highest)
        return mixed_values.reshape(count_of_rows, QUERY_HEADS * HEAD_SIZE)
    return jax.checkpoint(attend)

def reference(hidden_in, attn_gain, query_weight, key_matrix, value_matrix, query_gain, key_gain, output_weight, ffn_gain, router_weight, gate_up, down_proj, routes, out_grad):
    every_token = N_DP * N_CTX * N_EXPERT * TOK_DEV
    slot_count = N_DP * N_CTX * N_EXPERT * CAP
    pair_count = every_token * TOP
    flat_routes = routes.reshape(pair_count).astype(jnp.int32)
    onehot = (flat_routes[:, None] == jnp.arange(EXPERTS, dtype=jnp.int32)[None, :]).astype(jnp.int32)
    pair_rank = lax.optimization_barrier(jnp.sum((jnp.cumsum(onehot, axis=0) - onehot) * onehot, axis=1))
    pair_slot = flat_routes * slot_count + pair_rank
    slot_pair = jnp.full((EXPERTS * slot_count,), pair_count, dtype=jnp.int32).at[pair_slot].set(jnp.arange(pair_count, dtype=jnp.int32))
    slot_pair = slot_pair.reshape(EXPERTS, slot_count)
    slot_token = slot_pair // TOP
    position, seq_owner = group_layout()
    cosine, rope_sine = angles(position, HEAD_SIZE)
    cosine = cosine[None, :, None, :]
    rope_sine = rope_sine[None, :, None, :]
    attend = make_attend(position, seq_owner)

    def forward(inputs, attn_gain, query_weight, key_matrix, value_matrix, query_gain, key_gain, output_weight, ffn_gain, router_weight, gate_up, down_proj):
        normalized_input = reduced_precision(inputs * rms_scale(inputs) * attn_gain)
        query_pre = reduced_backward(matrix_product(normalized_input, query_weight)).reshape(every_token, QUERY_HEADS, HEAD_SIZE)
        key_before_norm = reduced_backward(matrix_product(normalized_input, key_matrix)).reshape(every_token, KEY_VALUE_HEADS, HEAD_SIZE)
        value_rows = reduced_precision(reduced_backward(matrix_product(normalized_input, value_matrix))).reshape(every_token, KEY_VALUE_HEADS, HEAD_SIZE)
        query_normed = query_pre * rms_scale(query_pre) * query_gain
        key_normed = key_before_norm * rms_scale(key_before_norm) * key_gain
        query_rows = reduced_precision(rotate(regroup(query_normed), cosine, rope_sine))
        keys = reduced_precision(rotate(regroup(key_normed), cosine, rope_sine))
        attended = ungroup(lax.map(attend, (query_rows, keys, regroup(value_rows))))
        attended = reduced_backward(reduced_precision(attended))
        residual = inputs + reduced_backward(matrix_product(attended, output_weight))
        ffn_in = reduced_precision(residual * rms_scale(residual) * ffn_gain)
        logits = matrix_product(ffn_in, router_weight)
        gate_weights = jax.nn.softmax(jnp.take_along_axis(logits, routes, axis=1), axis=-1)
        padded = jnp.concatenate([ffn_in, jnp.zeros((1, MODEL_WIDTH), jnp.float32)], axis=0)
        gate_flat = jnp.concatenate([gate_weights.reshape(pair_count), jnp.zeros((1,), jnp.float32)], axis=0)

        def expert_step(running, operands):
            tokens_here, pairs_here, gate_here, down_here = operands
            slot_rows = reduced_backward(padded[tokens_here])
            projected = reduced_backward(matrix_product(slot_rows, gate_here))
            hidden_low = reduced_precision(jax.nn.silu(projected[:, :FF]) * projected[:, FF:])
            expert_out = reduced_backward(reduced_precision(matrix_product(hidden_low, down_here)))
            weighted = gate_flat[pairs_here][:, None] * expert_out
            return (running + jax.ops.segment_sum(weighted, tokens_here, num_segments=every_token + 1), None)
        moe_sum = lax.scan(jax.checkpoint(expert_step), jnp.zeros((every_token + 1, MODEL_WIDTH), jnp.float32), (slot_token, slot_pair, gate_up, down_proj))[0]
        return residual + moe_sum[:every_token]
    floats = (hidden_in.astype(jnp.float32), attn_gain.astype(jnp.float32), query_weight.astype(jnp.float32), key_matrix.astype(jnp.float32), value_matrix.astype(jnp.float32), query_gain.astype(jnp.float32), key_gain.astype(jnp.float32), output_weight.astype(jnp.float32), ffn_gain.astype(jnp.float32), router_weight.astype(jnp.float32), gate_up.astype(jnp.float32), down_proj.astype(jnp.float32))
    block_out, pullback = jax.vjp(forward, *floats)
    grads = pullback(out_grad.astype(jnp.float32))
    return (block_out.astype(jnp.bfloat16), grads[0], grads[1], grads[2], grads[3], grads[4], grads[5], grads[6], grads[7], grads[8], grads[9], grads[10], grads[11])
```

```python
import math

import jax
import jax.numpy as jnp
from jax import lax
from jax.sharding import PartitionSpec as P

MODEL_WIDTH = 2048
QUERY_HEADS = 32
KEY_VALUE_HEADS = 4
HEAD_SIZE = 128
TOP = 8
PROMPT_DEV = 128


highest = lax.Precision.HIGHEST
epsilon = 1e-06
rope_base = 1000000.0
masked = -1e30
every = ("dp", "ctx", "expert")
plane = ("ctx", "expert")
bf16 = jnp.bfloat16
f32 = jnp.float32


def rms_scale(value_rows):
    return lax.rsqrt(jnp.mean(value_rows * value_rows, axis=-1, keepdims=True) + epsilon)


def norm_back(inputs, inv_rms, norm_gain, gradient):
    weighted = gradient * norm_gain
    return inv_rms * weighted - inputs * inv_rms**3 * jnp.mean(
        weighted * inputs, axis=-1, keepdims=True
    )


def angles(position, head_width):
    freq_index = jnp.arange(head_width // 2, dtype=f32)
    inverse = jnp.exp(-(2.0 * freq_index / head_width) * math.log(rope_base))
    rope_angle = position.astype(f32)[:, None] * inverse[None, :]
    rope_angle = jnp.concatenate([rope_angle, rope_angle], axis=-1)
    return (jnp.cos(rope_angle), jnp.sin(rope_angle))


def rotate(value_rows, cosine, rope_sine):
    half_width = value_rows.shape[-1] // 2
    turned = jnp.concatenate([-value_rows[..., half_width:], value_rows[..., :half_width]], axis=-1)
    return value_rows * cosine + turned * rope_sine


def rotate_back(gradient, cosine, rope_sine):
    shifted = gradient * rope_sine
    half_width = gradient.shape[-1] // 2
    return gradient * cosine + jnp.concatenate(
        [shifted[..., half_width:], -shifted[..., :half_width]], axis=-1
    )


def small_plane():
    return lax.axis_size("ctx") == 4 and lax.axis_size("expert") == 2


def swap(v, axis, bit):
    return lax.ppermute(v, axis, [(i, i ^ bit) for i in range(lax.axis_size(axis))])


def core(v):
    return swap(v, "ctx", 1)


def over_x(v):
    return swap(v, "ctx", 2)


def over_y(v):
    return swap(v, "expert", 1)


def relative():
    count = lax.axis_size(plane)
    me = lax.axis_index(plane)
    if small_plane():
        return [me ^ r for r in range(count)]
    return list(range(count))


def gather_plane(v):
    if not small_plane():
        out = lax.all_gather(v, plane, axis=0, tiled=False)
        return [out[i] for i in range(out.shape[0])]
    half = v.shape[0] // 2
    vy, vx, vc = over_y(v), over_x(v), core(v)
    top, low = over_x(vy[:half]), over_y(vx[half:])
    vyc, vxc = core(vy), core(vx)
    vxy = jnp.concatenate([top, low], axis=0)
    vxyc = jnp.concatenate([core(top), core(low)], axis=0)
    return [v, vy, vc, vyc, vx, vxy, vxc, vxyc]


def scatter_plane(blocks):
    if not small_plane():
        return lax.psum_scatter(
            jnp.concatenate(blocks, axis=0), plane, scatter_dimension=0, tiled=True
        )
    half = blocks[0].shape[0] // 2

    def add(a, b):
        return (a.astype(f32) + b.astype(f32)).astype(bf16)

    here = {}
    for r in (5, 4, 1, 0):
        here[r] = add(blocks[r], core(blocks[r ^ 2]))
    from_x = over_x(here[5][:half])
    from_y = over_y(here[5][half:])
    y_part = jnp.concatenate([add(here[1][:half], from_x), here[1][half:]], axis=0)
    x_part = jnp.concatenate([here[4][:half], add(here[4][half:], from_y)], axis=0)
    return here[0].astype(f32) + over_x(x_part).astype(f32) + over_y(y_part).astype(f32)


def exchange_plane(blocks):
    if not small_plane():
        out = lax.all_to_all(jnp.stack(blocks), plane, split_axis=0, concat_axis=0, tiled=True)
        return [out[i] for i in range(out.shape[0])]
    out = [blocks[0]]
    for r in range(1, 8):
        pairs = [(i, i ^ r) for i in range(8)]
        out.append(lax.ppermute(blocks[r], plane, pairs))
    return out


def piece_starts(total):
    if not small_plane():
        return [(0, total)]
    half, quarter = total // 2, total // 8
    mine = lax.axis_index("expert") * half
    other = half - mine
    member = lax.axis_index("ctx")
    return [(mine, half)] + [(other + (member ^ j) * quarter, quarter) for j in range(4)]


def fetch(weight):
    if not small_plane():
        return lax.all_gather(weight, "expert", axis=0, tiled=True)
    quarter = weight.shape[0] // 4
    member = lax.axis_index("ctx")
    mine = lax.dynamic_slice_in_dim(weight, member * quarter, quarter, axis=0)
    first = over_y(mine)
    second = core(first)
    third = over_x(first)
    fourth = core(third)
    return jnp.concatenate([weight, first, second, third, fourth], axis=0)


def reorder(v, axis):
    total = v.shape[axis]
    return jnp.concatenate(
        [
            lax.dynamic_slice_in_dim(v, start, size, axis=axis)
            for start, size in piece_starts(total)
        ],
        axis=axis,
    )


def restore(v, axis):
    total = v.shape[axis]
    out = jnp.zeros_like(v)
    at = 0
    for start, size in piece_starts(total):
        piece = lax.slice_in_dim(v, at, at + size, axis=axis)
        out = lax.dynamic_update_slice_in_dim(out, piece, start, axis=axis)
        at += size
    return out


def ctx_blocks(v):
    count = lax.axis_size("ctx")
    member = lax.axis_index("ctx")
    if count != 4:
        out = lax.all_gather(v, "ctx", axis=0, tiled=False)
        return [out[i] for i in range(count)], [jnp.int32(i) for i in range(count)]
    vc, vx = core(v), over_x(v)
    return [v, vc, vx, core(vx)], [member ^ j for j in range(4)]


def ctx_sum(blocks):
    count = lax.axis_size("ctx")
    if count != 4:
        return lax.psum_scatter(
            jnp.concatenate(blocks, axis=0), "ctx", scatter_dimension=0, tiled=True
        ).astype(f32)
    near = blocks[0].astype(f32) + core(blocks[1]).astype(f32)
    far = (blocks[2].astype(f32) + core(blocks[3]).astype(f32)).astype(bf16)
    return near + over_x(far).astype(f32)


def body(
    hidden_in,
    attn_gain,
    query_weight,
    key_matrix,
    value_matrix,
    query_gain,
    key_gain,
    output_weight,
    ffn_gain,
    router_weight,
    gate_up,
    down_proj,
    routes,
    out_grad,
):
    ctx_count = lax.axis_size("ctx")
    spread_count = lax.axis_size(plane)
    dp_count = lax.axis_size("dp")
    device_count = dp_count * spread_count
    local_experts = gate_up.shape[0]
    count_of_rows = hidden_in.shape[0]
    prompt_all = PROMPT_DEV * ctx_count
    heads_per_group = QUERY_HEADS // KEY_VALUE_HEADS
    score_scale = HEAD_SIZE ** (-0.5)
    hidden_ff = gate_up.shape[2] // 2
    full_query, full_key, full_value, full_output = (
        fetch(query_weight),
        fetch(key_matrix),
        fetch(value_matrix),
        fetch(output_weight),
    )
    order = relative()
    g_rows = jnp.concatenate(gather_plane(out_grad), axis=0)
    route_rows = jnp.concatenate(gather_plane(routes), axis=0)

    inputs = hidden_in.astype(f32)
    scale_in = rms_scale(inputs)
    normalized_input = (inputs * scale_in * attn_gain).astype(bf16)
    normed_reordered = reorder(normalized_input, 1)
    query_pre = jnp.dot(normed_reordered, full_query, preferred_element_type=f32).reshape(
        count_of_rows, QUERY_HEADS, HEAD_SIZE
    )
    key_before_norm = jnp.dot(normed_reordered, full_key, preferred_element_type=f32).reshape(
        count_of_rows, KEY_VALUE_HEADS, HEAD_SIZE
    )
    value_low = (
        jnp.dot(normed_reordered, full_value, preferred_element_type=f32)
        .astype(bf16)
        .reshape(count_of_rows, KEY_VALUE_HEADS, HEAD_SIZE)
    )
    query_inv = rms_scale(query_pre)
    key_inv = rms_scale(key_before_norm)
    member = lax.axis_index("ctx")
    offsets = jnp.arange(count_of_rows, dtype=jnp.int32)
    position = jnp.where(
        offsets < PROMPT_DEV, member * PROMPT_DEV + offsets, prompt_all + offsets - PROMPT_DEV
    )
    cosine, rope_sine = angles(position, HEAD_SIZE)
    cosine = cosine[:, None, :]
    rope_sine = rope_sine[:, None, :]
    query_reduced = rotate(query_pre * query_inv * query_gain, cosine, rope_sine).astype(bf16)
    key_low = rotate(key_before_norm * key_inv * key_gain, cosine, rope_sine).astype(bf16)
    pair_blocks, members = ctx_blocks(
        jnp.stack([key_low[:PROMPT_DEV], value_low[:PROMPT_DEV]])
    )
    keys_all = jnp.concatenate([b[0] for b in pair_blocks] + [key_low[PROMPT_DEV:]], axis=0)
    values_all = jnp.concatenate([b[1] for b in pair_blocks] + [value_low[PROMPT_DEV:]], axis=0)
    prompt_offsets = jnp.arange(PROMPT_DEV, dtype=jnp.int32)
    key_position = jnp.concatenate(
        [m * PROMPT_DEV + prompt_offsets for m in members]
        + [prompt_all + jnp.arange(count_of_rows - PROMPT_DEV, dtype=jnp.int32)]
    )
    visible = key_position[None, :] <= position[:, None]
    grouped_queries = query_reduced.reshape(
        count_of_rows, KEY_VALUE_HEADS, heads_per_group, HEAD_SIZE
    )

    def scores_of():
        raw_scores = (
            jnp.einsum("rkgd,skd->kgrs", grouped_queries, keys_all, preferred_element_type=f32)
            * score_scale
        )
        return jnp.where(visible, raw_scores, masked)

    scores = scores_of()
    row_max = jnp.max(scores, axis=-1, keepdims=True)
    weights = jnp.exp(scores - row_max)
    row_total = jnp.sum(weights, axis=-1, keepdims=True)
    log_total = row_max + jnp.log(row_total)
    attention = (weights / row_total).astype(bf16)
    attended = (
        jnp.einsum("kgrs,skd->rkgd", attention, values_all, preferred_element_type=f32)
        .reshape(count_of_rows, QUERY_HEADS * HEAD_SIZE)
        .astype(bf16)
    )
    residual = inputs + jnp.dot(reorder(attended, 1), full_output, preferred_element_type=f32)
    scale_ffn = rms_scale(residual)
    ffn_in = (residual * scale_ffn * ffn_gain).astype(bf16)

    rows = jnp.concatenate(gather_plane(ffn_in), axis=0)
    expert_count = local_experts * spread_count
    expert_ids = jnp.arange(expert_count, dtype=jnp.int32)

    def gates_of(some_rows, some_routes):
        logits = jnp.dot(some_rows, router_weight, preferred_element_type=f32)
        chosen = jnp.any(some_routes[:, :, None] == expert_ids[None, None, :], axis=1)
        logits = jnp.where(chosen, logits, masked)
        raised = jnp.where(
            chosen, jnp.exp(logits - jnp.max(logits, axis=-1, keepdims=True)), 0.0
        )
        return raised / jnp.sum(raised, axis=-1, keepdims=True)

    gates_all = gates_of(rows, route_rows)
    first_expert = lax.axis_index(plane) * local_experts
    gates_mine = lax.dynamic_slice_in_dim(gates_all, first_expert, local_experts, axis=1)
    moe_part = 0.0
    row_part = 0.0
    gate_grads = []
    gate_up_local = []
    down_local = []
    for which in range(local_experts):
        gate = gates_mine[:, which : which + 1]
        projected = jnp.dot(rows, gate_up[which], preferred_element_type=f32)
        back = jnp.dot(g_rows, down_proj[which].T, preferred_element_type=f32)
        gate_part = projected[:, :hidden_ff]
        up_part = projected[:, hidden_ff:]
        sigmoid_gate = jax.nn.sigmoid(gate_part)
        hidden = gate_part * sigmoid_gate * up_part
        gate_grads.append(jnp.sum(hidden * back, axis=-1))
        hidden_low = (gate * hidden).astype(bf16)
        hidden_back = gate * back
        gate_back = hidden_back * up_part * sigmoid_gate * (1.0 + gate_part * (1.0 - sigmoid_gate))
        up_back = hidden_back * gate_part * sigmoid_gate
        projected_grad = jnp.concatenate([gate_back, up_back], axis=-1).astype(bf16)
        moe_part = moe_part + jnp.dot(hidden_low, down_proj[which], preferred_element_type=f32)
        row_part = row_part + jnp.dot(
            projected_grad, gate_up[which].T, preferred_element_type=f32
        )
        gate_up_local.append(jnp.dot(rows.T, projected_grad, preferred_element_type=f32))
        down_local.append(jnp.dot(hidden_low.T, g_rows, preferred_element_type=f32))
    gate_up_grad, down_grad = (
        lax.psum_scatter(
            jnp.stack(gate_up_local).astype(bf16), "dp", scatter_dimension=1, tiled=True
        ).astype(f32),
        lax.psum_scatter(
            jnp.stack(down_local).astype(bf16), "dp", scatter_dimension=1, tiled=True
        ).astype(f32),
    )

    def blocks_of(v):
        return [
            v[i * count_of_rows : (i + 1) * count_of_rows] for i in range(spread_count)
        ]

    moe_sum = scatter_plane(blocks_of(moe_part.astype(bf16)))
    block_out = (residual + moe_sum).astype(bf16)
    back_sum = scatter_plane(blocks_of(row_part.astype(bf16)))
    gate_grad_blocks = exchange_plane(blocks_of(jnp.stack(gate_grads, axis=1)))
    gate_grad = jnp.zeros((count_of_rows, expert_count), f32)
    for r in range(spread_count):
        gate_grad = lax.dynamic_update_slice_in_dim(
            gate_grad, gate_grad_blocks[r], order[r] * local_experts, axis=1
        )
    gates = gates_of(ffn_in, routes)
    logit_grad = gates * (gate_grad - jnp.sum(gates * gate_grad, axis=-1, keepdims=True))

    grad_out = out_grad.astype(f32)
    router_local = jnp.dot(ffn_in.T, logit_grad, preferred_element_type=f32)
    ffn_in_grad = back_sum + jnp.dot(
        logit_grad, router_weight.astype(f32).T, precision=highest
    )
    residual_grad = grad_out + norm_back(residual, scale_ffn, ffn_gain, ffn_in_grad)
    ffn_gain_local = jnp.sum(ffn_in_grad * residual * scale_ffn, axis=0)
    branch_low = residual_grad.astype(bf16)
    branch_rows = jnp.concatenate(gather_plane(branch_low), axis=0)
    attended_grad = restore(
        jnp.dot(branch_low, full_output.T, preferred_element_type=f32).astype(bf16), 1
    ).reshape(count_of_rows, KEY_VALUE_HEADS, heads_per_group, HEAD_SIZE)
    attention_again = jnp.exp(scores_of() - log_total)
    prob_grad = jnp.einsum(
        "rkgd,skd->kgrs", attended_grad, values_all, preferred_element_type=f32
    )
    row_delta = jnp.sum(attention_again * prob_grad, axis=-1, keepdims=True)
    score_grad = (attention_again * (prob_grad - row_delta)).astype(bf16)
    query_grad = (
        jnp.einsum("kgrs,skd->rkgd", score_grad, keys_all, preferred_element_type=f32)
        * score_scale
    ).reshape(count_of_rows, QUERY_HEADS, HEAD_SIZE)
    key_grad_all = (
        jnp.einsum("kgrs,rkgd->skd", score_grad, grouped_queries, preferred_element_type=f32)
        * score_scale
    )
    value_grad_all = jnp.einsum(
        "kgrs,rkgd->skd",
        attention_again.astype(bf16),
        attended_grad,
        preferred_element_type=f32,
    )
    pair_grads = jnp.stack([key_grad_all[:prompt_all], value_grad_all[:prompt_all]]).astype(bf16)
    prompt_grads = ctx_sum(
        [pair_grads[:, i * PROMPT_DEV : (i + 1) * PROMPT_DEV] for i in range(ctx_count)]
        if ctx_count == 4
        else [pair_grads]
    )
    key_grad = jnp.concatenate([prompt_grads[0], key_grad_all[prompt_all:]], axis=0)
    value_gradient = jnp.concatenate([prompt_grads[1], value_grad_all[prompt_all:]], axis=0)
    query_rot_grad = rotate_back(query_grad, cosine, rope_sine)
    key_rot_grad = rotate_back(key_grad, cosine, rope_sine)
    query_gain_local = jnp.sum(query_rot_grad * query_pre * query_inv, axis=(0, 1))
    key_gain_local = jnp.sum(key_rot_grad * key_before_norm * key_inv, axis=(0, 1))
    query_pre_grad = (
        norm_back(query_pre, query_inv, query_gain, query_rot_grad)
        .astype(bf16)
        .reshape(count_of_rows, QUERY_HEADS * HEAD_SIZE)
    )
    key_pre_grad = (
        norm_back(key_before_norm, key_inv, key_gain, key_rot_grad)
        .astype(bf16)
        .reshape(count_of_rows, KEY_VALUE_HEADS * HEAD_SIZE)
    )
    value_before_norm_gradient = value_gradient.astype(bf16).reshape(
        count_of_rows, KEY_VALUE_HEADS * HEAD_SIZE
    )
    normed_grad = jnp.dot(query_pre_grad, full_query.T, preferred_element_type=f32)
    normed_grad = normed_grad + jnp.dot(key_pre_grad, full_key.T, preferred_element_type=f32)
    normed_grad = normed_grad + jnp.dot(
        value_before_norm_gradient, full_value.T, preferred_element_type=f32
    )
    normed_grad = restore(normed_grad, 1)
    attn_gain_local = jnp.sum(normed_grad * inputs * scale_in, axis=0)
    hidden_grad = residual_grad + norm_back(inputs, scale_in, attn_gain, normed_grad)

    pre_rows = jnp.concatenate(
        gather_plane(
            jnp.concatenate([query_pre_grad, key_pre_grad, value_before_norm_gradient], axis=1)
        ),
        axis=0,
    )

    def owned(v):
        width = v.shape[1] // device_count
        split = v.reshape(count_of_rows, dp_count, spread_count, width)
        parts = [
            lax.dynamic_index_in_dim(split, o, axis=2, keepdims=False).reshape(
                count_of_rows, dp_count * width
            )
            for o in order
        ]
        return jnp.concatenate(exchange_plane(parts), axis=0)

    normed_owned = owned(normalized_input)
    attended_owned = owned(attended)
    pre_local = jnp.dot(normed_owned.T, pre_rows, preferred_element_type=f32)
    output_local = jnp.dot(attended_owned.T, branch_rows, preferred_element_type=f32)
    pre_sum = lax.psum_scatter(pre_local.astype(bf16), "dp", scatter_dimension=0, tiled=True).astype(
        f32
    )
    output_sum = lax.psum_scatter(
        output_local.astype(bf16), "dp", scatter_dimension=0, tiled=True
    ).astype(f32)
    wide = QUERY_HEADS * HEAD_SIZE
    narrow = KEY_VALUE_HEADS * HEAD_SIZE

    small = jnp.concatenate(
        [
            v.reshape(device_count, -1)
            for v in (
                attn_gain_local,
                ffn_gain_local,
                query_gain_local,
                key_gain_local,
                router_local,
            )
        ],
        axis=1,
    )
    small = lax.all_to_all(small[:, None], every, split_axis=0, concat_axis=0, tiled=True)
    small = jnp.sum(small[:, 0], axis=0)
    share = MODEL_WIDTH // device_count
    head_share = HEAD_SIZE // device_count
    cuts = [share, share, head_share, head_share, share * expert_count]
    ends = [sum(cuts[: i + 1]) for i in range(5)]
    a_grad, f_grad, q_grad, k_grad, r_grad = [
        small[end - cut : end] for end, cut in zip(ends, cuts)
    ]
    return (
        block_out,
        hidden_grad,
        a_grad,
        pre_sum[:, :wide],
        pre_sum[:, wide : wide + narrow],
        pre_sum[:, wide + narrow :],
        q_grad,
        k_grad,
        output_sum,
        f_grad,
        r_grad.reshape(share, expert_count),
        gate_up_grad,
        down_grad,
    )


def solution(mesh):
    placed = (
        P(("dp", "ctx", "expert"), None),
        P(),
        P("expert", None),
        P("expert", None),
        P("expert", None),
        P(),
        P(),
        P("expert", None),
        P(),
        P(),
        P(("ctx", "expert"), None, None),
        P(("ctx", "expert"), None, None),
        P(("dp", "ctx", "expert"), None),
        P(("dp", "ctx", "expert"), None),
    )
    return jax.shard_map(
        body,
        mesh=mesh,
        in_specs=placed,
        out_specs=(
            P(("dp", "ctx", "expert"), None),
            P(("dp", "ctx", "expert"), None),
            P(("dp", "ctx", "expert")),
            P(("dp", "ctx", "expert"), None),
            P(("dp", "ctx", "expert"), None),
            P(("dp", "ctx", "expert"), None),
            P(("dp", "ctx", "expert")),
            P(("dp", "ctx", "expert")),
            P(("dp", "ctx", "expert"), None),
            P(("dp", "ctx", "expert")),
            P(("dp", "ctx", "expert"), None),
            P(("ctx", "expert"), "dp", None),
            P(("ctx", "expert"), "dp", None),
        ),
        check_vma=False,
    )
```

```python
import math

import jax
import jax.numpy as jnp
from jax import lax
from jax.experimental import pallas as pl
from jax.experimental.pallas import tpu as pltpu
from jax.sharding import PartitionSpec as P

MODEL_WIDTH = 2048
QUERY_HEADS = 32
KEY_VALUE_HEADS = 4
HEAD_SIZE = 128
TOP = 8
PROMPT_DEV = 128


highest = lax.Precision.HIGHEST
epsilon = 1e-06
rope_base = 1000000.0
masked = -1e30
every = ("dp", "ctx", "expert")
plane = ("ctx", "expert")
bf16 = jnp.bfloat16
f32 = jnp.float32


def rms_scale(value_rows):
    return lax.rsqrt(jnp.mean(value_rows * value_rows, axis=-1, keepdims=True) + epsilon)


def norm_back(inputs, inv_rms, norm_gain, gradient):
    weighted = gradient * norm_gain
    return inv_rms * weighted - inputs * inv_rms**3 * jnp.mean(
        weighted * inputs, axis=-1, keepdims=True
    )


def angles(position, head_width):
    freq_index = jnp.arange(head_width // 2, dtype=f32)
    inverse = jnp.exp(-(2.0 * freq_index / head_width) * math.log(rope_base))
    rope_angle = position.astype(f32)[:, None] * inverse[None, :]
    rope_angle = jnp.concatenate([rope_angle, rope_angle], axis=-1)
    return (jnp.cos(rope_angle), jnp.sin(rope_angle))


def rotate(value_rows, cosine, rope_sine):
    half_width = value_rows.shape[-1] // 2
    turned = jnp.concatenate([-value_rows[..., half_width:], value_rows[..., :half_width]], axis=-1)
    return value_rows * cosine + turned * rope_sine


def rotate_back(gradient, cosine, rope_sine):
    shifted = gradient * rope_sine
    half_width = gradient.shape[-1] // 2
    return gradient * cosine + jnp.concatenate(
        [shifted[..., half_width:], -shifted[..., :half_width]], axis=-1
    )


def small_plane():
    return lax.axis_size("ctx") == 4 and lax.axis_size("expert") == 2


def swap(v, axis, bit):
    return lax.ppermute(v, axis, [(i, i ^ bit) for i in range(lax.axis_size(axis))])


def core(v):
    return swap(v, "ctx", 1)


def over_x(v):
    return swap(v, "ctx", 2)


def over_y(v):
    return swap(v, "expert", 1)


def relative():
    count = lax.axis_size(plane)
    me = lax.axis_index(plane)
    if small_plane():
        return [me ^ r for r in range(count)]
    return list(range(count))


def gather_plane(v):
    if not small_plane():
        out = lax.all_gather(v, plane, axis=0, tiled=False)
        return [out[i] for i in range(out.shape[0])]
    half = v.shape[0] // 2
    vy, vx, vc = over_y(v), over_x(v), core(v)
    top, low = over_x(vy[:half]), over_y(vx[half:])
    vyc, vxc = core(vy), core(vx)
    vxy = jnp.concatenate([top, low], axis=0)
    vxyc = jnp.concatenate([core(top), core(low)], axis=0)
    return [v, vy, vc, vyc, vx, vxy, vxc, vxyc]


def scatter_plane(blocks):
    if not small_plane():
        return lax.psum_scatter(
            jnp.concatenate(blocks, axis=0), plane, scatter_dimension=0, tiled=True
        )
    half = blocks[0].shape[0] // 2

    def add(a, b):
        return (a.astype(f32) + b.astype(f32)).astype(bf16)

    here = {}
    for r in (5, 4, 1, 0):
        here[r] = add(blocks[r], core(blocks[r ^ 2]))
    from_x = over_x(here[5][:half])
    from_y = over_y(here[5][half:])
    y_part = jnp.concatenate([add(here[1][:half], from_x), here[1][half:]], axis=0)
    x_part = jnp.concatenate([here[4][:half], add(here[4][half:], from_y)], axis=0)
    return here[0].astype(f32) + over_x(x_part).astype(f32) + over_y(y_part).astype(f32)


def exchange_plane(blocks):
    if not small_plane():
        out = lax.all_to_all(jnp.stack(blocks), plane, split_axis=0, concat_axis=0, tiled=True)
        return [out[i] for i in range(out.shape[0])]
    out = [blocks[0]]
    for r in range(1, 8):
        pairs = [(i, i ^ r) for i in range(8)]
        out.append(lax.ppermute(blocks[r], plane, pairs))
    return out


def over_z(v):
    return swap(v, "dp", 1)


def after(v, *earlier):
    return lax.optimization_barrier((v, *earlier))[0]


class Places:
    def __init__(self):
        self.dp = lax.axis_index("dp")
        ctx = lax.axis_index("ctx")
        self.ctx = ctx
        self.z = lax.rem(self.dp, 2)
        self.x = lax.div(ctx, 2)
        self.c = lax.rem(ctx, 2)
        self.y = lax.axis_index("expert")
        self.to_x = {"ctx": (1 - self.x) * 2 + self.c}
        self.to_c = {"ctx": self.x * 2 + 1 - self.c}
        self.to_y = {"expert": 1 - self.y}
        self.to_z = {"dp": self.dp + 1 - 2 * self.z}


def plane_slot(x, c, y):
    return x * 4 + c * 2 + y


def greet(targets):
    barrier = pltpu.get_barrier_semaphore()
    for target in targets:
        pl.semaphore_signal(barrier, inc=1, device_id=target, device_id_type=pl.DeviceIdType.MESH)
    pl.semaphore_wait(barrier, len(targets))


class Sender:
    def __init__(self, send_sem, recv_sem):
        self.send_sem = send_sem
        self.recv_sem = recv_sem
        self.copies = []

    def __call__(self, source, target_ref, device):
        i = len(self.copies)
        copy = pltpu.make_async_remote_copy(
            src_ref=source,
            dst_ref=target_ref,
            send_sem=self.send_sem.at[i],
            recv_sem=self.recv_sem.at[i],
            device_id=device,
            device_id_type=pl.DeviceIdType.MESH,
        )
        copy.start()
        self.copies.append(copy)
        return copy

    def finish(self):
        for copy in self.copies:
            copy.wait_send()


def run_rounds(work, between):
    turns = max(i + len(todo) for i, todo in enumerate(work))
    for turn in range(turns):
        for i, todo in enumerate(work):
            if 0 <= turn - i < len(todo):
                todo[turn - i]()
        if turn in between:
            between[turn]()


def half_fetch(here, send, sources, other, columns, rows):
    def at(piece, part=None):
        first, size = piece * rows, rows
        if part is not None:
            size = rows // 2
            first = first + part * size
        return other.at[pl.ds(pl.multiple_of(first, size), size), columns]

    def piece(z, x, c):
        return z * 4 + x * 2 + c

    z, x, c = here.z, here.x, here.c
    got = {}

    def first():
        mine = piece(z, x, c)
        got["y"] = [
            send(
                source.at[pl.ds(pl.multiple_of(mine * rows, rows), rows), source_columns],
                other.at[pl.ds(pl.multiple_of(mine * rows, rows), rows), target_columns],
                here.to_y,
            )
            for source, source_columns, target_columns in sources
        ]

    def second():
        for copy in got["y"]:
            copy.wait_recv()
        mine = at(piece(z, x, c))
        got["x"] = send(mine, mine, here.to_x)
        got["z"] = send(mine, mine, here.to_z)
        got["c"] = send(mine, mine, here.to_c)

    def third():
        got["x"].wait_recv()
        from_x = piece(z, 1 - x, c)
        got["low"] = send(at(from_x, 1), at(from_x, 1), here.to_z)
        got["xc"] = send(at(from_x), at(from_x), here.to_c)
        got["z"].wait_recv()
        from_z = piece(1 - z, x, c)
        got["top"] = send(at(from_z, 0), at(from_z, 0), here.to_x)
        got["zc"] = send(at(from_z), at(from_z), here.to_c)

    def fourth():
        far = piece(1 - z, 1 - x, c)
        got["low"].wait_recv()
        got["lowc"] = send(at(far, 1), at(far, 1), here.to_c)
        got["top"].wait_recv()
        got["topc"] = send(at(far, 0), at(far, 0), here.to_c)

    def fifth():
        for name in ("c", "xc", "zc", "lowc", "topc"):
            got[name].wait_recv()

    return [first, second, third, fourth, fifth]


def block_gather(here, send, mine, local_sem, blocks):
    half = blocks.shape[1] // 2
    x, c, y = here.x, here.c, here.y
    got = {}

    def at(slot, part=None):
        if part is None:
            return blocks.at[slot]
        return blocks.at[slot, pl.ds(part * half, half)]

    def first():
        slot = plane_slot(x, c, y)
        got["own"] = pltpu.make_async_copy(mine, at(slot), local_sem)
        got["own"].start()
        got["y"] = send(mine, at(slot), here.to_y)
        got["x"] = send(mine, at(slot), here.to_x)
        got["c"] = send(mine, at(slot), here.to_c)

    def second():
        got["y"].wait_recv()
        from_y = plane_slot(x, c, 1 - y)
        got["top"] = send(at(from_y, 0), at(from_y, 0), here.to_x)
        got["yc"] = send(at(from_y), at(from_y), here.to_c)
        got["x"].wait_recv()
        from_x = plane_slot(1 - x, c, y)
        got["low"] = send(at(from_x, 1), at(from_x, 1), here.to_y)
        got["xc"] = send(at(from_x), at(from_x), here.to_c)

    def third():
        far = plane_slot(1 - x, c, 1 - y)
        got["top"].wait_recv()
        got["topc"] = send(at(far, 0), at(far, 0), here.to_c)
        got["low"].wait_recv()
        got["lowc"] = send(at(far, 1), at(far, 1), here.to_c)

    def fourth():
        for name in ("c", "yc", "xc", "topc", "lowc"):
            got[name].wait_recv()
        got["own"].wait()

    return [first, second, third, fourth]


def turn_half(v):
    return pltpu.roll(v, v.shape[-1] // 2, axis=1)


def head_norm(v):
    return lax.rsqrt(jnp.mean(v * v, axis=-1, keepdims=True) + epsilon)


def fetch_kernel(
    hidden_ref,
    attn_gain_ref,
    key_gain_ref,
    cosine_ref,
    sine_ref,
    key_ref,
    value_ref,
    query_ref,
    output_ref,
    grad_ref,
    kv_out,
    q_out,
    o_other,
    g_blocks,
    normed_ref,
    query_pre_ref,
    kv_pre_ref,
    kv_low_ref,
    kv_blocks,
    kv_own,
    kv_other,
    q_own,
    q_other,
    send_sem,
    recv_sem,
    local_sem,
):
    here = Places()
    greet([here.to_y, here.to_z, here.to_c, here.to_x])
    send = Sender(send_sem, recv_sem)
    width = hidden_ref.shape[1]
    half = width // 2
    narrow = key_ref.shape[1]
    wide = query_ref.shape[1]
    tile = 512
    loads = [
        pltpu.make_async_copy(key_ref, kv_own.at[:, pl.ds(0, narrow)], local_sem.at[0]),
        pltpu.make_async_copy(value_ref, kv_own.at[:, pl.ds(narrow, narrow)], local_sem.at[1]),
        pltpu.make_async_copy(query_ref, q_own, local_sem.at[2]),
    ]
    stores = [
        pltpu.make_async_copy(kv_other, kv_out, local_sem.at[3]),
        pltpu.make_async_copy(q_other, q_out, local_sem.at[4]),
    ]
    mine = pl.ds(pl.multiple_of(here.y * half, half), half)
    others = pl.ds(pl.multiple_of(half - here.y * half, half), half)

    def project(weight, out, rows, first, count, add):
        @pl.loop(first, first + count)
        def _(i):
            cols = pl.ds(pl.multiple_of(i * tile, tile), tile)
            part = jnp.dot(normed_ref[:, rows], weight[:, cols], preferred_element_type=f32)
            out[:, cols] = out[:, cols] + part if add else part

    def start():
        for load in loads:
            load.start()
        inputs = hidden_ref[...].astype(f32)
        normed_ref[...] = (inputs * head_norm(inputs) * attn_gain_ref[...]).astype(bf16)

    def own_part():
        for load in loads:
            load.wait()
        project(kv_own, kv_pre_ref, mine, 0, 2 * narrow // tile, False)
        project(q_own, query_pre_ref, mine, 0, wide // tile, False)

    exchange = {}

    def keys_part():
        project(kv_other, kv_pre_ref, others, 0, 2 * narrow // tile, True)
        stores[0].start()
        for h in range(narrow // HEAD_SIZE):
            cols = slice(h * HEAD_SIZE, (h + 1) * HEAD_SIZE)
            v = kv_pre_ref[:, cols]
            v = v * head_norm(v) * key_gain_ref[...]
            kv_low_ref[:, cols] = (v * cosine_ref[...] + turn_half(v) * sine_ref[...]).astype(bf16)
        kv_low_ref[:, narrow:] = kv_pre_ref[:, narrow:].astype(bf16)
        source = kv_low_ref.at[pl.ds(0, PROMPT_DEV)]
        slot = kv_blocks.at[here.ctx]
        exchange["own"] = pltpu.make_async_copy(source, slot, local_sem.at[5])
        exchange["own"].start()
        exchange["c"] = send(source, slot, here.to_c)
        exchange["x"] = send(source, slot, here.to_x)

    def keys_forward():
        exchange["x"].wait_recv()
        slot = kv_blocks.at[(1 - here.x) * 2 + here.c]
        exchange["xc"] = send(slot, slot, here.to_c)
        project(q_other, query_pre_ref, others, 0, wide // tile // 2, True)

    def queries_rest():
        stores[1].start()
        project(q_other, query_pre_ref, others, wide // tile // 2, wide // tile // 2, True)

    low, high = pl.ds(0, wide // 2), pl.ds(wide // 2, wide // 2)
    o_low, o_high = pl.ds(0, width // 2), pl.ds(width // 2, width // 2)
    rows, o_rows = half // 8, output_ref.shape[0] // 8
    work = [
        half_fetch(
            here,
            send,
            [
                (key_ref, pl.ds(0, narrow), pl.ds(0, narrow)),
                (value_ref, pl.ds(0, narrow), pl.ds(narrow, narrow)),
            ],
            kv_other,
            pl.ds(0, 2 * narrow),
            rows,
        ),
        half_fetch(here, send, [(query_ref, low, low)], q_other, low, rows),
        half_fetch(here, send, [(query_ref, high, high)], q_other, high, rows),
        half_fetch(here, send, [(output_ref, o_low, o_low)], o_other, o_low, o_rows),
        half_fetch(here, send, [(output_ref, o_high, o_high)], o_other, o_high, o_rows),
        block_gather(here, send, grad_ref, local_sem.at[6], g_blocks),
    ]
    run_rounds(
        work, {0: start, 2: own_part, 4: keys_part, 5: keys_forward, 6: queries_rest}
    )
    for name in ("c", "xc"):
        exchange[name].wait_recv()
    exchange["own"].wait()
    for store in stores:
        store.wait()
    send.finish()


def fetch_and_project(
    hidden_in, attn_gain, key_gain, cosine, sine, key_matrix, value_matrix, query_weight,
    output_weight, out_grad,
):
    rows, width = hidden_in.shape
    half, wide = query_weight.shape
    narrow = key_matrix.shape[1]
    spread = lax.axis_size(plane)
    vmem = pl.BlockSpec(memory_space=pltpu.VMEM)
    anywhere = pl.BlockSpec(memory_space=pl.ANY)
    copies = 5 * 10 + 1 + 9 + 3
    return pl.pallas_call(
        fetch_kernel,
        out_shape=[
            jax.ShapeDtypeStruct((half, 2 * narrow), bf16),
            jax.ShapeDtypeStruct((half, wide), bf16),
            jax.ShapeDtypeStruct(output_weight.shape, bf16),
            jax.ShapeDtypeStruct((spread, rows, width), bf16),
            jax.ShapeDtypeStruct((rows, width), bf16),
            jax.ShapeDtypeStruct((rows, wide), f32),
            jax.ShapeDtypeStruct((rows, 2 * narrow), f32),
            jax.ShapeDtypeStruct((rows, 2 * narrow), bf16),
            jax.ShapeDtypeStruct((lax.axis_size("ctx"), PROMPT_DEV, 2 * narrow), bf16),
        ],
        in_specs=[vmem] * 5 + [anywhere] * 5,
        out_specs=[anywhere] * 4 + [vmem] * 4 + [anywhere],
        scratch_shapes=[
            pltpu.VMEM((half, 2 * narrow), bf16),
            pltpu.VMEM((half, 2 * narrow), bf16),
            pltpu.VMEM((half, wide), bf16),
            pltpu.VMEM((half, wide), bf16),
            pltpu.SemaphoreType.DMA((copies,)),
            pltpu.SemaphoreType.DMA((copies,)),
            pltpu.SemaphoreType.DMA((7,)),
        ],
        compiler_params=pltpu.CompilerParams(
            collective_id=1, has_side_effects=True, vmem_limit_bytes=48 * 2**20
        ),
    )(
        hidden_in, attn_gain.reshape(1, width), key_gain.reshape(1, HEAD_SIZE), cosine, sine,
        key_matrix, value_matrix, query_weight, output_weight, out_grad,
    )


def gather_kernel(mine_ref, blocks, send_sem, recv_sem, local_sem):
    here = Places()
    greet([here.to_y, here.to_c, here.to_x])
    send = Sender(send_sem, recv_sem)
    run_rounds([block_gather(here, send, mine_ref, local_sem.at[0], blocks)], {})
    send.finish()


def gather_blocks(v, collective_id):
    anywhere = pl.BlockSpec(memory_space=pl.ANY)
    return pl.pallas_call(
        gather_kernel,
        out_shape=jax.ShapeDtypeStruct((lax.axis_size(plane),) + v.shape, v.dtype),
        in_specs=[anywhere],
        out_specs=anywhere,
        scratch_shapes=[
            pltpu.SemaphoreType.DMA((9,)),
            pltpu.SemaphoreType.DMA((9,)),
            pltpu.SemaphoreType.DMA((1,)),
        ],
        compiler_params=pltpu.CompilerParams(collective_id=collective_id, has_side_effects=True),
    )(v)


def gather_small(v):
    if not small_plane():
        return lax.all_gather(v, plane, axis=0, tiled=True)
    v = jnp.concatenate([v, over_y(v)], axis=0)
    v = jnp.concatenate([v, core(v)], axis=0)
    v = jnp.concatenate([v, over_x(v)], axis=0)
    blocks = v.reshape(lax.axis_size(plane), -1, v.shape[1])
    blocks = jnp.take(blocks, jnp.arange(blocks.shape[0]) ^ lax.axis_index(plane), axis=0)
    return blocks.reshape(v.shape)


def halves(v):
    half = v.shape[1] // 2
    mine = lax.axis_index("expert") * half
    return (
        lax.dynamic_slice_in_dim(v, mine, half, axis=1),
        lax.dynamic_slice_in_dim(v, half - mine, half, axis=1),
    )


def join_halves(mine, other):
    lower = lax.axis_index("expert") == 0
    return jnp.concatenate(
        [jnp.where(lower, mine, other), jnp.where(lower, other, mine)], axis=1
    )


def dot(a, b):
    return jnp.dot(a, b, preferred_element_type=f32)


def ctx_sum(v):
    if not small_plane():
        return lax.psum_scatter(v, "ctx", scatter_dimension=1, tiled=True).astype(f32)
    member = lax.axis_index("ctx")

    def block(j):
        return lax.dynamic_slice_in_dim(v, (member ^ j) * PROMPT_DEV, PROMPT_DEV, axis=1)

    near = block(0).astype(f32) + core(block(1)).astype(f32)
    far = (block(2).astype(f32) + core(block(3)).astype(f32)).astype(bf16)
    return near + over_x(far).astype(f32)


def body(
    hidden_in,
    attn_gain,
    query_weight,
    key_matrix,
    value_matrix,
    query_gain,
    key_gain,
    output_weight,
    ffn_gain,
    router_weight,
    gate_up,
    down_proj,
    routes,
    out_grad,
):
    ctx_count = lax.axis_size("ctx")
    spread_count = lax.axis_size(plane)
    dp_count = lax.axis_size("dp")
    device_count = dp_count * spread_count
    local_experts = gate_up.shape[0]
    count_of_rows = hidden_in.shape[0]
    prompt_all = PROMPT_DEV * ctx_count
    heads_per_group = QUERY_HEADS // KEY_VALUE_HEADS
    score_scale = HEAD_SIZE ** (-0.5)
    hidden_ff = gate_up.shape[2] // 2
    order = relative()
    member = lax.axis_index("ctx")
    offsets = jnp.arange(count_of_rows, dtype=jnp.int32)
    position = jnp.where(
        offsets < PROMPT_DEV, member * PROMPT_DEV + offsets, prompt_all + offsets - PROMPT_DEV
    )
    cosine, rope_sine = angles(position, HEAD_SIZE)
    narrow = KEY_VALUE_HEADS * HEAD_SIZE
    wide = QUERY_HEADS * HEAD_SIZE
    route_rows = gather_small(routes)
    inputs = hidden_in.astype(f32)
    scale_in = rms_scale(inputs)
    if small_plane():
        sign = jnp.where(jnp.arange(HEAD_SIZE) < HEAD_SIZE // 2, -1.0, 1.0)
        (
            kv_other,
            q_other,
            o_other,
            g_blocks,
            normalized_input,
            query_pre,
            key_value_pre,
            kv_low,
            kv_blocks,
        ) = fetch_and_project(
            hidden_in, attn_gain, key_gain, cosine, rope_sine * sign, key_matrix, value_matrix,
            query_weight, output_weight, out_grad,
        )
        kv_weights = [jnp.concatenate([key_matrix, value_matrix], axis=1), kv_other]
        q_weights = [query_weight, q_other]
        o_weights = [output_weight, o_other]
        g_rows = g_blocks.reshape(spread_count * count_of_rows, MODEL_WIDTH)
        kv_blocks = kv_blocks.reshape(prompt_all, 2 * narrow)
    else:
        full = [
            lax.all_gather(w, "expert", axis=0, tiled=True)
            for w in (
                jnp.concatenate([key_matrix, value_matrix], axis=1),
                query_weight,
                output_weight,
            )
        ]
        kv_weights, q_weights, o_weights = [[w] for w in full]
        g_rows = lax.all_gather(out_grad, plane, axis=0, tiled=True)
        normalized_input = (inputs * scale_in * attn_gain).astype(bf16)
        query_pre = dot(normalized_input, q_weights[0])
        key_value_pre = dot(normalized_input, kv_weights[0])
        key_pre = key_value_pre[:, :narrow].reshape(count_of_rows, KEY_VALUE_HEADS, HEAD_SIZE)
        key_low = rotate(
            key_pre * rms_scale(key_pre) * key_gain, cosine[:, None, :], rope_sine[:, None, :]
        ).astype(bf16)
        kv_low = jnp.concatenate(
            [key_low.reshape(count_of_rows, narrow), key_value_pre[:, narrow:].astype(bf16)],
            axis=1,
        )
        kv_blocks = lax.all_gather(kv_low[:PROMPT_DEV], "ctx", axis=0, tiled=True)

    def forward_dot(v, weights):
        if len(weights) == 1:
            return dot(v, weights[0])
        mine, other = halves(v)
        return dot(mine, weights[0]) + dot(other, weights[1])

    def backward_dot(v, weights):
        parts = [dot(v, w.T) for w in weights]
        return parts[0] if len(parts) == 1 else join_halves(*parts)

    query_pre = query_pre.reshape(count_of_rows, QUERY_HEADS, HEAD_SIZE)
    key_before_norm = key_value_pre[:, :narrow].reshape(
        count_of_rows, KEY_VALUE_HEADS, HEAD_SIZE
    )
    query_inv = rms_scale(query_pre)
    key_inv = rms_scale(key_before_norm)
    cosine = cosine[:, None, :]
    rope_sine = rope_sine[:, None, :]
    query_reduced = rotate(query_pre * query_inv * query_gain, cosine, rope_sine).astype(bf16)
    kv_all = jnp.concatenate([kv_blocks, kv_low[PROMPT_DEV:]], axis=0)
    keys_all, values_all = [
        v.reshape(kv_all.shape[0], KEY_VALUE_HEADS, HEAD_SIZE)
        for v in (kv_all[:, :narrow], kv_all[:, narrow:])
    ]
    key_position = jnp.arange(kv_all.shape[0], dtype=jnp.int32)
    visible = key_position[None, :] <= position[:, None]
    grouped_queries = query_reduced.reshape(
        count_of_rows, KEY_VALUE_HEADS, heads_per_group, HEAD_SIZE
    )

    def scores_of():
        raw_scores = (
            jnp.einsum("rkgd,skd->kgrs", grouped_queries, keys_all, preferred_element_type=f32)
            * score_scale
        )
        return jnp.where(visible, raw_scores, masked)

    scores = scores_of()
    row_max = jnp.max(scores, axis=-1, keepdims=True)
    weights = jnp.exp(scores - row_max)
    row_total = jnp.sum(weights, axis=-1, keepdims=True)
    log_total = row_max + jnp.log(row_total)
    attention = (weights / row_total).astype(bf16)
    attended = (
        jnp.einsum("kgrs,skd->rkgd", attention, values_all, preferred_element_type=f32)
        .reshape(count_of_rows, QUERY_HEADS * HEAD_SIZE)
        .astype(bf16)
    )
    residual = inputs + forward_dot(attended, o_weights)
    scale_ffn = rms_scale(residual)
    ffn_in = (residual * scale_ffn * ffn_gain).astype(bf16)

    if small_plane():
        rows = gather_blocks(ffn_in, 2).reshape(spread_count * count_of_rows, MODEL_WIDTH)
    else:
        rows = lax.all_gather(ffn_in, plane, axis=0, tiled=True)
    expert_count = local_experts * spread_count
    expert_ids = jnp.arange(expert_count, dtype=jnp.int32)

    def gates_of(some_rows, some_routes):
        logits = jnp.dot(some_rows, router_weight, preferred_element_type=f32)
        chosen = jnp.any(some_routes[:, :, None] == expert_ids[None, None, :], axis=1)
        logits = jnp.where(chosen, logits, masked)
        raised = jnp.where(
            chosen, jnp.exp(logits - jnp.max(logits, axis=-1, keepdims=True)), 0.0
        )
        return raised / jnp.sum(raised, axis=-1, keepdims=True)

    gates_all = gates_of(rows, route_rows)
    first_expert = lax.axis_index(plane) * local_experts
    gates_mine = lax.dynamic_slice_in_dim(gates_all, first_expert, local_experts, axis=1)
    moe_part = 0.0
    row_part = 0.0
    gate_grads = []
    hiddens = []
    projected_grads = []
    for which in range(local_experts):
        gate = gates_mine[:, which : which + 1]
        projected = jnp.dot(rows, gate_up[which], preferred_element_type=f32)
        back = jnp.dot(g_rows, down_proj[which].T, preferred_element_type=f32)
        gate_part = projected[:, :hidden_ff]
        up_part = projected[:, hidden_ff:]
        sigmoid_gate = jax.nn.sigmoid(gate_part)
        hidden = gate_part * sigmoid_gate * up_part
        gate_grads.append(jnp.sum(hidden * back, axis=-1))
        hidden_low = (gate * hidden).astype(bf16)
        hidden_back = gate * back
        gate_back = hidden_back * up_part * sigmoid_gate * (1.0 + gate_part * (1.0 - sigmoid_gate))
        up_back = hidden_back * gate_part * sigmoid_gate
        projected_grad = jnp.concatenate([gate_back, up_back], axis=-1).astype(bf16)
        hiddens.append(hidden_low)
        projected_grads.append(projected_grad)
    gate_up_local = jnp.stack(
        [jnp.dot(rows.T, v, preferred_element_type=f32).astype(bf16) for v in projected_grads]
    )
    down_local = jnp.stack(
        [jnp.dot(v.T, g_rows, preferred_element_type=f32).astype(bf16) for v in hiddens]
    )
    gate_up_low = lax.psum_scatter(gate_up_local, "dp", scatter_dimension=1, tiled=True)
    down_low = lax.psum_scatter(down_local, "dp", scatter_dimension=1, tiled=True)
    gate_up_grad = gate_up_low.astype(f32)
    down_grad = down_low.astype(f32)
    projected_grads, hiddens = lax.optimization_barrier(
        ((projected_grads, hiddens), gate_up_local, down_local)
    )[0]
    for which in range(local_experts):
        row_part = row_part + jnp.dot(
            projected_grads[which], gate_up[which].T, preferred_element_type=f32
        )
        moe_part = moe_part + jnp.dot(hiddens[which], down_proj[which], preferred_element_type=f32)

    def blocks_of(v):
        return [
            lax.dynamic_slice_in_dim(v, i * count_of_rows, count_of_rows, axis=0) for i in order
        ]

    moe_sum = scatter_plane(blocks_of(moe_part.astype(bf16)))
    block_out = (residual + moe_sum).astype(bf16)
    back_sum = scatter_plane(blocks_of(row_part.astype(bf16)))
    gate_grad_blocks = exchange_plane(blocks_of(jnp.stack(gate_grads, axis=1)))
    gate_grad = jnp.zeros((count_of_rows, expert_count), f32)
    for r in range(spread_count):
        gate_grad = lax.dynamic_update_slice_in_dim(
            gate_grad, gate_grad_blocks[r], order[r] * local_experts, axis=1
        )
    gates = gates_of(ffn_in, routes)
    logit_grad = gates * (gate_grad - jnp.sum(gates * gate_grad, axis=-1, keepdims=True))

    grad_out = out_grad.astype(f32)
    router_local = jnp.dot(ffn_in.T, logit_grad, preferred_element_type=f32)
    ffn_in_grad = back_sum + jnp.dot(
        logit_grad, router_weight.astype(f32).T, precision=highest
    )
    residual_grad = grad_out + norm_back(residual, scale_ffn, ffn_gain, ffn_in_grad)
    ffn_gain_local = jnp.sum(ffn_in_grad * residual * scale_ffn, axis=0)
    branch_low = residual_grad.astype(bf16)
    branch_rows = jnp.concatenate(gather_plane(branch_low), axis=0)
    attended_grad = (
        backward_dot(branch_low, o_weights)
        .astype(bf16)
        .reshape(count_of_rows, KEY_VALUE_HEADS, heads_per_group, HEAD_SIZE)
    )
    attention_again = jnp.exp(scores_of() - log_total)
    prob_grad = jnp.einsum(
        "rkgd,skd->kgrs", attended_grad, values_all, preferred_element_type=f32
    )
    row_delta = jnp.sum(attention_again * prob_grad, axis=-1, keepdims=True)
    score_grad = (attention_again * (prob_grad - row_delta)).astype(bf16)
    query_grad = (
        jnp.einsum("kgrs,skd->rkgd", score_grad, keys_all, preferred_element_type=f32)
        * score_scale
    ).reshape(count_of_rows, QUERY_HEADS, HEAD_SIZE)
    key_grad_all = (
        jnp.einsum("kgrs,rkgd->skd", score_grad, grouped_queries, preferred_element_type=f32)
        * score_scale
    )
    value_grad_all = jnp.einsum(
        "kgrs,rkgd->skd",
        attention_again.astype(bf16),
        attended_grad,
        preferred_element_type=f32,
    )
    pair_grads = jnp.stack([key_grad_all[:prompt_all], value_grad_all[:prompt_all]]).astype(bf16)
    prompt_grads = ctx_sum(pair_grads)
    key_grad = jnp.concatenate([prompt_grads[0], key_grad_all[prompt_all:]], axis=0)
    value_gradient = jnp.concatenate([prompt_grads[1], value_grad_all[prompt_all:]], axis=0)
    query_rot_grad = rotate_back(query_grad, cosine, rope_sine)
    key_rot_grad = rotate_back(key_grad, cosine, rope_sine)
    query_gain_local = jnp.sum(query_rot_grad * query_pre * query_inv, axis=(0, 1))
    key_gain_local = jnp.sum(key_rot_grad * key_before_norm * key_inv, axis=(0, 1))
    query_pre_grad = (
        norm_back(query_pre, query_inv, query_gain, query_rot_grad)
        .astype(bf16)
        .reshape(count_of_rows, QUERY_HEADS * HEAD_SIZE)
    )
    key_pre_grad = (
        norm_back(key_before_norm, key_inv, key_gain, key_rot_grad)
        .astype(bf16)
        .reshape(count_of_rows, KEY_VALUE_HEADS * HEAD_SIZE)
    )
    value_before_norm_gradient = value_gradient.astype(bf16).reshape(
        count_of_rows, KEY_VALUE_HEADS * HEAD_SIZE
    )
    key_value_grad = jnp.concatenate([key_pre_grad, value_before_norm_gradient], axis=1)
    normed_grad = backward_dot(query_pre_grad, q_weights) + backward_dot(
        key_value_grad, kv_weights
    )
    attn_gain_local = jnp.sum(normed_grad * inputs * scale_in, axis=0)
    hidden_grad = residual_grad + norm_back(inputs, scale_in, attn_gain, normed_grad)

    pre_rows = jnp.concatenate(
        gather_plane(
            jnp.concatenate([query_pre_grad, key_value_grad], axis=1)
        ),
        axis=0,
    )

    def owned(v):
        width = v.shape[1] // device_count
        split = v.reshape(count_of_rows, dp_count, spread_count, width)
        parts = [
            lax.dynamic_index_in_dim(split, o, axis=2, keepdims=False).reshape(
                count_of_rows, dp_count * width
            )
            for o in order
        ]
        return jnp.concatenate(exchange_plane(parts), axis=0)

    normed_owned = owned(after(normalized_input, rows))
    attended_owned = owned(after(attended, rows))
    pre_local = jnp.dot(normed_owned.T, pre_rows, preferred_element_type=f32)
    output_local = jnp.dot(attended_owned.T, branch_rows, preferred_element_type=f32)
    pre_local, output_local = lax.optimization_barrier(
        ((pre_local.astype(bf16), output_local.astype(bf16)), gate_up_low, down_low)
    )[0]
    output_sum = lax.psum_scatter(output_local, "dp", scatter_dimension=0, tiled=True).astype(f32)
    pre_sum = lax.psum_scatter(pre_local, "dp", scatter_dimension=0, tiled=True).astype(f32)

    small = jnp.concatenate(
        [
            v.reshape(device_count, -1)
            for v in (
                attn_gain_local,
                ffn_gain_local,
                query_gain_local,
                key_gain_local,
                router_local,
            )
        ],
        axis=1,
    )
    small = lax.all_to_all(small[:, None], every, split_axis=0, concat_axis=0, tiled=True)
    small = jnp.sum(small[:, 0], axis=0)
    share = MODEL_WIDTH // device_count
    head_share = HEAD_SIZE // device_count
    cuts = [share, share, head_share, head_share, share * expert_count]
    ends = [sum(cuts[: i + 1]) for i in range(5)]
    a_grad, f_grad, q_grad, k_grad, r_grad = [
        small[end - cut : end] for end, cut in zip(ends, cuts)
    ]
    return (
        block_out,
        hidden_grad,
        a_grad,
        pre_sum[:, :wide],
        pre_sum[:, wide : wide + narrow],
        pre_sum[:, wide + narrow :],
        q_grad,
        k_grad,
        output_sum,
        f_grad,
        r_grad.reshape(share, expert_count),
        gate_up_grad,
        down_grad,
    )


def solution(mesh):
    placed = (
        P(("dp", "ctx", "expert"), None),
        P(),
        P("expert", None),
        P("expert", None),
        P("expert", None),
        P(),
        P(),
        P("expert", None),
        P(),
        P(),
        P(("ctx", "expert"), None, None),
        P(("ctx", "expert"), None, None),
        P(("dp", "ctx", "expert"), None),
        P(("dp", "ctx", "expert"), None),
    )
    return jax.shard_map(
        body,
        mesh=mesh,
        in_specs=placed,
        out_specs=(
            P(("dp", "ctx", "expert"), None),
            P(("dp", "ctx", "expert"), None),
            P(("dp", "ctx", "expert")),
            P(("dp", "ctx", "expert"), None),
            P(("dp", "ctx", "expert"), None),
            P(("dp", "ctx", "expert"), None),
            P(("dp", "ctx", "expert")),
            P(("dp", "ctx", "expert")),
            P(("dp", "ctx", "expert"), None),
            P(("dp", "ctx", "expert")),
            P(("dp", "ctx", "expert"), None),
            P(("ctx", "expert"), "dp", None),
            P(("ctx", "expert"), "dp", None),
        ),
        check_vma=False,
    )
```

```python
import math

import jax
import jax.numpy as jnp
from jax import lax
from jax.experimental import pallas as pl
from jax.experimental.pallas import tpu as pltpu
from jax.sharding import PartitionSpec as P

MODEL_WIDTH = 2048
QUERY_HEADS = 32
KEY_VALUE_HEADS = 4
HEAD_SIZE = 128
TOP = 8
PROMPT_DEV = 128


highest = lax.Precision.HIGHEST
epsilon = 1e-06
rope_base = 1000000.0
masked = -1e30
every = ("dp", "ctx", "expert")
plane = ("ctx", "expert")
bf16 = jnp.bfloat16
f32 = jnp.float32


def rms_scale(value_rows):
    return lax.rsqrt(jnp.mean(value_rows * value_rows, axis=-1, keepdims=True) + epsilon)


def norm_back(inputs, inv_rms, norm_gain, gradient):
    weighted = gradient * norm_gain
    return inv_rms * weighted - inputs * inv_rms**3 * jnp.mean(
        weighted * inputs, axis=-1, keepdims=True
    )


def angles(position, head_width):
    freq_index = jnp.arange(head_width // 2, dtype=f32)
    inverse = jnp.exp(-(2.0 * freq_index / head_width) * math.log(rope_base))
    rope_angle = position.astype(f32)[:, None] * inverse[None, :]
    rope_angle = jnp.concatenate([rope_angle, rope_angle], axis=-1)
    return (jnp.cos(rope_angle), jnp.sin(rope_angle))


def rotate(value_rows, cosine, rope_sine):
    half_width = value_rows.shape[-1] // 2
    turned = jnp.concatenate([-value_rows[..., half_width:], value_rows[..., :half_width]], axis=-1)
    return value_rows * cosine + turned * rope_sine


def rotate_back(gradient, cosine, rope_sine):
    shifted = gradient * rope_sine
    half_width = gradient.shape[-1] // 2
    return gradient * cosine + jnp.concatenate(
        [shifted[..., half_width:], -shifted[..., :half_width]], axis=-1
    )


def small_plane():
    return lax.axis_size("ctx") == 4 and lax.axis_size("expert") == 2


def swap(v, axis, bit):
    return lax.ppermute(v, axis, [(i, i ^ bit) for i in range(lax.axis_size(axis))])


def core(v):
    return swap(v, "ctx", 1)


def over_x(v):
    return swap(v, "ctx", 2)


def over_y(v):
    return swap(v, "expert", 1)


def relative():
    count = lax.axis_size(plane)
    me = lax.axis_index(plane)
    if small_plane():
        return [me ^ r for r in range(count)]
    return list(range(count))


def gather_plane(v):
    if not small_plane():
        out = lax.all_gather(v, plane, axis=0, tiled=False)
        return [out[i] for i in range(out.shape[0])]
    half = v.shape[0] // 2
    vy, vx, vc = over_y(v), over_x(v), core(v)
    top, low = over_x(vy[:half]), over_y(vx[half:])
    vyc, vxc = core(vy), core(vx)
    vxy = jnp.concatenate([top, low], axis=0)
    vxyc = jnp.concatenate([core(top), core(low)], axis=0)
    return [v, vy, vc, vyc, vx, vxy, vxc, vxyc]


def exchange_plane(blocks):
    if not small_plane():
        out = lax.all_to_all(jnp.stack(blocks), plane, split_axis=0, concat_axis=0, tiled=True)
        return [out[i] for i in range(out.shape[0])]
    out = [blocks[0]]
    for r in range(1, 8):
        pairs = [(i, i ^ r) for i in range(8)]
        out.append(lax.ppermute(blocks[r], plane, pairs))
    return out


def over_z(v):
    return swap(v, "dp", 1)


def after(v, *earlier):
    return lax.optimization_barrier((v, *earlier))[0]


class Places:
    def __init__(self):
        self.dp = lax.axis_index("dp")
        ctx = lax.axis_index("ctx")
        self.ctx = ctx
        self.z = lax.rem(self.dp, 2)
        self.x = lax.div(ctx, 2)
        self.c = lax.rem(ctx, 2)
        self.y = lax.axis_index("expert")
        self.to_x = {"ctx": (1 - self.x) * 2 + self.c}
        self.to_c = {"ctx": self.x * 2 + 1 - self.c}
        self.to_y = {"expert": 1 - self.y}
        self.to_z = {"dp": self.dp + 1 - 2 * self.z}


def plane_slot(x, c, y):
    return x * 4 + y * 2 + c


def greet(targets):
    barrier = pltpu.get_barrier_semaphore()
    for target in targets:
        pl.semaphore_signal(barrier, inc=1, device_id=target, device_id_type=pl.DeviceIdType.MESH)
    pl.semaphore_wait(barrier, len(targets))


class Sender:
    def __init__(self, send_sem, recv_sem):
        self.send_sem = send_sem
        self.recv_sem = recv_sem
        self.copies = []

    def __call__(self, source, target_ref, device):
        i = len(self.copies)
        copy = pltpu.make_async_remote_copy(
            src_ref=source,
            dst_ref=target_ref,
            send_sem=self.send_sem.at[i],
            recv_sem=self.recv_sem.at[i],
            device_id=device,
            device_id_type=pl.DeviceIdType.MESH,
        )
        copy.start()
        self.copies.append(copy)
        return copy

    def finish(self):
        for copy in self.copies:
            copy.wait_send()


def run_rounds(work, between):
    turns = max(i + len(todo) for i, todo in enumerate(work))
    for turn in range(turns):
        for i, todo in enumerate(work):
            if 0 <= turn - i < len(todo):
                todo[turn - i]()
        if turn in between:
            between[turn]()


def half_fetch(here, send, sources, other, columns, rows):
    def at(piece, part=None):
        first, size = piece * rows, rows
        if part is not None:
            size = rows // 2
            first = first + part * size
        return other.at[pl.ds(pl.multiple_of(first, size), size), columns]

    def piece(z, x, c):
        return z * 4 + x * 2 + c

    z, x, c = here.z, here.x, here.c
    got = {}

    def first():
        mine = piece(z, x, c)
        got["y"] = [
            send(
                source.at[pl.ds(pl.multiple_of(mine * rows, rows), rows), source_columns],
                other.at[pl.ds(pl.multiple_of(mine * rows, rows), rows), target_columns],
                here.to_y,
            )
            for source, source_columns, target_columns in sources
        ]

    def second():
        for copy in got["y"]:
            copy.wait_recv()
        mine = at(piece(z, x, c))
        got["x"] = send(mine, mine, here.to_x)
        got["z"] = send(mine, mine, here.to_z)
        got["c"] = send(mine, mine, here.to_c)

    def third():
        got["x"].wait_recv()
        from_x = piece(z, 1 - x, c)
        got["low"] = send(at(from_x, 1), at(from_x, 1), here.to_z)
        got["xc"] = send(at(from_x), at(from_x), here.to_c)
        got["z"].wait_recv()
        from_z = piece(1 - z, x, c)
        got["top"] = send(at(from_z, 0), at(from_z, 0), here.to_x)
        got["zc"] = send(at(from_z), at(from_z), here.to_c)

    def fourth():
        far = piece(1 - z, 1 - x, c)
        got["low"].wait_recv()
        got["lowc"] = send(at(far, 1), at(far, 1), here.to_c)
        got["top"].wait_recv()
        got["topc"] = send(at(far, 0), at(far, 0), here.to_c)

    def fifth():
        for name in ("c", "xc", "zc", "lowc", "topc"):
            got[name].wait_recv()

    return [first, second, third, fourth, fifth]


def block_gather(here, send, mine, local_sem, blocks):
    rows = blocks.shape[0] // lax.axis_size(plane)
    half = rows // 2
    x, c, y = here.x, here.c, here.y
    got = {}

    def at(slot, part=None):
        first, size = slot * rows, rows
        if part is not None:
            first, size = first + part * half, half
        return blocks.at[pl.ds(pl.multiple_of(first, size), size)]

    def first():
        slot = plane_slot(x, c, y)
        got["own"] = pltpu.make_async_copy(mine, at(slot), local_sem)
        got["own"].start()
        got["y"] = send(mine, at(slot), here.to_y)
        got["x"] = send(mine, at(slot), here.to_x)
        got["c"] = send(mine, at(slot), here.to_c)

    def second():
        got["y"].wait_recv()
        from_y = plane_slot(x, c, 1 - y)
        got["top"] = send(at(from_y, 0), at(from_y, 0), here.to_x)
        got["yc"] = send(at(from_y), at(from_y), here.to_c)
        got["x"].wait_recv()
        from_x = plane_slot(1 - x, c, y)
        got["low"] = send(at(from_x, 1), at(from_x, 1), here.to_y)
        got["xc"] = send(at(from_x), at(from_x), here.to_c)

    def third():
        far = plane_slot(1 - x, c, 1 - y)
        got["top"].wait_recv()
        got["topc"] = send(at(far, 0), at(far, 0), here.to_c)
        got["low"].wait_recv()
        got["lowc"] = send(at(far, 1), at(far, 1), here.to_c)

    def fourth():
        for name in ("c", "yc", "xc", "topc", "lowc"):
            got[name].wait_recv()
        got["own"].wait()

    return [first, second, third, fourth], got


def turn_half(v):
    return pltpu.roll(v, v.shape[-1] // 2, axis=1)


def head_norm(v):
    return lax.rsqrt(jnp.mean(v * v, axis=-1, keepdims=True) + epsilon)


def fetch_kernel(
    hidden_ref,
    attn_gain_ref,
    key_gain_ref,
    cosine_ref,
    sine_ref,
    key_ref,
    value_ref,
    query_ref,
    output_ref,
    grad_ref,
    kv_out,
    q_out,
    o_other,
    g_blocks,
    normed_ref,
    query_pre_ref,
    kv_pre_ref,
    kv_low_ref,
    kv_blocks,
    kv_own,
    kv_other,
    q_own,
    q_other,
    send_sem,
    recv_sem,
    local_sem,
):
    here = Places()
    greet([here.to_y, here.to_z, here.to_c, here.to_x])
    send = Sender(send_sem, recv_sem)
    width = hidden_ref.shape[1]
    half = width // 2
    narrow = key_ref.shape[1]
    wide = query_ref.shape[1]
    tile = 512
    loads = [
        pltpu.make_async_copy(key_ref, kv_own.at[:, pl.ds(0, narrow)], local_sem.at[0]),
        pltpu.make_async_copy(value_ref, kv_own.at[:, pl.ds(narrow, narrow)], local_sem.at[1]),
        pltpu.make_async_copy(query_ref, q_own, local_sem.at[2]),
    ]
    stores = [
        pltpu.make_async_copy(kv_other, kv_out, local_sem.at[3]),
        pltpu.make_async_copy(q_other, q_out, local_sem.at[4]),
    ]
    mine = pl.ds(pl.multiple_of(here.y * half, half), half)
    others = pl.ds(pl.multiple_of(half - here.y * half, half), half)

    def project(weight, out, rows, first, count, add):
        @pl.loop(first, first + count)
        def _(i):
            cols = pl.ds(pl.multiple_of(i * tile, tile), tile)
            part = jnp.dot(normed_ref[:, rows], weight[:, cols], preferred_element_type=f32)
            out[:, cols] = out[:, cols] + part if add else part

    def start():
        for load in loads:
            load.start()
        inputs = hidden_ref[...].astype(f32)
        normed_ref[...] = (inputs * head_norm(inputs) * attn_gain_ref[...]).astype(bf16)

    def own_part():
        for load in loads:
            load.wait()
        project(kv_own, kv_pre_ref, mine, 0, 2 * narrow // tile, False)
        project(q_own, query_pre_ref, mine, 0, wide // tile, False)

    exchange = {}

    def keys_part():
        project(kv_other, kv_pre_ref, others, 0, 2 * narrow // tile, True)
        stores[0].start()
        for h in range(narrow // HEAD_SIZE):
            cols = slice(h * HEAD_SIZE, (h + 1) * HEAD_SIZE)
            v = kv_pre_ref[:, cols]
            v = v * head_norm(v) * key_gain_ref[...]
            kv_low_ref[:, cols] = (v * cosine_ref[...] + turn_half(v) * sine_ref[...]).astype(bf16)
        kv_low_ref[:, narrow:] = kv_pre_ref[:, narrow:].astype(bf16)
        source = kv_low_ref.at[pl.ds(0, PROMPT_DEV)]
        slot = kv_blocks.at[here.ctx]
        exchange["own"] = pltpu.make_async_copy(source, slot, local_sem.at[5])
        exchange["own"].start()
        exchange["c"] = send(source, slot, here.to_c)
        exchange["x"] = send(source, slot, here.to_x)

    def keys_forward():
        exchange["x"].wait_recv()
        slot = kv_blocks.at[(1 - here.x) * 2 + here.c]
        exchange["xc"] = send(slot, slot, here.to_c)
        project(q_other, query_pre_ref, others, 0, wide // tile // 2, True)

    def queries_rest():
        stores[1].start()
        project(q_other, query_pre_ref, others, wide // tile // 2, wide // tile // 2, True)

    low, high = pl.ds(0, wide // 2), pl.ds(wide // 2, wide // 2)
    o_low, o_high = pl.ds(0, width // 2), pl.ds(width // 2, width // 2)
    rows, o_rows = half // 8, output_ref.shape[0] // 8
    work = [
        half_fetch(
            here,
            send,
            [
                (key_ref, pl.ds(0, narrow), pl.ds(0, narrow)),
                (value_ref, pl.ds(0, narrow), pl.ds(narrow, narrow)),
            ],
            kv_other,
            pl.ds(0, 2 * narrow),
            rows,
        ),
        half_fetch(here, send, [(query_ref, low, low)], q_other, low, rows),
        half_fetch(here, send, [(query_ref, high, high)], q_other, high, rows),
        half_fetch(here, send, [(output_ref, o_low, o_low)], o_other, o_low, o_rows),
        half_fetch(here, send, [(output_ref, o_high, o_high)], o_other, o_high, o_rows),
        block_gather(here, send, grad_ref, local_sem.at[6], g_blocks)[0],
    ]
    run_rounds(
        work, {0: start, 2: own_part, 4: keys_part, 5: keys_forward, 6: queries_rest}
    )
    for name in ("c", "xc"):
        exchange[name].wait_recv()
    exchange["own"].wait()
    for store in stores:
        store.wait()
    send.finish()


def fetch_and_project(
    hidden_in, attn_gain, key_gain, cosine, sine, key_matrix, value_matrix, query_weight,
    output_weight, out_grad,
):
    rows, width = hidden_in.shape
    half, wide = query_weight.shape
    narrow = key_matrix.shape[1]
    spread = lax.axis_size(plane)
    vmem = pl.BlockSpec(memory_space=pltpu.VMEM)
    anywhere = pl.BlockSpec(memory_space=pl.ANY)
    copies = 5 * 10 + 1 + 9 + 3
    return pl.pallas_call(
        fetch_kernel,
        out_shape=[
            jax.ShapeDtypeStruct((half, 2 * narrow), bf16),
            jax.ShapeDtypeStruct((half, wide), bf16),
            jax.ShapeDtypeStruct(output_weight.shape, bf16),
            jax.ShapeDtypeStruct((spread * rows, width), bf16),
            jax.ShapeDtypeStruct((rows, width), bf16),
            jax.ShapeDtypeStruct((rows, wide), f32),
            jax.ShapeDtypeStruct((rows, 2 * narrow), f32),
            jax.ShapeDtypeStruct((rows, 2 * narrow), bf16),
            jax.ShapeDtypeStruct((lax.axis_size("ctx"), PROMPT_DEV, 2 * narrow), bf16),
        ],
        in_specs=[vmem] * 5 + [anywhere] * 5,
        out_specs=[anywhere] * 4 + [vmem] * 4 + [anywhere],
        scratch_shapes=[
            pltpu.VMEM((half, 2 * narrow), bf16),
            pltpu.VMEM((half, 2 * narrow), bf16),
            pltpu.VMEM((half, wide), bf16),
            pltpu.VMEM((half, wide), bf16),
            pltpu.SemaphoreType.DMA((copies,)),
            pltpu.SemaphoreType.DMA((copies,)),
            pltpu.SemaphoreType.DMA((7,)),
        ],
        compiler_params=pltpu.CompilerParams(
            collective_id=1, has_side_effects=True, vmem_limit_bytes=48 * 2**20
        ),
    )(
        hidden_in, attn_gain.reshape(1, width), key_gain.reshape(1, HEAD_SIZE), cosine, sine,
        key_matrix, value_matrix, query_weight, output_weight, out_grad,
    )


def chip_rows(x, y, rows):
    first = plane_slot(x, 0, y) * rows
    return pl.ds(pl.multiple_of(first, rows), 2 * rows)


def expert_kernel(
    ffn_ref,
    routes_ref,
    router_ref,
    g_hbm,
    gate_up_hbm,
    down_hbm,
    rows_out,
    hidden_out,
    grad_out,
    gate_grad_ref,
    rows_v,
    g_v,
    gate_up_v,
    down_v,
    hidden_v,
    grad_v,
    total_v,
    send_sem,
    recv_sem,
    local_sem,
):
    here = Places()
    greet([here.to_y, here.to_c, here.to_x])
    send = Sender(send_sem, recv_sem)
    count = ffn_ref.shape[0]
    experts = router_ref.shape[1]
    local_experts, ff, _ = down_hbm.shape
    tile = 256
    stages, got = block_gather(here, send, ffn_ref, local_sem.at[0], rows_v)
    stages[0]()
    loads = [
        pltpu.make_async_copy(gate_up_hbm, gate_up_v, local_sem.at[1]),
        pltpu.make_async_copy(down_hbm, down_v, local_sem.at[2]),
        pltpu.make_async_copy(g_hbm, g_v, local_sem.at[3]),
    ]
    for load in loads:
        load.start()
    first_expert = plane_index(here) * local_experts
    stores = []

    def chunk(x, y):
        some = chip_rows(x, y, count)
        logits = dot(rows_v[some, :], router_ref[...])
        ids = lax.broadcasted_iota(jnp.int32, logits.shape, 1)
        routes = routes_ref[some, :]
        chosen = ids < 0
        for k in range(routes.shape[1]):
            chosen = chosen | (routes[:, k : k + 1] == ids)
        logits = jnp.where(chosen, logits, masked)
        raised = jnp.exp(logits - jnp.max(logits, axis=-1, keepdims=True))
        raised = jnp.where(chosen, raised, 0.0)
        gates = raised / jnp.sum(raised, axis=-1, keepdims=True)
        lane = lax.broadcasted_iota(jnp.int32, total_v.shape, 1)
        total_v[...] = jnp.zeros(total_v.shape, f32)
        for e in range(local_experts):
            gate = jnp.sum(
                jnp.where(ids == first_expert + e, gates, 0.0), axis=-1, keepdims=True
            )
            here_lane = (lane == first_expert + e) | (lane == first_expert + e + experts)

            @pl.loop(0, ff // tile)
            def _(f, e=e, gate=gate, here_lane=here_lane):
                at = pl.multiple_of(f * tile, tile)
                a = dot(rows_v[some, :], gate_up_v[e, :, pl.ds(at, tile)])
                b = dot(rows_v[some, :], gate_up_v[e, :, pl.ds(ff + at, tile)])
                q = lax.dot_general(
                    g_v[some, :],
                    down_v[e, pl.ds(at, tile), :],
                    (((1,), (1,)), ((), ())),
                    preferred_element_type=f32,
                )
                s = 1.0 / (1.0 + jnp.exp(-a))
                raised_a = a * s
                hidden = raised_a * b
                total_v[...] = total_v[...] + jnp.where(
                    here_lane, jnp.sum(hidden * q, axis=-1, keepdims=True), 0.0
                )
                back = gate * q
                hidden_v[some, pl.ds(e * ff + at, tile)] = (gate * hidden).astype(bf16)
                grad_v[some, pl.ds(2 * e * ff + at, tile)] = (
                    back * b * s * (1.0 + a * (1.0 - s))
                ).astype(bf16)
                grad_v[some, pl.ds((2 * e + 1) * ff + at, tile)] = (back * raised_a).astype(bf16)

        total = total_v[...]
        high = total.astype(bf16).astype(f32)
        gate_grad_ref[some, :] = jnp.where(lane < experts, high, total - high).astype(bf16)
        for source, target in ((hidden_v, hidden_out), (grad_v, grad_out), (rows_v, rows_out)):
            store = pltpu.make_async_copy(
                source.at[some, :], target.at[some, :], local_sem.at[4 + len(stores)]
            )
            store.start()
            stores.append(store)

    x, y = here.x, here.y
    for name in ("c", "own"):
        arrive(got, name)
    for load in loads:
        load.wait()
    chunk(x, y)
    stages[1]()
    arrive(got, "yc")
    chunk(x, 1 - y)
    stages[2]()
    arrive(got, "xc")
    chunk(1 - x, y)
    arrive(got, "topc")
    arrive(got, "lowc")
    chunk(1 - x, 1 - y)
    for store in stores:
        store.wait()
    send.finish()


def arrive(got, name):
    copy = got[name]
    copy.wait() if name == "own" else copy.wait_recv()


def plane_index(here):
    return here.ctx * 2 + here.y


def experts_of_plane(ffn_in, route_rows, router_weight, g_rows, gate_up, down_proj):
    local_experts, ff, width = down_proj.shape
    total = route_rows.shape[0]
    vmem = pl.BlockSpec(memory_space=pltpu.VMEM)
    anywhere = pl.BlockSpec(memory_space=pl.ANY)
    return pl.pallas_call(
        expert_kernel,
        out_shape=[
            jax.ShapeDtypeStruct((total, width), bf16),
            jax.ShapeDtypeStruct((total, local_experts * ff), bf16),
            jax.ShapeDtypeStruct((total, 2 * local_experts * ff), bf16),
            jax.ShapeDtypeStruct((total, 128), bf16),
        ],
        in_specs=[vmem] * 3 + [anywhere] * 3,
        out_specs=[anywhere] * 3 + [vmem],
        scratch_shapes=[
            pltpu.VMEM((total, width), bf16),
            pltpu.VMEM((total, width), bf16),
            pltpu.VMEM(gate_up.shape, bf16),
            pltpu.VMEM(down_proj.shape, bf16),
            pltpu.VMEM((total, local_experts * ff), bf16),
            pltpu.VMEM((total, 2 * local_experts * ff), bf16),
            pltpu.VMEM((2 * ffn_in.shape[0], 128), f32),
            pltpu.SemaphoreType.DMA((9,)),
            pltpu.SemaphoreType.DMA((9,)),
            pltpu.SemaphoreType.DMA((16,)),
        ],
        compiler_params=pltpu.CompilerParams(
            collective_id=2, has_side_effects=True, vmem_limit_bytes=60 * 2**20
        ),
        cost_estimate=pl.CostEstimate(
            flops=2 * total * width * 3 * local_experts * ff,
            bytes_accessed=60 * 2**20,
            transcendentals=0,
        ),
    )(ffn_in, route_rows, router_weight, g_rows, gate_up, down_proj)


def plane_sum_kernel(across, *refs):
    if across:
        left_hbm, weight_hbm, extra_ref = refs[:3]
        refs = refs[3:]
    else:
        left_hbm, weight_hbm = refs[:2]
        extra_ref = None
        refs = refs[2:]
    (
        out_ref, left_v, weight_v, part_v, core_v, edge_v, last_v, send_sem, recv_sem, local_sem,
    ) = refs
    here = Places()
    greet([here.to_y, here.to_c, here.to_x])
    send = Sender(send_sem, recv_sem)
    count = out_ref.shape[0]
    half = count // 2
    experts = weight_hbm.shape[0]
    depth = left_hbm.shape[1] // experts
    width = weight_hbm.shape[1] if across else weight_hbm.shape[2]
    tile = 256
    x, y, c = here.x, here.y, here.c
    chips = [(1 - x, 1 - y), (1 - x, y), (x, 1 - y), (x, y)]
    weight_load = pltpu.make_async_copy(weight_hbm, weight_v, local_sem.at[0])
    weight_load.start()
    loads = []
    for k, (cx, cy) in enumerate(chips):
        load = pltpu.make_async_copy(
            left_hbm.at[chip_rows(cx, cy, count), :], left_v.at[k], local_sem.at[1 + k]
        )
        load.start()
        loads.append(load)
    weight_load.wait()
    to_core = []

    def compute(k):
        loads[k].wait()

        @pl.loop(0, width // tile)
        def _(n):
            cols = pl.ds(pl.multiple_of(n * tile, tile), tile)
            total = None
            for e in range(experts):
                left = left_v[k, :, e * depth : (e + 1) * depth]
                if across:
                    part = lax.dot_general(
                        left,
                        weight_v[e, cols, :],
                        (((1,), (1,)), ((), ())),
                        preferred_element_type=f32,
                    )
                else:
                    part = dot(left, weight_v[e, :, cols])
                total = part if total is None else total + part
            part_v[k, :, cols] = total.astype(bf16)

        if extra_ref is not None:
            part_v[k, :, width:] = extra_ref[chip_rows(*chips[k], count), :]
        to_core.append(
            send(
                part_v.at[k, pl.ds(pl.multiple_of((1 - c) * count, count), count)],
                core_v.at[k],
                here.to_c,
            )
        )

    mine = pl.ds(pl.multiple_of(c * count, count), count)

    def chip_sum(k):
        to_core[k].wait_recv()
        return part_v[k, mine, :].astype(f32) + core_v[k].astype(f32)

    compute(0)
    compute(1)
    core_v[0] = chip_sum(0).astype(bf16)
    from_x = send(core_v.at[0, pl.ds(0, half)], edge_v.at[0], here.to_x)
    from_y = send(core_v.at[0, pl.ds(half, half)], edge_v.at[1], here.to_y)
    compute(2)
    over_x_sum = chip_sum(1)
    core_v[1, :half] = over_x_sum[:half].astype(bf16)
    from_y.wait_recv()
    core_v[1, half:] = (over_x_sum[half:] + edge_v[1].astype(f32)).astype(bf16)
    last_x = send(core_v.at[1], last_v.at[0], here.to_x)
    over_y_sum = chip_sum(2)
    core_v[2, half:] = over_y_sum[half:].astype(bf16)
    from_x.wait_recv()
    core_v[2, :half] = (over_y_sum[:half] + edge_v[0].astype(f32)).astype(bf16)
    last_y = send(core_v.at[2], last_v.at[1], here.to_y)
    compute(3)
    out_ref[...] = chip_sum(3)
    last_x.wait_recv()
    last_y.wait_recv()
    out_ref[...] = out_ref[...] + last_v[0].astype(f32) + last_v[1].astype(f32)
    send.finish()


def plane_sum(left, weight, extra, collective_id):
    across = extra is not None
    count = left.shape[0] // lax.axis_size(plane)
    width = weight.shape[1] if across else weight.shape[2]
    wide = width + (extra.shape[1] if across else 0)
    vmem = pl.BlockSpec(memory_space=pltpu.VMEM)
    anywhere = pl.BlockSpec(memory_space=pl.ANY)

    def kernel(*refs):
        plane_sum_kernel(across, *refs)

    return pl.pallas_call(
        kernel,
        out_shape=jax.ShapeDtypeStruct((count, wide), f32),
        in_specs=[anywhere] * 2 + [vmem] * across,
        out_specs=vmem,
        scratch_shapes=[
            pltpu.VMEM((4, 2 * count, left.shape[1]), bf16),
            pltpu.VMEM(weight.shape, bf16),
            pltpu.VMEM((4, 2 * count, wide), bf16),
            pltpu.VMEM((4, count, wide), bf16),
            pltpu.VMEM((2, count // 2, wide), bf16),
            pltpu.VMEM((2, count, wide), bf16),
            pltpu.SemaphoreType.DMA((8,)),
            pltpu.SemaphoreType.DMA((8,)),
            pltpu.SemaphoreType.DMA((5,)),
        ],
        compiler_params=pltpu.CompilerParams(
            collective_id=collective_id, has_side_effects=True, vmem_limit_bytes=60 * 2**20
        ),
        cost_estimate=pl.CostEstimate(
            flops=2 * left.shape[0] * left.shape[1] * width,
            bytes_accessed=40 * 2**20,
            transcendentals=0,
        ),
    )(*([left, weight] + ([extra] if across else [])))


def head_softmax(queries, keys, visible):
    scores = lax.dot_general(
        queries, keys, (((1,), (1,)), ((), ())), preferred_element_type=f32
    ) * (HEAD_SIZE ** (-0.5))
    scores = jnp.where(visible, scores, masked)
    raised = jnp.exp(scores - jnp.max(scores, axis=-1, keepdims=True))
    return raised / jnp.sum(raised, axis=-1, keepdims=True)


def visible_keys(rows, keys):
    row = lax.broadcasted_iota(jnp.int32, (rows, keys), 0)
    key = lax.broadcasted_iota(jnp.int32, (rows, keys), 1)
    prompt_all = keys - (rows - PROMPT_DEV)
    own = lax.axis_index("ctx") * PROMPT_DEV + row
    position = jnp.where(row < PROMPT_DEV, own, prompt_all + row - PROMPT_DEV)
    return key <= position


def attention_kernel(
    query_pre_ref, gain_ref, cosine_ref, sine_ref, keys_ref, values_ref, queries_ref, attended_ref
):
    rows = query_pre_ref.shape[0]
    visible = visible_keys(rows, keys_ref.shape[0])
    keys = keys_ref[...]
    values = values_ref[...]
    for h in range(query_pre_ref.shape[1] // HEAD_SIZE):
        cols = slice(h * HEAD_SIZE, (h + 1) * HEAD_SIZE)
        v = query_pre_ref[:, cols]
        v = v * head_norm(v) * gain_ref[...]
        queries = (v * cosine_ref[...] + turn_half(v) * sine_ref[...]).astype(bf16)
        queries_ref[:, cols] = queries
        probs = head_softmax(queries, keys, visible).astype(bf16)
        attended_ref[:, cols] = dot(probs, values).astype(bf16)


def attention(query_pre, gain, cosine, sine, kv_all):
    rows, wide = query_pre.shape
    keys = kv_all.shape[0]
    group = wide // KEY_VALUE_HEADS
    small = pl.BlockSpec((rows, HEAD_SIZE), lambda i: (0, 0))
    block = pl.BlockSpec((rows, group), lambda i: (0, i))
    return pl.pallas_call(
        attention_kernel,
        grid=(KEY_VALUE_HEADS,),
        out_shape=[jax.ShapeDtypeStruct((rows, wide), bf16)] * 2,
        in_specs=[
            block,
            pl.BlockSpec((1, HEAD_SIZE), lambda i: (0, 0)),
            small,
            small,
            pl.BlockSpec((keys, HEAD_SIZE), lambda i: (0, i)),
            pl.BlockSpec((keys, HEAD_SIZE), lambda i: (0, KEY_VALUE_HEADS + i)),
        ],
        out_specs=[block, block],
        compiler_params=pltpu.CompilerParams(vmem_limit_bytes=48 * 2**20),
    )(query_pre, gain.reshape(1, HEAD_SIZE), cosine, sine, kv_all, kv_all)


def transposed_dot(a, b):
    return lax.dot_general(a, b, (((0,), (0,)), ((), ())), preferred_element_type=f32)


def attention_back_kernel(
    query_pre_ref,
    gain_ref,
    cosine_ref,
    sine_ref,
    keys_ref,
    values_ref,
    queries_ref,
    grad_ref,
    pre_grad_ref,
    key_grad_ref,
    value_grad_ref,
    gain_grad_ref,
):
    rows = query_pre_ref.shape[0]
    visible = visible_keys(rows, keys_ref.shape[0])
    keys = keys_ref[...]
    values = values_ref[...]
    scale = HEAD_SIZE ** (-0.5)
    gain_grad = jnp.zeros((rows, HEAD_SIZE), f32)
    key_grad = jnp.zeros(keys_ref.shape, f32)
    value_grad = jnp.zeros(keys_ref.shape, f32)
    for h in range(query_pre_ref.shape[1] // HEAD_SIZE):
        cols = slice(h * HEAD_SIZE, (h + 1) * HEAD_SIZE)
        queries = queries_ref[:, cols]
        grad = grad_ref[:, cols]
        probs = head_softmax(queries, keys, visible)
        prob_grad = lax.dot_general(
            grad, values, (((1,), (1,)), ((), ())), preferred_element_type=f32
        )
        delta = jnp.sum(probs * prob_grad, axis=-1, keepdims=True)
        score_grad = (probs * (prob_grad - delta)).astype(bf16)
        key_grad = key_grad + transposed_dot(score_grad, queries)
        value_grad = value_grad + transposed_dot(probs.astype(bf16), grad)
        u = dot(score_grad, keys) * scale
        u = u * cosine_ref[...] + turn_half(u * sine_ref[...])
        v = query_pre_ref[:, cols]
        inv = head_norm(v)
        gain_grad = gain_grad + u * v * inv
        pre_grad_ref[:, cols] = norm_back(v, inv, gain_ref[...], u).astype(bf16)
    key_grad_ref[...] = (key_grad * scale).astype(key_grad_ref.dtype)
    value_grad_ref[...] = value_grad.astype(value_grad_ref.dtype)
    gain_grad_ref[0] = jnp.sum(gain_grad, axis=0, keepdims=True)


def attention_back(query_pre, gain, cosine, sine, kv_all, queries, attended_grad):
    rows, wide = query_pre.shape
    keys, both = kv_all.shape
    group = wide // KEY_VALUE_HEADS
    small = pl.BlockSpec((rows, HEAD_SIZE), lambda i: (0, 0))
    block = pl.BlockSpec((rows, group), lambda i: (0, i))
    return pl.pallas_call(
        attention_back_kernel,
        grid=(KEY_VALUE_HEADS,),
        out_shape=[
            jax.ShapeDtypeStruct((rows, wide), bf16),
            jax.ShapeDtypeStruct((keys, both // 2), f32),
            jax.ShapeDtypeStruct((keys, both // 2), f32),
            jax.ShapeDtypeStruct((KEY_VALUE_HEADS, 1, HEAD_SIZE), f32),
        ],
        in_specs=[
            block,
            pl.BlockSpec((1, HEAD_SIZE), lambda i: (0, 0)),
            small,
            small,
            pl.BlockSpec((keys, HEAD_SIZE), lambda i: (0, i)),
            pl.BlockSpec((keys, HEAD_SIZE), lambda i: (0, KEY_VALUE_HEADS + i)),
            block,
            block,
        ],
        out_specs=[
            block,
            pl.BlockSpec((keys, HEAD_SIZE), lambda i: (0, i)),
            pl.BlockSpec((keys, HEAD_SIZE), lambda i: (0, i)),
            pl.BlockSpec((1, 1, HEAD_SIZE), lambda i: (i, 0, 0)),
        ],
        compiler_params=pltpu.CompilerParams(vmem_limit_bytes=48 * 2**20),
    )(
        query_pre, gain.reshape(1, HEAD_SIZE), cosine, sine, kv_all, kv_all, queries, attended_grad
    )


def gather_small(v):
    if not small_plane():
        return lax.all_gather(v, plane, axis=0, tiled=True)
    v = jnp.concatenate([v, over_y(v)], axis=0)
    v = jnp.concatenate([v, core(v)], axis=0)
    v = jnp.concatenate([v, over_x(v)], axis=0)
    blocks = v.reshape(lax.axis_size(plane), -1, v.shape[1])
    slot = jnp.arange(blocks.shape[0])
    device = slot // 4 * 4 + slot % 2 * 2 + slot // 2 % 2
    blocks = jnp.take(blocks, device ^ lax.axis_index(plane), axis=0)
    return blocks.reshape(v.shape)


def halves(v):
    half = v.shape[1] // 2
    mine = lax.axis_index("expert") * half
    return (
        lax.dynamic_slice_in_dim(v, mine, half, axis=1),
        lax.dynamic_slice_in_dim(v, half - mine, half, axis=1),
    )


def join_halves(mine, other):
    lower = lax.axis_index("expert") == 0
    return jnp.concatenate(
        [jnp.where(lower, mine, other), jnp.where(lower, other, mine)], axis=1
    )


def dot(a, b):
    return jnp.dot(a, b, preferred_element_type=f32)


def ctx_sum(v):
    if not small_plane():
        return lax.psum_scatter(v, "ctx", scatter_dimension=1, tiled=True).astype(f32)
    member = lax.axis_index("ctx")

    def block(j):
        return lax.dynamic_slice_in_dim(v, (member ^ j) * PROMPT_DEV, PROMPT_DEV, axis=1)

    near = block(0).astype(f32) + core(block(1)).astype(f32)
    far = (block(2).astype(f32) + core(block(3)).astype(f32)).astype(bf16)
    return near + over_x(far).astype(f32)


def body(
    hidden_in,
    attn_gain,
    query_weight,
    key_matrix,
    value_matrix,
    query_gain,
    key_gain,
    output_weight,
    ffn_gain,
    router_weight,
    gate_up,
    down_proj,
    routes,
    out_grad,
):
    ctx_count = lax.axis_size("ctx")
    spread_count = lax.axis_size(plane)
    dp_count = lax.axis_size("dp")
    device_count = dp_count * spread_count
    local_experts = gate_up.shape[0]
    count_of_rows = hidden_in.shape[0]
    prompt_all = PROMPT_DEV * ctx_count
    hidden_ff = gate_up.shape[2] // 2
    order = relative()
    member = lax.axis_index("ctx")
    offsets = jnp.arange(count_of_rows, dtype=jnp.int32)
    position = jnp.where(
        offsets < PROMPT_DEV, member * PROMPT_DEV + offsets, prompt_all + offsets - PROMPT_DEV
    )
    cosine, rope_sine = angles(position, HEAD_SIZE)
    narrow = KEY_VALUE_HEADS * HEAD_SIZE
    wide = QUERY_HEADS * HEAD_SIZE
    route_rows = gather_small(routes)
    inputs = hidden_in.astype(f32)
    scale_in = rms_scale(inputs)
    signed_sine = rope_sine * jnp.where(jnp.arange(HEAD_SIZE) < HEAD_SIZE // 2, -1.0, 1.0)
    if small_plane():
        (
            kv_other,
            q_other,
            o_other,
            g_rows,
            normalized_input,
            query_pre,
            key_value_pre,
            kv_low,
            kv_blocks,
        ) = fetch_and_project(
            hidden_in, attn_gain, key_gain, cosine, signed_sine, key_matrix, value_matrix,
            query_weight, output_weight, out_grad,
        )
        kv_weights = [jnp.concatenate([key_matrix, value_matrix], axis=1), kv_other]
        q_weights = [query_weight, q_other]
        o_weights = [output_weight, o_other]
        kv_blocks = kv_blocks.reshape(prompt_all, 2 * narrow)
    else:
        full = [
            lax.all_gather(w, "expert", axis=0, tiled=True)
            for w in (
                jnp.concatenate([key_matrix, value_matrix], axis=1),
                query_weight,
                output_weight,
            )
        ]
        kv_weights, q_weights, o_weights = [[w] for w in full]
        g_rows = lax.all_gather(out_grad, plane, axis=0, tiled=True)
        normalized_input = (inputs * scale_in * attn_gain).astype(bf16)
        query_pre = dot(normalized_input, q_weights[0])
        key_value_pre = dot(normalized_input, kv_weights[0])
        key_pre = key_value_pre[:, :narrow].reshape(count_of_rows, KEY_VALUE_HEADS, HEAD_SIZE)
        key_low = rotate(
            key_pre * rms_scale(key_pre) * key_gain, cosine[:, None, :], rope_sine[:, None, :]
        ).astype(bf16)
        kv_low = jnp.concatenate(
            [key_low.reshape(count_of_rows, narrow), key_value_pre[:, narrow:].astype(bf16)],
            axis=1,
        )
        kv_blocks = lax.all_gather(kv_low[:PROMPT_DEV], "ctx", axis=0, tiled=True)

    def forward_dot(v, weights):
        if len(weights) == 1:
            return dot(v, weights[0])
        mine, other = halves(v)
        return dot(mine, weights[0]) + dot(other, weights[1])

    def backward_dot(v, weights):
        parts = [dot(v, w.T) for w in weights]
        return parts[0] if len(parts) == 1 else join_halves(*parts)

    key_before_norm = key_value_pre[:, :narrow].reshape(
        count_of_rows, KEY_VALUE_HEADS, HEAD_SIZE
    )
    key_inv = rms_scale(key_before_norm)
    kv_all = jnp.concatenate([kv_blocks, kv_low[PROMPT_DEV:]], axis=0)
    queries, attended = attention(query_pre, query_gain, cosine, signed_sine, kv_all)
    residual = inputs + forward_dot(attended, o_weights)
    scale_ffn = rms_scale(residual)
    ffn_in = (residual * scale_ffn * ffn_gain).astype(bf16)

    expert_count = local_experts * spread_count
    expert_ids = jnp.arange(expert_count, dtype=jnp.int32)

    def gates_of(some_rows, some_routes):
        logits = dot(some_rows, router_weight)
        chosen = jnp.any(some_routes[:, :, None] == expert_ids[None, None, :], axis=1)
        logits = jnp.where(chosen, logits, masked)
        raised = jnp.where(
            chosen, jnp.exp(logits - jnp.max(logits, axis=-1, keepdims=True)), 0.0
        )
        return raised / jnp.sum(raised, axis=-1, keepdims=True)

    gates = gates_of(ffn_in, routes)
    if small_plane():
        rows, hidden_low, projected_grad, gate_grads = experts_of_plane(
            ffn_in, route_rows, router_weight, g_rows, gate_up, down_proj
        )
    else:
        rows = lax.all_gather(ffn_in, plane, axis=0, tiled=True)
        first_expert = lax.axis_index(plane) * local_experts
        gates_mine = lax.dynamic_slice_in_dim(
            gates_of(rows, route_rows), first_expert, local_experts, axis=1
        )
        gate_grads, hiddens, projected_grads = [], [], []
        for which in range(local_experts):
            gate = gates_mine[:, which : which + 1]
            projected = dot(rows, gate_up[which])
            back = dot(g_rows, down_proj[which].T)
            gate_part = projected[:, :hidden_ff]
            up_part = projected[:, hidden_ff:]
            sigmoid_gate = jax.nn.sigmoid(gate_part)
            hidden = gate_part * sigmoid_gate * up_part
            gate_grads.append(jnp.sum(hidden * back, axis=-1))
            hiddens.append((gate * hidden).astype(bf16))
            back = gate * back
            gate_back = back * up_part * sigmoid_gate * (1.0 + gate_part * (1.0 - sigmoid_gate))
            up_back = back * gate_part * sigmoid_gate
            projected_grads.append(jnp.concatenate([gate_back, up_back], axis=-1).astype(bf16))
        hidden_low = jnp.concatenate(hiddens, axis=1)
        projected_grad = jnp.concatenate(projected_grads, axis=1)
    down_local = dot(hidden_low.T, g_rows).astype(bf16)
    gate_up_local = dot(rows.T, projected_grad).astype(bf16)
    down_low = lax.psum_scatter(
        down_local.reshape(down_proj.shape), "dp", scatter_dimension=1, tiled=True
    )
    gate_up_low = lax.psum_scatter(gate_up_local, "dp", scatter_dimension=0, tiled=True)
    down_grad = down_low.astype(f32)
    gate_up_grad = jnp.stack(
        [
            gate_up_low[:, i * 2 * hidden_ff : (i + 1) * 2 * hidden_ff].astype(f32)
            for i in range(local_experts)
        ]
    )
    projected_grad, hidden_low = lax.optimization_barrier(
        ((projected_grad, hidden_low), gate_up_local, down_local)
    )[0]
    if small_plane():
        back = plane_sum(projected_grad, gate_up, gate_grads, 3)
        back_sum = back[:, :MODEL_WIDTH]
        gate_grad = (
            back[:, MODEL_WIDTH : MODEL_WIDTH + expert_count]
            + back[:, MODEL_WIDTH + expert_count : MODEL_WIDTH + 2 * expert_count]
        )
        moe_sum = plane_sum(after(hidden_low, back), down_proj, None, 4)
    else:
        moe_part = 0.0
        row_part = 0.0
        for which in range(local_experts):
            grads = projected_grad[:, which * 2 * hidden_ff : (which + 1) * 2 * hidden_ff]
            hidden = hidden_low[:, which * hidden_ff : (which + 1) * hidden_ff]
            row_part = row_part + dot(grads, gate_up[which].T)
            moe_part = moe_part + dot(hidden, down_proj[which])
        moe_sum, back_sum = [
            lax.psum_scatter(v.astype(bf16), plane, scatter_dimension=0, tiled=True).astype(f32)
            for v in (moe_part, row_part)
        ]
        gate_grad = lax.all_to_all(
            jnp.stack(gate_grads, axis=1).reshape(spread_count, count_of_rows, local_experts),
            plane,
            split_axis=0,
            concat_axis=0,
            tiled=True,
        )
        gate_grad = gate_grad.transpose(1, 0, 2).reshape(count_of_rows, expert_count)
    block_out = (residual + moe_sum).astype(bf16)
    logit_grad = gates * (gate_grad - jnp.sum(gates * gate_grad, axis=-1, keepdims=True))

    grad_out = out_grad.astype(f32)
    router_local = jnp.dot(ffn_in.T, logit_grad, preferred_element_type=f32)
    ffn_in_grad = back_sum + jnp.dot(
        logit_grad, router_weight.astype(f32).T, precision=highest
    )
    residual_grad = grad_out + norm_back(residual, scale_ffn, ffn_gain, ffn_in_grad)
    ffn_gain_local = jnp.sum(ffn_in_grad * residual * scale_ffn, axis=0)
    branch_low = residual_grad.astype(bf16)
    branch_rows = jnp.concatenate(gather_plane(branch_low), axis=0)
    attended_grad = backward_dot(branch_low, o_weights).astype(bf16)
    query_pre_grad, key_grad_all, value_grad_all, query_gain_parts = attention_back(
        query_pre, query_gain, cosine, signed_sine, kv_all, queries, attended_grad
    )
    query_gain_local = jnp.sum(query_gain_parts, axis=(0, 1))
    pair_grads = jnp.stack([key_grad_all[:prompt_all], value_grad_all[:prompt_all]]).astype(bf16)
    prompt_grads = ctx_sum(pair_grads)
    key_grad = jnp.concatenate([prompt_grads[0], key_grad_all[prompt_all:]], axis=0).reshape(
        count_of_rows, KEY_VALUE_HEADS, HEAD_SIZE
    )
    value_gradient = jnp.concatenate([prompt_grads[1], value_grad_all[prompt_all:]], axis=0)
    key_rot_grad = rotate_back(key_grad, cosine[:, None, :], rope_sine[:, None, :])
    key_gain_local = jnp.sum(key_rot_grad * key_before_norm * key_inv, axis=(0, 1))
    key_pre_grad = (
        norm_back(key_before_norm, key_inv, key_gain, key_rot_grad)
        .astype(bf16)
        .reshape(count_of_rows, KEY_VALUE_HEADS * HEAD_SIZE)
    )
    key_value_grad = jnp.concatenate([key_pre_grad, value_gradient.astype(bf16)], axis=1)
    normed_grad = backward_dot(query_pre_grad, q_weights) + backward_dot(
        key_value_grad, kv_weights
    )
    attn_gain_local = jnp.sum(normed_grad * inputs * scale_in, axis=0)
    hidden_grad = residual_grad + norm_back(inputs, scale_in, attn_gain, normed_grad)

    pre_rows = jnp.concatenate(
        gather_plane(
            jnp.concatenate([query_pre_grad, key_value_grad], axis=1)
        ),
        axis=0,
    )

    def owned(v):
        width = v.shape[1] // device_count
        split = v.reshape(count_of_rows, dp_count, spread_count, width)
        parts = [
            lax.dynamic_index_in_dim(split, o, axis=2, keepdims=False).reshape(
                count_of_rows, dp_count * width
            )
            for o in order
        ]
        return jnp.concatenate(exchange_plane(parts), axis=0)

    normed_owned = owned(after(normalized_input, rows))
    attended_owned = owned(after(attended, rows))
    pre_local = jnp.dot(normed_owned.T, pre_rows, preferred_element_type=f32)
    output_local = jnp.dot(attended_owned.T, branch_rows, preferred_element_type=f32)
    pre_local, output_local = lax.optimization_barrier(
        ((pre_local.astype(bf16), output_local.astype(bf16)), gate_up_low, down_low)
    )[0]
    output_sum = lax.psum_scatter(output_local, "dp", scatter_dimension=0, tiled=True).astype(f32)
    pre_sum = lax.psum_scatter(pre_local, "dp", scatter_dimension=0, tiled=True).astype(f32)

    small = jnp.concatenate(
        [
            v.reshape(device_count, -1)
            for v in (
                attn_gain_local,
                ffn_gain_local,
                query_gain_local,
                key_gain_local,
                router_local,
            )
        ],
        axis=1,
    )
    small = lax.all_to_all(small[:, None], every, split_axis=0, concat_axis=0, tiled=True)
    small = jnp.sum(small[:, 0], axis=0)
    share = MODEL_WIDTH // device_count
    head_share = HEAD_SIZE // device_count
    cuts = [share, share, head_share, head_share, share * expert_count]
    ends = [sum(cuts[: i + 1]) for i in range(5)]
    a_grad, f_grad, q_grad, k_grad, r_grad = [
        small[end - cut : end] for end, cut in zip(ends, cuts)
    ]
    return (
        block_out,
        hidden_grad,
        a_grad,
        pre_sum[:, :wide],
        pre_sum[:, wide : wide + narrow],
        pre_sum[:, wide + narrow :],
        q_grad,
        k_grad,
        output_sum,
        f_grad,
        r_grad.reshape(share, expert_count),
        gate_up_grad,
        down_grad,
    )


def solution(mesh):
    placed = (
        P(("dp", "ctx", "expert"), None),
        P(),
        P("expert", None),
        P("expert", None),
        P("expert", None),
        P(),
        P(),
        P("expert", None),
        P(),
        P(),
        P(("ctx", "expert"), None, None),
        P(("ctx", "expert"), None, None),
        P(("dp", "ctx", "expert"), None),
        P(("dp", "ctx", "expert"), None),
    )
    return jax.shard_map(
        body,
        mesh=mesh,
        in_specs=placed,
        out_specs=(
            P(("dp", "ctx", "expert"), None),
            P(("dp", "ctx", "expert"), None),
            P(("dp", "ctx", "expert")),
            P(("dp", "ctx", "expert"), None),
            P(("dp", "ctx", "expert"), None),
            P(("dp", "ctx", "expert"), None),
            P(("dp", "ctx", "expert")),
            P(("dp", "ctx", "expert")),
            P(("dp", "ctx", "expert"), None),
            P(("dp", "ctx", "expert")),
            P(("dp", "ctx", "expert"), None),
            P(("ctx", "expert"), "dp", None),
            P(("ctx", "expert"), "dp", None),
        ),
        check_vma=False,
    )
```

```python
import math

import jax
import jax.numpy as jnp
from jax import lax
from jax.experimental import pallas as pl
from jax.experimental.pallas import tpu as pltpu
from jax.sharding import PartitionSpec as P

MODEL_WIDTH = 2048
QUERY_HEADS = 32
KEY_VALUE_HEADS = 4
HEAD_SIZE = 128
TOP = 8
PROMPT_DEV = 128


highest = lax.Precision.HIGHEST
epsilon = 1e-06
rope_base = 1000000.0
masked = -1e30
every = ("dp", "ctx", "expert")
plane = ("ctx", "expert")
bf16 = jnp.bfloat16
f32 = jnp.float32


def rms_scale(value_rows):
    return lax.rsqrt(jnp.mean(value_rows * value_rows, axis=-1, keepdims=True) + epsilon)


def norm_back(inputs, inv_rms, norm_gain, gradient):
    weighted = gradient * norm_gain
    return inv_rms * weighted - inputs * inv_rms**3 * jnp.mean(
        weighted * inputs, axis=-1, keepdims=True
    )


def angles(position, head_width):
    freq_index = jnp.arange(head_width // 2, dtype=f32)
    inverse = jnp.exp(-(2.0 * freq_index / head_width) * math.log(rope_base))
    rope_angle = position.astype(f32)[:, None] * inverse[None, :]
    rope_angle = jnp.concatenate([rope_angle, rope_angle], axis=-1)
    return (jnp.cos(rope_angle), jnp.sin(rope_angle))


def rotate(value_rows, cosine, rope_sine):
    half_width = value_rows.shape[-1] // 2
    turned = jnp.concatenate([-value_rows[..., half_width:], value_rows[..., :half_width]], axis=-1)
    return value_rows * cosine + turned * rope_sine


def rotate_back(gradient, cosine, rope_sine):
    shifted = gradient * rope_sine
    half_width = gradient.shape[-1] // 2
    return gradient * cosine + jnp.concatenate(
        [shifted[..., half_width:], -shifted[..., :half_width]], axis=-1
    )


def small_plane():
    return [lax.axis_size(a) for a in every] == [4, 4, 2]


def swap(v, axis, bit):
    return lax.ppermute(v, axis, [(i, i ^ bit) for i in range(lax.axis_size(axis))])


def core(v):
    return swap(v, "ctx", 1)


def over_x(v):
    return swap(v, "ctx", 2)


def over_y(v):
    return swap(v, "expert", 1)


def over_z(v):
    return swap(v, "dp", 1)


def after(v, *earlier):
    return lax.optimization_barrier((v, *earlier))[0]


class Places:
    def __init__(self):
        self.dp = lax.axis_index("dp")
        ctx = lax.axis_index("ctx")
        self.ctx = ctx
        self.z = lax.rem(self.dp, 2)
        self.x = lax.div(ctx, 2)
        self.c = lax.rem(ctx, 2)
        self.y = lax.axis_index("expert")
        self.to_x = {"ctx": (1 - self.x) * 2 + self.c}
        self.to_c = {"ctx": self.x * 2 + 1 - self.c}
        self.to_y = {"expert": 1 - self.y}
        self.to_z = {"dp": self.dp + 1 - 2 * self.z}


def plane_slot(x, c, y):
    return x * 4 + y * 2 + c


def greet(targets):
    barrier = pltpu.get_barrier_semaphore()
    for target in targets:
        pl.semaphore_signal(barrier, inc=1, device_id=target, device_id_type=pl.DeviceIdType.MESH)
    pl.semaphore_wait(barrier, len(targets))


class Sender:
    def __init__(self, send_sem, recv_sem):
        self.send_sem = send_sem
        self.recv_sem = recv_sem
        self.copies = []

    def __call__(self, source, target_ref, device):
        i = len(self.copies)
        copy = pltpu.make_async_remote_copy(
            src_ref=source,
            dst_ref=target_ref,
            send_sem=self.send_sem.at[i],
            recv_sem=self.recv_sem.at[i],
            device_id=device,
            device_id_type=pl.DeviceIdType.MESH,
        )
        copy.start()
        self.copies.append(copy)
        return copy

    def finish(self):
        for copy in self.copies:
            copy.wait_send()


def half_fetch(here, send, sources, other, columns, rows, upper):
    def at(piece, part=None):
        first, size = piece * rows, rows
        if part == 0:
            size = upper
        elif part == 1:
            first, size = first + upper, rows - upper
        return other.at[pl.ds(pl.multiple_of(first, 16), size), columns]

    def piece(z, x, c):
        return z * 4 + x * 2 + c

    z, x, c = here.z, here.x, here.c
    got = {}

    def first():
        mine = piece(z, x, c)
        got["y"] = [
            send(
                source.at[pl.ds(pl.multiple_of(mine * rows, rows), rows), source_columns],
                other.at[pl.ds(pl.multiple_of(mine * rows, rows), rows), target_columns],
                here.to_y,
            )
            for source, source_columns, target_columns in sources
        ]

    def second():
        for copy in got["y"]:
            copy.wait_recv()
        mine = at(piece(z, x, c))
        got["x"] = send(mine, mine, here.to_x)
        got["z"] = send(mine, mine, here.to_z)
        got["c"] = send(mine, mine, here.to_c)

    def third():
        got["x"].wait_recv()
        from_x = piece(z, 1 - x, c)
        got["low"] = send(at(from_x, 1), at(from_x, 1), here.to_z)
        got["xc"] = send(at(from_x), at(from_x), here.to_c)
        got["z"].wait_recv()
        from_z = piece(1 - z, x, c)
        got["top"] = send(at(from_z, 0), at(from_z, 0), here.to_x)
        got["zc"] = send(at(from_z), at(from_z), here.to_c)

    def fourth():
        far = piece(1 - z, 1 - x, c)
        got["low"].wait_recv()
        got["lowc"] = send(at(far, 1), at(far, 1), here.to_c)
        got["top"].wait_recv()
        got["topc"] = send(at(far, 0), at(far, 0), here.to_c)

    def fifth():
        for name in ("c", "xc", "zc", "lowc", "topc"):
            got[name].wait_recv()

    return [first, second, third, fourth, fifth]


def block_gather(here, send, mine, local_sem, blocks, far_over_y=False, columns=None):
    rows = blocks.shape[0] // lax.axis_size(plane)
    half = rows // 2
    x, c, y = here.x, here.c, here.y
    got = {}

    def at(slot, part=None):
        first, size = slot * rows, rows
        if part is not None:
            first, size = first + part * half, half
        rows_of = pl.ds(pl.multiple_of(first, size), size)
        return blocks.at[rows_of] if columns is None else blocks.at[rows_of, columns]

    def first():
        slot = plane_slot(x, c, y)
        got["own"] = pltpu.make_async_copy(mine, at(slot), local_sem)
        got["own"].start()
        got["y"] = send(mine, at(slot), here.to_y)
        got["x"] = send(mine, at(slot), here.to_x)
        got["c"] = send(mine, at(slot), here.to_c)

    def second():
        got["y"].wait_recv()
        from_y = plane_slot(x, c, 1 - y)
        got["yc"] = send(at(from_y), at(from_y), here.to_c)
        if not far_over_y:
            got["top"] = send(at(from_y, 0), at(from_y, 0), here.to_x)
        got["x"].wait_recv()
        from_x = plane_slot(1 - x, c, y)
        got["xc"] = send(at(from_x), at(from_x), here.to_c)
        if far_over_y:
            got["top"] = send(at(from_x, 0), at(from_x, 0), here.to_y)
        got["low"] = send(at(from_x, 1), at(from_x, 1), here.to_y)

    def third():
        far = plane_slot(1 - x, c, 1 - y)
        got["top"].wait_recv()
        got["topc"] = send(at(far, 0), at(far, 0), here.to_c)
        got["low"].wait_recv()
        got["lowc"] = send(at(far, 1), at(far, 1), here.to_c)

    def fourth():
        for name in ("c", "yc", "xc", "topc", "lowc"):
            got[name].wait_recv()
        got["own"].wait()

    return [first, second, third, fourth], got


def turn_half(v):
    return pltpu.roll(v, v.shape[-1] // 2, axis=1)


def head_norm(v):
    return lax.rsqrt(jnp.mean(v * v, axis=-1, keepdims=True) + epsilon)


def fetch_kernel(
    hidden_ref,
    attn_gain_ref,
    query_gain_ref,
    key_gain_ref,
    ffn_gain_ref,
    cosine_ref,
    sine_ref,
    key_ref,
    value_ref,
    query_ref,
    output_ref,
    grad_ref,
    routes_ref,
    kv_out,
    q_out,
    o_out,
    g_blocks,
    route_blocks,
    kv_all_out,
    normed_owned,
    attended_owned,
    query_pre_ref,
    key_pre_ref,
    queries_ref,
    residual_ref,
    ffn_ref,
    normed_ref,
    attended_ref,
    kv_own,
    kv_other,
    q_own,
    q_other,
    o_own,
    o_other,
    kv_pre,
    kv_low,
    kv_all,
    send_sem,
    recv_sem,
    local_sem,
):
    here = Places()
    greet([here.to_y, here.to_z, here.to_c, here.to_x])
    send = Sender(send_sem, recv_sem)
    count, width = hidden_ref.shape
    half = width // 2
    narrow = key_ref.shape[1]
    wide = query_ref.shape[1]
    prompt_all = kv_all.shape[0] - (count - PROMPT_DEV)
    spread, groups = lax.axis_size(plane), lax.axis_size("dp")
    tile = 512
    loads = [
        pltpu.make_async_copy(key_ref, kv_own.at[:, pl.ds(0, narrow)], local_sem.at[0]),
        pltpu.make_async_copy(value_ref, kv_own.at[:, pl.ds(narrow, narrow)], local_sem.at[1]),
        pltpu.make_async_copy(query_ref, q_own, local_sem.at[2]),
        pltpu.make_async_copy(output_ref, o_own, local_sem.at[3]),
    ]
    stores = [
        pltpu.make_async_copy(kv_other, kv_out, local_sem.at[4]),
        pltpu.make_async_copy(q_other, q_out, local_sem.at[5]),
        pltpu.make_async_copy(o_other, o_out, local_sem.at[6]),
        pltpu.make_async_copy(kv_all, kv_all_out, local_sem.at[7]),
    ]

    def part_of(size, which):
        first = here.y * size if which == 0 else size - here.y * size
        return pl.ds(pl.multiple_of(first, size), size)

    def project(source, weight, out, which, first, count_of_tiles, add):
        rows = part_of(weight.shape[0], which)

        @pl.loop(first, first + count_of_tiles)
        def _(i):
            cols = pl.ds(pl.multiple_of(i * tile, tile), tile)
            part = dot(source[:, rows], weight[:, cols])
            out[:, cols] = out[:, cols] + part if add else part

    def start():
        for load in loads:
            load.start()
        inputs = hidden_ref[...].astype(f32)
        normed_ref[...] = (inputs * head_norm(inputs) * attn_gain_ref[...]).astype(bf16)

    def own_part():
        share = width // (spread * groups)
        for s in range(spread):
            normed_owned[s] = jnp.concatenate(
                [
                    normed_ref[:, (d * spread + s) * share : (d * spread + s + 1) * share]
                    for d in range(groups)
                ],
                axis=1,
            )
        for load in loads[:3]:
            load.wait()
        project(normed_ref, kv_own, kv_pre, 0, 0, 2 * narrow // tile, False)
        project(normed_ref, q_own, query_pre_ref, 0, 0, wide // tile, False)

    exchange = {}

    def keys_part():
        project(normed_ref, kv_other, kv_pre, 1, 0, 2 * narrow // tile, True)
        stores[0].start()
        key_pre_ref[...] = kv_pre[:, :narrow]
        for h in range(narrow // HEAD_SIZE):
            cols = slice(h * HEAD_SIZE, (h + 1) * HEAD_SIZE)
            v = kv_pre[:, cols]
            v = v * head_norm(v) * key_gain_ref[...]
            kv_low[:, cols] = (v * cosine_ref[...] + turn_half(v) * sine_ref[...]).astype(bf16)
        kv_low[:, narrow:] = kv_pre[:, narrow:].astype(bf16)
        kv_all[prompt_all:, :] = kv_low[PROMPT_DEV:, :]
        source = kv_low.at[pl.ds(0, PROMPT_DEV)]
        slot = kv_all.at[pl.ds(pl.multiple_of(here.ctx * PROMPT_DEV, PROMPT_DEV), PROMPT_DEV)]
        exchange["own"] = pltpu.make_async_copy(source, slot, local_sem.at[8])
        exchange["own"].start()
        exchange["c"] = send(source, slot, here.to_c)
        exchange["x"] = send(source, slot, here.to_x)

    def keys_forward():
        exchange["x"].wait_recv()
        first = ((1 - here.x) * 2 + here.c) * PROMPT_DEV
        slot = kv_all.at[pl.ds(pl.multiple_of(first, PROMPT_DEV), PROMPT_DEV)]
        exchange["xc"] = send(slot, slot, here.to_c)

    def queries_first():
        project(normed_ref, q_other, query_pre_ref, 1, 0, wide // tile // 2, True)

    def queries_rest():
        stores[1].start()
        project(
            normed_ref, q_other, query_pre_ref, 1, wide // tile // 2, wide // tile // 2, True
        )
        for name in ("c", "xc"):
            exchange[name].wait_recv()
        exchange["own"].wait()
        stores[3].start()

    group = 4
    pieces = 4

    def attend(part):
        visible = visible_keys(count, kv_all.shape[0])
        blocks = wide // HEAD_SIZE // group // pieces

        @pl.loop(part * blocks, (part + 1) * blocks)
        def _(i):
            first = lax.div(i * group, wide // narrow) * HEAD_SIZE
            keys = kv_all[:, pl.ds(pl.multiple_of(first, HEAD_SIZE), HEAD_SIZE)]
            values = kv_all[:, pl.ds(pl.multiple_of(narrow + first, HEAD_SIZE), HEAD_SIZE)]
            for h in range(group):
                cols = pl.ds(pl.multiple_of((i * group + h) * HEAD_SIZE, HEAD_SIZE), HEAD_SIZE)
                v = query_pre_ref[:, cols]
                v = v * head_norm(v) * query_gain_ref[...]
                queries = (v * cosine_ref[...] + turn_half(v) * sine_ref[...]).astype(bf16)
                queries_ref[:, cols] = queries
                probs = head_softmax(queries, keys, visible).astype(bf16)
                attended = dot(probs, values).astype(bf16)
                attended_ref[:, cols] = attended
                head = i * group + h
                at = pl.multiple_of(lax.div(head, spread) * HEAD_SIZE, HEAD_SIZE)
                attended_owned[lax.rem(head, spread), :, pl.ds(at, HEAD_SIZE)] = attended

    def output_own():
        loads[3].wait()
        project(attended_ref, o_own, residual_ref, 0, 0, width // tile, False)

    def finish_rows():
        stores[2].start()
        project(attended_ref, o_other, residual_ref, 1, 0, width // tile, True)
        residual = residual_ref[...] + hidden_ref[...].astype(f32)
        residual_ref[...] = residual
        ffn_ref[...] = (residual * head_norm(residual) * ffn_gain_ref[...]).astype(bf16)

    low, high = pl.ds(0, wide // 2), pl.ds(wide // 2, wide // 2)
    o_low, o_high = pl.ds(0, width // 2), pl.ds(width // 2, width // 2)
    rows, o_rows = half // 8, output_ref.shape[0] // 8
    kv, qa, qb, oa, ob, g, r = [
        half_fetch(
            here,
            send,
            [
                (key_ref, pl.ds(0, narrow), pl.ds(0, narrow)),
                (value_ref, pl.ds(0, narrow), pl.ds(narrow, narrow)),
            ],
            kv_other,
            pl.ds(0, 2 * narrow),
            rows,
            rows // 2,
        ),
        half_fetch(here, send, [(query_ref, low, low)], q_other, low, rows, rows // 2),
        half_fetch(here, send, [(query_ref, high, high)], q_other, high, rows, rows // 2),
        half_fetch(here, send, [(output_ref, o_low, o_low)], o_other, o_low, o_rows, o_rows // 4),
        half_fetch(
            here, send, [(output_ref, o_high, o_high)], o_other, o_high, o_rows, o_rows // 4
        ),
        block_gather(here, send, grad_ref, local_sem.at[9], g_blocks, True)[0],
        block_gather(here, send, routes_ref, local_sem.at[10], route_blocks)[0],
    ]
    steps = [
        kv[0], start, kv[1], qa[0], kv[2], own_part, qa[1], qb[0],
        kv[3], qa[2], qb[1], oa[0], kv[4], keys_part, qa[3], qb[2], oa[1], ob[0],
        keys_forward, qa[4], queries_first, qb[3], ob[1], qb[4], queries_rest,
        oa[2], g[0], r[0], lambda: attend(0), lambda: attend(1),
        oa[3], ob[2], g[1], r[1], lambda: attend(2), lambda: attend(3), oa[4], output_own,
        ob[3], g[2], r[2], ob[4], finish_rows, g[3], r[3],
    ]
    for step in steps:
        step()
    for store in stores:
        store.wait()
    send.finish()


def fetch_and_attend(
    hidden_in, attn_gain, query_gain, key_gain, ffn_gain, cosine, sine, key_matrix, value_matrix,
    query_weight, output_weight, out_grad, routes,
):
    rows, width = hidden_in.shape
    half, wide = query_weight.shape
    narrow = key_matrix.shape[1]
    spread = lax.axis_size(plane)
    keys = lax.axis_size("ctx") * PROMPT_DEV + rows - PROMPT_DEV
    vmem = pl.BlockSpec(memory_space=pltpu.VMEM)
    anywhere = pl.BlockSpec(memory_space=pl.ANY)
    copies = 5 * 10 + 1 + 2 * 9 + 3
    return pl.pallas_call(
        fetch_kernel,
        out_shape=[
            jax.ShapeDtypeStruct((half, 2 * narrow), bf16),
            jax.ShapeDtypeStruct((half, wide), bf16),
            jax.ShapeDtypeStruct(output_weight.shape, bf16),
            jax.ShapeDtypeStruct((spread * rows, width), bf16),
            jax.ShapeDtypeStruct((spread * rows, routes.shape[1]), jnp.int32),
            jax.ShapeDtypeStruct((keys, 2 * narrow), bf16),
            jax.ShapeDtypeStruct((spread, rows, width // spread), bf16),
            jax.ShapeDtypeStruct((spread, rows, wide // spread), bf16),
            jax.ShapeDtypeStruct((rows, wide), f32),
            jax.ShapeDtypeStruct((rows, narrow), f32),
            jax.ShapeDtypeStruct((rows, wide), bf16),
            jax.ShapeDtypeStruct((rows, width), f32),
            jax.ShapeDtypeStruct((rows, width), bf16),
        ],
        in_specs=[vmem] * 7 + [anywhere] * 6,
        out_specs=[anywhere] * 6 + [vmem] * 7,
        scratch_shapes=[
            pltpu.VMEM((rows, width), bf16),
            pltpu.VMEM((rows, wide), bf16),
            pltpu.VMEM((half, 2 * narrow), bf16),
            pltpu.VMEM((half, 2 * narrow), bf16),
            pltpu.VMEM((half, wide), bf16),
            pltpu.VMEM((half, wide), bf16),
            pltpu.VMEM(output_weight.shape, bf16),
            pltpu.VMEM(output_weight.shape, bf16),
            pltpu.VMEM((rows, 2 * narrow), f32),
            pltpu.VMEM((rows, 2 * narrow), bf16),
            pltpu.VMEM((keys, 2 * narrow), bf16),
            pltpu.SemaphoreType.DMA((copies,)),
            pltpu.SemaphoreType.DMA((copies,)),
            pltpu.SemaphoreType.DMA((11,)),
        ],
        compiler_params=pltpu.CompilerParams(
            collective_id=1, has_side_effects=True, vmem_limit_bytes=60 * 2**20
        ),
        cost_estimate=pl.CostEstimate(
            flops=2 * rows * width * (2 * wide + 2 * narrow) * 2,
            bytes_accessed=60 * 2**20,
            transcendentals=0,
        ),
    )(
        hidden_in, attn_gain.reshape(1, width), query_gain.reshape(1, HEAD_SIZE),
        key_gain.reshape(1, HEAD_SIZE), ffn_gain.reshape(1, width), cosine, sine,
        key_matrix, value_matrix, query_weight, output_weight, out_grad, routes,
    )


def chip_rows(x, y, rows):
    first = plane_slot(x, 0, y) * rows
    return pl.ds(pl.multiple_of(first, rows), 2 * rows)


def expert_chunk(some, first, rows_v, g_v, gate_up_v, down_v, hidden_v, grad_v, total_v, gate, mark):
    ff = down_v.shape[0]
    tile = 256

    @pl.loop(0, ff // tile, unroll=True)
    def _(f):
        at = pl.multiple_of(f * tile, tile)
        a = dot(rows_v[some, :], gate_up_v[:, pl.ds(at, tile)])
        b = dot(rows_v[some, :], gate_up_v[:, pl.ds(ff + at, tile)])
        q = lax.dot_general(
            g_v[some, :],
            down_v[pl.ds(at, tile), :],
            (((1,), (1,)), ((), ())),
            preferred_element_type=f32,
        )
        s = 1.0 / (1.0 + jnp.exp(-a))
        raised_a = a * s
        hidden = raised_a * b
        total_v[...] = total_v[...] + jnp.where(
            mark, jnp.sum(hidden * q, axis=-1, keepdims=True), 0.0
        )
        back = gate * q
        hidden_v[some, pl.ds(at, tile)] = (gate * hidden).astype(bf16)
        grad_v[some, pl.ds(at, tile)] = (back * b * s * (1.0 + a * (1.0 - s))).astype(bf16)
        grad_v[some, pl.ds(ff + at, tile)] = (back * raised_a).astype(bf16)


def first_expert_kernel(
    ffn_ref,
    routes_ref,
    router_ref,
    g_hbm,
    gate_up_hbm,
    down_hbm,
    rows_out,
    hidden_out,
    grad_out,
    gates_ref,
    gate_grad_ref,
    rows_v,
    g_v,
    gate_up_v,
    down_v,
    hidden_v,
    grad_v,
    total_v,
    send_sem,
    recv_sem,
    local_sem,
):
    here = Places()
    greet([here.to_y, here.to_c, here.to_x])
    send = Sender(send_sem, recv_sem)
    count = ffn_ref.shape[0]
    experts = router_ref.shape[1]
    local_experts = down_hbm.shape[0]
    stages, got = block_gather(here, send, ffn_ref, local_sem.at[0], rows_v)
    stages[0]()
    loads = [
        pltpu.make_async_copy(gate_up_hbm.at[0], gate_up_v, local_sem.at[1]),
        pltpu.make_async_copy(down_hbm.at[0], down_v, local_sem.at[2]),
        pltpu.make_async_copy(g_hbm, g_v, local_sem.at[3]),
    ]
    for load in loads:
        load.start()
    first_expert = plane_index(here) * local_experts
    stores = []

    def chunk(x, y):
        some = chip_rows(x, y, count)
        logits = dot(rows_v[some, :], router_ref[...])
        ids = lax.broadcasted_iota(jnp.int32, logits.shape, 1)
        routes = routes_ref[some, :]
        chosen = ids < 0
        for k in range(routes.shape[1]):
            chosen = chosen | (routes[:, k : k + 1] == ids)
        logits = jnp.where(chosen, logits, masked)
        raised = jnp.exp(logits - jnp.max(logits, axis=-1, keepdims=True))
        raised = jnp.where(chosen, raised, 0.0)
        gates = raised / jnp.sum(raised, axis=-1, keepdims=True)
        lane = lax.broadcasted_iota(jnp.int32, total_v.shape, 1)
        total_v[...] = jnp.zeros(total_v.shape, f32)
        columns = [
            jnp.sum(jnp.where(ids == first_expert + e, gates, 0.0), axis=-1, keepdims=True)
            for e in range(local_experts)
        ]
        spread = jnp.zeros(total_v.shape, f32)
        for e in range(local_experts):
            spread = jnp.where(lane == e, columns[e], spread)
        gates_ref[some, :] = spread
        mark = (lane == first_expert) | (lane == first_expert + experts)
        expert_chunk(
            some, 0, rows_v, g_v, gate_up_v, down_v, hidden_v, grad_v, total_v, columns[0], mark
        )
        gate_grad_ref[some, :] = total_v[...]
        for source, target in ((hidden_v, hidden_out), (grad_v, grad_out), (rows_v, rows_out)):
            store = pltpu.make_async_copy(
                source.at[some, :], target.at[some, :], local_sem.at[4 + len(stores)]
            )
            store.start()
            stores.append(store)

    x, y = here.x, here.y
    for name in ("c", "own"):
        arrive(got, name)
    for load in loads:
        load.wait()
    chunk(x, y)
    stages[1]()
    arrive(got, "yc")
    chunk(x, 1 - y)
    stages[2]()
    arrive(got, "xc")
    chunk(1 - x, y)
    arrive(got, "topc")
    arrive(got, "lowc")
    chunk(1 - x, 1 - y)
    for store in stores:
        store.wait()
    send.finish()


def gather_first_expert(ffn_in, route_rows, router_weight, g_rows, gate_up, down_proj):
    ff, width = down_proj.shape[1:]
    total = route_rows.shape[0]
    vmem = pl.BlockSpec(memory_space=pltpu.VMEM)
    anywhere = pl.BlockSpec(memory_space=pl.ANY)
    return pl.pallas_call(
        first_expert_kernel,
        out_shape=[
            jax.ShapeDtypeStruct((total, width), bf16),
            jax.ShapeDtypeStruct((total, ff), bf16),
            jax.ShapeDtypeStruct((total, 2 * ff), bf16),
            jax.ShapeDtypeStruct((total, 128), f32),
            jax.ShapeDtypeStruct((total, 128), f32),
        ],
        in_specs=[vmem] * 3 + [anywhere] * 3,
        out_specs=[anywhere] * 3 + [vmem] * 2,
        scratch_shapes=[
            pltpu.VMEM((total, width), bf16),
            pltpu.VMEM((total, width), bf16),
            pltpu.VMEM(gate_up.shape[1:], bf16),
            pltpu.VMEM(down_proj.shape[1:], bf16),
            pltpu.VMEM((total, ff), bf16),
            pltpu.VMEM((total, 2 * ff), bf16),
            pltpu.VMEM((2 * ffn_in.shape[0], 128), f32),
            pltpu.SemaphoreType.DMA((9,)),
            pltpu.SemaphoreType.DMA((9,)),
            pltpu.SemaphoreType.DMA((16,)),
        ],
        compiler_params=pltpu.CompilerParams(
            collective_id=2, has_side_effects=True, vmem_limit_bytes=56 * 2**20
        ),
        cost_estimate=pl.CostEstimate(
            flops=2 * total * width * 3 * ff,
            bytes_accessed=40 * 2**20,
            transcendentals=0,
        ),
    )(ffn_in, route_rows, router_weight, g_rows, gate_up, down_proj)


def next_expert_kernel(
    which, experts, rows_v, g_v, gates_ref, totals_ref, gate_up_v, down_v, hidden_v, grad_v,
    gate_grad_ref, total_v,
):
    lane = lax.broadcasted_iota(jnp.int32, total_v.shape, 1)
    expert = lax.axis_index(plane) * lax.div(experts, lax.axis_size(plane)) + which
    mark = (lane == expert) | (lane == expert + experts)
    total_v[...] = totals_ref[...]
    gate = jnp.sum(jnp.where(lane == which, gates_ref[...], 0.0), axis=-1, keepdims=True)
    some = pl.ds(0, rows_v.shape[0])
    expert_chunk(
        some, 0, rows_v, g_v, gate_up_v.at[0], down_v.at[0], hidden_v, grad_v, total_v, gate, mark
    )
    total = total_v[...]
    high = total.astype(bf16).astype(f32)
    gate_grad_ref[...] = jnp.where(lane < experts, high, total - high).astype(bf16)


def last_expert(which, experts, rows, g_rows, gates, totals, gate_up, down_proj):
    ff, width = down_proj.shape[1:]
    total = rows.shape[0]
    step = total // 4

    def block(columns):
        return pl.BlockSpec((step, columns), lambda i: (i, 0))

    def whole(shape):
        return pl.BlockSpec((1,) + shape[1:], lambda i: (which, 0, 0))

    def kernel(*refs):
        next_expert_kernel(which, experts, *refs)

    return pl.pallas_call(
        kernel,
        grid=(4,),
        out_shape=[
            jax.ShapeDtypeStruct((total, ff), bf16),
            jax.ShapeDtypeStruct((total, 2 * ff), bf16),
            jax.ShapeDtypeStruct((total, 128), bf16),
        ],
        in_specs=[
            block(width), block(width), block(128), block(128),
            whole(gate_up.shape), whole(down_proj.shape),
        ],
        out_specs=[block(ff), block(2 * ff), block(128)],
        scratch_shapes=[pltpu.VMEM((step, 128), f32)],
        compiler_params=pltpu.CompilerParams(vmem_limit_bytes=56 * 2**20),
        cost_estimate=pl.CostEstimate(flops=10**6, bytes_accessed=10**6, transcendentals=0),
    )(rows, g_rows, gates, totals, gate_up, down_proj)


def weight_grad_kernel(
    query_grad, kv_grad, branch, attended_owned, normed_owned, out_local, pre_local,
    pre_v, branch_v, attended_v, normed_v, send_sem, recv_sem, local_sem,
):
    here = Places()
    greet([here.to_y, here.to_c, here.to_x])
    send = Sender(send_sem, recv_sem)
    count, wide = query_grad.shape
    narrow = kv_grad.shape[1]
    spread = lax.axis_size(plane)
    tile = 1024
    half = wide // 2
    low, high, last = pl.ds(0, half), pl.ds(half, half), pl.ds(wide, narrow)
    b, _ = block_gather(here, send, branch, local_sem.at[0], branch_v)
    qa, _ = block_gather(
        here, send, query_grad.at[:, low], local_sem.at[1], pre_v, False, low
    )
    qb, _ = block_gather(
        here, send, query_grad.at[:, high], local_sem.at[2], pre_v, False, high
    )
    kv, _ = block_gather(here, send, kv_grad, local_sem.at[3], pre_v, False, last)
    loads = []
    for device in range(spread):
        slot = plane_slot(device // 4, device // 2 % 2, device % 2)
        rows = pl.ds(slot * count, count)
        for source, target in ((attended_owned, attended_v), (normed_owned, normed_v)):
            loads.append(
                pltpu.make_async_copy(
                    source.at[device], target.at[rows], local_sem.at[4 + len(loads)]
                )
            )

    def start():
        for load in loads:
            load.start()

    def product(left, right, out, first, tiles):
        @pl.loop(first, first + tiles)
        def _(i):
            cols = pl.ds(pl.multiple_of(i * tile, tile), tile)
            out[:, cols] = transposed_dot(left[...], right[:, cols]).astype(bf16)

    def output_product():
        for load in loads:
            load.wait()
        product(attended_v, branch_v, out_local, 0, branch.shape[1] // tile)

    steps = [
        b[0], start, b[1], qa[0], b[2], qa[1], qb[0], b[3], output_product,
        qa[2], qb[1], kv[0], qa[3],
        lambda: product(normed_v, pre_v, pre_local, 0, half // tile),
        qb[2], kv[1], qb[3],
        lambda: product(normed_v, pre_v, pre_local, half // tile, half // tile),
        kv[2], kv[3],
        lambda: product(normed_v, pre_v, pre_local, wide // tile, narrow // tile),
    ]
    for step in steps:
        step()
    send.finish()


def weight_grads(query_grad, kv_grad, branch, attended_owned, normed_owned):
    count, wide = query_grad.shape
    narrow, width = kv_grad.shape[1], branch.shape[1]
    spread = lax.axis_size(plane)
    vmem = pl.BlockSpec(memory_space=pltpu.VMEM)
    anywhere = pl.BlockSpec(memory_space=pl.ANY)
    return pl.pallas_call(
        weight_grad_kernel,
        out_shape=[
            jax.ShapeDtypeStruct((attended_owned.shape[2], width), bf16),
            jax.ShapeDtypeStruct((normed_owned.shape[2], wide + narrow), bf16),
        ],
        in_specs=[anywhere] * 5,
        out_specs=[vmem] * 2,
        scratch_shapes=[
            pltpu.VMEM((spread * count, wide + narrow), bf16),
            pltpu.VMEM((spread * count, width), bf16),
            pltpu.VMEM((spread * count, attended_owned.shape[2]), bf16),
            pltpu.VMEM((spread * count, normed_owned.shape[2]), bf16),
            pltpu.SemaphoreType.DMA((36,)),
            pltpu.SemaphoreType.DMA((36,)),
            pltpu.SemaphoreType.DMA((4 + 2 * spread,)),
        ],
        compiler_params=pltpu.CompilerParams(
            collective_id=5, has_side_effects=True, vmem_limit_bytes=56 * 2**20
        ),
        cost_estimate=pl.CostEstimate(flops=10**6, bytes_accessed=10**6, transcendentals=0),
    )(query_grad, kv_grad, branch, attended_owned, normed_owned)


def arrive(got, name):
    copy = got[name]
    copy.wait() if name == "own" else copy.wait_recv()


def plane_index(here):
    return here.ctx * 2 + here.y


def plane_sum_kernel(across, experts, *refs):
    lefts, weight_hbm = refs[:experts], refs[experts]
    extra_ref = refs[experts + 1] if across else None
    refs = refs[experts + 1 + across :]
    (
        out_ref, left_v, weight_v, part_v, core_v, edge_v, last_v, send_sem, recv_sem, local_sem,
    ) = refs
    here = Places()
    greet([here.to_y, here.to_c, here.to_x])
    send = Sender(send_sem, recv_sem)
    count = out_ref.shape[0]
    half = count // 2
    depth = lefts[0].shape[1]
    width = weight_hbm.shape[1] if across else weight_hbm.shape[2]
    tile = 256
    x, y, c = here.x, here.y, here.c
    chips = [(1 - x, 1 - y), (1 - x, y), (x, 1 - y), (x, y)]
    weight_load = pltpu.make_async_copy(weight_hbm, weight_v, local_sem.at[0])
    weight_load.start()
    loads = []
    for k, (cx, cy) in enumerate(chips):
        some = chip_rows(cx, cy, count)
        loads.append(
            [
                pltpu.make_async_copy(
                    left.at[some, :],
                    left_v.at[k, :, pl.ds(e * depth, depth)],
                    local_sem.at[1 + experts * k + e],
                )
                for e, left in enumerate(lefts)
            ]
        )
        for load in loads[-1]:
            load.start()
    weight_load.wait()
    to_core = []

    def compute(k):
        for load in loads[k]:
            load.wait()

        @pl.loop(0, width // tile)
        def _(n):
            cols = pl.ds(pl.multiple_of(n * tile, tile), tile)
            total = None
            for e in range(experts):
                left = left_v[k, :, e * depth : (e + 1) * depth]
                if across:
                    part = lax.dot_general(
                        left,
                        weight_v[e, cols, :],
                        (((1,), (1,)), ((), ())),
                        preferred_element_type=f32,
                    )
                else:
                    part = dot(left, weight_v[e, :, cols])
                total = part if total is None else total + part
            part_v[k, :, cols] = total.astype(bf16)

        if extra_ref is not None:
            part_v[k, :, width:] = extra_ref[chip_rows(*chips[k], count), :]
        to_core.append(
            send(
                part_v.at[k, pl.ds(pl.multiple_of((1 - c) * count, count), count)],
                core_v.at[k],
                here.to_c,
            )
        )

    mine = pl.ds(pl.multiple_of(c * count, count), count)

    def chip_sum(k):
        to_core[k].wait_recv()
        return part_v[k, mine, :].astype(f32) + core_v[k].astype(f32)

    compute(0)
    compute(1)
    core_v[0] = chip_sum(0).astype(bf16)
    from_x = send(core_v.at[0, pl.ds(0, half)], edge_v.at[0], here.to_x)
    from_y = send(core_v.at[0, pl.ds(half, half)], edge_v.at[1], here.to_y)
    compute(2)
    over_x_sum = chip_sum(1)
    core_v[1, :half] = over_x_sum[:half].astype(bf16)
    from_y.wait_recv()
    core_v[1, half:] = (over_x_sum[half:] + edge_v[1].astype(f32)).astype(bf16)
    last_x = send(core_v.at[1], last_v.at[0], here.to_x)
    over_y_sum = chip_sum(2)
    core_v[2, half:] = over_y_sum[half:].astype(bf16)
    from_x.wait_recv()
    core_v[2, :half] = (over_y_sum[:half] + edge_v[0].astype(f32)).astype(bf16)
    last_y = send(core_v.at[2], last_v.at[1], here.to_y)
    compute(3)
    out_ref[...] = chip_sum(3)
    last_x.wait_recv()
    last_y.wait_recv()
    out_ref[...] = out_ref[...] + last_v[0].astype(f32) + last_v[1].astype(f32)
    send.finish()


def plane_sum(lefts, weight, extra, collective_id):
    across = extra is not None
    count = lefts[0].shape[0] // lax.axis_size(plane)
    width = weight.shape[1] if across else weight.shape[2]
    wide = width + (extra.shape[1] if across else 0)
    experts, depth = len(lefts), lefts[0].shape[1]
    vmem = pl.BlockSpec(memory_space=pltpu.VMEM)
    anywhere = pl.BlockSpec(memory_space=pl.ANY)

    def kernel(*refs):
        plane_sum_kernel(across, experts, *refs)

    return pl.pallas_call(
        kernel,
        out_shape=jax.ShapeDtypeStruct((count, wide), f32),
        in_specs=[anywhere] * (experts + 1) + [vmem] * across,
        out_specs=vmem,
        scratch_shapes=[
            pltpu.VMEM((4, 2 * count, experts * depth), bf16),
            pltpu.VMEM(weight.shape, bf16),
            pltpu.VMEM((4, 2 * count, wide), bf16),
            pltpu.VMEM((4, count, wide), bf16),
            pltpu.VMEM((2, count // 2, wide), bf16),
            pltpu.VMEM((2, count, wide), bf16),
            pltpu.SemaphoreType.DMA((8,)),
            pltpu.SemaphoreType.DMA((8,)),
            pltpu.SemaphoreType.DMA((1 + 4 * experts,)),
        ],
        compiler_params=pltpu.CompilerParams(
            collective_id=collective_id, has_side_effects=True, vmem_limit_bytes=60 * 2**20
        ),
        cost_estimate=pl.CostEstimate(flops=10**6, bytes_accessed=10**6, transcendentals=0),
    )(*lefts, weight, *([extra] if across else []))


def head_softmax(queries, keys, visible):
    scores = lax.dot_general(
        queries, keys, (((1,), (1,)), ((), ())), preferred_element_type=f32
    ) * (HEAD_SIZE ** (-0.5))
    scores = jnp.where(visible, scores, masked)
    raised = jnp.exp(scores - jnp.max(scores, axis=-1, keepdims=True))
    return raised / jnp.sum(raised, axis=-1, keepdims=True)


def visible_keys(rows, keys):
    row = lax.broadcasted_iota(jnp.int32, (rows, keys), 0)
    key = lax.broadcasted_iota(jnp.int32, (rows, keys), 1)
    prompt_all = keys - (rows - PROMPT_DEV)
    own = lax.axis_index("ctx") * PROMPT_DEV + row
    position = jnp.where(row < PROMPT_DEV, own, prompt_all + row - PROMPT_DEV)
    return key <= position


def attention_kernel(
    query_pre_ref, gain_ref, cosine_ref, sine_ref, keys_ref, values_ref, queries_ref, attended_ref
):
    rows = query_pre_ref.shape[0]
    visible = visible_keys(rows, keys_ref.shape[0])
    keys = keys_ref[...]
    values = values_ref[...]
    for h in range(query_pre_ref.shape[1] // HEAD_SIZE):
        cols = slice(h * HEAD_SIZE, (h + 1) * HEAD_SIZE)
        v = query_pre_ref[:, cols]
        v = v * head_norm(v) * gain_ref[...]
        queries = (v * cosine_ref[...] + turn_half(v) * sine_ref[...]).astype(bf16)
        queries_ref[:, cols] = queries
        probs = head_softmax(queries, keys, visible).astype(bf16)
        attended_ref[:, cols] = dot(probs, values).astype(bf16)


def attention(query_pre, gain, cosine, sine, kv_all):
    rows, wide = query_pre.shape
    keys = kv_all.shape[0]
    group = wide // KEY_VALUE_HEADS
    small = pl.BlockSpec((rows, HEAD_SIZE), lambda i: (0, 0))
    block = pl.BlockSpec((rows, group), lambda i: (0, i))
    return pl.pallas_call(
        attention_kernel,
        grid=(KEY_VALUE_HEADS,),
        out_shape=[jax.ShapeDtypeStruct((rows, wide), bf16)] * 2,
        in_specs=[
            block,
            pl.BlockSpec((1, HEAD_SIZE), lambda i: (0, 0)),
            small,
            small,
            pl.BlockSpec((keys, HEAD_SIZE), lambda i: (0, i)),
            pl.BlockSpec((keys, HEAD_SIZE), lambda i: (0, KEY_VALUE_HEADS + i)),
        ],
        out_specs=[block, block],
        compiler_params=pltpu.CompilerParams(vmem_limit_bytes=48 * 2**20),
    )(query_pre, gain.reshape(1, HEAD_SIZE), cosine, sine, kv_all, kv_all)


def transposed_dot(a, b):
    return lax.dot_general(a, b, (((0,), (0,)), ((), ())), preferred_element_type=f32)


def attention_back_kernel(
    query_pre_ref,
    gain_ref,
    cosine_ref,
    sine_ref,
    keys_ref,
    values_ref,
    queries_ref,
    grad_ref,
    pre_grad_ref,
    key_grad_ref,
    value_grad_ref,
    gain_grad_ref,
):
    rows = query_pre_ref.shape[0]
    visible = visible_keys(rows, keys_ref.shape[0])
    keys = keys_ref[...]
    values = values_ref[...]
    scale = HEAD_SIZE ** (-0.5)
    gain_grad = jnp.zeros((rows, HEAD_SIZE), f32)
    key_grad = jnp.zeros(keys_ref.shape, f32)
    value_grad = jnp.zeros(keys_ref.shape, f32)
    for h in range(query_pre_ref.shape[1] // HEAD_SIZE):
        cols = slice(h * HEAD_SIZE, (h + 1) * HEAD_SIZE)
        queries = queries_ref[:, cols]
        grad = grad_ref[:, cols]
        probs = head_softmax(queries, keys, visible)
        prob_grad = lax.dot_general(
            grad, values, (((1,), (1,)), ((), ())), preferred_element_type=f32
        )
        delta = jnp.sum(probs * prob_grad, axis=-1, keepdims=True)
        score_grad = (probs * (prob_grad - delta)).astype(bf16)
        key_grad = key_grad + transposed_dot(score_grad, queries)
        value_grad = value_grad + transposed_dot(probs.astype(bf16), grad)
        u = dot(score_grad, keys) * scale
        u = u * cosine_ref[...] + turn_half(u * sine_ref[...])
        v = query_pre_ref[:, cols]
        inv = head_norm(v)
        gain_grad = gain_grad + u * v * inv
        pre_grad_ref[:, cols] = norm_back(v, inv, gain_ref[...], u).astype(bf16)
    key_grad_ref[...] = (key_grad * scale).astype(key_grad_ref.dtype)
    value_grad_ref[...] = value_grad.astype(value_grad_ref.dtype)
    gain_grad_ref[0] = jnp.sum(gain_grad, axis=0, keepdims=True)


def attention_back(query_pre, gain, cosine, sine, kv_all, queries, attended_grad):
    rows, wide = query_pre.shape
    keys, both = kv_all.shape
    group = wide // KEY_VALUE_HEADS
    small = pl.BlockSpec((rows, HEAD_SIZE), lambda i: (0, 0))
    block = pl.BlockSpec((rows, group), lambda i: (0, i))
    return pl.pallas_call(
        attention_back_kernel,
        grid=(KEY_VALUE_HEADS,),
        out_shape=[
            jax.ShapeDtypeStruct((rows, wide), bf16),
            jax.ShapeDtypeStruct((keys, both // 2), f32),
            jax.ShapeDtypeStruct((keys, both // 2), f32),
            jax.ShapeDtypeStruct((KEY_VALUE_HEADS, 1, HEAD_SIZE), f32),
        ],
        in_specs=[
            block,
            pl.BlockSpec((1, HEAD_SIZE), lambda i: (0, 0)),
            small,
            small,
            pl.BlockSpec((keys, HEAD_SIZE), lambda i: (0, i)),
            pl.BlockSpec((keys, HEAD_SIZE), lambda i: (0, KEY_VALUE_HEADS + i)),
            block,
            block,
        ],
        out_specs=[
            block,
            pl.BlockSpec((keys, HEAD_SIZE), lambda i: (0, i)),
            pl.BlockSpec((keys, HEAD_SIZE), lambda i: (0, i)),
            pl.BlockSpec((1, 1, HEAD_SIZE), lambda i: (i, 0, 0)),
        ],
        cost_estimate=pl.CostEstimate(flops=10**6, bytes_accessed=10**6, transcendentals=0),
        compiler_params=pltpu.CompilerParams(vmem_limit_bytes=48 * 2**20),
    )(
        query_pre, gain.reshape(1, HEAD_SIZE), cosine, sine, kv_all, kv_all, queries, attended_grad
    )


def join_halves(mine, other):
    lower = lax.axis_index("expert") == 0
    return jnp.concatenate(
        [jnp.where(lower, mine, other), jnp.where(lower, other, mine)], axis=1
    )


def dot(a, b):
    return jnp.dot(a, b, preferred_element_type=f32)


def ctx_sum(v):
    if not small_plane():
        return lax.psum_scatter(v, "ctx", scatter_dimension=1, tiled=True).astype(f32)
    member = lax.axis_index("ctx")

    def block(j):
        return lax.dynamic_slice_in_dim(v, (member ^ j) * PROMPT_DEV, PROMPT_DEV, axis=1)

    near = block(0).astype(f32) + core(block(1)).astype(f32)
    far = (block(2).astype(f32) + core(block(3)).astype(f32)).astype(bf16)
    return near + over_x(far).astype(f32)


def body(
    hidden_in,
    attn_gain,
    query_weight,
    key_matrix,
    value_matrix,
    query_gain,
    key_gain,
    output_weight,
    ffn_gain,
    router_weight,
    gate_up,
    down_proj,
    routes,
    out_grad,
):
    ctx_count = lax.axis_size("ctx")
    spread_count = lax.axis_size(plane)
    dp_count = lax.axis_size("dp")
    device_count = dp_count * spread_count
    local_experts = gate_up.shape[0]
    count_of_rows = hidden_in.shape[0]
    prompt_all = PROMPT_DEV * ctx_count
    hidden_ff = gate_up.shape[2] // 2
    member = lax.axis_index("ctx")
    offsets = jnp.arange(count_of_rows, dtype=jnp.int32)
    position = jnp.where(
        offsets < PROMPT_DEV, member * PROMPT_DEV + offsets, prompt_all + offsets - PROMPT_DEV
    )
    cosine, rope_sine = angles(position, HEAD_SIZE)
    narrow = KEY_VALUE_HEADS * HEAD_SIZE
    wide = QUERY_HEADS * HEAD_SIZE
    inputs = hidden_in.astype(f32)
    scale_in = rms_scale(inputs)

    def by_owner(v):
        v = v.reshape(count_of_rows, dp_count, spread_count, -1)
        return v.transpose(2, 0, 1, 3).reshape(spread_count, count_of_rows, -1)

    signed_sine = rope_sine * jnp.where(jnp.arange(HEAD_SIZE) < HEAD_SIZE // 2, -1.0, 1.0)
    if small_plane():
        (
            kv_other,
            q_other,
            o_other,
            g_rows,
            route_rows,
            kv_all,
            normed_owned,
            attended_owned,
            query_pre,
            key_pre,
            queries,
            residual,
            ffn_in,
        ) = fetch_and_attend(
            hidden_in, attn_gain, query_gain, key_gain, ffn_gain, cosine, signed_sine,
            key_matrix, value_matrix, query_weight, output_weight, out_grad, routes,
        )
        kv_weights = [jnp.concatenate([key_matrix, value_matrix], axis=1), kv_other]
        q_weights = [query_weight, q_other]
        o_weights = [output_weight, o_other]
    else:
        full = [
            lax.all_gather(w, "expert", axis=0, tiled=True)
            for w in (
                jnp.concatenate([key_matrix, value_matrix], axis=1),
                query_weight,
                output_weight,
            )
        ]
        kv_weights, q_weights, o_weights = [[w] for w in full]
        g_rows = lax.all_gather(out_grad, plane, axis=0, tiled=True)
        route_rows = lax.all_gather(routes, plane, axis=0, tiled=True)
        normalized_input = (inputs * scale_in * attn_gain).astype(bf16)
        query_pre = dot(normalized_input, q_weights[0])
        key_value_pre = dot(normalized_input, kv_weights[0])
        key_pre = key_value_pre[:, :narrow]
        key_heads = key_pre.reshape(count_of_rows, KEY_VALUE_HEADS, HEAD_SIZE)
        key_low = rotate(
            key_heads * rms_scale(key_heads) * key_gain, cosine[:, None, :], rope_sine[:, None, :]
        ).astype(bf16)
        kv_low = jnp.concatenate(
            [key_low.reshape(count_of_rows, narrow), key_value_pre[:, narrow:].astype(bf16)],
            axis=1,
        )
        kv_blocks = lax.all_gather(kv_low[:PROMPT_DEV], "ctx", axis=0, tiled=True)
        kv_all = jnp.concatenate([kv_blocks, kv_low[PROMPT_DEV:]], axis=0)
        queries, attended = attention(query_pre, query_gain, cosine, signed_sine, kv_all)
        residual = inputs + dot(attended, o_weights[0])
        ffn_in = (residual * rms_scale(residual) * ffn_gain).astype(bf16)
        normed_owned = by_owner(normalized_input)
        attended_owned = by_owner(attended)

    def owned(v):
        return lax.all_to_all(v, plane, split_axis=0, concat_axis=0, tiled=True)

    def backward_dot(v, weights):
        parts = [dot(v, w.T) for w in weights]
        return parts[0] if len(parts) == 1 else join_halves(*parts)

    key_before_norm = key_pre.reshape(count_of_rows, KEY_VALUE_HEADS, HEAD_SIZE)
    key_inv = rms_scale(key_before_norm)
    scale_ffn = rms_scale(residual)

    expert_count = local_experts * spread_count
    expert_ids = jnp.arange(expert_count, dtype=jnp.int32)

    def gates_of(some_rows, some_routes):
        logits = dot(some_rows, router_weight)
        chosen = jnp.any(some_routes[:, :, None] == expert_ids[None, None, :], axis=1)
        logits = jnp.where(chosen, logits, masked)
        raised = jnp.where(
            chosen, jnp.exp(logits - jnp.max(logits, axis=-1, keepdims=True)), 0.0
        )
        return raised / jnp.sum(raised, axis=-1, keepdims=True)

    def reduce_expert(which, rows, hidden, grads, g_rows):
        down_part = dot(hidden.T, g_rows).astype(bf16)
        gate_up_part = dot(rows.T, grads).astype(bf16)
        return (
            lax.psum_scatter(down_part, "dp", scatter_dimension=0, tiled=True),
            lax.psum_scatter(gate_up_part, "dp", scatter_dimension=0, tiled=True),
            down_part,
            gate_up_part,
        )

    gates = gates_of(ffn_in, routes)
    if small_plane():
        rows, hidden, grads, gates_mine, totals = gather_first_expert(
            ffn_in, route_rows, router_weight, g_rows, gate_up, down_proj
        )
        hiddens, projected_grads = [hidden], [grads]
        sums = [reduce_expert(0, rows, hidden, grads, g_rows)]
        rows = after(rows, *sums[0][2:])
        attended_owned, normed_owned = [
            owned(after(v, *sums[0][2:])) for v in (attended_owned, normed_owned)
        ]
        for which in range(1, local_experts):
            hidden, grads, gate_grads = last_expert(
                which, expert_count, rows, g_rows, gates_mine, totals, gate_up, down_proj
            )
            hiddens.append(hidden)
            projected_grads.append(grads)
            sums.append(reduce_expert(which, rows, hidden, grads, g_rows))
    else:
        rows = lax.all_gather(ffn_in, plane, axis=0, tiled=True)
        first_expert = lax.axis_index(plane) * local_experts
        gates_mine = lax.dynamic_slice_in_dim(
            gates_of(rows, route_rows), first_expert, local_experts, axis=1
        )
        gate_grads, hiddens, projected_grads = [], [], []
        for which in range(local_experts):
            gate = gates_mine[:, which : which + 1]
            projected = dot(rows, gate_up[which])
            back = dot(g_rows, down_proj[which].T)
            gate_part = projected[:, :hidden_ff]
            up_part = projected[:, hidden_ff:]
            sigmoid_gate = jax.nn.sigmoid(gate_part)
            hidden = gate_part * sigmoid_gate * up_part
            gate_grads.append(jnp.sum(hidden * back, axis=-1))
            hiddens.append((gate * hidden).astype(bf16))
            back = gate * back
            gate_back = back * up_part * sigmoid_gate * (1.0 + gate_part * (1.0 - sigmoid_gate))
            up_back = back * gate_part * sigmoid_gate
            projected_grads.append(jnp.concatenate([gate_back, up_back], axis=-1).astype(bf16))
        attended_owned, normed_owned = owned(attended_owned), owned(normed_owned)
        sums = [
            reduce_expert(i, rows, hidden, grads, g_rows)
            for i, (hidden, grads) in enumerate(zip(hiddens, projected_grads))
        ]
    down_low = [v[0] for v in sums]
    gate_up_low = [v[1] for v in sums]
    down_grad = jnp.stack([v.astype(f32) for v in down_low])
    gate_up_grad = jnp.stack([v.astype(f32) for v in gate_up_low])
    projected_grads, hiddens = lax.optimization_barrier(
        ((projected_grads, hiddens), [v[2:] for v in sums], attended_owned, normed_owned)
    )[0]
    if small_plane():
        back = plane_sum(projected_grads, gate_up, gate_grads, 3)
        back_sum = back[:, :MODEL_WIDTH]
        gate_grad = (
            back[:, MODEL_WIDTH : MODEL_WIDTH + expert_count]
            + back[:, MODEL_WIDTH + expert_count : MODEL_WIDTH + 2 * expert_count]
        )
        moe_sum = None
    else:
        moe_part = 0.0
        row_part = 0.0
        for which in range(local_experts):
            row_part = row_part + dot(projected_grads[which], gate_up[which].T)
            moe_part = moe_part + dot(hiddens[which], down_proj[which])
        moe_sum, back_sum = [
            lax.psum_scatter(v.astype(bf16), plane, scatter_dimension=0, tiled=True).astype(f32)
            for v in (moe_part, row_part)
        ]
        gate_grad = lax.all_to_all(
            jnp.stack(gate_grads, axis=1).reshape(spread_count, count_of_rows, local_experts),
            plane,
            split_axis=0,
            concat_axis=0,
            tiled=True,
        )
        gate_grad = gate_grad.transpose(1, 0, 2).reshape(count_of_rows, expert_count)
    logit_grad = gates * (gate_grad - jnp.sum(gates * gate_grad, axis=-1, keepdims=True))

    grad_out = out_grad.astype(f32)
    router_local = jnp.dot(ffn_in.T, logit_grad, preferred_element_type=f32)
    ffn_in_grad = back_sum + jnp.dot(
        logit_grad, router_weight.astype(f32).T, precision=highest
    )
    residual_grad = grad_out + norm_back(residual, scale_ffn, ffn_gain, ffn_in_grad)
    ffn_gain_local = jnp.sum(ffn_in_grad * residual * scale_ffn, axis=0)
    branch_low = residual_grad.astype(bf16)
    attended_grad = backward_dot(branch_low, o_weights).astype(bf16)
    query_pre_grad, key_grad_all, value_grad_all, query_gain_parts = attention_back(
        query_pre, query_gain, cosine, signed_sine, kv_all, queries, attended_grad
    )
    query_gain_local = jnp.sum(query_gain_parts, axis=(0, 1))
    pair_grads = jnp.stack([key_grad_all[:prompt_all], value_grad_all[:prompt_all]]).astype(bf16)
    prompt_grads = ctx_sum(pair_grads)
    key_grad = jnp.concatenate([prompt_grads[0], key_grad_all[prompt_all:]], axis=0).reshape(
        count_of_rows, KEY_VALUE_HEADS, HEAD_SIZE
    )
    value_gradient = jnp.concatenate([prompt_grads[1], value_grad_all[prompt_all:]], axis=0)
    key_rot_grad = rotate_back(key_grad, cosine[:, None, :], rope_sine[:, None, :])
    key_gain_local = jnp.sum(key_rot_grad * key_before_norm * key_inv, axis=(0, 1))
    key_pre_grad = (
        norm_back(key_before_norm, key_inv, key_gain, key_rot_grad)
        .astype(bf16)
        .reshape(count_of_rows, KEY_VALUE_HEADS * HEAD_SIZE)
    )
    key_value_grad = jnp.concatenate([key_pre_grad, value_gradient.astype(bf16)], axis=1)
    if small_plane():
        output_local, pre_local = weight_grads(
            query_pre_grad, key_value_grad, branch_low, attended_owned, normed_owned
        )
    else:
        branch_rows = lax.all_gather(branch_low, plane, axis=0, tiled=True)
        pre_rows = lax.all_gather(
            jnp.concatenate([query_pre_grad, key_value_grad], axis=1), plane, axis=0, tiled=True
        )
        attended_owned, normed_owned = [
            v.reshape(spread_count * count_of_rows, -1) for v in (attended_owned, normed_owned)
        ]
        output_local = dot(attended_owned.T, branch_rows).astype(bf16)
        pre_local = dot(normed_owned.T, pre_rows).astype(bf16)
    query_pre_grad, key_value_grad = lax.optimization_barrier(
        ((query_pre_grad, key_value_grad), pre_local)
    )[0]
    normed_grad = backward_dot(query_pre_grad, q_weights) + backward_dot(
        key_value_grad, kv_weights
    )
    attn_gain_local = jnp.sum(normed_grad * inputs * scale_in, axis=0)
    hidden_grad = residual_grad + norm_back(inputs, scale_in, attn_gain, normed_grad)
    if small_plane():
        moe_sum = plane_sum(after(hiddens, pre_local), down_proj, None, 4)
    block_out = (residual + moe_sum).astype(bf16)
    output_local, pre_local = lax.optimization_barrier(
        ((output_local, pre_local), gate_up_low, down_low)
    )[0]
    output_sum, pre_sum = [
        lax.psum_scatter(v, "dp", scatter_dimension=0, tiled=True).astype(f32)
        for v in (output_local, pre_local)
    ]

    small = jnp.concatenate(
        [
            v.reshape(device_count, -1)
            for v in (
                attn_gain_local,
                ffn_gain_local,
                query_gain_local,
                key_gain_local,
                router_local,
            )
        ],
        axis=1,
    )
    small = lax.all_to_all(small[:, None], every, split_axis=0, concat_axis=0, tiled=True)
    small = jnp.sum(small[:, 0], axis=0)
    share = MODEL_WIDTH // device_count
    head_share = HEAD_SIZE // device_count
    cuts = [share, share, head_share, head_share, share * expert_count]
    ends = [sum(cuts[: i + 1]) for i in range(5)]
    a_grad, f_grad, q_grad, k_grad, r_grad = [
        small[end - cut : end] for end, cut in zip(ends, cuts)
    ]
    return (
        block_out,
        hidden_grad,
        a_grad,
        pre_sum[:, :wide],
        pre_sum[:, wide : wide + narrow],
        pre_sum[:, wide + narrow :],
        q_grad,
        k_grad,
        output_sum,
        f_grad,
        r_grad.reshape(share, expert_count),
        gate_up_grad,
        down_grad,
    )


def solution(mesh):
    placed = (
        P(("dp", "ctx", "expert"), None),
        P(),
        P("expert", None),
        P("expert", None),
        P("expert", None),
        P(),
        P(),
        P("expert", None),
        P(),
        P(),
        P(("ctx", "expert"), None, None),
        P(("ctx", "expert"), None, None),
        P(("dp", "ctx", "expert"), None),
        P(("dp", "ctx", "expert"), None),
    )
    return jax.shard_map(
        body,
        mesh=mesh,
        in_specs=placed,
        out_specs=(
            P(("dp", "ctx", "expert"), None),
            P(("dp", "ctx", "expert"), None),
            P(("dp", "ctx", "expert")),
            P(("dp", "ctx", "expert"), None),
            P(("dp", "ctx", "expert"), None),
            P(("dp", "ctx", "expert"), None),
            P(("dp", "ctx", "expert")),
            P(("dp", "ctx", "expert")),
            P(("dp", "ctx", "expert"), None),
            P(("dp", "ctx", "expert")),
            P(("dp", "ctx", "expert"), None),
            P(("ctx", "expert"), "dp", None),
            P(("ctx", "expert"), "dp", None),
        ),
        check_vma=False,
    )
```

```python
import math

import jax
import jax.numpy as jnp
from jax import lax
from jax.experimental import pallas as pl
from jax.experimental.pallas import tpu as pltpu
from jax.sharding import PartitionSpec as P

MODEL_WIDTH = 2048
QUERY_HEADS = 32
KEY_VALUE_HEADS = 4
HEAD_SIZE = 128
TOP = 8
PROMPT_DEV = 128


highest = lax.Precision.HIGHEST
epsilon = 1e-06
rope_base = 1000000.0
masked = -1e30
every = ("dp", "ctx", "expert")
plane = ("ctx", "expert")
bf16 = jnp.bfloat16
f32 = jnp.float32


def rms_scale(value_rows):
    return lax.rsqrt(jnp.mean(value_rows * value_rows, axis=-1, keepdims=True) + epsilon)


def norm_back(inputs, inv_rms, norm_gain, gradient):
    weighted = gradient * norm_gain
    return inv_rms * weighted - inputs * inv_rms**3 * jnp.mean(
        weighted * inputs, axis=-1, keepdims=True
    )


def angles(position, head_width):
    freq_index = jnp.arange(head_width // 2, dtype=f32)
    inverse = jnp.exp(-(2.0 * freq_index / head_width) * math.log(rope_base))
    rope_angle = position.astype(f32)[:, None] * inverse[None, :]
    rope_angle = jnp.concatenate([rope_angle, rope_angle], axis=-1)
    return (jnp.cos(rope_angle), jnp.sin(rope_angle))


def rotate(value_rows, cosine, rope_sine):
    half_width = value_rows.shape[-1] // 2
    turned = jnp.concatenate([-value_rows[..., half_width:], value_rows[..., :half_width]], axis=-1)
    return value_rows * cosine + turned * rope_sine


def rotate_back(gradient, cosine, rope_sine):
    shifted = gradient * rope_sine
    half_width = gradient.shape[-1] // 2
    return gradient * cosine + jnp.concatenate(
        [shifted[..., half_width:], -shifted[..., :half_width]], axis=-1
    )


def small_plane():
    return [lax.axis_size(a) for a in every] == [4, 4, 2]


def swap(v, axis, bit):
    return lax.ppermute(v, axis, [(i, i ^ bit) for i in range(lax.axis_size(axis))])


def core(v):
    return swap(v, "ctx", 1)


def over_x(v):
    return swap(v, "ctx", 2)


def over_y(v):
    return swap(v, "expert", 1)


def over_z(v):
    return swap(v, "dp", 1)


def after(v, *earlier):
    return lax.optimization_barrier((v, *earlier))[0]


class Places:
    def __init__(self):
        self.dp = lax.axis_index("dp")
        ctx = lax.axis_index("ctx")
        self.ctx = ctx
        self.z = lax.rem(self.dp, 2)
        self.x = lax.div(ctx, 2)
        self.c = lax.rem(ctx, 2)
        self.y = lax.axis_index("expert")
        self.to_x = {"ctx": (1 - self.x) * 2 + self.c}
        self.to_c = {"ctx": self.x * 2 + 1 - self.c}
        self.to_y = {"expert": 1 - self.y}
        self.to_z = {"dp": self.dp + 1 - 2 * self.z}


def plane_slot(x, c, y):
    return x * 4 + y * 2 + c


def greet(targets):
    barrier = pltpu.get_barrier_semaphore()
    for target in targets:
        pl.semaphore_signal(barrier, inc=1, device_id=target, device_id_type=pl.DeviceIdType.MESH)
    pl.semaphore_wait(barrier, len(targets))


class Sender:
    def __init__(self, send_sem, recv_sem):
        self.send_sem = send_sem
        self.recv_sem = recv_sem
        self.copies = []

    def __call__(self, source, target_ref, device):
        i = len(self.copies)
        copy = pltpu.make_async_remote_copy(
            src_ref=source,
            dst_ref=target_ref,
            send_sem=self.send_sem.at[i],
            recv_sem=self.recv_sem.at[i],
            device_id=device,
            device_id_type=pl.DeviceIdType.MESH,
        )
        copy.start()
        self.copies.append(copy)
        return copy

    def finish(self):
        for copy in self.copies:
            copy.wait_send()


def half_fetch(here, send, sources, other, columns, rows, upper):
    def at(piece, part=None):
        first, size = piece * rows, rows
        if part == 0:
            size = upper
        elif part == 1:
            first, size = first + upper, rows - upper
        return other.at[pl.ds(pl.multiple_of(first, 16), size), columns]

    def piece(z, x, c):
        return z * 4 + x * 2 + c

    z, x, c = here.z, here.x, here.c
    got = {}

    def first():
        mine = piece(z, x, c)
        got["y"] = [
            send(
                source.at[pl.ds(pl.multiple_of(mine * rows, rows), rows), source_columns],
                other.at[pl.ds(pl.multiple_of(mine * rows, rows), rows), target_columns],
                here.to_y,
            )
            for source, source_columns, target_columns in sources
        ]

    def second():
        for copy in got["y"]:
            copy.wait_recv()
        mine = at(piece(z, x, c))
        got["x"] = send(mine, mine, here.to_x)
        got["z"] = send(mine, mine, here.to_z)
        got["c"] = send(mine, mine, here.to_c)

    def third():
        got["x"].wait_recv()
        from_x = piece(z, 1 - x, c)
        got["low"] = send(at(from_x, 1), at(from_x, 1), here.to_z)
        got["xc"] = send(at(from_x), at(from_x), here.to_c)
        got["z"].wait_recv()
        from_z = piece(1 - z, x, c)
        got["top"] = send(at(from_z, 0), at(from_z, 0), here.to_x)
        got["zc"] = send(at(from_z), at(from_z), here.to_c)

    def fourth():
        far = piece(1 - z, 1 - x, c)
        got["low"].wait_recv()
        got["lowc"] = send(at(far, 1), at(far, 1), here.to_c)
        got["top"].wait_recv()
        got["topc"] = send(at(far, 0), at(far, 0), here.to_c)

    def fifth():
        for name in ("c", "xc", "zc", "lowc", "topc"):
            got[name].wait_recv()

    return [first, second, third, fourth, fifth]


def block_gather(here, send, mine, local_sem, blocks, far_over_y=False, columns=None):
    rows = blocks.shape[0] // lax.axis_size(plane)
    half = rows // 2
    x, c, y = here.x, here.c, here.y
    got = {}

    def at(slot, part=None):
        first, size = slot * rows, rows
        if part is not None:
            first, size = first + part * half, half
        rows_of = pl.ds(pl.multiple_of(first, size), size)
        return blocks.at[rows_of] if columns is None else blocks.at[rows_of, columns]

    def first():
        slot = plane_slot(x, c, y)
        got["own"] = pltpu.make_async_copy(mine, at(slot), local_sem)
        got["own"].start()
        got["y"] = send(mine, at(slot), here.to_y)
        got["x"] = send(mine, at(slot), here.to_x)
        got["c"] = send(mine, at(slot), here.to_c)

    def second():
        got["y"].wait_recv()
        from_y = plane_slot(x, c, 1 - y)
        got["yc"] = send(at(from_y), at(from_y), here.to_c)
        if not far_over_y:
            got["top"] = send(at(from_y, 0), at(from_y, 0), here.to_x)
        got["x"].wait_recv()
        from_x = plane_slot(1 - x, c, y)
        got["xc"] = send(at(from_x), at(from_x), here.to_c)
        if far_over_y:
            got["top"] = send(at(from_x, 0), at(from_x, 0), here.to_y)
        got["low"] = send(at(from_x, 1), at(from_x, 1), here.to_y)

    def third():
        far = plane_slot(1 - x, c, 1 - y)
        got["top"].wait_recv()
        got["topc"] = send(at(far, 0), at(far, 0), here.to_c)
        got["low"].wait_recv()
        got["lowc"] = send(at(far, 1), at(far, 1), here.to_c)

    def fourth():
        for name in ("c", "yc", "xc", "topc", "lowc"):
            got[name].wait_recv()
        got["own"].wait()

    return [first, second, third, fourth], got


def turn_half(v):
    return pltpu.roll(v, v.shape[-1] // 2, axis=1)


def head_norm(v):
    return lax.rsqrt(jnp.mean(v * v, axis=-1, keepdims=True) + epsilon)


def fetch_kernel(
    hidden_ref,
    attn_gain_ref,
    query_gain_ref,
    key_gain_ref,
    ffn_gain_ref,
    cosine_ref,
    sine_ref,
    key_ref,
    value_ref,
    query_ref,
    output_ref,
    grad_ref,
    routes_ref,
    kv_out,
    q_out,
    o_out,
    g_blocks,
    route_blocks,
    kv_all_out,
    normed_owned,
    attended_owned,
    query_pre_ref,
    key_pre_ref,
    queries_ref,
    residual_ref,
    ffn_ref,
    normed_ref,
    attended_ref,
    kv_own,
    kv_other,
    q_own,
    q_other,
    o_own,
    o_other,
    kv_pre,
    kv_low,
    kv_all,
    send_sem,
    recv_sem,
    local_sem,
):
    here = Places()
    greet([here.to_y, here.to_z, here.to_c, here.to_x])
    send = Sender(send_sem, recv_sem)
    count, width = hidden_ref.shape
    half = width // 2
    narrow = key_ref.shape[1]
    wide = query_ref.shape[1]
    prompt_all = kv_all.shape[0] - (count - PROMPT_DEV)
    spread, groups = lax.axis_size(plane), lax.axis_size("dp")
    tile = 512
    loads = [
        pltpu.make_async_copy(key_ref, kv_own.at[:, pl.ds(0, narrow)], local_sem.at[0]),
        pltpu.make_async_copy(value_ref, kv_own.at[:, pl.ds(narrow, narrow)], local_sem.at[1]),
        pltpu.make_async_copy(query_ref, q_own, local_sem.at[2]),
        pltpu.make_async_copy(output_ref, o_own, local_sem.at[3]),
    ]
    stores = [
        pltpu.make_async_copy(kv_other, kv_out, local_sem.at[4]),
        pltpu.make_async_copy(q_other, q_out, local_sem.at[5]),
        pltpu.make_async_copy(o_other, o_out, local_sem.at[6]),
        pltpu.make_async_copy(kv_all, kv_all_out, local_sem.at[7]),
    ]

    def part_of(size, which):
        first = here.y * size if which == 0 else size - here.y * size
        return pl.ds(pl.multiple_of(first, size), size)

    def project(source, weight, out, which, first, count_of_tiles, add):
        rows = part_of(weight.shape[0], which)

        @pl.loop(first, first + count_of_tiles)
        def _(i):
            cols = pl.ds(pl.multiple_of(i * tile, tile), tile)
            part = dot(source[:, rows], weight[:, cols])
            out[:, cols] = out[:, cols] + part if add else part

    def start():
        for load in loads:
            load.start()
        inputs = hidden_ref[...].astype(f32)
        normed_ref[...] = (inputs * head_norm(inputs) * attn_gain_ref[...]).astype(bf16)

    def own_part():
        share = width // (spread * groups)
        for s in range(spread):
            normed_owned[s] = jnp.concatenate(
                [
                    normed_ref[:, (d * spread + s) * share : (d * spread + s + 1) * share]
                    for d in range(groups)
                ],
                axis=1,
            )
        for load in loads[:3]:
            load.wait()
        project(normed_ref, kv_own, kv_pre, 0, 0, 2 * narrow // tile, False)
        project(normed_ref, q_own, query_pre_ref, 0, 0, wide // tile, False)

    exchange = {}

    def keys_part():
        project(normed_ref, kv_other, kv_pre, 1, 0, 2 * narrow // tile, True)
        stores[0].start()
        key_pre_ref[...] = kv_pre[:, :narrow]
        for h in range(narrow // HEAD_SIZE):
            cols = slice(h * HEAD_SIZE, (h + 1) * HEAD_SIZE)
            v = kv_pre[:, cols]
            v = v * head_norm(v) * key_gain_ref[...]
            kv_low[:, cols] = (v * cosine_ref[...] + turn_half(v) * sine_ref[...]).astype(bf16)
        kv_low[:, narrow:] = kv_pre[:, narrow:].astype(bf16)
        kv_all[prompt_all:, :] = kv_low[PROMPT_DEV:, :]
        source = kv_low.at[pl.ds(0, PROMPT_DEV)]
        slot = kv_all.at[pl.ds(pl.multiple_of(here.ctx * PROMPT_DEV, PROMPT_DEV), PROMPT_DEV)]
        exchange["own"] = pltpu.make_async_copy(source, slot, local_sem.at[8])
        exchange["own"].start()
        exchange["c"] = send(source, slot, here.to_c)
        exchange["x"] = send(source, slot, here.to_x)

    def keys_forward():
        exchange["x"].wait_recv()
        first = ((1 - here.x) * 2 + here.c) * PROMPT_DEV
        slot = kv_all.at[pl.ds(pl.multiple_of(first, PROMPT_DEV), PROMPT_DEV)]
        exchange["xc"] = send(slot, slot, here.to_c)

    def queries_first():
        project(normed_ref, q_other, query_pre_ref, 1, 0, wide // tile // 2, True)

    def queries_rest():
        stores[1].start()
        project(
            normed_ref, q_other, query_pre_ref, 1, wide // tile // 2, wide // tile // 2, True
        )
        for name in ("c", "xc"):
            exchange[name].wait_recv()
        exchange["own"].wait()
        stores[3].start()

    group = 4
    pieces = 4

    def attend(part):
        visible = visible_keys(count, kv_all.shape[0])
        blocks = wide // HEAD_SIZE // group // pieces

        @pl.loop(part * blocks, (part + 1) * blocks)
        def _(i):
            first = lax.div(i * group, wide // narrow) * HEAD_SIZE
            keys = kv_all[:, pl.ds(pl.multiple_of(first, HEAD_SIZE), HEAD_SIZE)]
            values = kv_all[:, pl.ds(pl.multiple_of(narrow + first, HEAD_SIZE), HEAD_SIZE)]
            for h in range(group):
                cols = pl.ds(pl.multiple_of((i * group + h) * HEAD_SIZE, HEAD_SIZE), HEAD_SIZE)
                v = query_pre_ref[:, cols]
                v = v * head_norm(v) * query_gain_ref[...]
                queries = (v * cosine_ref[...] + turn_half(v) * sine_ref[...]).astype(bf16)
                queries_ref[:, cols] = queries
                probs = head_softmax(queries, keys, visible).astype(bf16)
                attended = dot(probs, values).astype(bf16)
                attended_ref[:, cols] = attended
                head = i * group + h
                at = pl.multiple_of(lax.div(head, spread) * HEAD_SIZE, HEAD_SIZE)
                attended_owned[lax.rem(head, spread), :, pl.ds(at, HEAD_SIZE)] = attended

    def output_own():
        loads[3].wait()
        project(attended_ref, o_own, residual_ref, 0, 0, width // tile, False)

    def finish_rows():
        stores[2].start()
        project(attended_ref, o_other, residual_ref, 1, 0, width // tile, True)
        residual = residual_ref[...] + hidden_ref[...].astype(f32)
        residual_ref[...] = residual
        ffn_ref[...] = (residual * head_norm(residual) * ffn_gain_ref[...]).astype(bf16)

    low, high = pl.ds(0, wide // 2), pl.ds(wide // 2, wide // 2)
    o_low, o_high = pl.ds(0, width // 2), pl.ds(width // 2, width // 2)
    rows, o_rows = half // 8, output_ref.shape[0] // 8
    kv, qa, qb, oa, ob, g, r = [
        half_fetch(
            here,
            send,
            [
                (key_ref, pl.ds(0, narrow), pl.ds(0, narrow)),
                (value_ref, pl.ds(0, narrow), pl.ds(narrow, narrow)),
            ],
            kv_other,
            pl.ds(0, 2 * narrow),
            rows,
            rows // 2,
        ),
        half_fetch(here, send, [(query_ref, low, low)], q_other, low, rows, rows // 2),
        half_fetch(here, send, [(query_ref, high, high)], q_other, high, rows, rows // 2),
        half_fetch(here, send, [(output_ref, o_low, o_low)], o_other, o_low, o_rows, o_rows // 4),
        half_fetch(
            here, send, [(output_ref, o_high, o_high)], o_other, o_high, o_rows, o_rows // 4
        ),
        block_gather(here, send, grad_ref, local_sem.at[9], g_blocks, True)[0],
        block_gather(here, send, routes_ref, local_sem.at[10], route_blocks)[0],
    ]
    steps = [
        kv[0], qa[0], qb[0], oa[0], ob[0], g[0], start, kv[1], kv[2], own_part, qa[1],
        kv[3], qa[2], qb[1], kv[4], keys_part, qa[3], qb[2], oa[1],
        keys_forward, qa[4], queries_first, qb[3], ob[1], qb[4], queries_rest,
        oa[2], r[0], lambda: attend(0), lambda: attend(1),
        oa[3], ob[2], g[1], r[1], lambda: attend(2), lambda: attend(3), oa[4], output_own,
        ob[3], g[2], r[2], ob[4], finish_rows, g[3], r[3],
    ]
    for step in steps:
        step()
    for store in stores:
        store.wait()
    send.finish()


def fetch_and_attend(
    hidden_in, attn_gain, query_gain, key_gain, ffn_gain, cosine, sine, key_matrix, value_matrix,
    query_weight, output_weight, out_grad, routes,
):
    rows, width = hidden_in.shape
    half, wide = query_weight.shape
    narrow = key_matrix.shape[1]
    spread = lax.axis_size(plane)
    keys = lax.axis_size("ctx") * PROMPT_DEV + rows - PROMPT_DEV
    vmem = pl.BlockSpec(memory_space=pltpu.VMEM)
    anywhere = pl.BlockSpec(memory_space=pl.ANY)
    copies = 5 * 10 + 1 + 2 * 9 + 3
    return pl.pallas_call(
        fetch_kernel,
        out_shape=[
            jax.ShapeDtypeStruct((half, 2 * narrow), bf16),
            jax.ShapeDtypeStruct((half, wide), bf16),
            jax.ShapeDtypeStruct(output_weight.shape, bf16),
            jax.ShapeDtypeStruct((spread * rows, width), bf16),
            jax.ShapeDtypeStruct((spread * rows, routes.shape[1]), jnp.int32),
            jax.ShapeDtypeStruct((keys, 2 * narrow), bf16),
            jax.ShapeDtypeStruct((spread, rows, width // spread), bf16),
            jax.ShapeDtypeStruct((spread, rows, wide // spread), bf16),
            jax.ShapeDtypeStruct((rows, wide), f32),
            jax.ShapeDtypeStruct((rows, narrow), f32),
            jax.ShapeDtypeStruct((rows, wide), bf16),
            jax.ShapeDtypeStruct((rows, width), f32),
            jax.ShapeDtypeStruct((rows, width), bf16),
        ],
        in_specs=[vmem] * 7 + [anywhere] * 6,
        out_specs=[anywhere] * 6 + [vmem] * 7,
        scratch_shapes=[
            pltpu.VMEM((rows, width), bf16),
            pltpu.VMEM((rows, wide), bf16),
            pltpu.VMEM((half, 2 * narrow), bf16),
            pltpu.VMEM((half, 2 * narrow), bf16),
            pltpu.VMEM((half, wide), bf16),
            pltpu.VMEM((half, wide), bf16),
            pltpu.VMEM(output_weight.shape, bf16),
            pltpu.VMEM(output_weight.shape, bf16),
            pltpu.VMEM((rows, 2 * narrow), f32),
            pltpu.VMEM((rows, 2 * narrow), bf16),
            pltpu.VMEM((keys, 2 * narrow), bf16),
            pltpu.SemaphoreType.DMA((copies,)),
            pltpu.SemaphoreType.DMA((copies,)),
            pltpu.SemaphoreType.DMA((11,)),
        ],
        compiler_params=pltpu.CompilerParams(
            collective_id=1, has_side_effects=True, vmem_limit_bytes=60 * 2**20
        ),
        cost_estimate=pl.CostEstimate(
            flops=2 * rows * width * (2 * wide + 2 * narrow) * 2,
            bytes_accessed=60 * 2**20,
            transcendentals=0,
        ),
    )(
        hidden_in, attn_gain.reshape(1, width), query_gain.reshape(1, HEAD_SIZE),
        key_gain.reshape(1, HEAD_SIZE), ffn_gain.reshape(1, width), cosine, sine,
        key_matrix, value_matrix, query_weight, output_weight, out_grad, routes,
    )


def chip_rows(x, y, rows):
    first = plane_slot(x, 0, y) * rows
    return pl.ds(pl.multiple_of(first, rows), 2 * rows)


def expert_chunk(some, first, rows_v, g_v, gate_up_v, down_v, hidden_v, grad_v, total_v, gate, mark):
    ff = down_v.shape[0]
    tile = 256

    @pl.loop(0, ff // tile, unroll=True)
    def _(f):
        at = pl.multiple_of(f * tile, tile)
        a = dot(rows_v[some, :], gate_up_v[:, pl.ds(at, tile)])
        b = dot(rows_v[some, :], gate_up_v[:, pl.ds(ff + at, tile)])
        q = lax.dot_general(
            g_v[some, :],
            down_v[pl.ds(at, tile), :],
            (((1,), (1,)), ((), ())),
            preferred_element_type=f32,
        )
        s = 1.0 / (1.0 + jnp.exp(-a))
        raised_a = a * s
        hidden = raised_a * b
        total_v[...] = total_v[...] + jnp.where(
            mark, jnp.sum(hidden * q, axis=-1, keepdims=True), 0.0
        )
        back = gate * q
        hidden_v[some, pl.ds(at, tile)] = (gate * hidden).astype(bf16)
        grad_v[some, pl.ds(at, tile)] = (back * b * s * (1.0 + a * (1.0 - s))).astype(bf16)
        grad_v[some, pl.ds(ff + at, tile)] = (back * raised_a).astype(bf16)


def first_expert_kernel(
    ffn_ref,
    routes_ref,
    router_ref,
    g_hbm,
    gate_up_hbm,
    down_hbm,
    rows_out,
    hidden_out,
    grad_out,
    gates_ref,
    gate_grad_ref,
    rows_v,
    g_v,
    gate_up_v,
    down_v,
    hidden_v,
    grad_v,
    total_v,
    send_sem,
    recv_sem,
    local_sem,
):
    here = Places()
    greet([here.to_y, here.to_c, here.to_x])
    send = Sender(send_sem, recv_sem)
    count = ffn_ref.shape[0]
    experts = router_ref.shape[1]
    local_experts = down_hbm.shape[0]
    stages, got = block_gather(here, send, ffn_ref, local_sem.at[0], rows_v)
    stages[0]()
    loads = [
        pltpu.make_async_copy(gate_up_hbm.at[0], gate_up_v, local_sem.at[1]),
        pltpu.make_async_copy(down_hbm.at[0], down_v, local_sem.at[2]),
        pltpu.make_async_copy(g_hbm, g_v, local_sem.at[3]),
    ]
    for load in loads:
        load.start()
    first_expert = plane_index(here) * local_experts
    stores = []

    def chunk(x, y):
        some = chip_rows(x, y, count)
        logits = dot(rows_v[some, :], router_ref[...])
        ids = lax.broadcasted_iota(jnp.int32, logits.shape, 1)
        routes = routes_ref[some, :]
        chosen = ids < 0
        for k in range(routes.shape[1]):
            chosen = chosen | (routes[:, k : k + 1] == ids)
        logits = jnp.where(chosen, logits, masked)
        raised = jnp.exp(logits - jnp.max(logits, axis=-1, keepdims=True))
        raised = jnp.where(chosen, raised, 0.0)
        gates = raised / jnp.sum(raised, axis=-1, keepdims=True)
        lane = lax.broadcasted_iota(jnp.int32, total_v.shape, 1)
        total_v[...] = jnp.zeros(total_v.shape, f32)
        columns = [
            jnp.sum(jnp.where(ids == first_expert + e, gates, 0.0), axis=-1, keepdims=True)
            for e in range(local_experts)
        ]
        spread = jnp.zeros(total_v.shape, f32)
        for e in range(local_experts):
            spread = jnp.where(lane == e, columns[e], spread)
        gates_ref[some, :] = spread
        mark = (lane == first_expert) | (lane == first_expert + experts)
        expert_chunk(
            some, 0, rows_v, g_v, gate_up_v, down_v, hidden_v, grad_v, total_v, columns[0], mark
        )
        gate_grad_ref[some, :] = total_v[...]
        for source, target in ((hidden_v, hidden_out), (grad_v, grad_out), (rows_v, rows_out)):
            columns = pl.ds(0, source.shape[1])
            store = pltpu.make_async_copy(
                source.at[some, :], target.at[some, columns], local_sem.at[4 + len(stores)]
            )
            store.start()
            stores.append(store)

    x, y = here.x, here.y
    for name in ("c", "own"):
        arrive(got, name)
    for load in loads:
        load.wait()
    chunk(x, y)
    stages[1]()
    arrive(got, "yc")
    chunk(x, 1 - y)
    stages[2]()
    arrive(got, "xc")
    chunk(1 - x, y)
    arrive(got, "topc")
    arrive(got, "lowc")
    chunk(1 - x, 1 - y)
    for store in stores:
        store.wait()
    send.finish()


def gather_first_expert(ffn_in, route_rows, router_weight, g_rows, gate_up, down_proj):
    experts, ff, width = down_proj.shape
    total = route_rows.shape[0]
    vmem = pl.BlockSpec(memory_space=pltpu.VMEM)
    anywhere = pl.BlockSpec(memory_space=pl.ANY)
    return pl.pallas_call(
        first_expert_kernel,
        out_shape=[
            jax.ShapeDtypeStruct((total, width), bf16),
            jax.ShapeDtypeStruct((total, ff), bf16),
            jax.ShapeDtypeStruct((total, 2 * experts * ff), bf16),
            jax.ShapeDtypeStruct((total, 128), f32),
            jax.ShapeDtypeStruct((total, 128), f32),
        ],
        in_specs=[vmem] * 3 + [anywhere] * 3,
        out_specs=[anywhere] * 3 + [vmem] * 2,
        scratch_shapes=[
            pltpu.VMEM((total, width), bf16),
            pltpu.VMEM((total, width), bf16),
            pltpu.VMEM(gate_up.shape[1:], bf16),
            pltpu.VMEM(down_proj.shape[1:], bf16),
            pltpu.VMEM((total, ff), bf16),
            pltpu.VMEM((total, 2 * ff), bf16),
            pltpu.VMEM((2 * ffn_in.shape[0], 128), f32),
            pltpu.SemaphoreType.DMA((9,)),
            pltpu.SemaphoreType.DMA((9,)),
            pltpu.SemaphoreType.DMA((16,)),
        ],
        compiler_params=pltpu.CompilerParams(
            collective_id=2, has_side_effects=True, vmem_limit_bytes=56 * 2**20
        ),
        cost_estimate=pl.CostEstimate(
            flops=2 * total * width * 3 * ff,
            bytes_accessed=40 * 2**20,
            transcendentals=0,
        ),
    )(ffn_in, route_rows, router_weight, g_rows, gate_up, down_proj)


def next_expert_kernel(
    which, experts, rows_v, g_v, gates_ref, totals_ref, gate_up_v, down_v, _, hidden_v, grad_v,
    gate_grad_ref, total_v,
):
    lane = lax.broadcasted_iota(jnp.int32, total_v.shape, 1)
    expert = lax.axis_index(plane) * lax.div(experts, lax.axis_size(plane)) + which
    mark = (lane == expert) | (lane == expert + experts)
    total_v[...] = totals_ref[...]
    gate = jnp.sum(jnp.where(lane == which, gates_ref[...], 0.0), axis=-1, keepdims=True)
    some = pl.ds(0, rows_v.shape[0])
    expert_chunk(
        some, 0, rows_v, g_v, gate_up_v.at[0], down_v.at[0], hidden_v, grad_v, total_v, gate, mark
    )
    total = total_v[...]
    high = total.astype(bf16).astype(f32)
    gate_grad_ref[...] = jnp.where(lane < experts, high, total - high).astype(bf16)


def last_expert(which, experts, rows, g_rows, gates, totals, gate_up, down_proj, grads):
    ff, width = down_proj.shape[1:]
    total = rows.shape[0]
    step = total // 4

    def block(columns):
        return pl.BlockSpec((step, columns), lambda i: (i, 0))

    def whole(shape):
        return pl.BlockSpec((1,) + shape[1:], lambda i: (which, 0, 0))

    def kernel(*refs):
        next_expert_kernel(which, experts, *refs)

    return pl.pallas_call(
        kernel,
        grid=(4,),
        out_shape=[
            jax.ShapeDtypeStruct((total, ff), bf16),
            jax.ShapeDtypeStruct(grads.shape, bf16),
            jax.ShapeDtypeStruct((total, 128), bf16),
        ],
        in_specs=[
            block(width), block(width), block(128), block(128),
            whole(gate_up.shape), whole(down_proj.shape), pl.BlockSpec(memory_space=pl.ANY),
        ],
        out_specs=[
            block(ff), pl.BlockSpec((step, 2 * ff), lambda i: (i, which)), block(128)
        ],
        input_output_aliases={6: 1},
        scratch_shapes=[pltpu.VMEM((step, 128), f32)],
        compiler_params=pltpu.CompilerParams(vmem_limit_bytes=56 * 2**20),
        cost_estimate=pl.CostEstimate(flops=10**6, bytes_accessed=10**6, transcendentals=0),
    )(rows, g_rows, gates, totals, gate_up, down_proj, grads)


def weight_grad_kernel(
    query_grad, kv_grad, branch, attended_owned, normed_owned, sums_ref,
    pre_v, branch_v, attended_v, normed_v, send_sem, recv_sem, local_sem,
):
    here = Places()
    greet([here.to_y, here.to_c, here.to_x])
    send = Sender(send_sem, recv_sem)
    count, wide = query_grad.shape
    narrow = kv_grad.shape[1]
    spread = lax.axis_size(plane)
    tile = sums_ref.shape[1]
    groups = lax.axis_size("dp")
    half = wide // 2
    low, high, last = pl.ds(0, half), pl.ds(half, half), pl.ds(wide, narrow)
    b, _ = block_gather(here, send, branch, local_sem.at[0], branch_v)
    qa, _ = block_gather(
        here, send, query_grad.at[:, low], local_sem.at[1], pre_v, False, low
    )
    qb, _ = block_gather(
        here, send, query_grad.at[:, high], local_sem.at[2], pre_v, False, high
    )
    kv, _ = block_gather(here, send, kv_grad, local_sem.at[3], pre_v, False, last)
    loads = []
    for device in range(spread):
        slot = plane_slot(device // 4, device // 2 % 2, device % 2)
        rows = pl.ds(slot * count, count)
        for source, target in ((attended_owned, attended_v), (normed_owned, normed_v)):
            loads.append(
                pltpu.make_async_copy(
                    source.at[device], target.at[rows], local_sem.at[4 + len(loads)]
                )
            )

    def start():
        for load in loads:
            load.start()

    def product(left, right, base, first, tiles):
        rows = left.shape[1] // groups

        @pl.loop(first, first + tiles)
        def _(i):
            cols = pl.ds(pl.multiple_of(i * tile, tile), tile)
            part = transposed_dot(left[...], right[:, cols]).astype(bf16)
            for d in range(groups):
                at = d * (sums_ref.shape[0] // groups) + base + i * rows
                sums_ref[pl.ds(pl.multiple_of(at, 64), rows), :] = part[
                    d * rows : (d + 1) * rows
                ]

    output_rows = attended_v.shape[1] // groups * (branch.shape[1] // tile)

    def output_product():
        for load in loads:
            load.wait()
        product(attended_v, branch_v, 0, 0, branch.shape[1] // tile)

    steps = [
        b[0], start, b[1], qa[0], b[2], qa[1], qb[0], b[3], output_product,
        qa[2], qb[1], kv[0], qa[3],
        lambda: product(normed_v, pre_v, output_rows, 0, half // tile),
        qb[2], kv[1], qb[3],
        lambda: product(normed_v, pre_v, output_rows, half // tile, half // tile),
        kv[2], kv[3],
        lambda: product(normed_v, pre_v, output_rows, wide // tile, narrow // tile),
    ]
    for step in steps:
        step()
    send.finish()


def weight_grads(query_grad, kv_grad, branch, attended_owned, normed_owned):
    count, wide = query_grad.shape
    narrow, width = kv_grad.shape[1], branch.shape[1]
    spread = lax.axis_size(plane)
    tile = narrow
    elements = attended_owned.shape[2] * width + normed_owned.shape[2] * (wide + narrow)
    vmem = pl.BlockSpec(memory_space=pltpu.VMEM)
    anywhere = pl.BlockSpec(memory_space=pl.ANY)
    return pl.pallas_call(
        weight_grad_kernel,
        out_shape=jax.ShapeDtypeStruct((elements // tile, tile), bf16),
        in_specs=[anywhere] * 5,
        out_specs=vmem,
        scratch_shapes=[
            pltpu.VMEM((spread * count, wide + narrow), bf16),
            pltpu.VMEM((spread * count, width), bf16),
            pltpu.VMEM((spread * count, attended_owned.shape[2]), bf16),
            pltpu.VMEM((spread * count, normed_owned.shape[2]), bf16),
            pltpu.SemaphoreType.DMA((36,)),
            pltpu.SemaphoreType.DMA((36,)),
            pltpu.SemaphoreType.DMA((4 + 2 * spread,)),
        ],
        compiler_params=pltpu.CompilerParams(
            collective_id=5, has_side_effects=True, vmem_limit_bytes=56 * 2**20
        ),
        cost_estimate=pl.CostEstimate(flops=10**6, bytes_accessed=10**6, transcendentals=0),
    )(query_grad, kv_grad, branch, attended_owned, normed_owned)


def arrive(got, name):
    copy = got[name]
    copy.wait() if name == "own" else copy.wait_recv()


def plane_index(here):
    return here.ctx * 2 + here.y


def plane_sum_kernel(across, parts, *refs):
    lefts, weight_hbm = refs[:parts], refs[parts]
    extra_ref = refs[parts + 1] if across else None
    refs = refs[parts + 1 + across :]
    (
        out_ref, left_v, weight_v, part_v, core_v, edge_v, last_v, send_sem, recv_sem, local_sem,
    ) = refs
    here = Places()
    greet([here.to_y, here.to_c, here.to_x])
    send = Sender(send_sem, recv_sem)
    count = out_ref.shape[0]
    half = count // 2
    experts = weight_hbm.shape[0]
    part_depth = lefts[0].shape[1]
    depth = part_depth * parts // experts
    width = weight_hbm.shape[1] if across else weight_hbm.shape[2]
    tile = 256
    x, y, c = here.x, here.y, here.c
    chips = [(1 - x, 1 - y), (1 - x, y), (x, 1 - y), (x, y)]
    weight_load = pltpu.make_async_copy(weight_hbm, weight_v, local_sem.at[0])
    weight_load.start()
    loads = []
    for k, (cx, cy) in enumerate(chips):
        some = chip_rows(cx, cy, count)
        loads.append(
            [
                pltpu.make_async_copy(
                    left.at[some, :],
                    left_v.at[k, :, pl.ds(e * part_depth, part_depth)],
                    local_sem.at[1 + parts * k + e],
                )
                for e, left in enumerate(lefts)
            ]
        )
        for load in loads[-1]:
            load.start()
    weight_load.wait()
    to_core = []

    def compute(k):
        for load in loads[k]:
            load.wait()

        @pl.loop(0, width // tile)
        def _(n):
            cols = pl.ds(pl.multiple_of(n * tile, tile), tile)
            total = None
            for e in range(experts):
                left = left_v[k, :, e * depth : (e + 1) * depth]
                if across:
                    part = lax.dot_general(
                        left,
                        weight_v[e, cols, :],
                        (((1,), (1,)), ((), ())),
                        preferred_element_type=f32,
                    )
                else:
                    part = dot(left, weight_v[e, :, cols])
                total = part if total is None else total + part
            part_v[k, :, cols] = total.astype(bf16)

        if extra_ref is not None:
            part_v[k, :, width:] = extra_ref[chip_rows(*chips[k], count), :]
        to_core.append(
            send(
                part_v.at[k, pl.ds(pl.multiple_of((1 - c) * count, count), count)],
                core_v.at[k],
                here.to_c,
            )
        )

    mine = pl.ds(pl.multiple_of(c * count, count), count)

    def chip_sum(k):
        to_core[k].wait_recv()
        return part_v[k, mine, :].astype(f32) + core_v[k].astype(f32)

    compute(0)
    compute(1)
    core_v[0] = chip_sum(0).astype(bf16)
    from_x = send(core_v.at[0, pl.ds(0, half)], edge_v.at[0], here.to_x)
    from_y = send(core_v.at[0, pl.ds(half, half)], edge_v.at[1], here.to_y)
    compute(2)
    over_x_sum = chip_sum(1)
    core_v[1, :half] = over_x_sum[:half].astype(bf16)
    from_y.wait_recv()
    core_v[1, half:] = (over_x_sum[half:] + edge_v[1].astype(f32)).astype(bf16)
    last_x = send(core_v.at[1], last_v.at[0], here.to_x)
    over_y_sum = chip_sum(2)
    core_v[2, half:] = over_y_sum[half:].astype(bf16)
    from_x.wait_recv()
    core_v[2, :half] = (over_y_sum[:half] + edge_v[0].astype(f32)).astype(bf16)
    last_y = send(core_v.at[2], last_v.at[1], here.to_y)
    compute(3)
    out_ref[...] = chip_sum(3)
    last_x.wait_recv()
    last_y.wait_recv()
    out_ref[...] = out_ref[...] + last_v[0].astype(f32) + last_v[1].astype(f32)
    send.finish()


def plane_sum(lefts, weight, extra, collective_id):
    across = extra is not None
    count = lefts[0].shape[0] // lax.axis_size(plane)
    width = weight.shape[1] if across else weight.shape[2]
    wide = width + (extra.shape[1] if across else 0)
    parts, depth = len(lefts), lefts[0].shape[1]
    vmem = pl.BlockSpec(memory_space=pltpu.VMEM)
    anywhere = pl.BlockSpec(memory_space=pl.ANY)

    def kernel(*refs):
        plane_sum_kernel(across, parts, *refs)

    return pl.pallas_call(
        kernel,
        out_shape=jax.ShapeDtypeStruct((count, wide), f32),
        in_specs=[anywhere] * (parts + 1) + [vmem] * across,
        out_specs=vmem,
        scratch_shapes=[
            pltpu.VMEM((4, 2 * count, parts * depth), bf16),
            pltpu.VMEM(weight.shape, bf16),
            pltpu.VMEM((4, 2 * count, wide), bf16),
            pltpu.VMEM((4, count, wide), bf16),
            pltpu.VMEM((2, count // 2, wide), bf16),
            pltpu.VMEM((2, count, wide), bf16),
            pltpu.SemaphoreType.DMA((8,)),
            pltpu.SemaphoreType.DMA((8,)),
            pltpu.SemaphoreType.DMA((1 + 4 * parts,)),
        ],
        compiler_params=pltpu.CompilerParams(
            collective_id=collective_id, has_side_effects=True, vmem_limit_bytes=60 * 2**20
        ),
        cost_estimate=pl.CostEstimate(flops=10**6, bytes_accessed=10**6, transcendentals=0),
    )(*lefts, weight, *([extra] if across else []))


def head_softmax(queries, keys, visible):
    scores = lax.dot_general(
        queries, keys, (((1,), (1,)), ((), ())), preferred_element_type=f32
    ) * (HEAD_SIZE ** (-0.5))
    scores = jnp.where(visible, scores, masked)
    raised = jnp.exp(scores - jnp.max(scores, axis=-1, keepdims=True))
    return raised / jnp.sum(raised, axis=-1, keepdims=True)


def visible_keys(rows, keys):
    row = lax.broadcasted_iota(jnp.int32, (rows, keys), 0)
    key = lax.broadcasted_iota(jnp.int32, (rows, keys), 1)
    prompt_all = keys - (rows - PROMPT_DEV)
    own = lax.axis_index("ctx") * PROMPT_DEV + row
    position = jnp.where(row < PROMPT_DEV, own, prompt_all + row - PROMPT_DEV)
    return key <= position


def attention_kernel(
    query_pre_ref, gain_ref, cosine_ref, sine_ref, keys_ref, values_ref, queries_ref, attended_ref
):
    rows = query_pre_ref.shape[0]
    visible = visible_keys(rows, keys_ref.shape[0])
    keys = keys_ref[...]
    values = values_ref[...]
    for h in range(query_pre_ref.shape[1] // HEAD_SIZE):
        cols = slice(h * HEAD_SIZE, (h + 1) * HEAD_SIZE)
        v = query_pre_ref[:, cols]
        v = v * head_norm(v) * gain_ref[...]
        queries = (v * cosine_ref[...] + turn_half(v) * sine_ref[...]).astype(bf16)
        queries_ref[:, cols] = queries
        probs = head_softmax(queries, keys, visible).astype(bf16)
        attended_ref[:, cols] = dot(probs, values).astype(bf16)


def attention(query_pre, gain, cosine, sine, kv_all):
    rows, wide = query_pre.shape
    keys = kv_all.shape[0]
    group = wide // KEY_VALUE_HEADS
    small = pl.BlockSpec((rows, HEAD_SIZE), lambda i: (0, 0))
    block = pl.BlockSpec((rows, group), lambda i: (0, i))
    return pl.pallas_call(
        attention_kernel,
        grid=(KEY_VALUE_HEADS,),
        out_shape=[jax.ShapeDtypeStruct((rows, wide), bf16)] * 2,
        in_specs=[
            block,
            pl.BlockSpec((1, HEAD_SIZE), lambda i: (0, 0)),
            small,
            small,
            pl.BlockSpec((keys, HEAD_SIZE), lambda i: (0, i)),
            pl.BlockSpec((keys, HEAD_SIZE), lambda i: (0, KEY_VALUE_HEADS + i)),
        ],
        out_specs=[block, block],
        compiler_params=pltpu.CompilerParams(vmem_limit_bytes=48 * 2**20),
    )(query_pre, gain.reshape(1, HEAD_SIZE), cosine, sine, kv_all, kv_all)


def transposed_dot(a, b):
    return lax.dot_general(a, b, (((0,), (0,)), ((), ())), preferred_element_type=f32)


def attention_back_kernel(
    query_pre_ref,
    gain_ref,
    cosine_ref,
    sine_ref,
    keys_ref,
    values_ref,
    queries_ref,
    grad_ref,
    pre_grad_ref,
    key_grad_ref,
    value_grad_ref,
    gain_grad_ref,
):
    rows = query_pre_ref.shape[0]
    visible = visible_keys(rows, keys_ref.shape[0])
    keys = keys_ref[...]
    values = values_ref[...]
    scale = HEAD_SIZE ** (-0.5)
    gain_grad = jnp.zeros((rows, HEAD_SIZE), f32)
    key_grad = jnp.zeros(keys_ref.shape, f32)
    value_grad = jnp.zeros(keys_ref.shape, f32)
    for h in range(query_pre_ref.shape[1] // HEAD_SIZE):
        cols = slice(h * HEAD_SIZE, (h + 1) * HEAD_SIZE)
        queries = queries_ref[:, cols]
        grad = grad_ref[:, cols]
        probs = head_softmax(queries, keys, visible)
        prob_grad = lax.dot_general(
            grad, values, (((1,), (1,)), ((), ())), preferred_element_type=f32
        )
        delta = jnp.sum(probs * prob_grad, axis=-1, keepdims=True)
        score_grad = (probs * (prob_grad - delta)).astype(bf16)
        key_grad = key_grad + transposed_dot(score_grad, queries)
        value_grad = value_grad + transposed_dot(probs.astype(bf16), grad)
        u = dot(score_grad, keys) * scale
        u = u * cosine_ref[...] + turn_half(u * sine_ref[...])
        v = query_pre_ref[:, cols]
        inv = head_norm(v)
        gain_grad = gain_grad + u * v * inv
        pre_grad_ref[:, cols] = norm_back(v, inv, gain_ref[...], u).astype(bf16)
    key_grad_ref[...] = (key_grad * scale).astype(key_grad_ref.dtype)
    value_grad_ref[...] = value_grad.astype(value_grad_ref.dtype)
    gain_grad_ref[0] = jnp.sum(gain_grad, axis=0, keepdims=True)


def attention_back(query_pre, gain, cosine, sine, kv_all, queries, attended_grad):
    rows, wide = query_pre.shape
    keys, both = kv_all.shape
    group = wide // KEY_VALUE_HEADS
    small = pl.BlockSpec((rows, HEAD_SIZE), lambda i: (0, 0))
    block = pl.BlockSpec((rows, group), lambda i: (0, i))
    return pl.pallas_call(
        attention_back_kernel,
        grid=(KEY_VALUE_HEADS,),
        out_shape=[
            jax.ShapeDtypeStruct((rows, wide), bf16),
            jax.ShapeDtypeStruct((keys, both // 2), f32),
            jax.ShapeDtypeStruct((keys, both // 2), f32),
            jax.ShapeDtypeStruct((KEY_VALUE_HEADS, 1, HEAD_SIZE), f32),
        ],
        in_specs=[
            block,
            pl.BlockSpec((1, HEAD_SIZE), lambda i: (0, 0)),
            small,
            small,
            pl.BlockSpec((keys, HEAD_SIZE), lambda i: (0, i)),
            pl.BlockSpec((keys, HEAD_SIZE), lambda i: (0, KEY_VALUE_HEADS + i)),
            block,
            block,
        ],
        out_specs=[
            block,
            pl.BlockSpec((keys, HEAD_SIZE), lambda i: (0, i)),
            pl.BlockSpec((keys, HEAD_SIZE), lambda i: (0, i)),
            pl.BlockSpec((1, 1, HEAD_SIZE), lambda i: (i, 0, 0)),
        ],
        cost_estimate=pl.CostEstimate(flops=10**6, bytes_accessed=10**6, transcendentals=0),
        compiler_params=pltpu.CompilerParams(vmem_limit_bytes=48 * 2**20),
    )(
        query_pre, gain.reshape(1, HEAD_SIZE), cosine, sine, kv_all, kv_all, queries, attended_grad
    )


def join_halves(mine, other):
    lower = lax.axis_index("expert") == 0
    return jnp.concatenate(
        [jnp.where(lower, mine, other), jnp.where(lower, other, mine)], axis=1
    )


def dot(a, b):
    return jnp.dot(a, b, preferred_element_type=f32)


def ctx_sum(v):
    if not small_plane():
        return lax.psum_scatter(v, "ctx", scatter_dimension=1, tiled=True).astype(f32)
    member = lax.axis_index("ctx")

    def block(j):
        return lax.dynamic_slice_in_dim(v, (member ^ j) * PROMPT_DEV, PROMPT_DEV, axis=1)

    near = block(0).astype(f32) + core(block(1)).astype(f32)
    far = (block(2).astype(f32) + core(block(3)).astype(f32)).astype(bf16)
    return near + over_x(far).astype(f32)


def body(
    hidden_in,
    attn_gain,
    query_weight,
    key_matrix,
    value_matrix,
    query_gain,
    key_gain,
    output_weight,
    ffn_gain,
    router_weight,
    gate_up,
    down_proj,
    routes,
    out_grad,
):
    ctx_count = lax.axis_size("ctx")
    spread_count = lax.axis_size(plane)
    dp_count = lax.axis_size("dp")
    device_count = dp_count * spread_count
    local_experts = gate_up.shape[0]
    count_of_rows = hidden_in.shape[0]
    prompt_all = PROMPT_DEV * ctx_count
    hidden_ff = gate_up.shape[2] // 2
    member = lax.axis_index("ctx")
    offsets = jnp.arange(count_of_rows, dtype=jnp.int32)
    position = jnp.where(
        offsets < PROMPT_DEV, member * PROMPT_DEV + offsets, prompt_all + offsets - PROMPT_DEV
    )
    cosine, rope_sine = angles(position, HEAD_SIZE)
    narrow = KEY_VALUE_HEADS * HEAD_SIZE
    wide = QUERY_HEADS * HEAD_SIZE
    inputs = hidden_in.astype(f32)
    scale_in = rms_scale(inputs)

    def by_owner(v):
        v = v.reshape(count_of_rows, dp_count, spread_count, -1)
        return v.transpose(2, 0, 1, 3).reshape(spread_count, count_of_rows, -1)

    signed_sine = rope_sine * jnp.where(jnp.arange(HEAD_SIZE) < HEAD_SIZE // 2, -1.0, 1.0)
    if small_plane():
        (
            kv_other,
            q_other,
            o_other,
            g_rows,
            route_rows,
            kv_all,
            normed_owned,
            attended_owned,
            query_pre,
            key_pre,
            queries,
            residual,
            ffn_in,
        ) = fetch_and_attend(
            hidden_in, attn_gain, query_gain, key_gain, ffn_gain, cosine, signed_sine,
            key_matrix, value_matrix, query_weight, output_weight, out_grad, routes,
        )
        kv_weights = [jnp.concatenate([key_matrix, value_matrix], axis=1), kv_other]
        q_weights = [query_weight, q_other]
        o_weights = [output_weight, o_other]
    else:
        full = [
            lax.all_gather(w, "expert", axis=0, tiled=True)
            for w in (
                jnp.concatenate([key_matrix, value_matrix], axis=1),
                query_weight,
                output_weight,
            )
        ]
        kv_weights, q_weights, o_weights = [[w] for w in full]
        g_rows = lax.all_gather(out_grad, plane, axis=0, tiled=True)
        route_rows = lax.all_gather(routes, plane, axis=0, tiled=True)
        normalized_input = (inputs * scale_in * attn_gain).astype(bf16)
        query_pre = dot(normalized_input, q_weights[0])
        key_value_pre = dot(normalized_input, kv_weights[0])
        key_pre = key_value_pre[:, :narrow]
        key_heads = key_pre.reshape(count_of_rows, KEY_VALUE_HEADS, HEAD_SIZE)
        key_low = rotate(
            key_heads * rms_scale(key_heads) * key_gain, cosine[:, None, :], rope_sine[:, None, :]
        ).astype(bf16)
        kv_low = jnp.concatenate(
            [key_low.reshape(count_of_rows, narrow), key_value_pre[:, narrow:].astype(bf16)],
            axis=1,
        )
        kv_blocks = lax.all_gather(kv_low[:PROMPT_DEV], "ctx", axis=0, tiled=True)
        kv_all = jnp.concatenate([kv_blocks, kv_low[PROMPT_DEV:]], axis=0)
        queries, attended = attention(query_pre, query_gain, cosine, signed_sine, kv_all)
        residual = inputs + dot(attended, o_weights[0])
        ffn_in = (residual * rms_scale(residual) * ffn_gain).astype(bf16)
        normed_owned = by_owner(normalized_input)
        attended_owned = by_owner(attended)

    def owned(v):
        return lax.all_to_all(v, plane, split_axis=0, concat_axis=0, tiled=True)

    def backward_dot(v, weights):
        parts = [dot(v, w.T) for w in weights]
        return parts[0] if len(parts) == 1 else join_halves(*parts)

    key_before_norm = key_pre.reshape(count_of_rows, KEY_VALUE_HEADS, HEAD_SIZE)
    key_inv = rms_scale(key_before_norm)
    scale_ffn = rms_scale(residual)

    expert_count = local_experts * spread_count
    expert_ids = jnp.arange(expert_count, dtype=jnp.int32)

    def gates_of(some_rows, some_routes):
        logits = dot(some_rows, router_weight)
        chosen = jnp.any(some_routes[:, :, None] == expert_ids[None, None, :], axis=1)
        logits = jnp.where(chosen, logits, masked)
        raised = jnp.where(
            chosen, jnp.exp(logits - jnp.max(logits, axis=-1, keepdims=True)), 0.0
        )
        return raised / jnp.sum(raised, axis=-1, keepdims=True)

    gates = gates_of(ffn_in, routes)
    if small_plane():
        rows, hidden, grads, gates_mine, totals = gather_first_expert(
            ffn_in, route_rows, router_weight, g_rows, gate_up, down_proj
        )
        hiddens = [hidden]
        down_parts = [dot(hidden.T, g_rows).astype(bf16)]
        rows, grads, attended_owned, normed_owned = lax.optimization_barrier(
            ((rows, grads, attended_owned, normed_owned), down_parts)
        )[0]
        attended_owned, normed_owned = owned(attended_owned), owned(normed_owned)
        hidden, grads, gate_grads = last_expert(
            1, expert_count, rows, g_rows, gates_mine, totals, gate_up, down_proj, grads
        )
        hiddens.append(hidden)
        projected_grads = [grads]
        down_parts.append(dot(hidden.T, g_rows).astype(bf16))
        gate_up_parts = [dot(after(rows, down_parts).T, grads).astype(bf16)]
    else:
        rows = lax.all_gather(ffn_in, plane, axis=0, tiled=True)
        first_expert = lax.axis_index(plane) * local_experts
        gates_mine = lax.dynamic_slice_in_dim(
            gates_of(rows, route_rows), first_expert, local_experts, axis=1
        )
        gate_grads, hiddens, projected_grads = [], [], []
        for which in range(local_experts):
            gate = gates_mine[:, which : which + 1]
            projected = dot(rows, gate_up[which])
            back = dot(g_rows, down_proj[which].T)
            gate_part = projected[:, :hidden_ff]
            up_part = projected[:, hidden_ff:]
            sigmoid_gate = jax.nn.sigmoid(gate_part)
            hidden = gate_part * sigmoid_gate * up_part
            gate_grads.append(jnp.sum(hidden * back, axis=-1))
            hiddens.append((gate * hidden).astype(bf16))
            back = gate * back
            gate_back = back * up_part * sigmoid_gate * (1.0 + gate_part * (1.0 - sigmoid_gate))
            up_back = back * gate_part * sigmoid_gate
            projected_grads.append(jnp.concatenate([gate_back, up_back], axis=-1).astype(bf16))
        attended_owned, normed_owned = owned(attended_owned), owned(normed_owned)
        down_parts = [dot(v.T, g_rows).astype(bf16) for v in hiddens]
        gate_up_parts = [dot(rows.T, v).astype(bf16) for v in projected_grads]
    down_low, gate_up_low = [
        [lax.psum_scatter(v, "dp", scatter_dimension=0, tiled=True) for v in parts]
        for parts in (down_parts, gate_up_parts)
    ]
    down_grad = jnp.stack([v.astype(f32) for v in down_low])
    gate_up_grad = jnp.stack(
        [
            part.astype(f32)
            for v in gate_up_low
            for part in jnp.split(v, v.shape[1] // (2 * hidden_ff), axis=1)
        ]
    )
    projected_grads, hiddens = lax.optimization_barrier(
        ((projected_grads, hiddens), down_parts, gate_up_parts, attended_owned, normed_owned)
    )[0]
    if small_plane():
        back = plane_sum(projected_grads, gate_up, gate_grads, 3)
        back_sum = back[:, :MODEL_WIDTH]
        gate_grad = (
            back[:, MODEL_WIDTH : MODEL_WIDTH + expert_count]
            + back[:, MODEL_WIDTH + expert_count : MODEL_WIDTH + 2 * expert_count]
        )
        moe_sum = None
    else:
        moe_part = 0.0
        row_part = 0.0
        for which in range(local_experts):
            row_part = row_part + dot(projected_grads[which], gate_up[which].T)
            moe_part = moe_part + dot(hiddens[which], down_proj[which])
        moe_sum, back_sum = [
            lax.psum_scatter(v.astype(bf16), plane, scatter_dimension=0, tiled=True).astype(f32)
            for v in (moe_part, row_part)
        ]
        gate_grad = lax.all_to_all(
            jnp.stack(gate_grads, axis=1).reshape(spread_count, count_of_rows, local_experts),
            plane,
            split_axis=0,
            concat_axis=0,
            tiled=True,
        )
        gate_grad = gate_grad.transpose(1, 0, 2).reshape(count_of_rows, expert_count)
    logit_grad = gates * (gate_grad - jnp.sum(gates * gate_grad, axis=-1, keepdims=True))

    grad_out = out_grad.astype(f32)
    router_local = jnp.dot(ffn_in.T, logit_grad, preferred_element_type=f32)
    ffn_in_grad = back_sum + jnp.dot(
        logit_grad, router_weight.astype(f32).T, precision=highest
    )
    residual_grad = grad_out + norm_back(residual, scale_ffn, ffn_gain, ffn_in_grad)
    ffn_gain_local = jnp.sum(ffn_in_grad * residual * scale_ffn, axis=0)
    branch_low = residual_grad.astype(bf16)
    attended_grad = backward_dot(branch_low, o_weights).astype(bf16)
    query_pre_grad, key_grad_all, value_grad_all, query_gain_parts = attention_back(
        query_pre, query_gain, cosine, signed_sine, kv_all, queries, attended_grad
    )
    query_gain_local = jnp.sum(query_gain_parts, axis=(0, 1))
    pair_grads = jnp.stack([key_grad_all[:prompt_all], value_grad_all[:prompt_all]]).astype(bf16)
    prompt_grads = ctx_sum(pair_grads)
    key_grad = jnp.concatenate([prompt_grads[0], key_grad_all[prompt_all:]], axis=0).reshape(
        count_of_rows, KEY_VALUE_HEADS, HEAD_SIZE
    )
    value_gradient = jnp.concatenate([prompt_grads[1], value_grad_all[prompt_all:]], axis=0)
    key_rot_grad = rotate_back(key_grad, cosine[:, None, :], rope_sine[:, None, :])
    key_gain_local = jnp.sum(key_rot_grad * key_before_norm * key_inv, axis=(0, 1))
    key_pre_grad = (
        norm_back(key_before_norm, key_inv, key_gain, key_rot_grad)
        .astype(bf16)
        .reshape(count_of_rows, KEY_VALUE_HEADS * HEAD_SIZE)
    )
    key_value_grad = jnp.concatenate([key_pre_grad, value_gradient.astype(bf16)], axis=1)
    if small_plane():
        local = [
            weight_grads(query_pre_grad, key_value_grad, branch_low, attended_owned, normed_owned)
        ]
    else:
        branch_rows = lax.all_gather(branch_low, plane, axis=0, tiled=True)
        pre_rows = lax.all_gather(
            jnp.concatenate([query_pre_grad, key_value_grad], axis=1), plane, axis=0, tiled=True
        )
        attended_owned, normed_owned = [
            v.reshape(spread_count * count_of_rows, -1) for v in (attended_owned, normed_owned)
        ]
        local = [
            dot(attended_owned.T, branch_rows).astype(bf16),
            dot(normed_owned.T, pre_rows).astype(bf16),
        ]
    query_pre_grad, key_value_grad = lax.optimization_barrier(
        ((query_pre_grad, key_value_grad), local)
    )[0]
    normed_grad = backward_dot(query_pre_grad, q_weights) + backward_dot(
        key_value_grad, kv_weights
    )
    attn_gain_local = jnp.sum(normed_grad * inputs * scale_in, axis=0)
    hidden_grad = residual_grad + norm_back(inputs, scale_in, attn_gain, normed_grad)
    if small_plane():
        moe_sum = plane_sum(after(hiddens, local), down_proj, None, 4)
    block_out = (residual + moe_sum).astype(bf16)
    local = lax.optimization_barrier((local, gate_up_low, down_low))[0]
    summed = [
        lax.psum_scatter(v, "dp", scatter_dimension=0, tiled=True).astype(f32) for v in local
    ]
    share = MODEL_WIDTH // device_count
    if small_plane():
        tile = summed[0].shape[1]
        cut = wide // device_count * (MODEL_WIDTH // tile)

        def untile(v, rows):
            return jnp.concatenate(
                [v[i : i + rows] for i in range(0, v.shape[0], rows)], axis=1
            )

        output_sum = untile(summed[0][:cut], wide // device_count)
        pre_sum = untile(summed[0][cut:], share)
    else:
        output_sum, pre_sum = summed

    small = jnp.concatenate(
        [
            v.reshape(device_count, -1)
            for v in (
                attn_gain_local,
                ffn_gain_local,
                query_gain_local,
                key_gain_local,
                router_local,
            )
        ],
        axis=1,
    )
    small = lax.all_to_all(small[:, None], every, split_axis=0, concat_axis=0, tiled=True)
    small = jnp.sum(small[:, 0], axis=0)
    head_share = HEAD_SIZE // device_count
    cuts = [share, share, head_share, head_share, share * expert_count]
    ends = [sum(cuts[: i + 1]) for i in range(5)]
    a_grad, f_grad, q_grad, k_grad, r_grad = [
        small[end - cut : end] for end, cut in zip(ends, cuts)
    ]
    return (
        block_out,
        hidden_grad,
        a_grad,
        pre_sum[:, :wide],
        pre_sum[:, wide : wide + narrow],
        pre_sum[:, wide + narrow :],
        q_grad,
        k_grad,
        output_sum,
        f_grad,
        r_grad.reshape(share, expert_count),
        gate_up_grad,
        down_grad,
    )


def solution(mesh):
    placed = (
        P(("dp", "ctx", "expert"), None),
        P(),
        P("expert", None),
        P("expert", None),
        P("expert", None),
        P(),
        P(),
        P("expert", None),
        P(),
        P(),
        P(("ctx", "expert"), None, None),
        P(("ctx", "expert"), None, None),
        P(("dp", "ctx", "expert"), None),
        P(("dp", "ctx", "expert"), None),
    )
    return jax.shard_map(
        body,
        mesh=mesh,
        in_specs=placed,
        out_specs=(
            P(("dp", "ctx", "expert"), None),
            P(("dp", "ctx", "expert"), None),
            P(("dp", "ctx", "expert")),
            P(("dp", "ctx", "expert"), None),
            P(("dp", "ctx", "expert"), None),
            P(("dp", "ctx", "expert"), None),
            P(("dp", "ctx", "expert")),
            P(("dp", "ctx", "expert")),
            P(("dp", "ctx", "expert"), None),
            P(("dp", "ctx", "expert")),
            P(("dp", "ctx", "expert"), None),
            P(("ctx", "expert"), "dp", None),
            P(("ctx", "expert"), "dp", None),
        ),
        check_vma=False,
    )
```

```python
import math

import jax
import jax.numpy as jnp
from jax import lax
from jax.experimental import pallas as pl
from jax.experimental.pallas import tpu as pltpu
from jax.sharding import PartitionSpec as P

MODEL_WIDTH = 2048
QUERY_HEADS = 32
KEY_VALUE_HEADS = 4
HEAD_SIZE = 128
TOP = 8
PROMPT_DEV = 128


highest = lax.Precision.HIGHEST
epsilon = 1e-06
rope_base = 1000000.0
masked = -1e30
every = ("dp", "ctx", "expert")
plane = ("ctx", "expert")
bf16 = jnp.bfloat16
f32 = jnp.float32


def rms_scale(value_rows):
    return lax.rsqrt(jnp.mean(value_rows * value_rows, axis=-1, keepdims=True) + epsilon)


def norm_back(inputs, inv_rms, norm_gain, gradient):
    weighted = gradient * norm_gain
    return inv_rms * weighted - inputs * inv_rms**3 * jnp.mean(
        weighted * inputs, axis=-1, keepdims=True
    )


def angles(position, head_width):
    freq_index = jnp.arange(head_width // 2, dtype=f32)
    inverse = jnp.exp(-(2.0 * freq_index / head_width) * math.log(rope_base))
    rope_angle = position.astype(f32)[:, None] * inverse[None, :]
    rope_angle = jnp.concatenate([rope_angle, rope_angle], axis=-1)
    return (jnp.cos(rope_angle), jnp.sin(rope_angle))


def rotate(value_rows, cosine, rope_sine):
    half_width = value_rows.shape[-1] // 2
    turned = jnp.concatenate([-value_rows[..., half_width:], value_rows[..., :half_width]], axis=-1)
    return value_rows * cosine + turned * rope_sine


def rotate_back(gradient, cosine, rope_sine):
    shifted = gradient * rope_sine
    half_width = gradient.shape[-1] // 2
    return gradient * cosine + jnp.concatenate(
        [shifted[..., half_width:], -shifted[..., :half_width]], axis=-1
    )


def small_plane():
    return [lax.axis_size(a) for a in every] == [4, 4, 2]


def swap(v, axis, bit):
    return lax.ppermute(v, axis, [(i, i ^ bit) for i in range(lax.axis_size(axis))])


def core(v):
    return swap(v, "ctx", 1)


def over_x(v):
    return swap(v, "ctx", 2)


def over_y(v):
    return swap(v, "expert", 1)


def over_z(v):
    return swap(v, "dp", 1)


def after(v, *earlier):
    return lax.optimization_barrier((v, *earlier))[0]


class Places:
    def __init__(self):
        self.dp = lax.axis_index("dp")
        ctx = lax.axis_index("ctx")
        self.ctx = ctx
        self.z = lax.rem(self.dp, 2)
        self.x = lax.div(ctx, 2)
        self.c = lax.rem(ctx, 2)
        self.y = lax.axis_index("expert")
        self.to_x = {"ctx": (1 - self.x) * 2 + self.c}
        self.to_c = {"ctx": self.x * 2 + 1 - self.c}
        self.to_y = {"expert": 1 - self.y}
        self.to_z = {"dp": self.dp + 1 - 2 * self.z}

    def peers(self):
        found = []
        for r in range(1, 8):
            x, c, y = [
                1 - v if r & bit else v for v, bit in ((self.x, 4), (self.c, 2), (self.y, 1))
            ]
            found.append((x * 4 + c * 2 + y, {"ctx": x * 2 + c, "expert": y}))
        return found


def plane_slot(x, c, y):
    return x * 4 + y * 2 + c


def greet(targets):
    barrier = pltpu.get_barrier_semaphore()
    for target in targets:
        pl.semaphore_signal(barrier, inc=1, device_id=target, device_id_type=pl.DeviceIdType.MESH)
    pl.semaphore_wait(barrier, len(targets))


class Sender:
    def __init__(self, send_sem, recv_sem):
        self.send_sem = send_sem
        self.recv_sem = recv_sem
        self.copies = []

    def __call__(self, source, target_ref, device):
        i = len(self.copies)
        copy = pltpu.make_async_remote_copy(
            src_ref=source,
            dst_ref=target_ref,
            send_sem=self.send_sem.at[i],
            recv_sem=self.recv_sem.at[i],
            device_id=device,
            device_id_type=pl.DeviceIdType.MESH,
        )
        copy.start()
        self.copies.append(copy)
        return copy

    def finish(self):
        for copy in self.copies:
            copy.wait_send()


def half_fetch(here, send, sources, other, columns, rows, upper):
    def at(piece, part=None):
        first, size = piece * rows, rows
        if part == 0:
            size = upper
        elif part == 1:
            first, size = first + upper, rows - upper
        return other.at[pl.ds(pl.multiple_of(first, 16), size), columns]

    def piece(z, x, c):
        return z * 4 + x * 2 + c

    z, x, c = here.z, here.x, here.c
    got = {}

    def first():
        mine = piece(z, x, c)
        got["y"] = [
            send(
                source.at[pl.ds(pl.multiple_of(mine * rows, rows), rows), source_columns],
                other.at[pl.ds(pl.multiple_of(mine * rows, rows), rows), target_columns],
                here.to_y,
            )
            for source, source_columns, target_columns in sources
        ]

    def second():
        for copy in got["y"]:
            copy.wait_recv()
        mine = at(piece(z, x, c))
        got["x"] = send(mine, mine, here.to_x)
        got["z"] = send(mine, mine, here.to_z)
        got["c"] = send(mine, mine, here.to_c)

    def third():
        got["x"].wait_recv()
        from_x = piece(z, 1 - x, c)
        got["low"] = send(at(from_x, 1), at(from_x, 1), here.to_z)
        got["xc"] = send(at(from_x), at(from_x), here.to_c)
        got["z"].wait_recv()
        from_z = piece(1 - z, x, c)
        got["top"] = send(at(from_z, 0), at(from_z, 0), here.to_x)
        got["zc"] = send(at(from_z), at(from_z), here.to_c)

    def fourth():
        far = piece(1 - z, 1 - x, c)
        got["low"].wait_recv()
        got["lowc"] = send(at(far, 1), at(far, 1), here.to_c)
        got["top"].wait_recv()
        got["topc"] = send(at(far, 0), at(far, 0), here.to_c)

    def fifth():
        for name in ("c", "xc", "zc", "lowc", "topc"):
            got[name].wait_recv()

    return [first, second, third, fourth, fifth]


def block_gather(here, send, mine, local_sem, blocks, far_over_y=False, columns=None):
    rows = blocks.shape[0] // lax.axis_size(plane)
    half = rows // 2
    x, c, y = here.x, here.c, here.y
    got = {}

    def at(slot, part=None):
        first, size = slot * rows, rows
        if part is not None:
            first, size = first + part * half, half
        rows_of = pl.ds(pl.multiple_of(first, size), size)
        return blocks.at[rows_of] if columns is None else blocks.at[rows_of, columns]

    def first():
        slot = plane_slot(x, c, y)
        got["own"] = pltpu.make_async_copy(mine, at(slot), local_sem)
        got["own"].start()
        got["y"] = send(mine, at(slot), here.to_y)
        got["x"] = send(mine, at(slot), here.to_x)
        got["c"] = send(mine, at(slot), here.to_c)

    def second():
        got["y"].wait_recv()
        from_y = plane_slot(x, c, 1 - y)
        got["yc"] = send(at(from_y), at(from_y), here.to_c)
        if not far_over_y:
            got["top"] = send(at(from_y, 0), at(from_y, 0), here.to_x)
        got["x"].wait_recv()
        from_x = plane_slot(1 - x, c, y)
        got["xc"] = send(at(from_x), at(from_x), here.to_c)
        if far_over_y:
            got["top"] = send(at(from_x, 0), at(from_x, 0), here.to_y)
        got["low"] = send(at(from_x, 1), at(from_x, 1), here.to_y)

    def third():
        far = plane_slot(1 - x, c, 1 - y)
        got["top"].wait_recv()
        got["topc"] = send(at(far, 0), at(far, 0), here.to_c)
        got["low"].wait_recv()
        got["lowc"] = send(at(far, 1), at(far, 1), here.to_c)

    def fourth():
        for name in ("c", "yc", "xc", "topc", "lowc"):
            got[name].wait_recv()
        got["own"].wait()

    return [first, second, third, fourth], got


def turn_half(v):
    return pltpu.roll(v, v.shape[-1] // 2, axis=1)


def head_norm(v):
    return lax.rsqrt(jnp.mean(v * v, axis=-1, keepdims=True) + epsilon)


def fetch_kernel(
    hidden_ref,
    attn_gain_ref,
    query_gain_ref,
    key_gain_ref,
    ffn_gain_ref,
    cosine_ref,
    sine_ref,
    key_ref,
    value_ref,
    query_ref,
    output_ref,
    grad_ref,
    routes_ref,
    kv_out,
    q_out,
    o_out,
    g_blocks,
    route_blocks,
    kv_all_out,
    normed_owned,
    attended_owned,
    query_pre_ref,
    key_pre_ref,
    queries_ref,
    residual_ref,
    ffn_ref,
    normed_ref,
    attended_ref,
    kv_own,
    kv_other,
    q_own,
    q_other,
    o_own,
    o_other,
    kv_pre,
    kv_low,
    kv_all,
    send_sem,
    recv_sem,
    local_sem,
):
    here = Places()
    greet([here.to_y, here.to_z, here.to_c, here.to_x])
    send = Sender(send_sem, recv_sem)
    count, width = hidden_ref.shape
    half = width // 2
    narrow = key_ref.shape[1]
    wide = query_ref.shape[1]
    prompt_all = kv_all.shape[0] - (count - PROMPT_DEV)
    spread, groups = lax.axis_size(plane), lax.axis_size("dp")
    tile = 512
    loads = [
        pltpu.make_async_copy(key_ref, kv_own.at[:, pl.ds(0, narrow)], local_sem.at[0]),
        pltpu.make_async_copy(value_ref, kv_own.at[:, pl.ds(narrow, narrow)], local_sem.at[1]),
        pltpu.make_async_copy(query_ref, q_own, local_sem.at[2]),
        pltpu.make_async_copy(output_ref, o_own, local_sem.at[3]),
    ]
    stores = [
        pltpu.make_async_copy(kv_other, kv_out, local_sem.at[4]),
        pltpu.make_async_copy(q_other, q_out, local_sem.at[5]),
        pltpu.make_async_copy(o_other, o_out, local_sem.at[6]),
        pltpu.make_async_copy(kv_all, kv_all_out, local_sem.at[7]),
    ]

    def part_of(size, which):
        first = here.y * size if which == 0 else size - here.y * size
        return pl.ds(pl.multiple_of(first, size), size)

    def project(source, weight, out, which, first, count_of_tiles, add):
        rows = part_of(weight.shape[0], which)

        @pl.loop(first, first + count_of_tiles)
        def _(i):
            cols = pl.ds(pl.multiple_of(i * tile, tile), tile)
            part = dot(source[:, rows], weight[:, cols])
            out[:, cols] = out[:, cols] + part if add else part

    def start():
        for load in loads:
            load.start()
        inputs = hidden_ref[...].astype(f32)
        normed_ref[...] = (inputs * head_norm(inputs) * attn_gain_ref[...]).astype(bf16)

    def own_part():
        share = width // (spread * groups)
        for s in range(spread):
            normed_owned[s] = jnp.concatenate(
                [
                    normed_ref[:, (d * spread + s) * share : (d * spread + s + 1) * share]
                    for d in range(groups)
                ],
                axis=1,
            )
        for load in loads[:3]:
            load.wait()
        project(normed_ref, kv_own, kv_pre, 0, 0, 2 * narrow // tile, False)
        project(normed_ref, q_own, query_pre_ref, 0, 0, wide // tile, False)

    exchange = {}

    def keys_part():
        project(normed_ref, kv_other, kv_pre, 1, 0, 2 * narrow // tile, True)
        stores[0].start()
        key_pre_ref[...] = kv_pre[:, :narrow]
        for h in range(narrow // HEAD_SIZE):
            cols = slice(h * HEAD_SIZE, (h + 1) * HEAD_SIZE)
            v = kv_pre[:, cols]
            v = v * head_norm(v) * key_gain_ref[...]
            kv_low[:, cols] = (v * cosine_ref[...] + turn_half(v) * sine_ref[...]).astype(bf16)
        kv_low[:, narrow:] = kv_pre[:, narrow:].astype(bf16)
        kv_all[prompt_all:, :] = kv_low[PROMPT_DEV:, :]
        source = kv_low.at[pl.ds(0, PROMPT_DEV)]
        slot = kv_all.at[pl.ds(pl.multiple_of(here.ctx * PROMPT_DEV, PROMPT_DEV), PROMPT_DEV)]
        exchange["own"] = pltpu.make_async_copy(source, slot, local_sem.at[8])
        exchange["own"].start()
        exchange["c"] = send(source, slot, here.to_c)
        exchange["x"] = send(source, slot, here.to_x)

    def keys_forward():
        exchange["x"].wait_recv()
        first = ((1 - here.x) * 2 + here.c) * PROMPT_DEV
        slot = kv_all.at[pl.ds(pl.multiple_of(first, PROMPT_DEV), PROMPT_DEV)]
        exchange["xc"] = send(slot, slot, here.to_c)

    def queries_first():
        project(normed_ref, q_other, query_pre_ref, 1, 0, wide // tile // 2, True)

    def queries_rest():
        stores[1].start()
        project(
            normed_ref, q_other, query_pre_ref, 1, wide // tile // 2, wide // tile // 2, True
        )
        for name in ("c", "xc"):
            exchange[name].wait_recv()
        exchange["own"].wait()
        stores[3].start()

    group = 4
    pieces = 4

    def attend(part):
        visible = visible_keys(count, kv_all.shape[0])
        blocks = wide // HEAD_SIZE // group // pieces

        @pl.loop(part * blocks, (part + 1) * blocks)
        def _(i):
            first = lax.div(i * group, wide // narrow) * HEAD_SIZE
            keys = kv_all[:, pl.ds(pl.multiple_of(first, HEAD_SIZE), HEAD_SIZE)]
            values = kv_all[:, pl.ds(pl.multiple_of(narrow + first, HEAD_SIZE), HEAD_SIZE)]
            for h in range(group):
                cols = pl.ds(pl.multiple_of((i * group + h) * HEAD_SIZE, HEAD_SIZE), HEAD_SIZE)
                v = query_pre_ref[:, cols]
                v = v * head_norm(v) * query_gain_ref[...]
                queries = (v * cosine_ref[...] + turn_half(v) * sine_ref[...]).astype(bf16)
                queries_ref[:, cols] = queries
                probs = head_softmax(queries, keys, visible).astype(bf16)
                attended = dot(probs, values).astype(bf16)
                attended_ref[:, cols] = attended
                head = i * group + h
                at = pl.multiple_of(lax.div(head, spread) * HEAD_SIZE, HEAD_SIZE)
                attended_owned[lax.rem(head, spread), :, pl.ds(at, HEAD_SIZE)] = attended

    def output_own():
        loads[3].wait()
        project(attended_ref, o_own, residual_ref, 0, 0, width // tile, False)

    def finish_rows():
        stores[2].start()
        project(attended_ref, o_other, residual_ref, 1, 0, width // tile, True)
        residual = residual_ref[...] + hidden_ref[...].astype(f32)
        residual_ref[...] = residual
        ffn_ref[...] = (residual * head_norm(residual) * ffn_gain_ref[...]).astype(bf16)

    low, high = pl.ds(0, wide // 2), pl.ds(wide // 2, wide // 2)
    o_low, o_high = pl.ds(0, width // 2), pl.ds(width // 2, width // 2)
    rows, o_rows = half // 8, output_ref.shape[0] // 8
    kv, qa, qb, oa, ob, g, r = [
        half_fetch(
            here,
            send,
            [
                (key_ref, pl.ds(0, narrow), pl.ds(0, narrow)),
                (value_ref, pl.ds(0, narrow), pl.ds(narrow, narrow)),
            ],
            kv_other,
            pl.ds(0, 2 * narrow),
            rows,
            rows // 2,
        ),
        half_fetch(here, send, [(query_ref, low, low)], q_other, low, rows, rows // 2),
        half_fetch(here, send, [(query_ref, high, high)], q_other, high, rows, rows // 2),
        half_fetch(here, send, [(output_ref, o_low, o_low)], o_other, o_low, o_rows, o_rows // 4),
        half_fetch(
            here, send, [(output_ref, o_high, o_high)], o_other, o_high, o_rows, o_rows // 4
        ),
        block_gather(here, send, grad_ref, local_sem.at[9], g_blocks, True)[0],
        block_gather(here, send, routes_ref, local_sem.at[10], route_blocks)[0],
    ]
    steps = [
        kv[0], qa[0], qb[0], oa[0], ob[0], g[0], start, kv[1], kv[2], own_part, qa[1],
        kv[3], qa[2], qb[1], kv[4], keys_part, qa[3], qb[2], oa[1],
        keys_forward, qa[4], queries_first, qb[3], ob[1], qb[4], queries_rest,
        oa[2], r[0], lambda: attend(0), lambda: attend(1),
        oa[3], ob[2], g[1], r[1], lambda: attend(2), lambda: attend(3), oa[4], output_own,
        ob[3], g[2], r[2], ob[4], finish_rows, g[3], r[3],
    ]
    for step in steps:
        step()
    for store in stores:
        store.wait()
    send.finish()


def fetch_and_attend(
    hidden_in, attn_gain, query_gain, key_gain, ffn_gain, cosine, sine, key_matrix, value_matrix,
    query_weight, output_weight, out_grad, routes,
):
    rows, width = hidden_in.shape
    half, wide = query_weight.shape
    narrow = key_matrix.shape[1]
    spread = lax.axis_size(plane)
    keys = lax.axis_size("ctx") * PROMPT_DEV + rows - PROMPT_DEV
    vmem = pl.BlockSpec(memory_space=pltpu.VMEM)
    anywhere = pl.BlockSpec(memory_space=pl.ANY)
    copies = 5 * 10 + 1 + 2 * 9 + 3
    return pl.pallas_call(
        fetch_kernel,
        out_shape=[
            jax.ShapeDtypeStruct((half, 2 * narrow), bf16),
            jax.ShapeDtypeStruct((half, wide), bf16),
            jax.ShapeDtypeStruct(output_weight.shape, bf16),
            jax.ShapeDtypeStruct((spread * rows, width), bf16),
            jax.ShapeDtypeStruct((spread * rows, routes.shape[1]), jnp.int32),
            jax.ShapeDtypeStruct((keys, 2 * narrow), bf16),
            jax.ShapeDtypeStruct((spread, rows, width // spread), bf16),
            jax.ShapeDtypeStruct((spread, rows, wide // spread), bf16),
            jax.ShapeDtypeStruct((rows, wide), f32),
            jax.ShapeDtypeStruct((rows, narrow), f32),
            jax.ShapeDtypeStruct((rows, wide), bf16),
            jax.ShapeDtypeStruct((rows, width), f32),
            jax.ShapeDtypeStruct((rows, width), bf16),
        ],
        in_specs=[vmem] * 7 + [anywhere] * 6,
        out_specs=[anywhere] * 6 + [vmem] * 7,
        scratch_shapes=[
            pltpu.VMEM((rows, width), bf16),
            pltpu.VMEM((rows, wide), bf16),
            pltpu.VMEM((half, 2 * narrow), bf16),
            pltpu.VMEM((half, 2 * narrow), bf16),
            pltpu.VMEM((half, wide), bf16),
            pltpu.VMEM((half, wide), bf16),
            pltpu.VMEM(output_weight.shape, bf16),
            pltpu.VMEM(output_weight.shape, bf16),
            pltpu.VMEM((rows, 2 * narrow), f32),
            pltpu.VMEM((rows, 2 * narrow), bf16),
            pltpu.VMEM((keys, 2 * narrow), bf16),
            pltpu.SemaphoreType.DMA((copies,)),
            pltpu.SemaphoreType.DMA((copies,)),
            pltpu.SemaphoreType.DMA((11,)),
        ],
        compiler_params=pltpu.CompilerParams(
            collective_id=1, has_side_effects=True, vmem_limit_bytes=60 * 2**20
        ),
        cost_estimate=pl.CostEstimate(
            flops=2 * rows * width * (2 * wide + 2 * narrow) * 2,
            bytes_accessed=60 * 2**20,
            transcendentals=0,
        ),
    )(
        hidden_in, attn_gain.reshape(1, width), query_gain.reshape(1, HEAD_SIZE),
        key_gain.reshape(1, HEAD_SIZE), ffn_gain.reshape(1, width), cosine, sine,
        key_matrix, value_matrix, query_weight, output_weight, out_grad, routes,
    )


def chip_rows(x, y, rows):
    first = plane_slot(x, 0, y) * rows
    return pl.ds(pl.multiple_of(first, rows), 2 * rows)


def expert_chunk(some, first, rows_v, g_v, gate_up_v, down_v, hidden_v, grad_v, total_v, gate, mark):
    ff = down_v.shape[0]
    tile = 256

    @pl.loop(0, ff // tile, unroll=True)
    def _(f):
        at = pl.multiple_of(f * tile, tile)
        a = dot(rows_v[some, :], gate_up_v[:, pl.ds(at, tile)])
        b = dot(rows_v[some, :], gate_up_v[:, pl.ds(ff + at, tile)])
        q = lax.dot_general(
            g_v[some, :],
            down_v[pl.ds(at, tile), :],
            (((1,), (1,)), ((), ())),
            preferred_element_type=f32,
        )
        s = 1.0 / (1.0 + jnp.exp(-a))
        raised_a = a * s
        hidden = raised_a * b
        total_v[...] = total_v[...] + jnp.where(
            mark, jnp.sum(hidden * q, axis=-1, keepdims=True), 0.0
        )
        back = gate * q
        hidden_v[some, pl.ds(at, tile)] = (gate * hidden).astype(bf16)
        grad_v[some, pl.ds(at, tile)] = (back * b * s * (1.0 + a * (1.0 - s))).astype(bf16)
        grad_v[some, pl.ds(ff + at, tile)] = (back * raised_a).astype(bf16)


def first_expert_kernel(
    ffn_ref,
    routes_ref,
    router_ref,
    g_hbm,
    gate_up_hbm,
    down_hbm,
    rows_out,
    hidden_out,
    grad_out,
    gates_ref,
    gate_grad_ref,
    down_grad_ref,
    rows_v,
    g_v,
    gate_up_v,
    down_v,
    hidden_v,
    grad_v,
    total_v,
    down_total,
    send_sem,
    recv_sem,
    local_sem,
):
    here = Places()
    greet([here.to_y, here.to_c, here.to_x])
    send = Sender(send_sem, recv_sem)
    count = ffn_ref.shape[0]
    experts = router_ref.shape[0]
    local_experts = down_hbm.shape[0]
    stages, got = block_gather(here, send, ffn_ref, local_sem.at[0], rows_v)
    stages[0]()
    loads = [
        pltpu.make_async_copy(gate_up_hbm.at[0], gate_up_v, local_sem.at[1]),
        pltpu.make_async_copy(down_hbm.at[0], down_v, local_sem.at[2]),
        pltpu.make_async_copy(g_hbm, g_v, local_sem.at[3]),
    ]
    for load in loads:
        load.start()
    first_expert = plane_index(here) * local_experts
    stores = []

    def chunk(x, y):
        some = chip_rows(x, y, count)
        logits = lax.dot_general(
            rows_v[some, :],
            router_ref[...],
            (((1,), (1,)), ((), ())),
            preferred_element_type=f32,
        )
        ids = lax.broadcasted_iota(jnp.int32, logits.shape, 1)
        routes = routes_ref[some, :]
        chosen = ids < 0
        for k in range(routes.shape[1]):
            chosen = chosen | (routes[:, k : k + 1] == ids)
        logits = jnp.where(chosen, logits, masked)
        raised = jnp.exp(logits - jnp.max(logits, axis=-1, keepdims=True))
        raised = jnp.where(chosen, raised, 0.0)
        gates = raised / jnp.sum(raised, axis=-1, keepdims=True)
        lane = lax.broadcasted_iota(jnp.int32, total_v.shape, 1)
        total_v[...] = jnp.zeros(total_v.shape, f32)
        columns = [
            jnp.sum(jnp.where(ids == first_expert + e, gates, 0.0), axis=-1, keepdims=True)
            for e in range(local_experts)
        ]
        spread = jnp.zeros(total_v.shape, f32)
        for e in range(local_experts):
            spread = jnp.where(lane == e, columns[e], spread)
        gates_ref[some, :] = spread
        mark = (lane == first_expert) | (lane == first_expert + experts)
        expert_chunk(
            some, 0, rows_v, g_v, gate_up_v, down_v, hidden_v, grad_v, total_v, columns[0], mark
        )
        gate_grad_ref[some, :] = total_v[...]
        for source, target in ((hidden_v, hidden_out), (grad_v, grad_out), (rows_v, rows_out)):
            columns = pl.ds(0, source.shape[1])
            store = pltpu.make_async_copy(
                source.at[some, :], target.at[some, columns], local_sem.at[4 + len(stores)]
            )
            store.start()
            stores.append(store)
        add_down(some, len(stores) == 3, len(stores) == 12)

    def add_down(some, is_first, is_last):
        tile = 512

        @pl.loop(0, down_total.shape[1] // tile)
        def _(i):
            cols = pl.ds(pl.multiple_of(i * tile, tile), tile)
            part = transposed_dot(hidden_v[some, :], g_v[some, cols])
            if not is_first:
                part = part + down_total[:, cols]
            if is_last:
                down_grad_ref[:, cols] = part.astype(bf16)
            else:
                down_total[:, cols] = part

    x, y = here.x, here.y
    for name in ("c", "own"):
        arrive(got, name)
    for load in loads:
        load.wait()
    chunk(x, y)
    stages[1]()
    arrive(got, "yc")
    chunk(x, 1 - y)
    stages[2]()
    arrive(got, "xc")
    chunk(1 - x, y)
    arrive(got, "topc")
    arrive(got, "lowc")
    chunk(1 - x, 1 - y)
    for store in stores:
        store.wait()
    send.finish()


def gather_first_expert(ffn_in, route_rows, router_weight, g_rows, gate_up, down_proj):
    experts, ff, width = down_proj.shape
    total = route_rows.shape[0]
    vmem = pl.BlockSpec(memory_space=pltpu.VMEM)
    anywhere = pl.BlockSpec(memory_space=pl.ANY)
    return pl.pallas_call(
        first_expert_kernel,
        out_shape=[
            jax.ShapeDtypeStruct((total, width), bf16),
            jax.ShapeDtypeStruct((total, ff), bf16),
            jax.ShapeDtypeStruct((total, 2 * experts * ff), bf16),
            jax.ShapeDtypeStruct((total, 128), f32),
            jax.ShapeDtypeStruct((total, 128), f32),
            jax.ShapeDtypeStruct((ff, width), bf16),
        ],
        in_specs=[vmem] * 3 + [anywhere] * 3,
        out_specs=[anywhere] * 3 + [vmem] * 3,
        scratch_shapes=[
            pltpu.VMEM((total, width), bf16),
            pltpu.VMEM((total, width), bf16),
            pltpu.VMEM(gate_up.shape[1:], bf16),
            pltpu.VMEM(down_proj.shape[1:], bf16),
            pltpu.VMEM((total, ff), bf16),
            pltpu.VMEM((total, 2 * ff), bf16),
            pltpu.VMEM((2 * ffn_in.shape[0], 128), f32),
            pltpu.VMEM((ff, width), f32),
            pltpu.SemaphoreType.DMA((9,)),
            pltpu.SemaphoreType.DMA((9,)),
            pltpu.SemaphoreType.DMA((16,)),
        ],
        compiler_params=pltpu.CompilerParams(
            collective_id=2, has_side_effects=True, vmem_limit_bytes=56 * 2**20
        ),
        cost_estimate=pl.CostEstimate(
            flops=2 * total * width * 3 * ff,
            bytes_accessed=40 * 2**20,
            transcendentals=0,
        ),
    )(ffn_in, route_rows, router_weight.T, g_rows, gate_up, down_proj)


def next_expert_kernel(
    which, experts, rows_v, g_v, gates_ref, totals_ref, gate_up_v, down_v, _, hidden_v, grad_v,
    gate_grad_ref, total_v,
):
    lane = lax.broadcasted_iota(jnp.int32, total_v.shape, 1)
    expert = lax.axis_index(plane) * lax.div(experts, lax.axis_size(plane)) + which
    mark = (lane == expert) | (lane == expert + experts)
    total_v[...] = totals_ref[...]
    gate = jnp.sum(jnp.where(lane == which, gates_ref[...], 0.0), axis=-1, keepdims=True)
    some = pl.ds(0, rows_v.shape[0])
    expert_chunk(
        some, 0, rows_v, g_v, gate_up_v.at[0], down_v.at[0], hidden_v, grad_v, total_v, gate, mark
    )
    total = total_v[...]
    high = total.astype(bf16).astype(f32)
    gate_grad_ref[...] = jnp.where(lane < experts, high, total - high).astype(bf16)


def last_expert(which, experts, rows, g_rows, gates, totals, gate_up, down_proj, grads):
    ff, width = down_proj.shape[1:]
    total = rows.shape[0]
    step = total // 4

    def block(columns):
        return pl.BlockSpec((step, columns), lambda i: (i, 0))

    def whole(shape):
        return pl.BlockSpec((1,) + shape[1:], lambda i: (which, 0, 0))

    def kernel(*refs):
        next_expert_kernel(which, experts, *refs)

    return pl.pallas_call(
        kernel,
        grid=(4,),
        out_shape=[
            jax.ShapeDtypeStruct((total, ff), bf16),
            jax.ShapeDtypeStruct(grads.shape, bf16),
            jax.ShapeDtypeStruct((total, 128), bf16),
        ],
        in_specs=[
            block(width), block(width), block(128), block(128),
            whole(gate_up.shape), whole(down_proj.shape), pl.BlockSpec(memory_space=pl.ANY),
        ],
        out_specs=[
            block(ff), pl.BlockSpec((step, 2 * ff), lambda i: (i, which)), block(128)
        ],
        input_output_aliases={6: 1},
        scratch_shapes=[pltpu.VMEM((step, 128), f32)],
        compiler_params=pltpu.CompilerParams(vmem_limit_bytes=56 * 2**20),
        cost_estimate=pl.CostEstimate(flops=10**6, bytes_accessed=10**6, transcendentals=0),
    )(rows, g_rows, gates, totals, gate_up, down_proj, grads)


def weight_grad_kernel(
    query_grad, kv_grad, branch, attended_owned, normed_owned, down_part, sums_ref,
    pre_v, branch_v, attended_v, normed_v, send_sem, recv_sem, local_sem,
):
    here = Places()
    greet([here.to_y, here.to_c, here.to_x])
    send = Sender(send_sem, recv_sem)
    count, wide = query_grad.shape
    narrow = kv_grad.shape[1]
    spread = lax.axis_size(plane)
    tile = sums_ref.shape[1]
    groups = lax.axis_size("dp")
    half = wide // 2
    low, high, last = pl.ds(0, half), pl.ds(half, half), pl.ds(wide, narrow)
    qa, _ = block_gather(
        here, send, query_grad.at[:, low], local_sem.at[1], pre_v, False, low
    )
    qb, _ = block_gather(
        here, send, query_grad.at[:, high], local_sem.at[2], pre_v, False, high
    )
    kv, _ = block_gather(here, send, kv_grad, local_sem.at[3], pre_v, False, last)
    loads = [pltpu.make_async_copy(branch, branch_v, local_sem.at[0])]
    for device in range(spread):
        slot = plane_slot(device // 4, device // 2 % 2, device % 2)
        rows = pl.ds(slot * count, count)
        for source, target in ((attended_owned, attended_v), (normed_owned, normed_v)):
            loads.append(
                pltpu.make_async_copy(
                    source.at[device], target.at[rows], local_sem.at[3 + len(loads)]
                )
            )

    output_rows = attended_v.shape[1] // groups * (branch.shape[1] // tile)
    pre_rows = normed_v.shape[1] // groups * ((wide + narrow) // tile)
    down_rows = down_part.shape[0] // groups
    kept = [
        pltpu.make_async_copy(
            down_part.at[pl.ds(d * down_rows, down_rows), pl.ds(i * tile, tile)],
            sums_ref.at[
                pl.ds(
                    d * (sums_ref.shape[0] // groups) + output_rows + pre_rows + i * down_rows,
                    down_rows,
                )
            ],
            local_sem.at[4 + 2 * spread + d * (down_part.shape[1] // tile) + i],
        )
        for d in range(groups)
        for i in range(down_part.shape[1] // tile)
    ]

    def start():
        for copy in loads + kept:
            copy.start()

    def product(left, right, base, first, tiles):
        rows = left.shape[1] // groups

        @pl.loop(first, first + tiles)
        def _(i):
            cols = pl.ds(pl.multiple_of(i * tile, tile), tile)
            part = transposed_dot(left[...], right[:, cols]).astype(bf16)
            for d in range(groups):
                at = d * (sums_ref.shape[0] // groups) + base + i * rows
                sums_ref[pl.ds(pl.multiple_of(at, 64), rows), :] = part[
                    d * rows : (d + 1) * rows
                ]

    def output_product():
        for load in loads:
            load.wait()
        product(attended_v, branch_v, 0, 0, branch.shape[1] // tile)

    steps = [
        qa[0], qb[0], kv[0], start, output_product, qa[1], qb[1], qa[2], kv[1], qb[2], qa[3],
        lambda: product(normed_v, pre_v, output_rows, 0, half // tile),
        kv[2], qb[3],
        lambda: product(normed_v, pre_v, output_rows, half // tile, half // tile),
        kv[3],
        lambda: product(normed_v, pre_v, output_rows, wide // tile, narrow // tile),
    ]
    for step in steps:
        step()
    for copy in kept:
        copy.wait()
    send.finish()


def weight_grads(query_grad, kv_grad, branch, attended_owned, normed_owned, down_part):
    count, wide = query_grad.shape
    narrow, width = kv_grad.shape[1], branch.shape[1]
    spread = lax.axis_size(plane)
    tile = narrow
    elements = attended_owned.shape[2] * width + normed_owned.shape[2] * (wide + narrow)
    elements += math.prod(down_part.shape)
    groups = lax.axis_size("dp")
    vmem = pl.BlockSpec(memory_space=pltpu.VMEM)
    anywhere = pl.BlockSpec(memory_space=pl.ANY)
    return pl.pallas_call(
        weight_grad_kernel,
        out_shape=jax.ShapeDtypeStruct((elements // tile, tile), bf16),
        in_specs=[anywhere] * 6,
        out_specs=vmem,
        scratch_shapes=[
            pltpu.VMEM((spread * count, wide + narrow), bf16),
            pltpu.VMEM((spread * count, width), bf16),
            pltpu.VMEM((spread * count, attended_owned.shape[2]), bf16),
            pltpu.VMEM((spread * count, normed_owned.shape[2]), bf16),
            pltpu.SemaphoreType.DMA((27,)),
            pltpu.SemaphoreType.DMA((27,)),
            pltpu.SemaphoreType.DMA((4 + 2 * spread + groups * (down_part.shape[1] // tile),)),
        ],
        compiler_params=pltpu.CompilerParams(
            collective_id=5, has_side_effects=True, vmem_limit_bytes=56 * 2**20
        ),
        cost_estimate=pl.CostEstimate(flops=10**6, bytes_accessed=10**6, transcendentals=0),
    )(query_grad, kv_grad, branch, attended_owned, normed_owned, down_part)


def arrive(got, name):
    copy = got[name]
    copy.wait() if name == "own" else copy.wait_recv()


def plane_index(here):
    return here.ctx * 2 + here.y


def plane_sum_kernel(across, parts, *refs):
    lefts, weight_hbm = refs[:parts], refs[parts]
    refs = refs[parts + 1 :]
    extra_ref, sources, targets = None, [], []
    if across:
        extra_ref, sources, targets = refs[0], refs[1:3], refs[4:6]
        refs = (refs[3],) + refs[6:]
    (
        out_ref, left_v, weight_v, part_v, core_v, edge_v, last_v, send_sem, recv_sem, local_sem,
    ) = refs
    here = Places()
    peers = here.peers() if across else []
    greet([device for _, device in peers] or [here.to_y, here.to_c, here.to_x])
    send = Sender(send_sem, recv_sem)
    count = out_ref.shape[0]
    half = count // 2
    experts = weight_hbm.shape[0]
    part_depth = lefts[0].shape[1]
    depth = part_depth * parts // experts
    width = weight_hbm.shape[1] if across else weight_hbm.shape[2]
    tile = 256
    x, y, c = here.x, here.y, here.c
    chips = [(1 - x, 1 - y), (1 - x, y), (x, 1 - y), (x, y)]
    weight_load = pltpu.make_async_copy(weight_hbm, weight_v, local_sem.at[0])
    weight_load.start()
    loads = []
    for k, (cx, cy) in enumerate(chips):
        some = chip_rows(cx, cy, count)
        loads.append(
            [
                pltpu.make_async_copy(
                    left.at[some, :],
                    left_v.at[k, :, pl.ds(e * part_depth, part_depth)],
                    local_sem.at[1 + parts * k + e],
                )
                for e, left in enumerate(lefts)
            ]
        )
        for load in loads[-1]:
            load.start()
    owned = []
    for index, device in peers:
        for source, target in zip(sources, targets):
            owned.append(send(source.at[index], target.at[plane_index(here)], device))
    kept = [
        pltpu.make_async_copy(
            source.at[plane_index(here)],
            target.at[plane_index(here)],
            local_sem.at[1 + 4 * parts + i],
        )
        for i, (source, target) in enumerate(zip(sources, targets))
    ]
    for copy in kept:
        copy.start()
    weight_load.wait()
    to_core = []

    def compute(k):
        for load in loads[k]:
            load.wait()

        @pl.loop(0, width // tile)
        def _(n):
            cols = pl.ds(pl.multiple_of(n * tile, tile), tile)
            total = None
            for e in range(experts):
                left = left_v[k, :, e * depth : (e + 1) * depth]
                if across:
                    part = lax.dot_general(
                        left,
                        weight_v[e, cols, :],
                        (((1,), (1,)), ((), ())),
                        preferred_element_type=f32,
                    )
                else:
                    part = dot(left, weight_v[e, :, cols])
                total = part if total is None else total + part
            part_v[k, :, cols] = total.astype(bf16)

        if extra_ref is not None:
            part_v[k, :, width:] = extra_ref[chip_rows(*chips[k], count), :]
        to_core.append(
            send(
                part_v.at[k, pl.ds(pl.multiple_of((1 - c) * count, count), count)],
                core_v.at[k],
                here.to_c,
            )
        )

    mine = pl.ds(pl.multiple_of(c * count, count), count)

    def chip_sum(k):
        to_core[k].wait_recv()
        return part_v[k, mine, :].astype(f32) + core_v[k].astype(f32)

    compute(0)
    compute(1)
    core_v[0] = chip_sum(0).astype(bf16)
    from_x = send(core_v.at[0, pl.ds(0, half)], edge_v.at[0], here.to_x)
    from_y = send(core_v.at[0, pl.ds(half, half)], edge_v.at[1], here.to_y)
    compute(2)
    over_x_sum = chip_sum(1)
    core_v[1, :half] = over_x_sum[:half].astype(bf16)
    from_y.wait_recv()
    core_v[1, half:] = (over_x_sum[half:] + edge_v[1].astype(f32)).astype(bf16)
    last_x = send(core_v.at[1], last_v.at[0], here.to_x)
    over_y_sum = chip_sum(2)
    core_v[2, half:] = over_y_sum[half:].astype(bf16)
    from_x.wait_recv()
    core_v[2, :half] = (over_y_sum[:half] + edge_v[0].astype(f32)).astype(bf16)
    last_y = send(core_v.at[2], last_v.at[1], here.to_y)
    compute(3)
    out_ref[...] = chip_sum(3)
    last_x.wait_recv()
    last_y.wait_recv()
    out_ref[...] = out_ref[...] + last_v[0].astype(f32) + last_v[1].astype(f32)
    for copy in owned:
        copy.wait_recv()
    for copy in kept:
        copy.wait()
    send.finish()


def plane_sum(lefts, weight, extra, owned, collective_id):
    across = extra is not None
    count = lefts[0].shape[0] // lax.axis_size(plane)
    width = weight.shape[1] if across else weight.shape[2]
    wide = width + (extra.shape[1] if across else 0)
    parts, depth = len(lefts), lefts[0].shape[1]
    vmem = pl.BlockSpec(memory_space=pltpu.VMEM)
    anywhere = pl.BlockSpec(memory_space=pl.ANY)

    def kernel(*refs):
        plane_sum_kernel(across, parts, *refs)

    return pl.pallas_call(
        kernel,
        out_shape=[jax.ShapeDtypeStruct((count, wide), f32)]
        + [jax.ShapeDtypeStruct(v.shape, v.dtype) for v in owned],
        in_specs=[anywhere] * (parts + 1) + [vmem] * across + [anywhere] * len(owned),
        out_specs=[vmem] + [anywhere] * len(owned),
        scratch_shapes=[
            pltpu.VMEM((4, 2 * count, parts * depth), bf16),
            pltpu.VMEM(weight.shape, bf16),
            pltpu.VMEM((4, 2 * count, wide), bf16),
            pltpu.VMEM((4, count, wide), bf16),
            pltpu.VMEM((2, count // 2, wide), bf16),
            pltpu.VMEM((2, count, wide), bf16),
            pltpu.SemaphoreType.DMA((8 + 7 * len(owned),)),
            pltpu.SemaphoreType.DMA((8 + 7 * len(owned),)),
            pltpu.SemaphoreType.DMA((1 + 4 * parts + len(owned),)),
        ],
        compiler_params=pltpu.CompilerParams(
            collective_id=collective_id, has_side_effects=True, vmem_limit_bytes=60 * 2**20
        ),
        cost_estimate=pl.CostEstimate(flops=10**6, bytes_accessed=10**6, transcendentals=0),
    )(*lefts, weight, *([extra] if across else []), *owned)


def head_softmax(queries, keys, visible):
    scores = lax.dot_general(
        queries, keys, (((1,), (1,)), ((), ())), preferred_element_type=f32
    ) * (HEAD_SIZE ** (-0.5))
    scores = jnp.where(visible, scores, masked)
    raised = jnp.exp(scores - jnp.max(scores, axis=-1, keepdims=True))
    return raised / jnp.sum(raised, axis=-1, keepdims=True)


def visible_keys(rows, keys):
    row = lax.broadcasted_iota(jnp.int32, (rows, keys), 0)
    key = lax.broadcasted_iota(jnp.int32, (rows, keys), 1)
    prompt_all = keys - (rows - PROMPT_DEV)
    own = lax.axis_index("ctx") * PROMPT_DEV + row
    position = jnp.where(row < PROMPT_DEV, own, prompt_all + row - PROMPT_DEV)
    return key <= position


def attention_kernel(
    query_pre_ref, gain_ref, cosine_ref, sine_ref, keys_ref, values_ref, queries_ref, attended_ref
):
    rows = query_pre_ref.shape[0]
    visible = visible_keys(rows, keys_ref.shape[0])
    keys = keys_ref[...]
    values = values_ref[...]
    for h in range(query_pre_ref.shape[1] // HEAD_SIZE):
        cols = slice(h * HEAD_SIZE, (h + 1) * HEAD_SIZE)
        v = query_pre_ref[:, cols]
        v = v * head_norm(v) * gain_ref[...]
        queries = (v * cosine_ref[...] + turn_half(v) * sine_ref[...]).astype(bf16)
        queries_ref[:, cols] = queries
        probs = head_softmax(queries, keys, visible).astype(bf16)
        attended_ref[:, cols] = dot(probs, values).astype(bf16)


def attention(query_pre, gain, cosine, sine, kv_all):
    rows, wide = query_pre.shape
    keys = kv_all.shape[0]
    group = wide // KEY_VALUE_HEADS
    small = pl.BlockSpec((rows, HEAD_SIZE), lambda i: (0, 0))
    block = pl.BlockSpec((rows, group), lambda i: (0, i))
    return pl.pallas_call(
        attention_kernel,
        grid=(KEY_VALUE_HEADS,),
        out_shape=[jax.ShapeDtypeStruct((rows, wide), bf16)] * 2,
        in_specs=[
            block,
            pl.BlockSpec((1, HEAD_SIZE), lambda i: (0, 0)),
            small,
            small,
            pl.BlockSpec((keys, HEAD_SIZE), lambda i: (0, i)),
            pl.BlockSpec((keys, HEAD_SIZE), lambda i: (0, KEY_VALUE_HEADS + i)),
        ],
        out_specs=[block, block],
        compiler_params=pltpu.CompilerParams(vmem_limit_bytes=48 * 2**20),
    )(query_pre, gain.reshape(1, HEAD_SIZE), cosine, sine, kv_all, kv_all)


def transposed_dot(a, b):
    return lax.dot_general(a, b, (((0,), (0,)), ((), ())), preferred_element_type=f32)


def back_heads(
    first,
    key_at,
    value_at,
    out_at,
    query_pre_ref,
    gain_ref,
    cosine_ref,
    sine_ref,
    keys_ref,
    values_ref,
    queries_ref,
    grad_ref,
    pre_grad_ref,
    key_grad_ref,
    value_grad_ref,
):
    rows = query_pre_ref.shape[0]
    visible = visible_keys(rows, keys_ref.shape[0])
    keys = keys_ref[:, pl.ds(key_at, HEAD_SIZE)]
    values = values_ref[:, pl.ds(value_at, HEAD_SIZE)]
    scale = HEAD_SIZE ** (-0.5)
    gain_grad = jnp.zeros((rows, HEAD_SIZE), f32)
    key_grad = jnp.zeros(keys.shape, f32)
    value_grad = jnp.zeros(keys.shape, f32)
    for h in range(QUERY_HEADS // KEY_VALUE_HEADS):
        cols = pl.ds(first + h * HEAD_SIZE, HEAD_SIZE)
        queries = queries_ref[:, cols]
        grad = grad_ref[:, cols]
        probs = head_softmax(queries, keys, visible)
        prob_grad = lax.dot_general(
            grad, values, (((1,), (1,)), ((), ())), preferred_element_type=f32
        )
        delta = jnp.sum(probs * prob_grad, axis=-1, keepdims=True)
        score_grad = (probs * (prob_grad - delta)).astype(bf16)
        key_grad = key_grad + transposed_dot(score_grad, queries)
        value_grad = value_grad + transposed_dot(probs.astype(bf16), grad)
        u = dot(score_grad, keys) * scale
        u = u * cosine_ref[...] + turn_half(u * sine_ref[...])
        v = query_pre_ref[:, cols]
        inv = head_norm(v)
        gain_grad = gain_grad + u * v * inv
        pre_grad_ref[:, cols] = norm_back(v, inv, gain_ref[...], u).astype(bf16)
    out = pl.ds(out_at, HEAD_SIZE)
    key_grad_ref[:, out] = (key_grad * scale).astype(key_grad_ref.dtype)
    value_grad_ref[:, out] = value_grad.astype(value_grad_ref.dtype)
    return jnp.sum(gain_grad, axis=0, keepdims=True)


def attention_back_kernel(*refs):
    refs[-1][0] = back_heads(0, 0, 0, 0, *refs[:-1])


def attention_back_gather_kernel(
    query_pre_ref, gain_ref, cosine_ref, sine_ref, kv_ref, queries_ref, grad_ref, branch,
    pre_grad_ref, key_grad_ref, value_grad_ref, gain_grad_ref, branch_rows,
    send_sem, recv_sem, local_sem,
):
    here = Places()
    greet([here.to_y, here.to_c, here.to_x])
    send = Sender(send_sem, recv_sem)
    stages, _ = block_gather(here, send, branch, local_sem.at[0], branch_rows)
    group = query_pre_ref.shape[1] // KEY_VALUE_HEADS
    narrow = kv_ref.shape[1] // 2

    def heads(first, count):
        @pl.loop(first, first + count)
        def _(i):
            at = pl.multiple_of(i * HEAD_SIZE, HEAD_SIZE)
            gain_grad_ref[i] = back_heads(
                pl.multiple_of(i * group, group),
                at,
                pl.multiple_of(narrow + i * HEAD_SIZE, HEAD_SIZE),
                at,
                query_pre_ref,
                gain_ref,
                cosine_ref,
                sine_ref,
                kv_ref,
                kv_ref,
                queries_ref,
                grad_ref,
                pre_grad_ref,
                key_grad_ref,
                value_grad_ref,
            )

    stages[0]()
    heads(0, KEY_VALUE_HEADS - 1)
    stages[1]()
    heads(KEY_VALUE_HEADS - 1, 1)
    stages[2]()
    stages[3]()
    send.finish()


def attention_back_gather(query_pre, gain, cosine, sine, kv_all, queries, attended_grad, branch):
    rows, wide = query_pre.shape
    keys, both = kv_all.shape
    vmem = pl.BlockSpec(memory_space=pltpu.VMEM)
    anywhere = pl.BlockSpec(memory_space=pl.ANY)
    return pl.pallas_call(
        attention_back_gather_kernel,
        out_shape=[
            jax.ShapeDtypeStruct((rows, wide), bf16),
            jax.ShapeDtypeStruct((keys, both // 2), f32),
            jax.ShapeDtypeStruct((keys, both // 2), f32),
            jax.ShapeDtypeStruct((KEY_VALUE_HEADS, 1, HEAD_SIZE), f32),
            jax.ShapeDtypeStruct((lax.axis_size(plane) * rows, branch.shape[1]), bf16),
        ],
        in_specs=[vmem] * 7 + [anywhere],
        out_specs=[vmem] * 4 + [anywhere],
        scratch_shapes=[
            pltpu.SemaphoreType.DMA((9,)),
            pltpu.SemaphoreType.DMA((9,)),
            pltpu.SemaphoreType.DMA((1,)),
        ],
        compiler_params=pltpu.CompilerParams(
            collective_id=6, has_side_effects=True, vmem_limit_bytes=48 * 2**20
        ),
        cost_estimate=pl.CostEstimate(flops=10**6, bytes_accessed=10**6, transcendentals=0),
    )(
        query_pre, gain.reshape(1, HEAD_SIZE), cosine, sine, kv_all, queries, attended_grad, branch
    )


def attention_back(query_pre, gain, cosine, sine, kv_all, queries, attended_grad):
    rows, wide = query_pre.shape
    keys, both = kv_all.shape
    group = wide // KEY_VALUE_HEADS
    small = pl.BlockSpec((rows, HEAD_SIZE), lambda i: (0, 0))
    block = pl.BlockSpec((rows, group), lambda i: (0, i))
    return pl.pallas_call(
        attention_back_kernel,
        grid=(KEY_VALUE_HEADS,),
        out_shape=[
            jax.ShapeDtypeStruct((rows, wide), bf16),
            jax.ShapeDtypeStruct((keys, both // 2), f32),
            jax.ShapeDtypeStruct((keys, both // 2), f32),
            jax.ShapeDtypeStruct((KEY_VALUE_HEADS, 1, HEAD_SIZE), f32),
        ],
        in_specs=[
            block,
            pl.BlockSpec((1, HEAD_SIZE), lambda i: (0, 0)),
            small,
            small,
            pl.BlockSpec((keys, HEAD_SIZE), lambda i: (0, i)),
            pl.BlockSpec((keys, HEAD_SIZE), lambda i: (0, KEY_VALUE_HEADS + i)),
            block,
            block,
        ],
        out_specs=[
            block,
            pl.BlockSpec((keys, HEAD_SIZE), lambda i: (0, i)),
            pl.BlockSpec((keys, HEAD_SIZE), lambda i: (0, i)),
            pl.BlockSpec((1, 1, HEAD_SIZE), lambda i: (i, 0, 0)),
        ],
        cost_estimate=pl.CostEstimate(flops=10**6, bytes_accessed=10**6, transcendentals=0),
        compiler_params=pltpu.CompilerParams(vmem_limit_bytes=48 * 2**20),
    )(
        query_pre, gain.reshape(1, HEAD_SIZE), cosine, sine, kv_all, kv_all, queries, attended_grad
    )


def join_halves(mine, other):
    lower = lax.axis_index("expert") == 0
    return jnp.concatenate(
        [jnp.where(lower, mine, other), jnp.where(lower, other, mine)], axis=1
    )


def dot(a, b):
    return jnp.dot(a, b, preferred_element_type=f32)


def ctx_sum(v):
    if not small_plane():
        return lax.psum_scatter(v, "ctx", scatter_dimension=1, tiled=True).astype(f32)
    member = lax.axis_index("ctx")

    def block(j):
        return lax.dynamic_slice_in_dim(v, (member ^ j) * PROMPT_DEV, PROMPT_DEV, axis=1)

    near = block(0).astype(f32) + core(block(1)).astype(f32)
    far = (block(2).astype(f32) + core(block(3)).astype(f32)).astype(bf16)
    return near + over_x(far).astype(f32)


def body(
    hidden_in,
    attn_gain,
    query_weight,
    key_matrix,
    value_matrix,
    query_gain,
    key_gain,
    output_weight,
    ffn_gain,
    router_weight,
    gate_up,
    down_proj,
    routes,
    out_grad,
):
    ctx_count = lax.axis_size("ctx")
    spread_count = lax.axis_size(plane)
    dp_count = lax.axis_size("dp")
    device_count = dp_count * spread_count
    local_experts = gate_up.shape[0]
    count_of_rows = hidden_in.shape[0]
    prompt_all = PROMPT_DEV * ctx_count
    hidden_ff = gate_up.shape[2] // 2
    member = lax.axis_index("ctx")
    offsets = jnp.arange(count_of_rows, dtype=jnp.int32)
    position = jnp.where(
        offsets < PROMPT_DEV, member * PROMPT_DEV + offsets, prompt_all + offsets - PROMPT_DEV
    )
    cosine, rope_sine = angles(position, HEAD_SIZE)
    narrow = KEY_VALUE_HEADS * HEAD_SIZE
    wide = QUERY_HEADS * HEAD_SIZE
    inputs = hidden_in.astype(f32)
    scale_in = rms_scale(inputs)

    def by_owner(v):
        v = v.reshape(count_of_rows, dp_count, spread_count, -1)
        return v.transpose(2, 0, 1, 3).reshape(spread_count, count_of_rows, -1)

    signed_sine = rope_sine * jnp.where(jnp.arange(HEAD_SIZE) < HEAD_SIZE // 2, -1.0, 1.0)
    if small_plane():
        (
            kv_other,
            q_other,
            o_other,
            g_rows,
            route_rows,
            kv_all,
            normed_owned,
            attended_owned,
            query_pre,
            key_pre,
            queries,
            residual,
            ffn_in,
        ) = fetch_and_attend(
            hidden_in, attn_gain, query_gain, key_gain, ffn_gain, cosine, signed_sine,
            key_matrix, value_matrix, query_weight, output_weight, out_grad, routes,
        )
        kv_weights = [jnp.concatenate([key_matrix, value_matrix], axis=1), kv_other]
        q_weights = [query_weight, q_other]
        o_weights = [output_weight, o_other]
    else:
        full = [
            lax.all_gather(w, "expert", axis=0, tiled=True)
            for w in (
                jnp.concatenate([key_matrix, value_matrix], axis=1),
                query_weight,
                output_weight,
            )
        ]
        kv_weights, q_weights, o_weights = [[w] for w in full]
        g_rows = lax.all_gather(out_grad, plane, axis=0, tiled=True)
        route_rows = lax.all_gather(routes, plane, axis=0, tiled=True)
        normalized_input = (inputs * scale_in * attn_gain).astype(bf16)
        query_pre = dot(normalized_input, q_weights[0])
        key_value_pre = dot(normalized_input, kv_weights[0])
        key_pre = key_value_pre[:, :narrow]
        key_heads = key_pre.reshape(count_of_rows, KEY_VALUE_HEADS, HEAD_SIZE)
        key_low = rotate(
            key_heads * rms_scale(key_heads) * key_gain, cosine[:, None, :], rope_sine[:, None, :]
        ).astype(bf16)
        kv_low = jnp.concatenate(
            [key_low.reshape(count_of_rows, narrow), key_value_pre[:, narrow:].astype(bf16)],
            axis=1,
        )
        kv_blocks = lax.all_gather(kv_low[:PROMPT_DEV], "ctx", axis=0, tiled=True)
        kv_all = jnp.concatenate([kv_blocks, kv_low[PROMPT_DEV:]], axis=0)
        queries, attended = attention(query_pre, query_gain, cosine, signed_sine, kv_all)
        residual = inputs + dot(attended, o_weights[0])
        ffn_in = (residual * rms_scale(residual) * ffn_gain).astype(bf16)
        normed_owned = by_owner(normalized_input)
        attended_owned = by_owner(attended)

    def owned(v):
        return lax.all_to_all(v, plane, split_axis=0, concat_axis=0, tiled=True)

    def backward_dot(v, weights):
        parts = [dot(v, w.T) for w in weights]
        return parts[0] if len(parts) == 1 else join_halves(*parts)

    key_before_norm = key_pre.reshape(count_of_rows, KEY_VALUE_HEADS, HEAD_SIZE)
    key_inv = rms_scale(key_before_norm)
    scale_ffn = rms_scale(residual)

    expert_count = local_experts * spread_count
    expert_ids = jnp.arange(expert_count, dtype=jnp.int32)

    def gates_of(some_rows, some_routes):
        logits = dot(some_rows, router_weight)
        chosen = jnp.any(some_routes[:, :, None] == expert_ids[None, None, :], axis=1)
        logits = jnp.where(chosen, logits, masked)
        raised = jnp.where(
            chosen, jnp.exp(logits - jnp.max(logits, axis=-1, keepdims=True)), 0.0
        )
        return raised / jnp.sum(raised, axis=-1, keepdims=True)

    gates = gates_of(ffn_in, routes)
    if small_plane():
        rows, hidden, grads, gates_mine, totals, down_part = gather_first_expert(
            ffn_in, route_rows, router_weight, g_rows, gate_up, down_proj
        )
        hiddens = [hidden]
        down_parts = [down_part]
        rows, grads = after((rows, grads), down_parts)
        hidden, grads, gate_grads = last_expert(
            1, expert_count, rows, g_rows, gates_mine, totals, gate_up, down_proj, grads
        )
        hiddens.append(hidden)
        projected_grads = [grads]
        gate_up_parts = [dot(rows.T, grads).astype(bf16)]
        down_late = dot(after(hidden, gate_up_parts).T, g_rows).astype(bf16)
    else:
        rows = lax.all_gather(ffn_in, plane, axis=0, tiled=True)
        first_expert = lax.axis_index(plane) * local_experts
        gates_mine = lax.dynamic_slice_in_dim(
            gates_of(rows, route_rows), first_expert, local_experts, axis=1
        )
        gate_grads, hiddens, projected_grads = [], [], []
        for which in range(local_experts):
            gate = gates_mine[:, which : which + 1]
            projected = dot(rows, gate_up[which])
            back = dot(g_rows, down_proj[which].T)
            gate_part = projected[:, :hidden_ff]
            up_part = projected[:, hidden_ff:]
            sigmoid_gate = jax.nn.sigmoid(gate_part)
            hidden = gate_part * sigmoid_gate * up_part
            gate_grads.append(jnp.sum(hidden * back, axis=-1))
            hiddens.append((gate * hidden).astype(bf16))
            back = gate * back
            gate_back = back * up_part * sigmoid_gate * (1.0 + gate_part * (1.0 - sigmoid_gate))
            up_back = back * gate_part * sigmoid_gate
            projected_grads.append(jnp.concatenate([gate_back, up_back], axis=-1).astype(bf16))
        attended_owned, normed_owned = owned(attended_owned), owned(normed_owned)
        down_parts = [dot(v.T, g_rows).astype(bf16) for v in hiddens]
        gate_up_parts = [dot(rows.T, v).astype(bf16) for v in projected_grads]
    down_low, gate_up_low = [
        [lax.psum_scatter(v, "dp", scatter_dimension=0, tiled=True) for v in parts]
        for parts in (down_parts, gate_up_parts)
    ]
    gate_up_grad = jnp.stack(
        [
            part.astype(f32)
            for v in gate_up_low
            for part in jnp.split(v, v.shape[1] // (2 * hidden_ff), axis=1)
        ]
    )
    projected_grads, hiddens = lax.optimization_barrier(
        ((projected_grads, hiddens), down_parts, gate_up_parts)
    )[0]
    if small_plane():
        back, attended_owned, normed_owned = plane_sum(
            projected_grads, gate_up, gate_grads, [attended_owned, normed_owned], 3
        )
        back_sum = back[:, :MODEL_WIDTH]
        gate_grad = (
            back[:, MODEL_WIDTH : MODEL_WIDTH + expert_count]
            + back[:, MODEL_WIDTH + expert_count : MODEL_WIDTH + 2 * expert_count]
        )
        moe_sum = None
    else:
        moe_part = 0.0
        row_part = 0.0
        for which in range(local_experts):
            row_part = row_part + dot(projected_grads[which], gate_up[which].T)
            moe_part = moe_part + dot(hiddens[which], down_proj[which])
        moe_sum, back_sum = [
            lax.psum_scatter(v.astype(bf16), plane, scatter_dimension=0, tiled=True).astype(f32)
            for v in (moe_part, row_part)
        ]
        gate_grad = lax.all_to_all(
            jnp.stack(gate_grads, axis=1).reshape(spread_count, count_of_rows, local_experts),
            plane,
            split_axis=0,
            concat_axis=0,
            tiled=True,
        )
        gate_grad = gate_grad.transpose(1, 0, 2).reshape(count_of_rows, expert_count)
    logit_grad = gates * (gate_grad - jnp.sum(gates * gate_grad, axis=-1, keepdims=True))

    grad_out = out_grad.astype(f32)
    router_local = jnp.dot(ffn_in.T, logit_grad, preferred_element_type=f32)
    ffn_in_grad = back_sum + jnp.dot(
        logit_grad, router_weight.astype(f32).T, precision=highest
    )
    residual_grad = grad_out + norm_back(residual, scale_ffn, ffn_gain, ffn_in_grad)
    ffn_gain_local = jnp.sum(ffn_in_grad * residual * scale_ffn, axis=0)
    branch_low = residual_grad.astype(bf16)
    attended_grad = backward_dot(branch_low, o_weights).astype(bf16)
    operands = (query_pre, query_gain, cosine, signed_sine, kv_all, queries, attended_grad)
    if small_plane():
        *attention_grads, branch_rows = attention_back_gather(*operands, branch_low)
    else:
        attention_grads = attention_back(*operands)
    query_pre_grad, key_grad_all, value_grad_all, query_gain_parts = attention_grads
    query_gain_local = jnp.sum(query_gain_parts, axis=(0, 1))
    pair_grads = jnp.stack([key_grad_all[:prompt_all], value_grad_all[:prompt_all]]).astype(bf16)
    prompt_grads = ctx_sum(pair_grads)
    key_grad = jnp.concatenate([prompt_grads[0], key_grad_all[prompt_all:]], axis=0).reshape(
        count_of_rows, KEY_VALUE_HEADS, HEAD_SIZE
    )
    value_gradient = jnp.concatenate([prompt_grads[1], value_grad_all[prompt_all:]], axis=0)
    key_rot_grad = rotate_back(key_grad, cosine[:, None, :], rope_sine[:, None, :])
    key_gain_local = jnp.sum(key_rot_grad * key_before_norm * key_inv, axis=(0, 1))
    key_pre_grad = (
        norm_back(key_before_norm, key_inv, key_gain, key_rot_grad)
        .astype(bf16)
        .reshape(count_of_rows, KEY_VALUE_HEADS * HEAD_SIZE)
    )
    key_value_grad = jnp.concatenate([key_pre_grad, value_gradient.astype(bf16)], axis=1)
    if small_plane():
        local = [
            weight_grads(
                query_pre_grad, key_value_grad, branch_rows, attended_owned, normed_owned, down_late
            )
        ]
    else:
        branch_rows = lax.all_gather(branch_low, plane, axis=0, tiled=True)
        pre_rows = lax.all_gather(
            jnp.concatenate([query_pre_grad, key_value_grad], axis=1), plane, axis=0, tiled=True
        )
        attended_owned, normed_owned = [
            v.reshape(spread_count * count_of_rows, -1) for v in (attended_owned, normed_owned)
        ]
        local = [
            dot(attended_owned.T, branch_rows).astype(bf16),
            dot(normed_owned.T, pre_rows).astype(bf16),
        ]
    query_pre_grad, key_value_grad = lax.optimization_barrier(
        ((query_pre_grad, key_value_grad), local)
    )[0]
    normed_grad = backward_dot(query_pre_grad, q_weights) + backward_dot(
        key_value_grad, kv_weights
    )
    attn_gain_local = jnp.sum(normed_grad * inputs * scale_in, axis=0)
    hidden_grad = residual_grad + norm_back(inputs, scale_in, attn_gain, normed_grad)
    if small_plane():
        moe_sum = plane_sum(after(hiddens, local), down_proj, None, [], 4)[0]
    block_out = (residual + moe_sum).astype(bf16)
    local = lax.optimization_barrier((local, gate_up_low, down_low))[0]
    summed = [
        lax.psum_scatter(v, "dp", scatter_dimension=0, tiled=True).astype(f32) for v in local
    ]
    share = MODEL_WIDTH // device_count
    if small_plane():
        tile = summed[0].shape[1]
        cut = wide // device_count * (MODEL_WIDTH // tile)

        def untile(v, rows):
            return jnp.concatenate(
                [v[i : i + rows] for i in range(0, v.shape[0], rows)], axis=1
            )

        end = cut + share * ((wide + 2 * narrow) // tile)
        output_sum = untile(summed[0][:cut], wide // device_count)
        pre_sum = untile(summed[0][cut:end], share)
        down_low.append(untile(summed[0][end:], hidden_ff // dp_count))
    else:
        output_sum, pre_sum = summed
    down_grad = jnp.stack([v.astype(f32) for v in down_low])

    small = jnp.concatenate(
        [
            v.reshape(device_count, -1)
            for v in (
                attn_gain_local,
                ffn_gain_local,
                query_gain_local,
                key_gain_local,
                router_local,
            )
        ],
        axis=1,
    )
    small = lax.all_to_all(small[:, None], every, split_axis=0, concat_axis=0, tiled=True)
    small = jnp.sum(small[:, 0], axis=0)
    head_share = HEAD_SIZE // device_count
    cuts = [share, share, head_share, head_share, share * expert_count]
    ends = [sum(cuts[: i + 1]) for i in range(5)]
    a_grad, f_grad, q_grad, k_grad, r_grad = [
        small[end - cut : end] for end, cut in zip(ends, cuts)
    ]
    return (
        block_out,
        hidden_grad,
        a_grad,
        pre_sum[:, :wide],
        pre_sum[:, wide : wide + narrow],
        pre_sum[:, wide + narrow :],
        q_grad,
        k_grad,
        output_sum,
        f_grad,
        r_grad.reshape(share, expert_count),
        gate_up_grad,
        down_grad,
    )


def solution(mesh):
    placed = (
        P(("dp", "ctx", "expert"), None),
        P(),
        P("expert", None),
        P("expert", None),
        P("expert", None),
        P(),
        P(),
        P("expert", None),
        P(),
        P(),
        P(("ctx", "expert"), None, None),
        P(("ctx", "expert"), None, None),
        P(("dp", "ctx", "expert"), None),
        P(("dp", "ctx", "expert"), None),
    )
    return jax.shard_map(
        body,
        mesh=mesh,
        in_specs=placed,
        out_specs=(
            P(("dp", "ctx", "expert"), None),
            P(("dp", "ctx", "expert"), None),
            P(("dp", "ctx", "expert")),
            P(("dp", "ctx", "expert"), None),
            P(("dp", "ctx", "expert"), None),
            P(("dp", "ctx", "expert"), None),
            P(("dp", "ctx", "expert")),
            P(("dp", "ctx", "expert")),
            P(("dp", "ctx", "expert"), None),
            P(("dp", "ctx", "expert")),
            P(("dp", "ctx", "expert"), None),
            P(("ctx", "expert"), "dp", None),
            P(("ctx", "expert"), "dp", None),
        ),
        check_vma=False,
    )
```

```python
import math

import jax
import jax.numpy as jnp
from jax import lax
from jax.experimental import pallas as pl
from jax.experimental.pallas import tpu as pltpu
from jax.sharding import PartitionSpec as P

MODEL_WIDTH = 2048
QUERY_HEADS = 32
KEY_VALUE_HEADS = 4
HEAD_SIZE = 128
TOP = 8
PROMPT_DEV = 128


highest = lax.Precision.HIGHEST
epsilon = 1e-06
rope_base = 1000000.0
masked = -1e30
every = ("dp", "ctx", "expert")
plane = ("ctx", "expert")
bf16 = jnp.bfloat16
f32 = jnp.float32


def rms_scale(value_rows):
    return lax.rsqrt(jnp.mean(value_rows * value_rows, axis=-1, keepdims=True) + epsilon)


def norm_back(inputs, inv_rms, norm_gain, gradient):
    weighted = gradient * norm_gain
    return inv_rms * weighted - inputs * inv_rms**3 * jnp.mean(
        weighted * inputs, axis=-1, keepdims=True
    )


def angles(position, head_width):
    freq_index = jnp.arange(head_width // 2, dtype=f32)
    inverse = jnp.exp(-(2.0 * freq_index / head_width) * math.log(rope_base))
    rope_angle = position.astype(f32)[:, None] * inverse[None, :]
    rope_angle = jnp.concatenate([rope_angle, rope_angle], axis=-1)
    return (jnp.cos(rope_angle), jnp.sin(rope_angle))


def rotate(value_rows, cosine, rope_sine):
    half_width = value_rows.shape[-1] // 2
    turned = jnp.concatenate([-value_rows[..., half_width:], value_rows[..., :half_width]], axis=-1)
    return value_rows * cosine + turned * rope_sine


def rotate_back(gradient, cosine, rope_sine):
    shifted = gradient * rope_sine
    half_width = gradient.shape[-1] // 2
    return gradient * cosine + jnp.concatenate(
        [shifted[..., half_width:], -shifted[..., :half_width]], axis=-1
    )


def small_plane():
    return [lax.axis_size(a) for a in every] == [4, 4, 2]


def swap(v, axis, bit):
    return lax.ppermute(v, axis, [(i, i ^ bit) for i in range(lax.axis_size(axis))])


def core(v):
    return swap(v, "ctx", 1)


def over_x(v):
    return swap(v, "ctx", 2)


def over_y(v):
    return swap(v, "expert", 1)


def over_z(v):
    return swap(v, "dp", 1)


def after(v, *earlier):
    return lax.optimization_barrier((v, *earlier))[0]


class Places:
    def __init__(self):
        self.dp = lax.axis_index("dp")
        ctx = lax.axis_index("ctx")
        self.ctx = ctx
        self.z = lax.rem(self.dp, 2)
        self.x = lax.div(ctx, 2)
        self.c = lax.rem(ctx, 2)
        self.y = lax.axis_index("expert")
        self.to_x = {"ctx": (1 - self.x) * 2 + self.c}
        self.to_c = {"ctx": self.x * 2 + 1 - self.c}
        self.to_y = {"expert": 1 - self.y}
        self.to_z = {"dp": self.dp + 1 - 2 * self.z}

    def peers(self):
        found = []
        for r in range(1, 8):
            x, c, y = [
                1 - v if r & bit else v for v, bit in ((self.x, 4), (self.c, 2), (self.y, 1))
            ]
            found.append((x * 4 + c * 2 + y, {"ctx": x * 2 + c, "expert": y}))
        return found


def plane_slot(x, c, y):
    return x * 4 + y * 2 + c


def greet(targets):
    barrier = pltpu.get_barrier_semaphore()
    for target in targets:
        pl.semaphore_signal(barrier, inc=1, device_id=target, device_id_type=pl.DeviceIdType.MESH)
    pl.semaphore_wait(barrier, len(targets))


class Sender:
    def __init__(self, send_sem, recv_sem):
        self.send_sem = send_sem
        self.recv_sem = recv_sem
        self.copies = []

    def __call__(self, source, target_ref, device):
        i = len(self.copies)
        copy = pltpu.make_async_remote_copy(
            src_ref=source,
            dst_ref=target_ref,
            send_sem=self.send_sem.at[i],
            recv_sem=self.recv_sem.at[i],
            device_id=device,
            device_id_type=pl.DeviceIdType.MESH,
        )
        copy.start()
        self.copies.append(copy)
        return copy

    def finish(self):
        for copy in self.copies:
            copy.wait_send()


def half_fetch(here, send, sources, other, columns, rows, upper):
    def at(piece, part=None):
        first, size = piece * rows, rows
        if part == 0:
            size = upper
        elif part == 1:
            first, size = first + upper, rows - upper
        return other.at[pl.ds(pl.multiple_of(first, 16), size), columns]

    def piece(z, x, c):
        return z * 4 + x * 2 + c

    z, x, c = here.z, here.x, here.c
    got = {}

    def first():
        mine = piece(z, x, c)
        got["y"] = [
            send(
                source.at[pl.ds(pl.multiple_of(mine * rows, rows), rows), source_columns],
                other.at[pl.ds(pl.multiple_of(mine * rows, rows), rows), target_columns],
                here.to_y,
            )
            for source, source_columns, target_columns in sources
        ]

    def second():
        for copy in got["y"]:
            copy.wait_recv()
        mine = at(piece(z, x, c))
        got["x"] = send(mine, mine, here.to_x)
        got["z"] = send(mine, mine, here.to_z)
        got["c"] = send(mine, mine, here.to_c)

    def third():
        got["x"].wait_recv()
        from_x = piece(z, 1 - x, c)
        got["low"] = send(at(from_x, 1), at(from_x, 1), here.to_z)
        got["xc"] = send(at(from_x), at(from_x), here.to_c)
        got["z"].wait_recv()
        from_z = piece(1 - z, x, c)
        got["top"] = send(at(from_z, 0), at(from_z, 0), here.to_x)
        got["zc"] = send(at(from_z), at(from_z), here.to_c)

    def fourth():
        far = piece(1 - z, 1 - x, c)
        got["low"].wait_recv()
        got["lowc"] = send(at(far, 1), at(far, 1), here.to_c)
        got["top"].wait_recv()
        got["topc"] = send(at(far, 0), at(far, 0), here.to_c)

    def fifth():
        for name in ("c", "xc", "zc", "lowc", "topc"):
            got[name].wait_recv()

    return [first, second, third, fourth, fifth]


def block_gather(here, send, mine, local_sem, blocks, far_over_y=False, columns=None):
    rows = blocks.shape[0] // lax.axis_size(plane)
    half = rows // 2
    x, c, y = here.x, here.c, here.y
    got = {}

    def at(slot, part=None):
        first, size = slot * rows, rows
        if part is not None:
            first, size = first + part * half, half
        rows_of = pl.ds(pl.multiple_of(first, size), size)
        return blocks.at[rows_of] if columns is None else blocks.at[rows_of, columns]

    def first():
        slot = plane_slot(x, c, y)
        got["own"] = pltpu.make_async_copy(mine, at(slot), local_sem)
        got["own"].start()
        got["y"] = send(mine, at(slot), here.to_y)
        got["x"] = send(mine, at(slot), here.to_x)
        got["c"] = send(mine, at(slot), here.to_c)

    def second():
        got["y"].wait_recv()
        from_y = plane_slot(x, c, 1 - y)
        got["yc"] = send(at(from_y), at(from_y), here.to_c)
        if not far_over_y:
            got["top"] = send(at(from_y, 0), at(from_y, 0), here.to_x)
        got["x"].wait_recv()
        from_x = plane_slot(1 - x, c, y)
        got["xc"] = send(at(from_x), at(from_x), here.to_c)
        if far_over_y:
            got["top"] = send(at(from_x, 0), at(from_x, 0), here.to_y)
        got["low"] = send(at(from_x, 1), at(from_x, 1), here.to_y)

    def third():
        far = plane_slot(1 - x, c, 1 - y)
        got["top"].wait_recv()
        got["topc"] = send(at(far, 0), at(far, 0), here.to_c)
        got["low"].wait_recv()
        got["lowc"] = send(at(far, 1), at(far, 1), here.to_c)

    def fourth():
        for name in ("c", "yc", "xc", "topc", "lowc"):
            got[name].wait_recv()
        got["own"].wait()

    return [first, second, third, fourth], got


def turn_half(v):
    return pltpu.roll(v, v.shape[-1] // 2, axis=1)


def head_norm(v):
    return lax.rsqrt(jnp.mean(v * v, axis=-1, keepdims=True) + epsilon)


def fetch_kernel(
    hidden_ref,
    attn_gain_ref,
    query_gain_ref,
    key_gain_ref,
    ffn_gain_ref,
    cosine_ref,
    sine_ref,
    key_ref,
    value_ref,
    query_ref,
    output_ref,
    grad_ref,
    routes_ref,
    kv_out,
    q_out,
    o_out,
    g_blocks,
    route_blocks,
    kv_all_out,
    normed_out,
    attended_out,
    query_pre_out,
    queries_out,
    key_pre_ref,
    residual_ref,
    ffn_ref,
    normed_owned,
    attended_owned,
    query_pre_ref,
    queries_ref,
    normed_ref,
    attended_ref,
    kv_own,
    kv_other,
    q_own,
    q_other,
    o_own,
    o_other,
    kv_pre,
    kv_low,
    kv_all,
    send_sem,
    recv_sem,
    local_sem,
):
    here = Places()
    greet([here.to_y, here.to_z, here.to_c, here.to_x])
    send = Sender(send_sem, recv_sem)
    count, width = hidden_ref.shape
    half = width // 2
    narrow = key_ref.shape[1]
    wide = query_ref.shape[1]
    prompt_all = kv_all.shape[0] - (count - PROMPT_DEV)
    spread, groups = lax.axis_size(plane), lax.axis_size("dp")
    tile = 512
    loads = [
        pltpu.make_async_copy(key_ref, kv_own.at[:, pl.ds(0, narrow)], local_sem.at[0]),
        pltpu.make_async_copy(value_ref, kv_own.at[:, pl.ds(narrow, narrow)], local_sem.at[1]),
        pltpu.make_async_copy(query_ref, q_own, local_sem.at[2]),
        pltpu.make_async_copy(output_ref, o_own, local_sem.at[3]),
    ]
    stores = [
        pltpu.make_async_copy(kv_other, kv_out, local_sem.at[4]),
        pltpu.make_async_copy(q_other, q_out, local_sem.at[5]),
        pltpu.make_async_copy(o_other, o_out, local_sem.at[6]),
        pltpu.make_async_copy(kv_all, kv_all_out, local_sem.at[7]),
        pltpu.make_async_copy(normed_owned, normed_out, local_sem.at[11]),
        pltpu.make_async_copy(attended_owned, attended_out, local_sem.at[12]),
        pltpu.make_async_copy(query_pre_ref, query_pre_out, local_sem.at[13]),
        pltpu.make_async_copy(queries_ref, queries_out, local_sem.at[14]),
    ]

    def part_of(size, which):
        first = here.y * size if which == 0 else size - here.y * size
        return pl.ds(pl.multiple_of(first, size), size)

    def project(source, weight, out, which, first, count_of_tiles, add):
        rows = part_of(weight.shape[0], which)

        @pl.loop(first, first + count_of_tiles)
        def _(i):
            cols = pl.ds(pl.multiple_of(i * tile, tile), tile)
            part = dot(source[:, rows], weight[:, cols])
            out[:, cols] = out[:, cols] + part if add else part

    def start():
        for load in loads:
            load.start()
        inputs = hidden_ref[...].astype(f32)
        normed_ref[...] = (inputs * head_norm(inputs) * attn_gain_ref[...]).astype(bf16)

    def own_part():
        share = width // (spread * groups)
        for s in range(spread):
            normed_owned[s] = jnp.concatenate(
                [
                    normed_ref[:, (d * spread + s) * share : (d * spread + s + 1) * share]
                    for d in range(groups)
                ],
                axis=1,
            )
        stores[4].start()
        for load in loads[:3]:
            load.wait()
        project(normed_ref, kv_own, kv_pre, 0, 0, 2 * narrow // tile, False)
        project(normed_ref, q_own, query_pre_ref, 0, 0, wide // tile, False)

    exchange = {}

    def keys_part():
        project(normed_ref, kv_other, kv_pre, 1, 0, 2 * narrow // tile, True)
        stores[0].start()
        key_pre_ref[...] = kv_pre[:, :narrow]
        for h in range(narrow // HEAD_SIZE):
            cols = slice(h * HEAD_SIZE, (h + 1) * HEAD_SIZE)
            v = kv_pre[:, cols]
            v = v * head_norm(v) * key_gain_ref[...]
            kv_low[:, cols] = (v * cosine_ref[...] + turn_half(v) * sine_ref[...]).astype(bf16)
        kv_low[:, narrow:] = kv_pre[:, narrow:].astype(bf16)
        kv_all[prompt_all:, :] = kv_low[PROMPT_DEV:, :]
        source = kv_low.at[pl.ds(0, PROMPT_DEV)]
        slot = kv_all.at[pl.ds(pl.multiple_of(here.ctx * PROMPT_DEV, PROMPT_DEV), PROMPT_DEV)]
        exchange["own"] = pltpu.make_async_copy(source, slot, local_sem.at[8])
        exchange["own"].start()
        exchange["c"] = send(source, slot, here.to_c)
        exchange["x"] = send(source, slot, here.to_x)

    def keys_forward():
        exchange["x"].wait_recv()
        first = ((1 - here.x) * 2 + here.c) * PROMPT_DEV
        slot = kv_all.at[pl.ds(pl.multiple_of(first, PROMPT_DEV), PROMPT_DEV)]
        exchange["xc"] = send(slot, slot, here.to_c)

    def queries_first():
        project(normed_ref, q_other, query_pre_ref, 1, 0, wide // tile // 2, True)

    def queries_rest():
        stores[1].start()
        project(
            normed_ref, q_other, query_pre_ref, 1, wide // tile // 2, wide // tile // 2, True
        )
        for name in ("c", "xc"):
            exchange[name].wait_recv()
        exchange["own"].wait()
        stores[3].start()
        stores[6].start()

    group = 4
    pieces = 4

    def attend(part):
        visible = visible_keys(count, kv_all.shape[0])
        blocks = wide // HEAD_SIZE // group // pieces

        @pl.loop(part * blocks, (part + 1) * blocks)
        def _(i):
            first = lax.div(i * group, wide // narrow) * HEAD_SIZE
            keys = kv_all[:, pl.ds(pl.multiple_of(first, HEAD_SIZE), HEAD_SIZE)]
            values = kv_all[:, pl.ds(pl.multiple_of(narrow + first, HEAD_SIZE), HEAD_SIZE)]
            for h in range(group):
                cols = pl.ds(pl.multiple_of((i * group + h) * HEAD_SIZE, HEAD_SIZE), HEAD_SIZE)
                v = query_pre_ref[:, cols]
                v = v * head_norm(v) * query_gain_ref[...]
                queries = (v * cosine_ref[...] + turn_half(v) * sine_ref[...]).astype(bf16)
                queries_ref[:, cols] = queries
                probs = head_softmax(queries, keys, visible).astype(bf16)
                attended = dot(probs, values).astype(bf16)
                attended_ref[:, cols] = attended
                head = i * group + h
                at = pl.multiple_of(lax.div(head, spread) * HEAD_SIZE, HEAD_SIZE)
                attended_owned[lax.rem(head, spread), :, pl.ds(at, HEAD_SIZE)] = attended

    def output_own():
        stores[5].start()
        stores[7].start()
        loads[3].wait()
        project(attended_ref, o_own, residual_ref, 0, 0, width // tile, False)

    def finish_rows():
        stores[2].start()
        project(attended_ref, o_other, residual_ref, 1, 0, width // tile, True)
        residual = residual_ref[...] + hidden_ref[...].astype(f32)
        residual_ref[...] = residual
        ffn_ref[...] = (residual * head_norm(residual) * ffn_gain_ref[...]).astype(bf16)

    low, high = pl.ds(0, wide // 2), pl.ds(wide // 2, wide // 2)
    o_low, o_high = pl.ds(0, width // 2), pl.ds(width // 2, width // 2)
    rows, o_rows = half // 8, output_ref.shape[0] // 8
    kv, qa, qb, oa, ob, g, r = [
        half_fetch(
            here,
            send,
            [
                (key_ref, pl.ds(0, narrow), pl.ds(0, narrow)),
                (value_ref, pl.ds(0, narrow), pl.ds(narrow, narrow)),
            ],
            kv_other,
            pl.ds(0, 2 * narrow),
            rows,
            rows // 2,
        ),
        half_fetch(here, send, [(query_ref, low, low)], q_other, low, rows, rows // 2),
        half_fetch(here, send, [(query_ref, high, high)], q_other, high, rows, rows // 2),
        half_fetch(here, send, [(output_ref, o_low, o_low)], o_other, o_low, o_rows, o_rows // 4),
        half_fetch(
            here, send, [(output_ref, o_high, o_high)], o_other, o_high, o_rows, o_rows // 4
        ),
        block_gather(here, send, grad_ref, local_sem.at[9], g_blocks, True)[0],
        block_gather(here, send, routes_ref, local_sem.at[10], route_blocks)[0],
    ]
    steps = [
        kv[0], qa[0], qb[0], oa[0], ob[0], g[0], start, kv[1], kv[2], own_part, qa[1],
        kv[3], qa[2], qb[1], kv[4], keys_part, qa[3], qb[2], oa[1],
        keys_forward, qa[4], queries_first, qb[3], ob[1], qb[4], queries_rest,
        oa[2], r[0], lambda: attend(0), lambda: attend(1),
        oa[3], ob[2], g[1], r[1], lambda: attend(2), lambda: attend(3), oa[4], output_own,
        ob[3], g[2], r[2], ob[4], finish_rows, g[3], r[3],
    ]
    for step in steps:
        step()
    for store in stores:
        store.wait()
    send.finish()


def fetch_and_attend(
    hidden_in, attn_gain, query_gain, key_gain, ffn_gain, cosine, sine, key_matrix, value_matrix,
    query_weight, output_weight, out_grad, routes,
):
    rows, width = hidden_in.shape
    half, wide = query_weight.shape
    narrow = key_matrix.shape[1]
    spread = lax.axis_size(plane)
    keys = lax.axis_size("ctx") * PROMPT_DEV + rows - PROMPT_DEV
    vmem = pl.BlockSpec(memory_space=pltpu.VMEM)
    anywhere = pl.BlockSpec(memory_space=pl.ANY)
    copies = 5 * 10 + 1 + 2 * 9 + 3
    return pl.pallas_call(
        fetch_kernel,
        out_shape=[
            jax.ShapeDtypeStruct((half, 2 * narrow), bf16),
            jax.ShapeDtypeStruct((half, wide), bf16),
            jax.ShapeDtypeStruct(output_weight.shape, bf16),
            jax.ShapeDtypeStruct((spread * rows, width), bf16),
            jax.ShapeDtypeStruct((spread * rows, routes.shape[1]), jnp.int32),
            jax.ShapeDtypeStruct((keys, 2 * narrow), bf16),
            jax.ShapeDtypeStruct((spread, rows, width // spread), bf16),
            jax.ShapeDtypeStruct((spread, rows, wide // spread), bf16),
            jax.ShapeDtypeStruct((rows, wide), f32),
            jax.ShapeDtypeStruct((rows, wide), bf16),
            jax.ShapeDtypeStruct((rows, narrow), f32),
            jax.ShapeDtypeStruct((rows, width), f32),
            jax.ShapeDtypeStruct((rows, width), bf16),
        ],
        in_specs=[vmem] * 7 + [anywhere] * 6,
        out_specs=[anywhere] * 10 + [vmem] * 3,
        scratch_shapes=[
            pltpu.VMEM((spread, rows, width // spread), bf16),
            pltpu.VMEM((spread, rows, wide // spread), bf16),
            pltpu.VMEM((rows, wide), f32),
            pltpu.VMEM((rows, wide), bf16),
            pltpu.VMEM((rows, width), bf16),
            pltpu.VMEM((rows, wide), bf16),
            pltpu.VMEM((half, 2 * narrow), bf16),
            pltpu.VMEM((half, 2 * narrow), bf16),
            pltpu.VMEM((half, wide), bf16),
            pltpu.VMEM((half, wide), bf16),
            pltpu.VMEM(output_weight.shape, bf16),
            pltpu.VMEM(output_weight.shape, bf16),
            pltpu.VMEM((rows, 2 * narrow), f32),
            pltpu.VMEM((rows, 2 * narrow), bf16),
            pltpu.VMEM((keys, 2 * narrow), bf16),
            pltpu.SemaphoreType.DMA((copies,)),
            pltpu.SemaphoreType.DMA((copies,)),
            pltpu.SemaphoreType.DMA((15,)),
        ],
        compiler_params=pltpu.CompilerParams(
            collective_id=1, has_side_effects=True, vmem_limit_bytes=60 * 2**20
        ),
        cost_estimate=pl.CostEstimate(
            flops=2 * rows * width * (2 * wide + 2 * narrow) * 2,
            bytes_accessed=60 * 2**20,
            transcendentals=0,
        ),
    )(
        hidden_in, attn_gain.reshape(1, width), query_gain.reshape(1, HEAD_SIZE),
        key_gain.reshape(1, HEAD_SIZE), ffn_gain.reshape(1, width), cosine, sine,
        key_matrix, value_matrix, query_weight, output_weight, out_grad, routes,
    )


def chip_rows(x, y, rows):
    first = plane_slot(x, 0, y) * rows
    return pl.ds(pl.multiple_of(first, rows), 2 * rows)


def expert_chunk(some, first, rows_v, g_v, gate_up_v, down_v, hidden_v, grad_v, total_v, gate, mark):
    ff = down_v.shape[0]
    tile = 256

    @pl.loop(0, ff // tile, unroll=True)
    def _(f):
        at = pl.multiple_of(f * tile, tile)
        a = dot(rows_v[some, :], gate_up_v[:, pl.ds(at, tile)])
        b = dot(rows_v[some, :], gate_up_v[:, pl.ds(ff + at, tile)])
        q = lax.dot_general(
            g_v[some, :],
            down_v[pl.ds(at, tile), :],
            (((1,), (1,)), ((), ())),
            preferred_element_type=f32,
        )
        s = 1.0 / (1.0 + jnp.exp(-a))
        raised_a = a * s
        hidden = raised_a * b
        total_v[...] = total_v[...] + jnp.where(
            mark, jnp.sum(hidden * q, axis=-1, keepdims=True), 0.0
        )
        back = gate * q
        hidden_v[some, pl.ds(at, tile)] = (gate * hidden).astype(bf16)
        grad_v[some, pl.ds(at, tile)] = (back * b * s * (1.0 + a * (1.0 - s))).astype(bf16)
        grad_v[some, pl.ds(ff + at, tile)] = (back * raised_a).astype(bf16)


def first_expert_kernel(
    ffn_ref,
    routes_ref,
    router_ref,
    g_hbm,
    gate_up_hbm,
    down_hbm,
    rows_out,
    hidden_out,
    grad_out,
    gates_ref,
    gate_grad_ref,
    down_grad_ref,
    rows_v,
    g_v,
    gate_up_v,
    down_v,
    hidden_v,
    grad_v,
    total_v,
    down_total,
    send_sem,
    recv_sem,
    local_sem,
):
    here = Places()
    greet([here.to_y, here.to_c, here.to_x])
    send = Sender(send_sem, recv_sem)
    count = ffn_ref.shape[0]
    experts = router_ref.shape[0]
    local_experts = down_hbm.shape[0]
    stages, got = block_gather(here, send, ffn_ref, local_sem.at[0], rows_v)
    stages[0]()
    loads = [
        pltpu.make_async_copy(gate_up_hbm.at[0], gate_up_v, local_sem.at[1]),
        pltpu.make_async_copy(down_hbm.at[0], down_v, local_sem.at[2]),
        pltpu.make_async_copy(g_hbm, g_v, local_sem.at[3]),
    ]
    for load in loads:
        load.start()
    first_expert = plane_index(here) * local_experts
    stores = []

    def chunk(x, y):
        some = chip_rows(x, y, count)
        logits = lax.dot_general(
            rows_v[some, :],
            router_ref[...],
            (((1,), (1,)), ((), ())),
            preferred_element_type=f32,
        )
        ids = lax.broadcasted_iota(jnp.int32, logits.shape, 1)
        routes = routes_ref[some, :]
        chosen = ids < 0
        for k in range(routes.shape[1]):
            chosen = chosen | (routes[:, k : k + 1] == ids)
        logits = jnp.where(chosen, logits, masked)
        raised = jnp.exp(logits - jnp.max(logits, axis=-1, keepdims=True))
        raised = jnp.where(chosen, raised, 0.0)
        gates = raised / jnp.sum(raised, axis=-1, keepdims=True)
        lane = lax.broadcasted_iota(jnp.int32, total_v.shape, 1)
        total_v[...] = jnp.zeros(total_v.shape, f32)
        columns = [
            jnp.sum(jnp.where(ids == first_expert + e, gates, 0.0), axis=-1, keepdims=True)
            for e in range(local_experts)
        ]
        spread = jnp.zeros(total_v.shape, f32)
        for e in range(local_experts):
            spread = jnp.where(lane == e, columns[e], spread)
        gates_ref[some, :] = spread
        mark = (lane == first_expert) | (lane == first_expert + experts)
        expert_chunk(
            some, 0, rows_v, g_v, gate_up_v, down_v, hidden_v, grad_v, total_v, columns[0], mark
        )
        gate_grad_ref[some, :] = total_v[...]
        for source, target in ((hidden_v, hidden_out), (grad_v, grad_out), (rows_v, rows_out)):
            columns = pl.ds(0, source.shape[1])
            store = pltpu.make_async_copy(
                source.at[some, :], target.at[some, columns], local_sem.at[4 + len(stores)]
            )
            store.start()
            stores.append(store)
        add_down(some, len(stores) == 3, len(stores) == 12)

    def add_down(some, is_first, is_last):
        tile = 512

        @pl.loop(0, down_total.shape[1] // tile)
        def _(i):
            cols = pl.ds(pl.multiple_of(i * tile, tile), tile)
            part = transposed_dot(hidden_v[some, :], g_v[some, cols])
            if not is_first:
                part = part + down_total[:, cols]
            if is_last:
                down_grad_ref[:, cols] = part.astype(bf16)
            else:
                down_total[:, cols] = part

    x, y = here.x, here.y
    for name in ("c", "own"):
        arrive(got, name)
    for load in loads:
        load.wait()
    chunk(x, y)
    stages[1]()
    arrive(got, "yc")
    chunk(x, 1 - y)
    stages[2]()
    arrive(got, "xc")
    chunk(1 - x, y)
    arrive(got, "topc")
    arrive(got, "lowc")
    chunk(1 - x, 1 - y)
    for store in stores:
        store.wait()
    send.finish()


def gather_first_expert(ffn_in, route_rows, router_weight, g_rows, gate_up, down_proj):
    experts, ff, width = down_proj.shape
    total = route_rows.shape[0]
    vmem = pl.BlockSpec(memory_space=pltpu.VMEM)
    anywhere = pl.BlockSpec(memory_space=pl.ANY)
    return pl.pallas_call(
        first_expert_kernel,
        out_shape=[
            jax.ShapeDtypeStruct((total, width), bf16),
            jax.ShapeDtypeStruct((total, ff), bf16),
            jax.ShapeDtypeStruct((total, 2 * experts * ff), bf16),
            jax.ShapeDtypeStruct((total, 128), f32),
            jax.ShapeDtypeStruct((total, 128), f32),
            jax.ShapeDtypeStruct((ff, width), bf16),
        ],
        in_specs=[anywhere] + [vmem] * 2 + [anywhere] * 3,
        out_specs=[anywhere] * 3 + [vmem] * 3,
        scratch_shapes=[
            pltpu.VMEM((total, width), bf16),
            pltpu.VMEM((total, width), bf16),
            pltpu.VMEM(gate_up.shape[1:], bf16),
            pltpu.VMEM(down_proj.shape[1:], bf16),
            pltpu.VMEM((total, ff), bf16),
            pltpu.VMEM((total, 2 * ff), bf16),
            pltpu.VMEM((2 * ffn_in.shape[0], 128), f32),
            pltpu.VMEM((ff, width), f32),
            pltpu.SemaphoreType.DMA((9,)),
            pltpu.SemaphoreType.DMA((9,)),
            pltpu.SemaphoreType.DMA((16,)),
        ],
        compiler_params=pltpu.CompilerParams(
            collective_id=2, has_side_effects=True, vmem_limit_bytes=56 * 2**20
        ),
        cost_estimate=pl.CostEstimate(
            flops=2 * total * width * 3 * ff,
            bytes_accessed=40 * 2**20,
            transcendentals=0,
        ),
    )(ffn_in, route_rows, router_weight.T, g_rows, gate_up, down_proj)


def next_expert_kernel(
    which, experts, rows_v, g_v, gates_ref, totals_ref, gate_up_v, down_v, _, hidden_v, grad_v,
    gate_grad_ref, total_v,
):
    lane = lax.broadcasted_iota(jnp.int32, total_v.shape, 1)
    expert = lax.axis_index(plane) * lax.div(experts, lax.axis_size(plane)) + which
    mark = (lane == expert) | (lane == expert + experts)
    total_v[...] = totals_ref[...]
    gate = jnp.sum(jnp.where(lane == which, gates_ref[...], 0.0), axis=-1, keepdims=True)
    some = pl.ds(0, rows_v.shape[0])
    expert_chunk(
        some, 0, rows_v, g_v, gate_up_v.at[0], down_v.at[0], hidden_v, grad_v, total_v, gate, mark
    )
    total = total_v[...]
    high = total.astype(bf16).astype(f32)
    gate_grad_ref[...] = jnp.where(lane < experts, high, total - high).astype(bf16)


def last_expert(which, experts, rows, g_rows, gates, totals, gate_up, down_proj, grads):
    ff, width = down_proj.shape[1:]
    total = rows.shape[0]
    step = total // 4

    def block(columns):
        return pl.BlockSpec((step, columns), lambda i: (i, 0))

    def whole(shape):
        return pl.BlockSpec((1,) + shape[1:], lambda i: (which, 0, 0))

    def kernel(*refs):
        next_expert_kernel(which, experts, *refs)

    return pl.pallas_call(
        kernel,
        grid=(4,),
        out_shape=[
            jax.ShapeDtypeStruct((total, ff), bf16),
            jax.ShapeDtypeStruct(grads.shape, bf16),
            jax.ShapeDtypeStruct((total, 128), bf16),
        ],
        in_specs=[
            block(width), block(width), block(128), block(128),
            whole(gate_up.shape), whole(down_proj.shape), pl.BlockSpec(memory_space=pl.ANY),
        ],
        out_specs=[
            block(ff), pl.BlockSpec((step, 2 * ff), lambda i: (i, which)), block(128)
        ],
        input_output_aliases={6: 1},
        scratch_shapes=[pltpu.VMEM((step, 128), f32)],
        compiler_params=pltpu.CompilerParams(vmem_limit_bytes=56 * 2**20),
        cost_estimate=pl.CostEstimate(flops=10**6, bytes_accessed=10**6, transcendentals=0),
    )(rows, g_rows, gates, totals, gate_up, down_proj, grads)


def weight_grad_kernel(
    query_grad, kv_grad, branch, attended_owned, normed_owned, down_part, sums_ref,
    pre_v, branch_v, attended_v, normed_v, send_sem, recv_sem, local_sem,
):
    here = Places()
    greet([here.to_y, here.to_c, here.to_x])
    send = Sender(send_sem, recv_sem)
    count, wide = query_grad.shape
    narrow = kv_grad.shape[1]
    spread = lax.axis_size(plane)
    tile = sums_ref.shape[1]
    groups = lax.axis_size("dp")
    half = wide // 2
    low, high, last = pl.ds(0, half), pl.ds(half, half), pl.ds(wide, narrow)
    qa, _ = block_gather(
        here, send, query_grad.at[:, low], local_sem.at[1], pre_v, False, low
    )
    qb, _ = block_gather(
        here, send, query_grad.at[:, high], local_sem.at[2], pre_v, False, high
    )
    kv, _ = block_gather(here, send, kv_grad, local_sem.at[3], pre_v, False, last)
    loads = [pltpu.make_async_copy(branch, branch_v, local_sem.at[0])]
    for device in range(spread):
        slot = plane_slot(device // 4, device // 2 % 2, device % 2)
        rows = pl.ds(slot * count, count)
        for source, target in ((attended_owned, attended_v), (normed_owned, normed_v)):
            loads.append(
                pltpu.make_async_copy(
                    source.at[device], target.at[rows], local_sem.at[3 + len(loads)]
                )
            )

    output_rows = attended_v.shape[1] // groups * (branch.shape[1] // tile)
    pre_rows = normed_v.shape[1] // groups * ((wide + narrow) // tile)
    down_rows = down_part.shape[0] // groups
    kept = [
        pltpu.make_async_copy(
            down_part.at[pl.ds(d * down_rows, down_rows), pl.ds(i * tile, tile)],
            sums_ref.at[
                pl.ds(
                    d * (sums_ref.shape[0] // groups) + output_rows + pre_rows + i * down_rows,
                    down_rows,
                )
            ],
            local_sem.at[4 + 2 * spread + d * (down_part.shape[1] // tile) + i],
        )
        for d in range(groups)
        for i in range(down_part.shape[1] // tile)
    ]

    def start():
        for copy in loads + kept:
            copy.start()

    def product(left, right, base, first, tiles):
        rows = left.shape[1] // groups

        @pl.loop(first, first + tiles)
        def _(i):
            cols = pl.ds(pl.multiple_of(i * tile, tile), tile)
            part = transposed_dot(left[...], right[:, cols]).astype(bf16)
            for d in range(groups):
                at = d * (sums_ref.shape[0] // groups) + base + i * rows
                sums_ref[pl.ds(pl.multiple_of(at, 64), rows), :] = part[
                    d * rows : (d + 1) * rows
                ]

    def output_product():
        for load in loads:
            load.wait()
        product(attended_v, branch_v, 0, 0, branch.shape[1] // tile)

    steps = [
        qa[0], qb[0], kv[0], start, output_product, qa[1], qb[1], qa[2], kv[1], qb[2], qa[3],
        lambda: product(normed_v, pre_v, output_rows, 0, half // tile),
        kv[2], qb[3],
        lambda: product(normed_v, pre_v, output_rows, half // tile, half // tile),
        kv[3],
        lambda: product(normed_v, pre_v, output_rows, wide // tile, narrow // tile),
    ]
    for step in steps:
        step()
    for copy in kept:
        copy.wait()
    send.finish()


def weight_grads(query_grad, kv_grad, branch, attended_owned, normed_owned, down_part):
    count, wide = query_grad.shape
    narrow, width = kv_grad.shape[1], branch.shape[1]
    spread = lax.axis_size(plane)
    tile = narrow
    elements = attended_owned.shape[2] * width + normed_owned.shape[2] * (wide + narrow)
    elements += math.prod(down_part.shape)
    groups = lax.axis_size("dp")
    vmem = pl.BlockSpec(memory_space=pltpu.VMEM)
    anywhere = pl.BlockSpec(memory_space=pl.ANY)
    return pl.pallas_call(
        weight_grad_kernel,
        out_shape=jax.ShapeDtypeStruct((elements // tile, tile), bf16),
        in_specs=[anywhere] * 6,
        out_specs=vmem,
        scratch_shapes=[
            pltpu.VMEM((spread * count, wide + narrow), bf16),
            pltpu.VMEM((spread * count, width), bf16),
            pltpu.VMEM((spread * count, attended_owned.shape[2]), bf16),
            pltpu.VMEM((spread * count, normed_owned.shape[2]), bf16),
            pltpu.SemaphoreType.DMA((27,)),
            pltpu.SemaphoreType.DMA((27,)),
            pltpu.SemaphoreType.DMA((4 + 2 * spread + groups * (down_part.shape[1] // tile),)),
        ],
        compiler_params=pltpu.CompilerParams(
            collective_id=5, has_side_effects=True, vmem_limit_bytes=56 * 2**20
        ),
        cost_estimate=pl.CostEstimate(flops=10**6, bytes_accessed=10**6, transcendentals=0),
    )(query_grad, kv_grad, branch, attended_owned, normed_owned, down_part)


def untile_kernel(sums_ref, down_ref, output_ref, query_ref, key_ref, value_ref, downs_ref):
    tile = sums_ref.shape[1]
    at = 0

    def take(rows):
        nonlocal at
        part = sums_ref[at : at + rows, :].astype(f32)
        at = at + rows
        return part

    for out in (output_ref, query_ref):
        for first in range(0, out.shape[1], tile):
            out[:, first : first + tile] = take(out.shape[0])
    both = take(key_ref.shape[0])
    key_ref[...] = both[:, : key_ref.shape[1]]
    value_ref[...] = both[:, key_ref.shape[1] :]
    downs_ref[0] = down_ref[...].astype(f32)
    for first in range(0, downs_ref.shape[2], tile):
        downs_ref[1, :, first : first + tile] = take(downs_ref.shape[1])


def untile(sums, down, output_rows, wide, share, narrow):
    vmem = pl.BlockSpec(memory_space=pltpu.VMEM)
    rows, width = down.shape
    shapes = [
        (output_rows, width), (share, wide), (share, narrow), (share, narrow), (2, rows, width)
    ]
    return pl.pallas_call(
        untile_kernel,
        out_shape=[jax.ShapeDtypeStruct(shape, f32) for shape in shapes],
        in_specs=[vmem] * 2,
        out_specs=[vmem] * 5,
        compiler_params=pltpu.CompilerParams(vmem_limit_bytes=32 * 2**20),
    )(sums, down)


def arrive(got, name):
    copy = got[name]
    copy.wait() if name == "own" else copy.wait_recv()


def plane_index(here):
    return here.ctx * 2 + here.y


def plane_sum_kernel(across, parts, *refs):
    lefts, weight_hbm = refs[:parts], refs[parts]
    refs = refs[parts + 1 :]
    extra_ref, sources, targets = None, [], []
    if across:
        extra_ref, sources, targets = refs[0], refs[1:3], refs[4:6]
        refs = (refs[3],) + refs[6:]
    (
        out_ref, left_v, weight_v, part_v, core_v, edge_v, last_v, send_sem, recv_sem, local_sem,
    ) = refs
    here = Places()
    peers = here.peers() if across else []
    greet([device for _, device in peers] or [here.to_y, here.to_c, here.to_x])
    send = Sender(send_sem, recv_sem)
    count = out_ref.shape[0]
    half = count // 2
    experts = weight_hbm.shape[0]
    part_depth = lefts[0].shape[1]
    depth = part_depth * parts // experts
    width = weight_hbm.shape[1] if across else weight_hbm.shape[2]
    tile = 256
    x, y, c = here.x, here.y, here.c
    chips = [(1 - x, 1 - y), (1 - x, y), (x, 1 - y), (x, y)]
    weight_load = pltpu.make_async_copy(weight_hbm, weight_v, local_sem.at[0])
    weight_load.start()
    loads = []
    for k, (cx, cy) in enumerate(chips):
        some = chip_rows(cx, cy, count)
        loads.append(
            [
                pltpu.make_async_copy(
                    left.at[some, :],
                    left_v.at[k, :, pl.ds(e * part_depth, part_depth)],
                    local_sem.at[1 + parts * k + e],
                )
                for e, left in enumerate(lefts)
            ]
        )
        for load in loads[-1]:
            load.start()
    owned = []
    for index, device in peers:
        for source, target in zip(sources, targets):
            owned.append(send(source.at[index], target.at[plane_index(here)], device))
    kept = [
        pltpu.make_async_copy(
            source.at[plane_index(here)],
            target.at[plane_index(here)],
            local_sem.at[1 + 4 * parts + i],
        )
        for i, (source, target) in enumerate(zip(sources, targets))
    ]
    for copy in kept:
        copy.start()
    weight_load.wait()
    to_core = []

    def compute(k):
        for load in loads[k]:
            load.wait()

        @pl.loop(0, width // tile)
        def _(n):
            cols = pl.ds(pl.multiple_of(n * tile, tile), tile)
            total = None
            for e in range(experts):
                left = left_v[k, :, e * depth : (e + 1) * depth]
                if across:
                    part = lax.dot_general(
                        left,
                        weight_v[e, cols, :],
                        (((1,), (1,)), ((), ())),
                        preferred_element_type=f32,
                    )
                else:
                    part = dot(left, weight_v[e, :, cols])
                total = part if total is None else total + part
            part_v[k, :, cols] = total.astype(bf16)

        if extra_ref is not None:
            part_v[k, :, width:] = extra_ref[chip_rows(*chips[k], count), :]
        to_core.append(
            send(
                part_v.at[k, pl.ds(pl.multiple_of((1 - c) * count, count), count)],
                core_v.at[k],
                here.to_c,
            )
        )

    mine = pl.ds(pl.multiple_of(c * count, count), count)

    def chip_sum(k):
        to_core[k].wait_recv()
        return part_v[k, mine, :].astype(f32) + core_v[k].astype(f32)

    compute(0)
    compute(1)
    core_v[0] = chip_sum(0).astype(bf16)
    from_x = send(core_v.at[0, pl.ds(0, half)], edge_v.at[0], here.to_x)
    from_y = send(core_v.at[0, pl.ds(half, half)], edge_v.at[1], here.to_y)
    compute(2)
    over_x_sum = chip_sum(1)
    core_v[1, :half] = over_x_sum[:half].astype(bf16)
    from_y.wait_recv()
    core_v[1, half:] = (over_x_sum[half:] + edge_v[1].astype(f32)).astype(bf16)
    last_x = send(core_v.at[1], last_v.at[0], here.to_x)
    over_y_sum = chip_sum(2)
    core_v[2, half:] = over_y_sum[half:].astype(bf16)
    from_x.wait_recv()
    core_v[2, :half] = (over_y_sum[:half] + edge_v[0].astype(f32)).astype(bf16)
    last_y = send(core_v.at[2], last_v.at[1], here.to_y)
    compute(3)
    out_ref[...] = chip_sum(3)
    last_x.wait_recv()
    last_y.wait_recv()
    out_ref[...] = out_ref[...] + last_v[0].astype(f32) + last_v[1].astype(f32)
    for copy in owned:
        copy.wait_recv()
    for copy in kept:
        copy.wait()
    send.finish()


def plane_sum(lefts, weight, extra, owned, collective_id):
    across = extra is not None
    count = lefts[0].shape[0] // lax.axis_size(plane)
    width = weight.shape[1] if across else weight.shape[2]
    wide = width + (extra.shape[1] if across else 0)
    parts, depth = len(lefts), lefts[0].shape[1]
    vmem = pl.BlockSpec(memory_space=pltpu.VMEM)
    anywhere = pl.BlockSpec(memory_space=pl.ANY)

    def kernel(*refs):
        plane_sum_kernel(across, parts, *refs)

    return pl.pallas_call(
        kernel,
        out_shape=[jax.ShapeDtypeStruct((count, wide), f32)]
        + [jax.ShapeDtypeStruct(v.shape, v.dtype) for v in owned],
        in_specs=[anywhere] * (parts + 1) + [vmem] * across + [anywhere] * len(owned),
        out_specs=[vmem] + [anywhere] * len(owned),
        scratch_shapes=[
            pltpu.VMEM((4, 2 * count, parts * depth), bf16),
            pltpu.VMEM(weight.shape, bf16),
            pltpu.VMEM((4, 2 * count, wide), bf16),
            pltpu.VMEM((4, count, wide), bf16),
            pltpu.VMEM((2, count // 2, wide), bf16),
            pltpu.VMEM((2, count, wide), bf16),
            pltpu.SemaphoreType.DMA((8 + 7 * len(owned),)),
            pltpu.SemaphoreType.DMA((8 + 7 * len(owned),)),
            pltpu.SemaphoreType.DMA((1 + 4 * parts + len(owned),)),
        ],
        compiler_params=pltpu.CompilerParams(
            collective_id=collective_id, has_side_effects=True, vmem_limit_bytes=60 * 2**20
        ),
        cost_estimate=pl.CostEstimate(flops=10**6, bytes_accessed=10**6, transcendentals=0),
    )(*lefts, weight, *([extra] if across else []), *owned)


def head_softmax(queries, keys, visible):
    scores = lax.dot_general(
        queries, keys, (((1,), (1,)), ((), ())), preferred_element_type=f32
    ) * (HEAD_SIZE ** (-0.5))
    scores = jnp.where(visible, scores, masked)
    raised = jnp.exp(scores - jnp.max(scores, axis=-1, keepdims=True))
    return raised / jnp.sum(raised, axis=-1, keepdims=True)


def visible_keys(rows, keys):
    row = lax.broadcasted_iota(jnp.int32, (rows, keys), 0)
    key = lax.broadcasted_iota(jnp.int32, (rows, keys), 1)
    prompt_all = keys - (rows - PROMPT_DEV)
    own = lax.axis_index("ctx") * PROMPT_DEV + row
    position = jnp.where(row < PROMPT_DEV, own, prompt_all + row - PROMPT_DEV)
    return key <= position


def attention_kernel(
    query_pre_ref, gain_ref, cosine_ref, sine_ref, keys_ref, values_ref, queries_ref, attended_ref
):
    rows = query_pre_ref.shape[0]
    visible = visible_keys(rows, keys_ref.shape[0])
    keys = keys_ref[...]
    values = values_ref[...]
    for h in range(query_pre_ref.shape[1] // HEAD_SIZE):
        cols = slice(h * HEAD_SIZE, (h + 1) * HEAD_SIZE)
        v = query_pre_ref[:, cols]
        v = v * head_norm(v) * gain_ref[...]
        queries = (v * cosine_ref[...] + turn_half(v) * sine_ref[...]).astype(bf16)
        queries_ref[:, cols] = queries
        probs = head_softmax(queries, keys, visible).astype(bf16)
        attended_ref[:, cols] = dot(probs, values).astype(bf16)


def attention(query_pre, gain, cosine, sine, kv_all):
    rows, wide = query_pre.shape
    keys = kv_all.shape[0]
    group = wide // KEY_VALUE_HEADS
    small = pl.BlockSpec((rows, HEAD_SIZE), lambda i: (0, 0))
    block = pl.BlockSpec((rows, group), lambda i: (0, i))
    return pl.pallas_call(
        attention_kernel,
        grid=(KEY_VALUE_HEADS,),
        out_shape=[jax.ShapeDtypeStruct((rows, wide), bf16)] * 2,
        in_specs=[
            block,
            pl.BlockSpec((1, HEAD_SIZE), lambda i: (0, 0)),
            small,
            small,
            pl.BlockSpec((keys, HEAD_SIZE), lambda i: (0, i)),
            pl.BlockSpec((keys, HEAD_SIZE), lambda i: (0, KEY_VALUE_HEADS + i)),
        ],
        out_specs=[block, block],
        compiler_params=pltpu.CompilerParams(vmem_limit_bytes=48 * 2**20),
    )(query_pre, gain.reshape(1, HEAD_SIZE), cosine, sine, kv_all, kv_all)


def transposed_dot(a, b):
    return lax.dot_general(a, b, (((0,), (0,)), ((), ())), preferred_element_type=f32)


def back_heads(
    first,
    key_at,
    value_at,
    out_at,
    query_pre_ref,
    gain_ref,
    cosine_ref,
    sine_ref,
    keys_ref,
    values_ref,
    queries_ref,
    grad_ref,
    pre_grad_ref,
    key_grad_ref,
    value_grad_ref,
):
    rows = query_pre_ref.shape[0]
    visible = visible_keys(rows, keys_ref.shape[0])
    keys = keys_ref[:, pl.ds(key_at, HEAD_SIZE)]
    values = values_ref[:, pl.ds(value_at, HEAD_SIZE)]
    scale = HEAD_SIZE ** (-0.5)
    gain_grad = jnp.zeros((rows, HEAD_SIZE), f32)
    key_grad = jnp.zeros(keys.shape, f32)
    value_grad = jnp.zeros(keys.shape, f32)
    for h in range(QUERY_HEADS // KEY_VALUE_HEADS):
        cols = pl.ds(first + h * HEAD_SIZE, HEAD_SIZE)
        queries = queries_ref[:, cols]
        grad = grad_ref[:, cols]
        probs = head_softmax(queries, keys, visible)
        prob_grad = lax.dot_general(
            grad, values, (((1,), (1,)), ((), ())), preferred_element_type=f32
        )
        delta = jnp.sum(probs * prob_grad, axis=-1, keepdims=True)
        score_grad = (probs * (prob_grad - delta)).astype(bf16)
        key_grad = key_grad + transposed_dot(score_grad, queries)
        value_grad = value_grad + transposed_dot(probs.astype(bf16), grad)
        u = dot(score_grad, keys) * scale
        u = u * cosine_ref[...] + turn_half(u * sine_ref[...])
        v = query_pre_ref[:, cols]
        inv = head_norm(v)
        gain_grad = gain_grad + u * v * inv
        pre_grad_ref[:, cols] = norm_back(v, inv, gain_ref[...], u).astype(bf16)
    out = pl.ds(out_at, HEAD_SIZE)
    key_grad_ref[:, out] = (key_grad * scale).astype(key_grad_ref.dtype)
    value_grad_ref[:, out] = value_grad.astype(value_grad_ref.dtype)
    return jnp.sum(gain_grad, axis=0, keepdims=True)


def attention_back_kernel(*refs):
    refs[-1][0] = back_heads(0, 0, 0, 0, *refs[:-1])


def attention_back_gather_kernel(
    query_pre_ref, gain_ref, cosine_ref, sine_ref, kv_ref, queries_ref, grad_ref, branch,
    pre_grad_ref, key_grad_ref, value_grad_ref, gain_grad_ref, branch_rows,
    send_sem, recv_sem, local_sem,
):
    here = Places()
    greet([here.to_y, here.to_c, here.to_x])
    send = Sender(send_sem, recv_sem)
    stages, _ = block_gather(here, send, branch, local_sem.at[0], branch_rows)
    group = query_pre_ref.shape[1] // KEY_VALUE_HEADS
    narrow = kv_ref.shape[1] // 2

    def heads(first, count):
        @pl.loop(first, first + count)
        def _(i):
            at = pl.multiple_of(i * HEAD_SIZE, HEAD_SIZE)
            gain_grad_ref[i] = back_heads(
                pl.multiple_of(i * group, group),
                at,
                pl.multiple_of(narrow + i * HEAD_SIZE, HEAD_SIZE),
                at,
                query_pre_ref,
                gain_ref,
                cosine_ref,
                sine_ref,
                kv_ref,
                kv_ref,
                queries_ref,
                grad_ref,
                pre_grad_ref,
                key_grad_ref,
                value_grad_ref,
            )

    stages[0]()
    heads(0, KEY_VALUE_HEADS - 1)
    stages[1]()
    heads(KEY_VALUE_HEADS - 1, 1)
    stages[2]()
    stages[3]()
    send.finish()


def attention_back_gather(query_pre, gain, cosine, sine, kv_all, queries, attended_grad, branch):
    rows, wide = query_pre.shape
    keys, both = kv_all.shape
    vmem = pl.BlockSpec(memory_space=pltpu.VMEM)
    anywhere = pl.BlockSpec(memory_space=pl.ANY)
    return pl.pallas_call(
        attention_back_gather_kernel,
        out_shape=[
            jax.ShapeDtypeStruct((rows, wide), bf16),
            jax.ShapeDtypeStruct((keys, both // 2), f32),
            jax.ShapeDtypeStruct((keys, both // 2), f32),
            jax.ShapeDtypeStruct((KEY_VALUE_HEADS, 1, HEAD_SIZE), f32),
            jax.ShapeDtypeStruct((lax.axis_size(plane) * rows, branch.shape[1]), bf16),
        ],
        in_specs=[vmem] * 7 + [anywhere],
        out_specs=[vmem] * 4 + [anywhere],
        scratch_shapes=[
            pltpu.SemaphoreType.DMA((9,)),
            pltpu.SemaphoreType.DMA((9,)),
            pltpu.SemaphoreType.DMA((1,)),
        ],
        compiler_params=pltpu.CompilerParams(
            collective_id=6, has_side_effects=True, vmem_limit_bytes=48 * 2**20
        ),
        cost_estimate=pl.CostEstimate(flops=10**6, bytes_accessed=10**6, transcendentals=0),
    )(
        query_pre, gain.reshape(1, HEAD_SIZE), cosine, sine, kv_all, queries, attended_grad, branch
    )


def attention_back(query_pre, gain, cosine, sine, kv_all, queries, attended_grad):
    rows, wide = query_pre.shape
    keys, both = kv_all.shape
    group = wide // KEY_VALUE_HEADS
    small = pl.BlockSpec((rows, HEAD_SIZE), lambda i: (0, 0))
    block = pl.BlockSpec((rows, group), lambda i: (0, i))
    return pl.pallas_call(
        attention_back_kernel,
        grid=(KEY_VALUE_HEADS,),
        out_shape=[
            jax.ShapeDtypeStruct((rows, wide), bf16),
            jax.ShapeDtypeStruct((keys, both // 2), f32),
            jax.ShapeDtypeStruct((keys, both // 2), f32),
            jax.ShapeDtypeStruct((KEY_VALUE_HEADS, 1, HEAD_SIZE), f32),
        ],
        in_specs=[
            block,
            pl.BlockSpec((1, HEAD_SIZE), lambda i: (0, 0)),
            small,
            small,
            pl.BlockSpec((keys, HEAD_SIZE), lambda i: (0, i)),
            pl.BlockSpec((keys, HEAD_SIZE), lambda i: (0, KEY_VALUE_HEADS + i)),
            block,
            block,
        ],
        out_specs=[
            block,
            pl.BlockSpec((keys, HEAD_SIZE), lambda i: (0, i)),
            pl.BlockSpec((keys, HEAD_SIZE), lambda i: (0, i)),
            pl.BlockSpec((1, 1, HEAD_SIZE), lambda i: (i, 0, 0)),
        ],
        cost_estimate=pl.CostEstimate(flops=10**6, bytes_accessed=10**6, transcendentals=0),
        compiler_params=pltpu.CompilerParams(vmem_limit_bytes=48 * 2**20),
    )(
        query_pre, gain.reshape(1, HEAD_SIZE), cosine, sine, kv_all, kv_all, queries, attended_grad
    )


def join_halves(mine, other):
    lower = lax.axis_index("expert") == 0
    return jnp.concatenate(
        [jnp.where(lower, mine, other), jnp.where(lower, other, mine)], axis=1
    )


def dot(a, b):
    return jnp.dot(a, b, preferred_element_type=f32)


def ctx_sum(v):
    if not small_plane():
        return lax.psum_scatter(v, "ctx", scatter_dimension=1, tiled=True).astype(f32)
    member = lax.axis_index("ctx")

    def block(j):
        return lax.dynamic_slice_in_dim(v, (member ^ j) * PROMPT_DEV, PROMPT_DEV, axis=1)

    near = block(0).astype(f32) + core(block(1)).astype(f32)
    far = (block(2).astype(f32) + core(block(3)).astype(f32)).astype(bf16)
    return near + over_x(far).astype(f32)


def body(
    hidden_in,
    attn_gain,
    query_weight,
    key_matrix,
    value_matrix,
    query_gain,
    key_gain,
    output_weight,
    ffn_gain,
    router_weight,
    gate_up,
    down_proj,
    routes,
    out_grad,
):
    ctx_count = lax.axis_size("ctx")
    spread_count = lax.axis_size(plane)
    dp_count = lax.axis_size("dp")
    device_count = dp_count * spread_count
    local_experts = gate_up.shape[0]
    count_of_rows = hidden_in.shape[0]
    prompt_all = PROMPT_DEV * ctx_count
    hidden_ff = gate_up.shape[2] // 2
    member = lax.axis_index("ctx")
    offsets = jnp.arange(count_of_rows, dtype=jnp.int32)
    position = jnp.where(
        offsets < PROMPT_DEV, member * PROMPT_DEV + offsets, prompt_all + offsets - PROMPT_DEV
    )
    cosine, rope_sine = angles(position, HEAD_SIZE)
    narrow = KEY_VALUE_HEADS * HEAD_SIZE
    wide = QUERY_HEADS * HEAD_SIZE
    inputs = hidden_in.astype(f32)
    scale_in = rms_scale(inputs)

    def by_owner(v):
        v = v.reshape(count_of_rows, dp_count, spread_count, -1)
        return v.transpose(2, 0, 1, 3).reshape(spread_count, count_of_rows, -1)

    signed_sine = rope_sine * jnp.where(jnp.arange(HEAD_SIZE) < HEAD_SIZE // 2, -1.0, 1.0)
    if small_plane():
        (
            kv_other,
            q_other,
            o_other,
            g_rows,
            route_rows,
            kv_all,
            normed_owned,
            attended_owned,
            query_pre,
            queries,
            key_pre,
            residual,
            ffn_in,
        ) = fetch_and_attend(
            hidden_in, attn_gain, query_gain, key_gain, ffn_gain, cosine, signed_sine,
            key_matrix, value_matrix, query_weight, output_weight, out_grad, routes,
        )
        kv_weights = [jnp.concatenate([key_matrix, value_matrix], axis=1), kv_other]
        q_weights = [query_weight, q_other]
        o_weights = [output_weight, o_other]
    else:
        full = [
            lax.all_gather(w, "expert", axis=0, tiled=True)
            for w in (
                jnp.concatenate([key_matrix, value_matrix], axis=1),
                query_weight,
                output_weight,
            )
        ]
        kv_weights, q_weights, o_weights = [[w] for w in full]
        g_rows = lax.all_gather(out_grad, plane, axis=0, tiled=True)
        route_rows = lax.all_gather(routes, plane, axis=0, tiled=True)
        normalized_input = (inputs * scale_in * attn_gain).astype(bf16)
        query_pre = dot(normalized_input, q_weights[0])
        key_value_pre = dot(normalized_input, kv_weights[0])
        key_pre = key_value_pre[:, :narrow]
        key_heads = key_pre.reshape(count_of_rows, KEY_VALUE_HEADS, HEAD_SIZE)
        key_low = rotate(
            key_heads * rms_scale(key_heads) * key_gain, cosine[:, None, :], rope_sine[:, None, :]
        ).astype(bf16)
        kv_low = jnp.concatenate(
            [key_low.reshape(count_of_rows, narrow), key_value_pre[:, narrow:].astype(bf16)],
            axis=1,
        )
        kv_blocks = lax.all_gather(kv_low[:PROMPT_DEV], "ctx", axis=0, tiled=True)
        kv_all = jnp.concatenate([kv_blocks, kv_low[PROMPT_DEV:]], axis=0)
        queries, attended = attention(query_pre, query_gain, cosine, signed_sine, kv_all)
        residual = inputs + dot(attended, o_weights[0])
        ffn_in = (residual * rms_scale(residual) * ffn_gain).astype(bf16)
        normed_owned = by_owner(normalized_input)
        attended_owned = by_owner(attended)

    def owned(v):
        return lax.all_to_all(v, plane, split_axis=0, concat_axis=0, tiled=True)

    def backward_dot(v, weights):
        parts = [dot(v, w.T) for w in weights]
        return parts[0] if len(parts) == 1 else join_halves(*parts)

    key_before_norm = key_pre.reshape(count_of_rows, KEY_VALUE_HEADS, HEAD_SIZE)
    key_inv = rms_scale(key_before_norm)
    scale_ffn = rms_scale(residual)

    expert_count = local_experts * spread_count
    expert_ids = jnp.arange(expert_count, dtype=jnp.int32)

    def gates_of(some_rows, some_routes):
        logits = dot(some_rows, router_weight)
        chosen = jnp.any(some_routes[:, :, None] == expert_ids[None, None, :], axis=1)
        logits = jnp.where(chosen, logits, masked)
        raised = jnp.where(
            chosen, jnp.exp(logits - jnp.max(logits, axis=-1, keepdims=True)), 0.0
        )
        return raised / jnp.sum(raised, axis=-1, keepdims=True)

    gates = gates_of(ffn_in, routes)
    if small_plane():
        rows, hidden, grads, gates_mine, totals, down_part = gather_first_expert(
            ffn_in, route_rows, router_weight, g_rows, gate_up, down_proj
        )
        hiddens = [hidden]
        down_parts = [down_part]
        rows, grads = after((rows, grads), down_parts)
        hidden, grads, gate_grads = last_expert(
            1, expert_count, rows, g_rows, gates_mine, totals, gate_up, down_proj, grads
        )
        hiddens.append(hidden)
        projected_grads = [grads]
        gate_up_parts = [dot(rows.T, grads).astype(bf16)]
        down_late = dot(after(hidden, gate_up_parts).T, g_rows).astype(bf16)
    else:
        rows = lax.all_gather(ffn_in, plane, axis=0, tiled=True)
        first_expert = lax.axis_index(plane) * local_experts
        gates_mine = lax.dynamic_slice_in_dim(
            gates_of(rows, route_rows), first_expert, local_experts, axis=1
        )
        gate_grads, hiddens, projected_grads = [], [], []
        for which in range(local_experts):
            gate = gates_mine[:, which : which + 1]
            projected = dot(rows, gate_up[which])
            back = dot(g_rows, down_proj[which].T)
            gate_part = projected[:, :hidden_ff]
            up_part = projected[:, hidden_ff:]
            sigmoid_gate = jax.nn.sigmoid(gate_part)
            hidden = gate_part * sigmoid_gate * up_part
            gate_grads.append(jnp.sum(hidden * back, axis=-1))
            hiddens.append((gate * hidden).astype(bf16))
            back = gate * back
            gate_back = back * up_part * sigmoid_gate * (1.0 + gate_part * (1.0 - sigmoid_gate))
            up_back = back * gate_part * sigmoid_gate
            projected_grads.append(jnp.concatenate([gate_back, up_back], axis=-1).astype(bf16))
        attended_owned, normed_owned = owned(attended_owned), owned(normed_owned)
        down_parts = [dot(v.T, g_rows).astype(bf16) for v in hiddens]
        gate_up_parts = [dot(rows.T, v).astype(bf16) for v in projected_grads]
    down_low, gate_up_low = [
        [lax.psum_scatter(v, "dp", scatter_dimension=0, tiled=True) for v in parts]
        for parts in (down_parts, gate_up_parts)
    ]
    gate_up_grad = jnp.stack(
        [
            part.astype(f32)
            for v in gate_up_low
            for part in jnp.split(v, v.shape[1] // (2 * hidden_ff), axis=1)
        ]
    )
    projected_grads, hiddens = lax.optimization_barrier(
        ((projected_grads, hiddens), down_parts, gate_up_parts)
    )[0]
    if small_plane():
        back, attended_owned, normed_owned = plane_sum(
            projected_grads, gate_up, gate_grads, [attended_owned, normed_owned], 3
        )
        back_sum = back[:, :MODEL_WIDTH]
        gate_grad = (
            back[:, MODEL_WIDTH : MODEL_WIDTH + expert_count]
            + back[:, MODEL_WIDTH + expert_count : MODEL_WIDTH + 2 * expert_count]
        )
        moe_sum = None
    else:
        moe_part = 0.0
        row_part = 0.0
        for which in range(local_experts):
            row_part = row_part + dot(projected_grads[which], gate_up[which].T)
            moe_part = moe_part + dot(hiddens[which], down_proj[which])
        moe_sum, back_sum = [
            lax.psum_scatter(v.astype(bf16), plane, scatter_dimension=0, tiled=True).astype(f32)
            for v in (moe_part, row_part)
        ]
        gate_grad = lax.all_to_all(
            jnp.stack(gate_grads, axis=1).reshape(spread_count, count_of_rows, local_experts),
            plane,
            split_axis=0,
            concat_axis=0,
            tiled=True,
        )
        gate_grad = gate_grad.transpose(1, 0, 2).reshape(count_of_rows, expert_count)
    logit_grad = gates * (gate_grad - jnp.sum(gates * gate_grad, axis=-1, keepdims=True))

    grad_out = out_grad.astype(f32)
    router_local = jnp.dot(ffn_in.T, logit_grad, preferred_element_type=f32)
    ffn_in_grad = back_sum + jnp.dot(
        logit_grad, router_weight.astype(f32).T, precision=highest
    )
    residual_grad = grad_out + norm_back(residual, scale_ffn, ffn_gain, ffn_in_grad)
    ffn_gain_local = jnp.sum(ffn_in_grad * residual * scale_ffn, axis=0)
    branch_low = residual_grad.astype(bf16)
    attended_grad = backward_dot(branch_low, o_weights).astype(bf16)
    operands = (query_pre, query_gain, cosine, signed_sine, kv_all, queries, attended_grad)
    if small_plane():
        *attention_grads, branch_rows = attention_back_gather(*operands, branch_low)
    else:
        attention_grads = attention_back(*operands)
    query_pre_grad, key_grad_all, value_grad_all, query_gain_parts = attention_grads
    query_gain_local = jnp.sum(query_gain_parts, axis=(0, 1))
    pair_grads = jnp.stack([key_grad_all[:prompt_all], value_grad_all[:prompt_all]]).astype(bf16)
    prompt_grads = ctx_sum(pair_grads)
    key_grad = jnp.concatenate([prompt_grads[0], key_grad_all[prompt_all:]], axis=0).reshape(
        count_of_rows, KEY_VALUE_HEADS, HEAD_SIZE
    )
    value_gradient = jnp.concatenate([prompt_grads[1], value_grad_all[prompt_all:]], axis=0)
    key_rot_grad = rotate_back(key_grad, cosine[:, None, :], rope_sine[:, None, :])
    key_gain_local = jnp.sum(key_rot_grad * key_before_norm * key_inv, axis=(0, 1))
    key_pre_grad = (
        norm_back(key_before_norm, key_inv, key_gain, key_rot_grad)
        .astype(bf16)
        .reshape(count_of_rows, KEY_VALUE_HEADS * HEAD_SIZE)
    )
    key_value_grad = jnp.concatenate([key_pre_grad, value_gradient.astype(bf16)], axis=1)
    if small_plane():
        local = [
            weight_grads(
                query_pre_grad, key_value_grad, branch_rows, attended_owned, normed_owned, down_late
            )
        ]
    else:
        branch_rows = lax.all_gather(branch_low, plane, axis=0, tiled=True)
        pre_rows = lax.all_gather(
            jnp.concatenate([query_pre_grad, key_value_grad], axis=1), plane, axis=0, tiled=True
        )
        attended_owned, normed_owned = [
            v.reshape(spread_count * count_of_rows, -1) for v in (attended_owned, normed_owned)
        ]
        local = [
            dot(attended_owned.T, branch_rows).astype(bf16),
            dot(normed_owned.T, pre_rows).astype(bf16),
        ]
    query_pre_grad, key_value_grad = lax.optimization_barrier(
        ((query_pre_grad, key_value_grad), local)
    )[0]
    normed_grad = backward_dot(query_pre_grad, q_weights) + backward_dot(
        key_value_grad, kv_weights
    )
    attn_gain_local = jnp.sum(normed_grad * inputs * scale_in, axis=0)
    hidden_grad = residual_grad + norm_back(inputs, scale_in, attn_gain, normed_grad)
    if small_plane():
        moe_sum = plane_sum(after(hiddens, local), down_proj, None, [], 4)[0]
    block_out = (residual + moe_sum).astype(bf16)
    local = lax.optimization_barrier((local, gate_up_low, down_low))[0]
    summed = [lax.psum_scatter(v, "dp", scatter_dimension=0, tiled=True) for v in local]
    share = MODEL_WIDTH // device_count
    if small_plane():
        output_sum, query_sum, key_sum, value_sum, down_grad = untile(
            summed[0], down_low[0], wide // device_count, wide, share, narrow
        )
    else:
        output_sum, pre_sum = [v.astype(f32) for v in summed]
        query_sum = pre_sum[:, :wide]
        key_sum = pre_sum[:, wide : wide + narrow]
        value_sum = pre_sum[:, wide + narrow :]
        down_grad = jnp.stack([v.astype(f32) for v in down_low])

    small = jnp.concatenate(
        [
            v.reshape(device_count, -1)
            for v in (
                attn_gain_local,
                ffn_gain_local,
                query_gain_local,
                key_gain_local,
                router_local,
            )
        ],
        axis=1,
    )
    small = lax.all_to_all(small[:, None], every, split_axis=0, concat_axis=0, tiled=True)
    small = jnp.sum(small[:, 0], axis=0)
    head_share = HEAD_SIZE // device_count
    cuts = [share, share, head_share, head_share, share * expert_count]
    ends = [sum(cuts[: i + 1]) for i in range(5)]
    a_grad, f_grad, q_grad, k_grad, r_grad = [
        small[end - cut : end] for end, cut in zip(ends, cuts)
    ]
    return (
        block_out,
        hidden_grad,
        a_grad,
        query_sum,
        key_sum,
        value_sum,
        q_grad,
        k_grad,
        output_sum,
        f_grad,
        r_grad.reshape(share, expert_count),
        gate_up_grad,
        down_grad,
    )


def solution(mesh):
    placed = (
        P(("dp", "ctx", "expert"), None),
        P(),
        P("expert", None),
        P("expert", None),
        P("expert", None),
        P(),
        P(),
        P("expert", None),
        P(),
        P(),
        P(("ctx", "expert"), None, None),
        P(("ctx", "expert"), None, None),
        P(("dp", "ctx", "expert"), None),
        P(("dp", "ctx", "expert"), None),
    )
    return jax.shard_map(
        body,
        mesh=mesh,
        in_specs=placed,
        out_specs=(
            P(("dp", "ctx", "expert"), None),
            P(("dp", "ctx", "expert"), None),
            P(("dp", "ctx", "expert")),
            P(("dp", "ctx", "expert"), None),
            P(("dp", "ctx", "expert"), None),
            P(("dp", "ctx", "expert"), None),
            P(("dp", "ctx", "expert")),
            P(("dp", "ctx", "expert")),
            P(("dp", "ctx", "expert"), None),
            P(("dp", "ctx", "expert")),
            P(("dp", "ctx", "expert"), None),
            P(("ctx", "expert"), "dp", None),
            P(("ctx", "expert"), "dp", None),
        ),
        check_vma=False,
    )
```

```python
import math

import jax
import jax.numpy as jnp
from jax import lax
from jax.experimental import pallas as pl
from jax.experimental.pallas import tpu as pltpu
from jax.sharding import PartitionSpec as P

MODEL_WIDTH = 2048
QUERY_HEADS = 32
KEY_VALUE_HEADS = 4
HEAD_SIZE = 128
TOP = 8
PROMPT_DEV = 128


highest = lax.Precision.HIGHEST
epsilon = 1e-06
rope_base = 1000000.0
masked = -1e30
every = ("dp", "ctx", "expert")
plane = ("ctx", "expert")
bf16 = jnp.bfloat16
f32 = jnp.float32


def rms_scale(value_rows):
    return lax.rsqrt(jnp.mean(value_rows * value_rows, axis=-1, keepdims=True) + epsilon)


def norm_back(inputs, inv_rms, norm_gain, gradient):
    weighted = gradient * norm_gain
    return inv_rms * weighted - inputs * inv_rms**3 * jnp.mean(
        weighted * inputs, axis=-1, keepdims=True
    )


def angles(position, head_width):
    freq_index = jnp.arange(head_width // 2, dtype=f32)
    inverse = jnp.exp(-(2.0 * freq_index / head_width) * math.log(rope_base))
    rope_angle = position.astype(f32)[:, None] * inverse[None, :]
    rope_angle = jnp.concatenate([rope_angle, rope_angle], axis=-1)
    return (jnp.cos(rope_angle), jnp.sin(rope_angle))


def rotate(value_rows, cosine, rope_sine):
    half_width = value_rows.shape[-1] // 2
    turned = jnp.concatenate([-value_rows[..., half_width:], value_rows[..., :half_width]], axis=-1)
    return value_rows * cosine + turned * rope_sine


def rotate_back(gradient, cosine, rope_sine):
    shifted = gradient * rope_sine
    half_width = gradient.shape[-1] // 2
    return gradient * cosine + jnp.concatenate(
        [shifted[..., half_width:], -shifted[..., :half_width]], axis=-1
    )


def small_plane():
    return [lax.axis_size(a) for a in every] == [4, 4, 2]


def swap(v, axis, bit):
    return lax.ppermute(v, axis, [(i, i ^ bit) for i in range(lax.axis_size(axis))])


def core(v):
    return swap(v, "ctx", 1)


def over_x(v):
    return swap(v, "ctx", 2)


def over_y(v):
    return swap(v, "expert", 1)


def over_z(v):
    return swap(v, "dp", 1)


def after(v, *earlier):
    return lax.optimization_barrier((v, *earlier))[0]


class Places:
    def __init__(self):
        self.dp = lax.axis_index("dp")
        ctx = lax.axis_index("ctx")
        self.ctx = ctx
        self.z = lax.rem(self.dp, 2)
        self.x = lax.div(ctx, 2)
        self.c = lax.rem(ctx, 2)
        self.y = lax.axis_index("expert")
        self.to_x = {"ctx": (1 - self.x) * 2 + self.c}
        self.to_c = {"ctx": self.x * 2 + 1 - self.c}
        self.to_y = {"expert": 1 - self.y}
        self.to_z = {"dp": self.dp + 1 - 2 * self.z}

    def peers(self):
        found = []
        for r in range(1, 8):
            x, c, y = [
                1 - v if r & bit else v for v, bit in ((self.x, 4), (self.c, 2), (self.y, 1))
            ]
            found.append((x * 4 + c * 2 + y, {"ctx": x * 2 + c, "expert": y}))
        return found


def plane_slot(x, c, y):
    return x * 4 + y * 2 + c


def greet(targets):
    barrier = pltpu.get_barrier_semaphore()
    for target in targets:
        pl.semaphore_signal(barrier, inc=1, device_id=target, device_id_type=pl.DeviceIdType.MESH)
    pl.semaphore_wait(barrier, len(targets))


class Sender:
    def __init__(self, send_sem, recv_sem):
        self.send_sem = send_sem
        self.recv_sem = recv_sem
        self.copies = []

    def __call__(self, source, target_ref, device):
        i = len(self.copies)
        copy = pltpu.make_async_remote_copy(
            src_ref=source,
            dst_ref=target_ref,
            send_sem=self.send_sem.at[i],
            recv_sem=self.recv_sem.at[i],
            device_id=device,
            device_id_type=pl.DeviceIdType.MESH,
        )
        copy.start()
        self.copies.append(copy)
        return copy

    def finish(self):
        for copy in self.copies:
            copy.wait_send()


def half_fetch(here, send, sources, other, columns, rows, upper):
    def at(piece, part=None):
        first, size = piece * rows, rows
        if part == 0:
            size = upper
        elif part == 1:
            first, size = first + upper, rows - upper
        return other.at[pl.ds(pl.multiple_of(first, 16), size), columns]

    def piece(z, x, c):
        return z * 4 + x * 2 + c

    z, x, c = here.z, here.x, here.c
    got = {}

    def first():
        mine = piece(z, x, c)
        got["y"] = [
            send(
                source.at[pl.ds(pl.multiple_of(mine * rows, rows), rows), source_columns],
                other.at[pl.ds(pl.multiple_of(mine * rows, rows), rows), target_columns],
                here.to_y,
            )
            for source, source_columns, target_columns in sources
        ]

    def second():
        for copy in got["y"]:
            copy.wait_recv()
        mine = at(piece(z, x, c))
        got["x"] = send(mine, mine, here.to_x)
        got["z"] = send(mine, mine, here.to_z)
        got["c"] = send(mine, mine, here.to_c)

    def third():
        got["x"].wait_recv()
        from_x = piece(z, 1 - x, c)
        got["low"] = send(at(from_x, 1), at(from_x, 1), here.to_z)
        got["xc"] = send(at(from_x), at(from_x), here.to_c)
        got["z"].wait_recv()
        from_z = piece(1 - z, x, c)
        got["top"] = send(at(from_z, 0), at(from_z, 0), here.to_x)
        got["zc"] = send(at(from_z), at(from_z), here.to_c)

    def fourth():
        far = piece(1 - z, 1 - x, c)
        got["low"].wait_recv()
        got["lowc"] = send(at(far, 1), at(far, 1), here.to_c)
        got["top"].wait_recv()
        got["topc"] = send(at(far, 0), at(far, 0), here.to_c)

    def fifth():
        for name in ("c", "xc", "zc", "lowc", "topc"):
            got[name].wait_recv()

    return [first, second, third, fourth, fifth]


def block_gather(here, send, mine, local_sem, blocks, far_over_y=False, columns=None):
    rows = blocks.shape[0] // lax.axis_size(plane)
    half = rows // 2
    x, c, y = here.x, here.c, here.y
    got = {}

    def at(slot, part=None):
        first, size = slot * rows, rows
        if part is not None:
            first, size = first + part * half, half
        rows_of = pl.ds(pl.multiple_of(first, size), size)
        return blocks.at[rows_of] if columns is None else blocks.at[rows_of, columns]

    def first():
        slot = plane_slot(x, c, y)
        got["own"] = pltpu.make_async_copy(mine, at(slot), local_sem)
        got["own"].start()
        got["y"] = send(mine, at(slot), here.to_y)
        got["x"] = send(mine, at(slot), here.to_x)
        got["c"] = send(mine, at(slot), here.to_c)

    def second():
        got["y"].wait_recv()
        from_y = plane_slot(x, c, 1 - y)
        got["yc"] = send(at(from_y), at(from_y), here.to_c)
        if not far_over_y:
            got["top"] = send(at(from_y, 0), at(from_y, 0), here.to_x)
        got["x"].wait_recv()
        from_x = plane_slot(1 - x, c, y)
        got["xc"] = send(at(from_x), at(from_x), here.to_c)
        if far_over_y:
            got["top"] = send(at(from_x, 0), at(from_x, 0), here.to_y)
        got["low"] = send(at(from_x, 1), at(from_x, 1), here.to_y)

    def third():
        far = plane_slot(1 - x, c, 1 - y)
        got["top"].wait_recv()
        got["topc"] = send(at(far, 0), at(far, 0), here.to_c)
        got["low"].wait_recv()
        got["lowc"] = send(at(far, 1), at(far, 1), here.to_c)

    def fourth():
        for name in ("c", "yc", "xc", "topc", "lowc"):
            got[name].wait_recv()
        got["own"].wait()

    return [first, second, third, fourth], got


def turn_half(v):
    return pltpu.roll(v, v.shape[-1] // 2, axis=1)


def head_norm(v):
    return lax.rsqrt(jnp.mean(v * v, axis=-1, keepdims=True) + epsilon)


def fetch_kernel(
    hidden_ref,
    attn_gain_ref,
    query_gain_ref,
    key_gain_ref,
    ffn_gain_ref,
    cosine_ref,
    sine_ref,
    key_ref,
    value_ref,
    query_ref,
    output_ref,
    grad_ref,
    routes_across,
    kv_out,
    q_out,
    o_out,
    g_blocks,
    route_blocks,
    kv_all_out,
    normed_out,
    attended_out,
    query_pre_out,
    queries_out,
    key_pre_ref,
    residual_ref,
    ffn_ref,
    normed_owned,
    attended_owned,
    query_pre_ref,
    queries_ref,
    normed_ref,
    attended_ref,
    kv_own,
    kv_other,
    q_own,
    q_other,
    o_own,
    o_other,
    kv_pre,
    kv_low,
    kv_all,
    routes_ref,
    send_sem,
    recv_sem,
    local_sem,
):
    here = Places()
    greet([here.to_y, here.to_z, here.to_c, here.to_x])
    send = Sender(send_sem, recv_sem)
    count, width = hidden_ref.shape
    half = width // 2
    narrow = key_ref.shape[1]
    wide = query_ref.shape[1]
    prompt_all = kv_all.shape[0] - (count - PROMPT_DEV)
    spread, groups = lax.axis_size(plane), lax.axis_size("dp")
    tile = 512
    loads = [
        pltpu.make_async_copy(key_ref, kv_own.at[:, pl.ds(0, narrow)], local_sem.at[0]),
        pltpu.make_async_copy(value_ref, kv_own.at[:, pl.ds(narrow, narrow)], local_sem.at[1]),
        pltpu.make_async_copy(query_ref, q_own, local_sem.at[2]),
        pltpu.make_async_copy(output_ref, o_own, local_sem.at[3]),
    ]
    stores = [
        pltpu.make_async_copy(kv_other, kv_out, local_sem.at[4]),
        pltpu.make_async_copy(q_other, q_out, local_sem.at[5]),
        pltpu.make_async_copy(o_other, o_out, local_sem.at[6]),
        pltpu.make_async_copy(kv_all, kv_all_out, local_sem.at[7]),
        pltpu.make_async_copy(normed_owned, normed_out, local_sem.at[11]),
        pltpu.make_async_copy(attended_owned, attended_out, local_sem.at[12]),
        pltpu.make_async_copy(query_pre_ref, query_pre_out, local_sem.at[13]),
        pltpu.make_async_copy(queries_ref, queries_out, local_sem.at[14]),
    ]

    def part_of(size, which):
        first = here.y * size if which == 0 else size - here.y * size
        return pl.ds(pl.multiple_of(first, size), size)

    def project(source, weight, out, which, first, count_of_tiles, add):
        rows = part_of(weight.shape[0], which)

        @pl.loop(first, first + count_of_tiles)
        def _(i):
            cols = pl.ds(pl.multiple_of(i * tile, tile), tile)
            part = dot(source[:, rows], weight[:, cols])
            out[:, cols] = out[:, cols] + part if add else part

    def start():
        for load in loads:
            load.start()
        routes_ref[...] = routes_across[...].T
        inputs = hidden_ref[...].astype(f32)
        normed_ref[...] = (inputs * head_norm(inputs) * attn_gain_ref[...]).astype(bf16)

    def own_part():
        share = width // (spread * groups)
        for s in range(spread):
            normed_owned[s] = jnp.concatenate(
                [
                    normed_ref[:, (d * spread + s) * share : (d * spread + s + 1) * share]
                    for d in range(groups)
                ],
                axis=1,
            )
        stores[4].start()
        for load in loads[:3]:
            load.wait()
        project(normed_ref, kv_own, kv_pre, 0, 0, 2 * narrow // tile, False)
        project(normed_ref, q_own, query_pre_ref, 0, 0, wide // tile, False)

    exchange = {}

    def keys_part():
        project(normed_ref, kv_other, kv_pre, 1, 0, 2 * narrow // tile, True)
        stores[0].start()
        key_pre_ref[...] = kv_pre[:, :narrow]
        for h in range(narrow // HEAD_SIZE):
            cols = slice(h * HEAD_SIZE, (h + 1) * HEAD_SIZE)
            v = kv_pre[:, cols]
            v = v * head_norm(v) * key_gain_ref[...]
            kv_low[:, cols] = (v * cosine_ref[...] + turn_half(v) * sine_ref[...]).astype(bf16)
        kv_low[:, narrow:] = kv_pre[:, narrow:].astype(bf16)
        kv_all[prompt_all:, :] = kv_low[PROMPT_DEV:, :]
        source = kv_low.at[pl.ds(0, PROMPT_DEV)]
        slot = kv_all.at[pl.ds(pl.multiple_of(here.ctx * PROMPT_DEV, PROMPT_DEV), PROMPT_DEV)]
        exchange["own"] = pltpu.make_async_copy(source, slot, local_sem.at[8])
        exchange["own"].start()
        exchange["c"] = send(source, slot, here.to_c)
        exchange["x"] = send(source, slot, here.to_x)

    def keys_forward():
        exchange["x"].wait_recv()
        first = ((1 - here.x) * 2 + here.c) * PROMPT_DEV
        slot = kv_all.at[pl.ds(pl.multiple_of(first, PROMPT_DEV), PROMPT_DEV)]
        exchange["xc"] = send(slot, slot, here.to_c)

    def queries_first():
        project(normed_ref, q_other, query_pre_ref, 1, 0, wide // tile // 2, True)

    def queries_rest():
        stores[1].start()
        project(
            normed_ref, q_other, query_pre_ref, 1, wide // tile // 2, wide // tile // 2, True
        )
        for name in ("c", "xc"):
            exchange[name].wait_recv()
        exchange["own"].wait()
        stores[3].start()
        stores[6].start()

    group = 4
    pieces = 4

    def attend(part):
        visible = visible_keys(count, kv_all.shape[0])
        blocks = wide // HEAD_SIZE // group // pieces

        @pl.loop(part * blocks, (part + 1) * blocks)
        def _(i):
            first = lax.div(i * group, wide // narrow) * HEAD_SIZE
            keys = kv_all[:, pl.ds(pl.multiple_of(first, HEAD_SIZE), HEAD_SIZE)]
            values = kv_all[:, pl.ds(pl.multiple_of(narrow + first, HEAD_SIZE), HEAD_SIZE)]
            for h in range(group):
                cols = pl.ds(pl.multiple_of((i * group + h) * HEAD_SIZE, HEAD_SIZE), HEAD_SIZE)
                v = query_pre_ref[:, cols]
                v = v * head_norm(v) * query_gain_ref[...]
                queries = (v * cosine_ref[...] + turn_half(v) * sine_ref[...]).astype(bf16)
                queries_ref[:, cols] = queries
                probs = head_softmax(queries, keys, visible).astype(bf16)
                attended = dot(probs, values).astype(bf16)
                attended_ref[:, cols] = attended
                head = i * group + h
                at = pl.multiple_of(lax.div(head, spread) * HEAD_SIZE, HEAD_SIZE)
                attended_owned[lax.rem(head, spread), :, pl.ds(at, HEAD_SIZE)] = attended

    def output_own():
        stores[5].start()
        stores[7].start()
        loads[3].wait()
        project(attended_ref, o_own, residual_ref, 0, 0, width // tile, False)

    def finish_rows():
        stores[2].start()
        project(attended_ref, o_other, residual_ref, 1, 0, width // tile, True)
        residual = residual_ref[...] + hidden_ref[...].astype(f32)
        residual_ref[...] = residual
        ffn_ref[...] = (residual * head_norm(residual) * ffn_gain_ref[...]).astype(bf16)

    low, high = pl.ds(0, wide // 2), pl.ds(wide // 2, wide // 2)
    o_low, o_high = pl.ds(0, width // 2), pl.ds(width // 2, width // 2)
    rows, o_rows = half // 8, output_ref.shape[0] // 8
    kv, qa, qb, oa, ob, g, r = [
        half_fetch(
            here,
            send,
            [
                (key_ref, pl.ds(0, narrow), pl.ds(0, narrow)),
                (value_ref, pl.ds(0, narrow), pl.ds(narrow, narrow)),
            ],
            kv_other,
            pl.ds(0, 2 * narrow),
            rows,
            rows // 2,
        ),
        half_fetch(here, send, [(query_ref, low, low)], q_other, low, rows, rows // 2),
        half_fetch(here, send, [(query_ref, high, high)], q_other, high, rows, rows // 2),
        half_fetch(here, send, [(output_ref, o_low, o_low)], o_other, o_low, o_rows, o_rows // 4),
        half_fetch(
            here, send, [(output_ref, o_high, o_high)], o_other, o_high, o_rows, o_rows // 4
        ),
        block_gather(here, send, grad_ref, local_sem.at[9], g_blocks, True)[0],
        block_gather(here, send, routes_ref, local_sem.at[10], route_blocks)[0],
    ]
    steps = [
        kv[0], qa[0], qb[0], oa[0], ob[0], g[0], start, kv[1], kv[2], own_part, qa[1],
        kv[3], qa[2], qb[1], kv[4], keys_part, qa[3], qb[2], oa[1],
        keys_forward, qa[4], queries_first, qb[3], ob[1], qb[4], queries_rest,
        oa[2], r[0], lambda: attend(0), lambda: attend(1),
        oa[3], ob[2], g[1], r[1], lambda: attend(2), lambda: attend(3), oa[4], output_own,
        ob[3], g[2], r[2], ob[4], finish_rows, g[3], r[3],
    ]
    for step in steps:
        step()
    for store in stores:
        store.wait()
    send.finish()


def fetch_and_attend(
    hidden_in, attn_gain, query_gain, key_gain, ffn_gain, cosine, sine, key_matrix, value_matrix,
    query_weight, output_weight, out_grad, routes,
):
    rows, width = hidden_in.shape
    half, wide = query_weight.shape
    narrow = key_matrix.shape[1]
    spread = lax.axis_size(plane)
    keys = lax.axis_size("ctx") * PROMPT_DEV + rows - PROMPT_DEV
    vmem = pl.BlockSpec(memory_space=pltpu.VMEM)
    anywhere = pl.BlockSpec(memory_space=pl.ANY)
    copies = 5 * 10 + 1 + 2 * 9 + 3
    return pl.pallas_call(
        fetch_kernel,
        out_shape=[
            jax.ShapeDtypeStruct((half, 2 * narrow), bf16),
            jax.ShapeDtypeStruct((half, wide), bf16),
            jax.ShapeDtypeStruct(output_weight.shape, bf16),
            jax.ShapeDtypeStruct((spread * rows, width), bf16),
            jax.ShapeDtypeStruct((spread * rows, routes.shape[1]), jnp.int32),
            jax.ShapeDtypeStruct((keys, 2 * narrow), bf16),
            jax.ShapeDtypeStruct((spread, rows, width // spread), bf16),
            jax.ShapeDtypeStruct((spread, rows, wide // spread), bf16),
            jax.ShapeDtypeStruct((rows, wide), f32),
            jax.ShapeDtypeStruct((rows, wide), bf16),
            jax.ShapeDtypeStruct((rows, narrow), f32),
            jax.ShapeDtypeStruct((rows, width), f32),
            jax.ShapeDtypeStruct((rows, width), bf16),
        ],
        in_specs=[vmem] * 7 + [anywhere] * 5 + [vmem],
        out_specs=[anywhere] * 10 + [vmem] * 3,
        scratch_shapes=[
            pltpu.VMEM((spread, rows, width // spread), bf16),
            pltpu.VMEM((spread, rows, wide // spread), bf16),
            pltpu.VMEM((rows, wide), f32),
            pltpu.VMEM((rows, wide), bf16),
            pltpu.VMEM((rows, width), bf16),
            pltpu.VMEM((rows, wide), bf16),
            pltpu.VMEM((half, 2 * narrow), bf16),
            pltpu.VMEM((half, 2 * narrow), bf16),
            pltpu.VMEM((half, wide), bf16),
            pltpu.VMEM((half, wide), bf16),
            pltpu.VMEM(output_weight.shape, bf16),
            pltpu.VMEM(output_weight.shape, bf16),
            pltpu.VMEM((rows, 2 * narrow), f32),
            pltpu.VMEM((rows, 2 * narrow), bf16),
            pltpu.VMEM((keys, 2 * narrow), bf16),
            pltpu.VMEM(routes.shape, jnp.int32),
            pltpu.SemaphoreType.DMA((copies,)),
            pltpu.SemaphoreType.DMA((copies,)),
            pltpu.SemaphoreType.DMA((15,)),
        ],
        compiler_params=pltpu.CompilerParams(
            collective_id=1, has_side_effects=True, vmem_limit_bytes=60 * 2**20
        ),
        cost_estimate=pl.CostEstimate(
            flops=2 * rows * width * (2 * wide + 2 * narrow) * 2,
            bytes_accessed=60 * 2**20,
            transcendentals=0,
        ),
    )(
        hidden_in, attn_gain.reshape(1, width), query_gain.reshape(1, HEAD_SIZE),
        key_gain.reshape(1, HEAD_SIZE), ffn_gain.reshape(1, width), cosine, sine,
        key_matrix, value_matrix, query_weight, output_weight, out_grad, routes.T,
    )


def chip_rows(x, y, rows):
    first = plane_slot(x, 0, y) * rows
    return pl.ds(pl.multiple_of(first, rows), 2 * rows)


def across_down(rows, down_rows):
    return lax.dot_general(rows, down_rows, (((1,), (1,)), ((), ())), preferred_element_type=f32)


def expert_chunk(
    some, rows_v, g_v, gate_up_v, down_v, hidden_v, grad_v, total_v, gate, mark, q_v=None
):
    ff = down_v.shape[0]
    tile = 256

    @pl.loop(0, ff // tile, unroll=True)
    def _(f):
        at = pl.multiple_of(f * tile, tile)
        a = dot(rows_v[some, :], gate_up_v[:, pl.ds(at, tile)])
        b = dot(rows_v[some, :], gate_up_v[:, pl.ds(ff + at, tile)])
        if q_v is None:
            q = across_down(g_v[some, :], down_v[pl.ds(at, tile), :])
        else:
            q = q_v[some, pl.ds(at, tile)]
        s = 1.0 / (1.0 + jnp.exp(-a))
        raised_a = a * s
        hidden = raised_a * b
        total_v[...] = total_v[...] + jnp.where(
            mark, jnp.sum(hidden * q, axis=-1, keepdims=True), 0.0
        )
        back = gate * q
        hidden_v[some, pl.ds(at, tile)] = (gate * hidden).astype(bf16)
        grad_v[some, pl.ds(at, tile)] = (back * b * s * (1.0 + a * (1.0 - s))).astype(bf16)
        grad_v[some, pl.ds(ff + at, tile)] = (back * raised_a).astype(bf16)


def first_expert_kernel(
    ffn_ref,
    routes_ref,
    router_ref,
    g_hbm,
    gate_up_hbm,
    down_hbm,
    rows_out,
    hidden_out,
    grad_out,
    gates_ref,
    gate_grad_ref,
    down_grad_ref,
    rows_v,
    g_v,
    gate_up_v,
    down_v,
    hidden_v,
    grad_v,
    total_v,
    down_total,
    q_v,
    send_sem,
    recv_sem,
    local_sem,
):
    here = Places()
    greet([here.to_y, here.to_c, here.to_x])
    send = Sender(send_sem, recv_sem)
    count = ffn_ref.shape[0]
    experts = router_ref.shape[0]
    local_experts = down_hbm.shape[0]
    stages, got = block_gather(here, send, ffn_ref, local_sem.at[0], rows_v)
    stages[0]()
    loads = [
        pltpu.make_async_copy(down_hbm.at[0], down_v, local_sem.at[2]),
        pltpu.make_async_copy(g_hbm, g_v, local_sem.at[3]),
        pltpu.make_async_copy(gate_up_hbm.at[0], gate_up_v, local_sem.at[1]),
    ]
    for load in loads:
        load.start()
    first_expert = plane_index(here) * local_experts
    stores = []

    def chunk(x, y):
        some = chip_rows(x, y, count)
        logits = lax.dot_general(
            rows_v[some, :],
            router_ref[...],
            (((1,), (1,)), ((), ())),
            preferred_element_type=f32,
        )
        ids = lax.broadcasted_iota(jnp.int32, logits.shape, 1)
        routes = routes_ref[some, :]
        chosen = ids < 0
        for k in range(routes.shape[1]):
            chosen = chosen | (routes[:, k : k + 1] == ids)
        logits = jnp.where(chosen, logits, masked)
        raised = jnp.exp(logits - jnp.max(logits, axis=-1, keepdims=True))
        raised = jnp.where(chosen, raised, 0.0)
        gates = raised / jnp.sum(raised, axis=-1, keepdims=True)
        lane = lax.broadcasted_iota(jnp.int32, total_v.shape, 1)
        total_v[...] = jnp.zeros(total_v.shape, f32)
        columns = [
            jnp.sum(jnp.where(ids == first_expert + e, gates, 0.0), axis=-1, keepdims=True)
            for e in range(local_experts)
        ]
        spread = jnp.zeros(total_v.shape, f32)
        for e in range(local_experts):
            spread = jnp.where(lane == e, columns[e], spread)
        gates_ref[some, :] = spread
        mark = (lane == first_expert) | (lane == first_expert + experts)
        expert_chunk(
            some, rows_v, g_v, gate_up_v, down_v, hidden_v, grad_v, total_v, columns[0], mark, q_v
        )
        gate_grad_ref[some, :] = total_v[...]
        for source, target in ((hidden_v, hidden_out), (grad_v, grad_out), (rows_v, rows_out)):
            columns = pl.ds(0, source.shape[1])
            store = pltpu.make_async_copy(
                source.at[some, :], target.at[some, columns], local_sem.at[4 + len(stores)]
            )
            store.start()
            stores.append(store)
        add_down(some, len(stores) == 3, len(stores) == 12)

    def add_down(some, is_first, is_last):
        tile = 512

        @pl.loop(0, down_total.shape[1] // tile)
        def _(i):
            cols = pl.ds(pl.multiple_of(i * tile, tile), tile)
            part = transposed_dot(hidden_v[some, :], g_v[some, cols])
            if not is_first:
                part = part + down_total[:, cols]
            if is_last:
                down_grad_ref[:, cols] = part.astype(bf16)
            else:
                down_total[:, cols] = part

    x, y = here.x, here.y
    for load in loads[:2]:
        load.wait()

    @pl.loop(0, rows_v.shape[0] // (2 * count))
    def _(i):
        some = pl.ds(pl.multiple_of(i * 2 * count, 2 * count), 2 * count)
        for at in range(0, down_v.shape[0], 256):
            q_v[some, at : at + 256] = across_down(g_v[some, :], down_v[at : at + 256, :])

    for name in ("c", "own"):
        arrive(got, name)
    loads[2].wait()
    chunk(x, y)
    stages[1]()
    arrive(got, "yc")
    chunk(x, 1 - y)
    stages[2]()
    arrive(got, "xc")
    chunk(1 - x, y)
    arrive(got, "topc")
    arrive(got, "lowc")
    chunk(1 - x, 1 - y)
    for store in stores:
        store.wait()
    send.finish()


def gather_first_expert(ffn_in, route_rows, router_weight, g_rows, gate_up, down_proj):
    experts, ff, width = down_proj.shape
    total = route_rows.shape[0]
    vmem = pl.BlockSpec(memory_space=pltpu.VMEM)
    anywhere = pl.BlockSpec(memory_space=pl.ANY)
    return pl.pallas_call(
        first_expert_kernel,
        out_shape=[
            jax.ShapeDtypeStruct((total, width), bf16),
            jax.ShapeDtypeStruct((total, ff), bf16),
            jax.ShapeDtypeStruct((total, 2 * experts * ff), bf16),
            jax.ShapeDtypeStruct((total, 128), f32),
            jax.ShapeDtypeStruct((total, 128), f32),
            jax.ShapeDtypeStruct((ff, width), bf16),
        ],
        in_specs=[anywhere] + [vmem] * 2 + [anywhere] * 3,
        out_specs=[anywhere] * 3 + [vmem] * 3,
        scratch_shapes=[
            pltpu.VMEM((total, width), bf16),
            pltpu.VMEM((total, width), bf16),
            pltpu.VMEM(gate_up.shape[1:], bf16),
            pltpu.VMEM(down_proj.shape[1:], bf16),
            pltpu.VMEM((total, ff), bf16),
            pltpu.VMEM((total, 2 * ff), bf16),
            pltpu.VMEM((2 * ffn_in.shape[0], 128), f32),
            pltpu.VMEM((ff, width), f32),
            pltpu.VMEM((total, ff), f32),
            pltpu.SemaphoreType.DMA((9,)),
            pltpu.SemaphoreType.DMA((9,)),
            pltpu.SemaphoreType.DMA((16,)),
        ],
        compiler_params=pltpu.CompilerParams(
            collective_id=2, has_side_effects=True, vmem_limit_bytes=56 * 2**20
        ),
        cost_estimate=pl.CostEstimate(
            flops=2 * total * width * 3 * ff,
            bytes_accessed=40 * 2**20,
            transcendentals=0,
        ),
    )(ffn_in, route_rows, router_weight.T, g_rows, gate_up, down_proj)


def next_expert_kernel(
    which, experts, rows_v, g_v, gates_ref, totals_ref, gate_up_v, down_v, _, hidden_v, grad_v,
    gate_grad_ref, total_v,
):
    lane = lax.broadcasted_iota(jnp.int32, total_v.shape, 1)
    expert = lax.axis_index(plane) * lax.div(experts, lax.axis_size(plane)) + which
    mark = (lane == expert) | (lane == expert + experts)
    total_v[...] = totals_ref[...]
    gate = jnp.sum(jnp.where(lane == which, gates_ref[...], 0.0), axis=-1, keepdims=True)
    some = pl.ds(0, rows_v.shape[0])
    expert_chunk(
        some, rows_v, g_v, gate_up_v.at[0], down_v.at[0], hidden_v, grad_v, total_v, gate, mark
    )
    total = total_v[...]
    high = total.astype(bf16).astype(f32)
    gate_grad_ref[...] = jnp.where(lane < experts, high, total - high).astype(bf16)


def last_expert(which, experts, rows, g_rows, gates, totals, gate_up, down_proj, grads):
    ff, width = down_proj.shape[1:]
    total = rows.shape[0]
    step = total // 4

    def block(columns):
        return pl.BlockSpec((step, columns), lambda i: (i, 0))

    def whole(shape):
        return pl.BlockSpec((1,) + shape[1:], lambda i: (which, 0, 0))

    def kernel(*refs):
        next_expert_kernel(which, experts, *refs)

    return pl.pallas_call(
        kernel,
        grid=(4,),
        out_shape=[
            jax.ShapeDtypeStruct((total, ff), bf16),
            jax.ShapeDtypeStruct(grads.shape, bf16),
            jax.ShapeDtypeStruct((total, 128), bf16),
        ],
        in_specs=[
            block(width), block(width), block(128), block(128),
            whole(gate_up.shape), whole(down_proj.shape), pl.BlockSpec(memory_space=pl.ANY),
        ],
        out_specs=[
            block(ff), pl.BlockSpec((step, 2 * ff), lambda i: (i, which)), block(128)
        ],
        input_output_aliases={6: 1},
        scratch_shapes=[pltpu.VMEM((step, 128), f32)],
        compiler_params=pltpu.CompilerParams(vmem_limit_bytes=56 * 2**20),
        cost_estimate=pl.CostEstimate(flops=10**6, bytes_accessed=10**6, transcendentals=0),
    )(rows, g_rows, gates, totals, gate_up, down_proj, grads)


def weight_grad_kernel(
    query_grad, kv_grad, branch, attended_owned, normed_owned, down_part, sums_ref,
    pre_v, branch_v, attended_v, normed_v, send_sem, recv_sem, local_sem,
):
    here = Places()
    greet([here.to_y, here.to_c, here.to_x])
    send = Sender(send_sem, recv_sem)
    count, wide = query_grad.shape
    narrow = kv_grad.shape[1]
    spread = lax.axis_size(plane)
    tile = sums_ref.shape[1]
    groups = lax.axis_size("dp")
    half = wide // 2
    low, high, last = pl.ds(0, half), pl.ds(half, half), pl.ds(wide, narrow)
    qa, _ = block_gather(
        here, send, query_grad.at[:, low], local_sem.at[1], pre_v, False, low
    )
    qb, _ = block_gather(
        here, send, query_grad.at[:, high], local_sem.at[2], pre_v, False, high
    )
    kv, _ = block_gather(here, send, kv_grad, local_sem.at[3], pre_v, False, last)
    loads = [pltpu.make_async_copy(branch, branch_v, local_sem.at[0])]
    for device in range(spread):
        slot = plane_slot(device // 4, device // 2 % 2, device % 2)
        rows = pl.ds(slot * count, count)
        for source, target in ((attended_owned, attended_v), (normed_owned, normed_v)):
            loads.append(
                pltpu.make_async_copy(
                    source.at[device], target.at[rows], local_sem.at[3 + len(loads)]
                )
            )

    output_rows = attended_v.shape[1] // groups * (branch.shape[1] // tile)
    pre_rows = normed_v.shape[1] // groups * ((wide + narrow) // tile)
    down_rows = down_part.shape[0] // groups
    kept = [
        pltpu.make_async_copy(
            down_part.at[pl.ds(d * down_rows, down_rows), pl.ds(i * tile, tile)],
            sums_ref.at[
                pl.ds(
                    d * (sums_ref.shape[0] // groups) + output_rows + pre_rows + i * down_rows,
                    down_rows,
                )
            ],
            local_sem.at[4 + 2 * spread + d * (down_part.shape[1] // tile) + i],
        )
        for d in range(groups)
        for i in range(down_part.shape[1] // tile)
    ]

    def start():
        for copy in loads + kept:
            copy.start()

    def product(left, right, base, first, tiles):
        rows = left.shape[1] // groups

        @pl.loop(first, first + tiles)
        def _(i):
            cols = pl.ds(pl.multiple_of(i * tile, tile), tile)
            part = transposed_dot(left[...], right[:, cols]).astype(bf16)
            for d in range(groups):
                at = d * (sums_ref.shape[0] // groups) + base + i * rows
                sums_ref[pl.ds(pl.multiple_of(at, 64), rows), :] = part[
                    d * rows : (d + 1) * rows
                ]

    def output_product():
        for load in loads:
            load.wait()
        product(attended_v, branch_v, 0, 0, branch.shape[1] // tile)

    steps = [
        qa[0], qb[0], kv[0], start, output_product, qa[1], qb[1], qa[2], kv[1], qb[2], qa[3],
        lambda: product(normed_v, pre_v, output_rows, 0, half // tile),
        kv[2], qb[3],
        lambda: product(normed_v, pre_v, output_rows, half // tile, half // tile),
        kv[3],
        lambda: product(normed_v, pre_v, output_rows, wide // tile, narrow // tile),
    ]
    for step in steps:
        step()
    for copy in kept:
        copy.wait()
    send.finish()


def weight_grads(query_grad, kv_grad, branch, attended_owned, normed_owned, down_part):
    count, wide = query_grad.shape
    narrow, width = kv_grad.shape[1], branch.shape[1]
    spread = lax.axis_size(plane)
    tile = narrow
    elements = attended_owned.shape[2] * width + normed_owned.shape[2] * (wide + narrow)
    elements += math.prod(down_part.shape)
    groups = lax.axis_size("dp")
    vmem = pl.BlockSpec(memory_space=pltpu.VMEM)
    anywhere = pl.BlockSpec(memory_space=pl.ANY)
    return pl.pallas_call(
        weight_grad_kernel,
        out_shape=jax.ShapeDtypeStruct((elements // tile, tile), bf16),
        in_specs=[anywhere] * 6,
        out_specs=vmem,
        scratch_shapes=[
            pltpu.VMEM((spread * count, wide + narrow), bf16),
            pltpu.VMEM((spread * count, width), bf16),
            pltpu.VMEM((spread * count, attended_owned.shape[2]), bf16),
            pltpu.VMEM((spread * count, normed_owned.shape[2]), bf16),
            pltpu.SemaphoreType.DMA((27,)),
            pltpu.SemaphoreType.DMA((27,)),
            pltpu.SemaphoreType.DMA((4 + 2 * spread + groups * (down_part.shape[1] // tile),)),
        ],
        compiler_params=pltpu.CompilerParams(
            collective_id=5, has_side_effects=True, vmem_limit_bytes=56 * 2**20
        ),
        cost_estimate=pl.CostEstimate(flops=10**6, bytes_accessed=10**6, transcendentals=0),
    )(query_grad, kv_grad, branch, attended_owned, normed_owned, down_part)


def untile_kernel(sums_ref, down_ref, output_ref, query_ref, key_ref, value_ref, downs_ref):
    tile = sums_ref.shape[1]
    at = 0

    def take(rows):
        nonlocal at
        part = sums_ref[at : at + rows, :].astype(f32)
        at = at + rows
        return part

    for out in (output_ref, query_ref):
        for first in range(0, out.shape[1], tile):
            out[:, first : first + tile] = take(out.shape[0])
    both = take(key_ref.shape[0])
    key_ref[...] = both[:, : key_ref.shape[1]]
    value_ref[...] = both[:, key_ref.shape[1] :]
    downs_ref[0] = down_ref[...].astype(f32)
    for first in range(0, downs_ref.shape[2], tile):
        downs_ref[1, :, first : first + tile] = take(downs_ref.shape[1])


def untile(sums, down, output_rows, wide, share, narrow):
    vmem = pl.BlockSpec(memory_space=pltpu.VMEM)
    rows, width = down.shape
    shapes = [
        (output_rows, width), (share, wide), (share, narrow), (share, narrow), (2, rows, width)
    ]
    return pl.pallas_call(
        untile_kernel,
        out_shape=[jax.ShapeDtypeStruct(shape, f32) for shape in shapes],
        in_specs=[vmem] * 2,
        out_specs=[vmem] * 5,
        compiler_params=pltpu.CompilerParams(vmem_limit_bytes=32 * 2**20),
    )(sums, down)


def arrive(got, name):
    copy = got[name]
    copy.wait() if name == "own" else copy.wait_recv()


def plane_index(here):
    return here.ctx * 2 + here.y


def plane_sum_kernel(across, parts, *refs):
    lefts, weight_hbm = refs[:parts], refs[parts]
    refs = refs[parts + 1 :]
    extra_ref, sources, targets = None, [], []
    if across:
        extra_ref, sources, targets = refs[0], refs[1:3], refs[4:6]
        refs = (refs[3],) + refs[6:]
    (
        out_ref, left_v, weight_v, part_v, core_v, edge_v, last_v, send_sem, recv_sem, local_sem,
    ) = refs
    here = Places()
    peers = here.peers() if across else []
    greet([device for _, device in peers] or [here.to_y, here.to_c, here.to_x])
    send = Sender(send_sem, recv_sem)
    count = out_ref.shape[0]
    half = count // 2
    experts = weight_hbm.shape[0]
    part_depth = lefts[0].shape[1]
    depth = part_depth * parts // experts
    width = weight_hbm.shape[1] if across else weight_hbm.shape[2]
    tile = 256
    x, y, c = here.x, here.y, here.c
    chips = [(1 - x, 1 - y), (1 - x, y), (x, 1 - y), (x, y)]
    weight_load = pltpu.make_async_copy(weight_hbm, weight_v, local_sem.at[0])
    weight_load.start()
    loads = []
    for k, (cx, cy) in enumerate(chips):
        some = chip_rows(cx, cy, count)
        loads.append(
            [
                pltpu.make_async_copy(
                    left.at[some, :],
                    left_v.at[k, :, pl.ds(e * part_depth, part_depth)],
                    local_sem.at[1 + parts * k + e],
                )
                for e, left in enumerate(lefts)
            ]
        )
        for load in loads[-1]:
            load.start()
    owned = []
    for index, device in peers:
        for source, target in zip(sources, targets):
            owned.append(send(source.at[index], target.at[plane_index(here)], device))
    kept = [
        pltpu.make_async_copy(
            source.at[plane_index(here)],
            target.at[plane_index(here)],
            local_sem.at[1 + 4 * parts + i],
        )
        for i, (source, target) in enumerate(zip(sources, targets))
    ]
    for copy in kept:
        copy.start()
    weight_load.wait()
    to_core = []

    def compute(k):
        for load in loads[k]:
            load.wait()

        @pl.loop(0, width // tile)
        def _(n):
            cols = pl.ds(pl.multiple_of(n * tile, tile), tile)
            total = None
            for e in range(experts):
                left = left_v[k, :, e * depth : (e + 1) * depth]
                if across:
                    part = lax.dot_general(
                        left,
                        weight_v[e, cols, :],
                        (((1,), (1,)), ((), ())),
                        preferred_element_type=f32,
                    )
                else:
                    part = dot(left, weight_v[e, :, cols])
                total = part if total is None else total + part
            part_v[k, :, cols] = total.astype(bf16)

        if extra_ref is not None:
            part_v[k, :, width:] = extra_ref[chip_rows(*chips[k], count), :]
        to_core.append(
            send(
                part_v.at[k, pl.ds(pl.multiple_of((1 - c) * count, count), count)],
                core_v.at[k],
                here.to_c,
            )
        )

    mine = pl.ds(pl.multiple_of(c * count, count), count)

    def chip_sum(k):
        to_core[k].wait_recv()
        return part_v[k, mine, :].astype(f32) + core_v[k].astype(f32)

    compute(0)
    compute(1)
    core_v[0] = chip_sum(0).astype(bf16)
    from_x = send(core_v.at[0, pl.ds(0, half)], edge_v.at[0], here.to_x)
    from_y = send(core_v.at[0, pl.ds(half, half)], edge_v.at[1], here.to_y)
    compute(2)
    over_x_sum = chip_sum(1)
    core_v[1, :half] = over_x_sum[:half].astype(bf16)
    from_y.wait_recv()
    core_v[1, half:] = (over_x_sum[half:] + edge_v[1].astype(f32)).astype(bf16)
    last_x = send(core_v.at[1], last_v.at[0], here.to_x)
    over_y_sum = chip_sum(2)
    core_v[2, half:] = over_y_sum[half:].astype(bf16)
    from_x.wait_recv()
    core_v[2, :half] = (over_y_sum[:half] + edge_v[0].astype(f32)).astype(bf16)
    last_y = send(core_v.at[2], last_v.at[1], here.to_y)
    compute(3)
    out_ref[...] = chip_sum(3)
    last_x.wait_recv()
    last_y.wait_recv()
    out_ref[...] = out_ref[...] + last_v[0].astype(f32) + last_v[1].astype(f32)
    for copy in owned:
        copy.wait_recv()
    for copy in kept:
        copy.wait()
    send.finish()


def plane_sum(lefts, weight, extra, owned, collective_id):
    across = extra is not None
    count = lefts[0].shape[0] // lax.axis_size(plane)
    width = weight.shape[1] if across else weight.shape[2]
    wide = width + (extra.shape[1] if across else 0)
    parts, depth = len(lefts), lefts[0].shape[1]
    vmem = pl.BlockSpec(memory_space=pltpu.VMEM)
    anywhere = pl.BlockSpec(memory_space=pl.ANY)

    def kernel(*refs):
        plane_sum_kernel(across, parts, *refs)

    return pl.pallas_call(
        kernel,
        out_shape=[jax.ShapeDtypeStruct((count, wide), f32)]
        + [jax.ShapeDtypeStruct(v.shape, v.dtype) for v in owned],
        in_specs=[anywhere] * (parts + 1) + [vmem] * across + [anywhere] * len(owned),
        out_specs=[vmem] + [anywhere] * len(owned),
        scratch_shapes=[
            pltpu.VMEM((4, 2 * count, parts * depth), bf16),
            pltpu.VMEM(weight.shape, bf16),
            pltpu.VMEM((4, 2 * count, wide), bf16),
            pltpu.VMEM((4, count, wide), bf16),
            pltpu.VMEM((2, count // 2, wide), bf16),
            pltpu.VMEM((2, count, wide), bf16),
            pltpu.SemaphoreType.DMA((8 + 7 * len(owned),)),
            pltpu.SemaphoreType.DMA((8 + 7 * len(owned),)),
            pltpu.SemaphoreType.DMA((1 + 4 * parts + len(owned),)),
        ],
        compiler_params=pltpu.CompilerParams(
            collective_id=collective_id, has_side_effects=True, vmem_limit_bytes=60 * 2**20
        ),
        cost_estimate=pl.CostEstimate(flops=10**6, bytes_accessed=10**6, transcendentals=0),
    )(*lefts, weight, *([extra] if across else []), *owned)


def head_softmax(queries, keys, visible):
    scores = lax.dot_general(
        queries, keys, (((1,), (1,)), ((), ())), preferred_element_type=f32
    ) * (HEAD_SIZE ** (-0.5))
    scores = jnp.where(visible, scores, masked)
    raised = jnp.exp(scores - jnp.max(scores, axis=-1, keepdims=True))
    return raised / jnp.sum(raised, axis=-1, keepdims=True)


def visible_keys(rows, keys):
    row = lax.broadcasted_iota(jnp.int32, (rows, keys), 0)
    key = lax.broadcasted_iota(jnp.int32, (rows, keys), 1)
    prompt_all = keys - (rows - PROMPT_DEV)
    own = lax.axis_index("ctx") * PROMPT_DEV + row
    position = jnp.where(row < PROMPT_DEV, own, prompt_all + row - PROMPT_DEV)
    return key <= position


def attention_kernel(
    query_pre_ref, gain_ref, cosine_ref, sine_ref, keys_ref, values_ref, queries_ref, attended_ref
):
    rows = query_pre_ref.shape[0]
    visible = visible_keys(rows, keys_ref.shape[0])
    keys = keys_ref[...]
    values = values_ref[...]
    for h in range(query_pre_ref.shape[1] // HEAD_SIZE):
        cols = slice(h * HEAD_SIZE, (h + 1) * HEAD_SIZE)
        v = query_pre_ref[:, cols]
        v = v * head_norm(v) * gain_ref[...]
        queries = (v * cosine_ref[...] + turn_half(v) * sine_ref[...]).astype(bf16)
        queries_ref[:, cols] = queries
        probs = head_softmax(queries, keys, visible).astype(bf16)
        attended_ref[:, cols] = dot(probs, values).astype(bf16)


def attention(query_pre, gain, cosine, sine, kv_all):
    rows, wide = query_pre.shape
    keys = kv_all.shape[0]
    group = wide // KEY_VALUE_HEADS
    small = pl.BlockSpec((rows, HEAD_SIZE), lambda i: (0, 0))
    block = pl.BlockSpec((rows, group), lambda i: (0, i))
    return pl.pallas_call(
        attention_kernel,
        grid=(KEY_VALUE_HEADS,),
        out_shape=[jax.ShapeDtypeStruct((rows, wide), bf16)] * 2,
        in_specs=[
            block,
            pl.BlockSpec((1, HEAD_SIZE), lambda i: (0, 0)),
            small,
            small,
            pl.BlockSpec((keys, HEAD_SIZE), lambda i: (0, i)),
            pl.BlockSpec((keys, HEAD_SIZE), lambda i: (0, KEY_VALUE_HEADS + i)),
        ],
        out_specs=[block, block],
        compiler_params=pltpu.CompilerParams(vmem_limit_bytes=48 * 2**20),
    )(query_pre, gain.reshape(1, HEAD_SIZE), cosine, sine, kv_all, kv_all)


def transposed_dot(a, b):
    return lax.dot_general(a, b, (((0,), (0,)), ((), ())), preferred_element_type=f32)


def back_heads(
    first,
    key_at,
    value_at,
    out_at,
    query_pre_ref,
    gain_ref,
    cosine_ref,
    sine_ref,
    keys_ref,
    values_ref,
    queries_ref,
    grad_ref,
    pre_grad_ref,
    key_grad_ref,
    value_grad_ref,
):
    rows = query_pre_ref.shape[0]
    visible = visible_keys(rows, keys_ref.shape[0])
    keys = keys_ref[:, pl.ds(key_at, HEAD_SIZE)]
    values = values_ref[:, pl.ds(value_at, HEAD_SIZE)]
    scale = HEAD_SIZE ** (-0.5)
    gain_grad = jnp.zeros((rows, HEAD_SIZE), f32)
    key_grad = jnp.zeros(keys.shape, f32)
    value_grad = jnp.zeros(keys.shape, f32)
    for h in range(QUERY_HEADS // KEY_VALUE_HEADS):
        cols = pl.ds(first + h * HEAD_SIZE, HEAD_SIZE)
        queries = queries_ref[:, cols]
        grad = grad_ref[:, cols]
        probs = head_softmax(queries, keys, visible)
        prob_grad = lax.dot_general(
            grad, values, (((1,), (1,)), ((), ())), preferred_element_type=f32
        )
        delta = jnp.sum(probs * prob_grad, axis=-1, keepdims=True)
        score_grad = (probs * (prob_grad - delta)).astype(bf16)
        key_grad = key_grad + transposed_dot(score_grad, queries)
        value_grad = value_grad + transposed_dot(probs.astype(bf16), grad)
        u = dot(score_grad, keys) * scale
        u = u * cosine_ref[...] + turn_half(u * sine_ref[...])
        v = query_pre_ref[:, cols]
        inv = head_norm(v)
        gain_grad = gain_grad + u * v * inv
        pre_grad_ref[:, cols] = norm_back(v, inv, gain_ref[...], u).astype(bf16)
    out = pl.ds(out_at, HEAD_SIZE)
    key_grad_ref[:, out] = (key_grad * scale).astype(key_grad_ref.dtype)
    value_grad_ref[:, out] = value_grad.astype(value_grad_ref.dtype)
    return jnp.sum(gain_grad, axis=0, keepdims=True)


def attention_back_kernel(*refs):
    refs[-1][0] = back_heads(0, 0, 0, 0, *refs[:-1])


def attention_back_gather_kernel(
    query_pre_ref, gain_ref, cosine_ref, sine_ref, kv_ref, queries_ref, grad_ref, branch,
    pre_grad_ref, key_grad_ref, value_grad_ref, gain_grad_ref, branch_rows,
    send_sem, recv_sem, local_sem,
):
    here = Places()
    greet([here.to_y, here.to_c, here.to_x])
    send = Sender(send_sem, recv_sem)
    stages, _ = block_gather(here, send, branch, local_sem.at[0], branch_rows)
    group = query_pre_ref.shape[1] // KEY_VALUE_HEADS
    narrow = kv_ref.shape[1] // 2

    def heads(first, count):
        @pl.loop(first, first + count)
        def _(i):
            at = pl.multiple_of(i * HEAD_SIZE, HEAD_SIZE)
            gain_grad_ref[i] = back_heads(
                pl.multiple_of(i * group, group),
                at,
                pl.multiple_of(narrow + i * HEAD_SIZE, HEAD_SIZE),
                at,
                query_pre_ref,
                gain_ref,
                cosine_ref,
                sine_ref,
                kv_ref,
                kv_ref,
                queries_ref,
                grad_ref,
                pre_grad_ref,
                key_grad_ref,
                value_grad_ref,
            )

    stages[0]()
    heads(0, KEY_VALUE_HEADS - 1)
    stages[1]()
    heads(KEY_VALUE_HEADS - 1, 1)
    stages[2]()
    stages[3]()
    send.finish()


def attention_back_gather(query_pre, gain, cosine, sine, kv_all, queries, attended_grad, branch):
    rows, wide = query_pre.shape
    keys, both = kv_all.shape
    vmem = pl.BlockSpec(memory_space=pltpu.VMEM)
    anywhere = pl.BlockSpec(memory_space=pl.ANY)
    return pl.pallas_call(
        attention_back_gather_kernel,
        out_shape=[
            jax.ShapeDtypeStruct((rows, wide), bf16),
            jax.ShapeDtypeStruct((keys, both // 2), f32),
            jax.ShapeDtypeStruct((keys, both // 2), f32),
            jax.ShapeDtypeStruct((KEY_VALUE_HEADS, 1, HEAD_SIZE), f32),
            jax.ShapeDtypeStruct((lax.axis_size(plane) * rows, branch.shape[1]), bf16),
        ],
        in_specs=[vmem] * 7 + [anywhere],
        out_specs=[vmem] * 4 + [anywhere],
        scratch_shapes=[
            pltpu.SemaphoreType.DMA((9,)),
            pltpu.SemaphoreType.DMA((9,)),
            pltpu.SemaphoreType.DMA((1,)),
        ],
        compiler_params=pltpu.CompilerParams(
            collective_id=6, has_side_effects=True, vmem_limit_bytes=48 * 2**20
        ),
        cost_estimate=pl.CostEstimate(flops=10**6, bytes_accessed=10**6, transcendentals=0),
    )(
        query_pre, gain.reshape(1, HEAD_SIZE), cosine, sine, kv_all, queries, attended_grad, branch
    )


def attention_back(query_pre, gain, cosine, sine, kv_all, queries, attended_grad):
    rows, wide = query_pre.shape
    keys, both = kv_all.shape
    group = wide // KEY_VALUE_HEADS
    small = pl.BlockSpec((rows, HEAD_SIZE), lambda i: (0, 0))
    block = pl.BlockSpec((rows, group), lambda i: (0, i))
    return pl.pallas_call(
        attention_back_kernel,
        grid=(KEY_VALUE_HEADS,),
        out_shape=[
            jax.ShapeDtypeStruct((rows, wide), bf16),
            jax.ShapeDtypeStruct((keys, both // 2), f32),
            jax.ShapeDtypeStruct((keys, both // 2), f32),
            jax.ShapeDtypeStruct((KEY_VALUE_HEADS, 1, HEAD_SIZE), f32),
        ],
        in_specs=[
            block,
            pl.BlockSpec((1, HEAD_SIZE), lambda i: (0, 0)),
            small,
            small,
            pl.BlockSpec((keys, HEAD_SIZE), lambda i: (0, i)),
            pl.BlockSpec((keys, HEAD_SIZE), lambda i: (0, KEY_VALUE_HEADS + i)),
            block,
            block,
        ],
        out_specs=[
            block,
            pl.BlockSpec((keys, HEAD_SIZE), lambda i: (0, i)),
            pl.BlockSpec((keys, HEAD_SIZE), lambda i: (0, i)),
            pl.BlockSpec((1, 1, HEAD_SIZE), lambda i: (i, 0, 0)),
        ],
        cost_estimate=pl.CostEstimate(flops=10**6, bytes_accessed=10**6, transcendentals=0),
        compiler_params=pltpu.CompilerParams(vmem_limit_bytes=48 * 2**20),
    )(
        query_pre, gain.reshape(1, HEAD_SIZE), cosine, sine, kv_all, kv_all, queries, attended_grad
    )


def join_halves(mine, other):
    lower = lax.axis_index("expert") == 0
    return jnp.concatenate(
        [jnp.where(lower, mine, other), jnp.where(lower, other, mine)], axis=1
    )


def dot(a, b):
    return jnp.dot(a, b, preferred_element_type=f32)


def ctx_sum(v):
    if not small_plane():
        return lax.psum_scatter(v, "ctx", scatter_dimension=1, tiled=True).astype(f32)
    member = lax.axis_index("ctx")

    def block(j):
        return lax.dynamic_slice_in_dim(v, (member ^ j) * PROMPT_DEV, PROMPT_DEV, axis=1)

    near = block(0).astype(f32) + core(block(1)).astype(f32)
    far = (block(2).astype(f32) + core(block(3)).astype(f32)).astype(bf16)
    return near + over_x(far).astype(f32)


def body(
    hidden_in,
    attn_gain,
    query_weight,
    key_matrix,
    value_matrix,
    query_gain,
    key_gain,
    output_weight,
    ffn_gain,
    router_weight,
    gate_up,
    down_proj,
    routes,
    out_grad,
):
    ctx_count = lax.axis_size("ctx")
    spread_count = lax.axis_size(plane)
    dp_count = lax.axis_size("dp")
    device_count = dp_count * spread_count
    local_experts = gate_up.shape[0]
    count_of_rows = hidden_in.shape[0]
    prompt_all = PROMPT_DEV * ctx_count
    hidden_ff = gate_up.shape[2] // 2
    member = lax.axis_index("ctx")
    offsets = jnp.arange(count_of_rows, dtype=jnp.int32)
    position = jnp.where(
        offsets < PROMPT_DEV, member * PROMPT_DEV + offsets, prompt_all + offsets - PROMPT_DEV
    )
    cosine, rope_sine = angles(position, HEAD_SIZE)
    narrow = KEY_VALUE_HEADS * HEAD_SIZE
    wide = QUERY_HEADS * HEAD_SIZE
    inputs = hidden_in.astype(f32)
    scale_in = rms_scale(inputs)

    def by_owner(v):
        v = v.reshape(count_of_rows, dp_count, spread_count, -1)
        return v.transpose(2, 0, 1, 3).reshape(spread_count, count_of_rows, -1)

    signed_sine = rope_sine * jnp.where(jnp.arange(HEAD_SIZE) < HEAD_SIZE // 2, -1.0, 1.0)
    if small_plane():
        (
            kv_other,
            q_other,
            o_other,
            g_rows,
            route_rows,
            kv_all,
            normed_owned,
            attended_owned,
            query_pre,
            queries,
            key_pre,
            residual,
            ffn_in,
        ) = fetch_and_attend(
            hidden_in, attn_gain, query_gain, key_gain, ffn_gain, cosine, signed_sine,
            key_matrix, value_matrix, query_weight, output_weight, out_grad, routes,
        )
        kv_weights = [jnp.concatenate([key_matrix, value_matrix], axis=1), kv_other]
        q_weights = [query_weight, q_other]
        o_weights = [output_weight, o_other]
    else:
        full = [
            lax.all_gather(w, "expert", axis=0, tiled=True)
            for w in (
                jnp.concatenate([key_matrix, value_matrix], axis=1),
                query_weight,
                output_weight,
            )
        ]
        kv_weights, q_weights, o_weights = [[w] for w in full]
        g_rows = lax.all_gather(out_grad, plane, axis=0, tiled=True)
        route_rows = lax.all_gather(routes, plane, axis=0, tiled=True)
        normalized_input = (inputs * scale_in * attn_gain).astype(bf16)
        query_pre = dot(normalized_input, q_weights[0])
        key_value_pre = dot(normalized_input, kv_weights[0])
        key_pre = key_value_pre[:, :narrow]
        key_heads = key_pre.reshape(count_of_rows, KEY_VALUE_HEADS, HEAD_SIZE)
        key_low = rotate(
            key_heads * rms_scale(key_heads) * key_gain, cosine[:, None, :], rope_sine[:, None, :]
        ).astype(bf16)
        kv_low = jnp.concatenate(
            [key_low.reshape(count_of_rows, narrow), key_value_pre[:, narrow:].astype(bf16)],
            axis=1,
        )
        kv_blocks = lax.all_gather(kv_low[:PROMPT_DEV], "ctx", axis=0, tiled=True)
        kv_all = jnp.concatenate([kv_blocks, kv_low[PROMPT_DEV:]], axis=0)
        queries, attended = attention(query_pre, query_gain, cosine, signed_sine, kv_all)
        residual = inputs + dot(attended, o_weights[0])
        ffn_in = (residual * rms_scale(residual) * ffn_gain).astype(bf16)
        normed_owned = by_owner(normalized_input)
        attended_owned = by_owner(attended)

    def owned(v):
        return lax.all_to_all(v, plane, split_axis=0, concat_axis=0, tiled=True)

    def backward_dot(v, weights):
        parts = [dot(v, w.T) for w in weights]
        return parts[0] if len(parts) == 1 else join_halves(*parts)

    key_before_norm = key_pre.reshape(count_of_rows, KEY_VALUE_HEADS, HEAD_SIZE)
    key_inv = rms_scale(key_before_norm)
    scale_ffn = rms_scale(residual)

    expert_count = local_experts * spread_count
    expert_ids = jnp.arange(expert_count, dtype=jnp.int32)

    def gates_of(some_rows, some_routes):
        logits = dot(some_rows, router_weight)
        chosen = jnp.any(some_routes[:, :, None] == expert_ids[None, None, :], axis=1)
        logits = jnp.where(chosen, logits, masked)
        raised = jnp.where(
            chosen, jnp.exp(logits - jnp.max(logits, axis=-1, keepdims=True)), 0.0
        )
        return raised / jnp.sum(raised, axis=-1, keepdims=True)

    gates = gates_of(ffn_in, routes)
    if small_plane():
        rows, hidden, grads, gates_mine, totals, down_part = gather_first_expert(
            ffn_in, route_rows, router_weight, g_rows, gate_up, down_proj
        )
        hiddens = [hidden]
        down_parts = [down_part]
        rows, grads = after((rows, grads), down_parts)
        hidden, grads, gate_grads = last_expert(
            1, expert_count, rows, g_rows, gates_mine, totals, gate_up, down_proj, grads
        )
        hiddens.append(hidden)
        projected_grads = [grads]
        gate_up_parts = [dot(rows.T, grads).astype(bf16)]
        down_late = dot(after(hidden, gate_up_parts).T, g_rows).astype(bf16)
    else:
        rows = lax.all_gather(ffn_in, plane, axis=0, tiled=True)
        first_expert = lax.axis_index(plane) * local_experts
        gates_mine = lax.dynamic_slice_in_dim(
            gates_of(rows, route_rows), first_expert, local_experts, axis=1
        )
        gate_grads, hiddens, projected_grads = [], [], []
        for which in range(local_experts):
            gate = gates_mine[:, which : which + 1]
            projected = dot(rows, gate_up[which])
            back = dot(g_rows, down_proj[which].T)
            gate_part = projected[:, :hidden_ff]
            up_part = projected[:, hidden_ff:]
            sigmoid_gate = jax.nn.sigmoid(gate_part)
            hidden = gate_part * sigmoid_gate * up_part
            gate_grads.append(jnp.sum(hidden * back, axis=-1))
            hiddens.append((gate * hidden).astype(bf16))
            back = gate * back
            gate_back = back * up_part * sigmoid_gate * (1.0 + gate_part * (1.0 - sigmoid_gate))
            up_back = back * gate_part * sigmoid_gate
            projected_grads.append(jnp.concatenate([gate_back, up_back], axis=-1).astype(bf16))
        attended_owned, normed_owned = owned(attended_owned), owned(normed_owned)
        down_parts = [dot(v.T, g_rows).astype(bf16) for v in hiddens]
        gate_up_parts = [dot(rows.T, v).astype(bf16) for v in projected_grads]
    down_low, gate_up_low = [
        [lax.psum_scatter(v, "dp", scatter_dimension=0, tiled=True) for v in parts]
        for parts in (down_parts, gate_up_parts)
    ]
    gate_up_grad = jnp.stack(
        [
            part.astype(f32)
            for v in gate_up_low
            for part in jnp.split(v, v.shape[1] // (2 * hidden_ff), axis=1)
        ]
    )
    projected_grads, hiddens = lax.optimization_barrier(
        ((projected_grads, hiddens), down_parts, gate_up_parts)
    )[0]
    if small_plane():
        back, attended_owned, normed_owned = plane_sum(
            projected_grads, gate_up, gate_grads, [attended_owned, normed_owned], 3
        )
        back_sum = back[:, :MODEL_WIDTH]
        gate_grad = (
            back[:, MODEL_WIDTH : MODEL_WIDTH + expert_count]
            + back[:, MODEL_WIDTH + expert_count : MODEL_WIDTH + 2 * expert_count]
        )
        moe_sum = None
    else:
        moe_part = 0.0
        row_part = 0.0
        for which in range(local_experts):
            row_part = row_part + dot(projected_grads[which], gate_up[which].T)
            moe_part = moe_part + dot(hiddens[which], down_proj[which])
        moe_sum, back_sum = [
            lax.psum_scatter(v.astype(bf16), plane, scatter_dimension=0, tiled=True).astype(f32)
            for v in (moe_part, row_part)
        ]
        gate_grad = lax.all_to_all(
            jnp.stack(gate_grads, axis=1).reshape(spread_count, count_of_rows, local_experts),
            plane,
            split_axis=0,
            concat_axis=0,
            tiled=True,
        )
        gate_grad = gate_grad.transpose(1, 0, 2).reshape(count_of_rows, expert_count)
    logit_grad = gates * (gate_grad - jnp.sum(gates * gate_grad, axis=-1, keepdims=True))

    grad_out = out_grad.astype(f32)
    router_local = jnp.dot(ffn_in.T, logit_grad, preferred_element_type=f32)
    ffn_in_grad = back_sum + jnp.dot(
        logit_grad, router_weight.astype(f32).T, precision=highest
    )
    residual_grad = grad_out + norm_back(residual, scale_ffn, ffn_gain, ffn_in_grad)
    ffn_gain_local = jnp.sum(ffn_in_grad * residual * scale_ffn, axis=0)
    branch_low = residual_grad.astype(bf16)
    attended_grad = backward_dot(branch_low, o_weights).astype(bf16)
    operands = (query_pre, query_gain, cosine, signed_sine, kv_all, queries, attended_grad)
    if small_plane():
        *attention_grads, branch_rows = attention_back_gather(*operands, branch_low)
    else:
        attention_grads = attention_back(*operands)
    query_pre_grad, key_grad_all, value_grad_all, query_gain_parts = attention_grads
    query_gain_local = jnp.sum(query_gain_parts, axis=(0, 1))
    pair_grads = jnp.stack([key_grad_all[:prompt_all], value_grad_all[:prompt_all]]).astype(bf16)
    prompt_grads = ctx_sum(pair_grads)
    key_grad = jnp.concatenate([prompt_grads[0], key_grad_all[prompt_all:]], axis=0).reshape(
        count_of_rows, KEY_VALUE_HEADS, HEAD_SIZE
    )
    value_gradient = jnp.concatenate([prompt_grads[1], value_grad_all[prompt_all:]], axis=0)
    key_rot_grad = rotate_back(key_grad, cosine[:, None, :], rope_sine[:, None, :])
    key_gain_local = jnp.sum(key_rot_grad * key_before_norm * key_inv, axis=(0, 1))
    key_pre_grad = (
        norm_back(key_before_norm, key_inv, key_gain, key_rot_grad)
        .astype(bf16)
        .reshape(count_of_rows, KEY_VALUE_HEADS * HEAD_SIZE)
    )
    key_value_grad = jnp.concatenate([key_pre_grad, value_gradient.astype(bf16)], axis=1)
    if small_plane():
        local = [
            weight_grads(
                query_pre_grad, key_value_grad, branch_rows, attended_owned, normed_owned, down_late
            )
        ]
    else:
        branch_rows = lax.all_gather(branch_low, plane, axis=0, tiled=True)
        pre_rows = lax.all_gather(
            jnp.concatenate([query_pre_grad, key_value_grad], axis=1), plane, axis=0, tiled=True
        )
        attended_owned, normed_owned = [
            v.reshape(spread_count * count_of_rows, -1) for v in (attended_owned, normed_owned)
        ]
        local = [
            dot(attended_owned.T, branch_rows).astype(bf16),
            dot(normed_owned.T, pre_rows).astype(bf16),
        ]
    query_pre_grad, key_value_grad = lax.optimization_barrier(
        ((query_pre_grad, key_value_grad), local)
    )[0]
    normed_grad = backward_dot(query_pre_grad, q_weights) + backward_dot(
        key_value_grad, kv_weights
    )
    attn_gain_local = jnp.sum(normed_grad * inputs * scale_in, axis=0)
    hidden_grad = residual_grad + norm_back(inputs, scale_in, attn_gain, normed_grad)
    if small_plane():
        moe_sum = plane_sum(after(hiddens, local), down_proj, None, [], 4)[0]
    block_out = (residual + moe_sum).astype(bf16)
    local = lax.optimization_barrier((local, gate_up_low, down_low))[0]
    summed = [lax.psum_scatter(v, "dp", scatter_dimension=0, tiled=True) for v in local]
    share = MODEL_WIDTH // device_count
    if small_plane():
        output_sum, query_sum, key_sum, value_sum, down_grad = untile(
            summed[0], down_low[0], wide // device_count, wide, share, narrow
        )
    else:
        output_sum, pre_sum = [v.astype(f32) for v in summed]
        query_sum = pre_sum[:, :wide]
        key_sum = pre_sum[:, wide : wide + narrow]
        value_sum = pre_sum[:, wide + narrow :]
        down_grad = jnp.stack([v.astype(f32) for v in down_low])

    small = jnp.concatenate(
        [
            v.reshape(device_count, -1)
            for v in (
                attn_gain_local,
                ffn_gain_local,
                query_gain_local,
                key_gain_local,
                router_local,
            )
        ],
        axis=1,
    )
    small = lax.all_to_all(small[:, None], every, split_axis=0, concat_axis=0, tiled=True)
    small = jnp.sum(small[:, 0], axis=0)
    head_share = HEAD_SIZE // device_count
    cuts = [share, share, head_share, head_share, share * expert_count]
    ends = [sum(cuts[: i + 1]) for i in range(5)]
    a_grad, f_grad, q_grad, k_grad, r_grad = [
        small[end - cut : end] for end, cut in zip(ends, cuts)
    ]
    return (
        block_out,
        hidden_grad,
        a_grad,
        query_sum,
        key_sum,
        value_sum,
        q_grad,
        k_grad,
        output_sum,
        f_grad,
        r_grad.reshape(share, expert_count),
        gate_up_grad,
        down_grad,
    )


def solution(mesh):
    placed = (
        P(("dp", "ctx", "expert"), None),
        P(),
        P("expert", None),
        P("expert", None),
        P("expert", None),
        P(),
        P(),
        P("expert", None),
        P(),
        P(),
        P(("ctx", "expert"), None, None),
        P(("ctx", "expert"), None, None),
        P(("dp", "ctx", "expert"), None),
        P(("dp", "ctx", "expert"), None),
    )
    return jax.shard_map(
        body,
        mesh=mesh,
        in_specs=placed,
        out_specs=(
            P(("dp", "ctx", "expert"), None),
            P(("dp", "ctx", "expert"), None),
            P(("dp", "ctx", "expert")),
            P(("dp", "ctx", "expert"), None),
            P(("dp", "ctx", "expert"), None),
            P(("dp", "ctx", "expert"), None),
            P(("dp", "ctx", "expert")),
            P(("dp", "ctx", "expert")),
            P(("dp", "ctx", "expert"), None),
            P(("dp", "ctx", "expert")),
            P(("dp", "ctx", "expert"), None),
            P(("ctx", "expert"), "dp", None),
            P(("ctx", "expert"), "dp", None),
        ),
        check_vma=False,
    )
```

```python
import math

import jax
import jax.numpy as jnp
from jax import lax
from jax.experimental import pallas as pl
from jax.experimental.pallas import tpu as pltpu
from jax.sharding import PartitionSpec as P

MODEL_WIDTH = 2048
QUERY_HEADS = 32
KEY_VALUE_HEADS = 4
HEAD_SIZE = 128
TOP = 8
PROMPT_DEV = 128


highest = lax.Precision.HIGHEST
epsilon = 1e-06
rope_base = 1000000.0
masked = -1e30
every = ("dp", "ctx", "expert")
plane = ("ctx", "expert")
bf16 = jnp.bfloat16
f32 = jnp.float32


def rms_scale(value_rows):
    return lax.rsqrt(jnp.mean(value_rows * value_rows, axis=-1, keepdims=True) + epsilon)


def norm_back(inputs, inv_rms, norm_gain, gradient):
    weighted = gradient * norm_gain
    return inv_rms * weighted - inputs * inv_rms**3 * jnp.mean(
        weighted * inputs, axis=-1, keepdims=True
    )


def angles(position, head_width):
    freq_index = jnp.arange(head_width // 2, dtype=f32)
    inverse = jnp.exp(-(2.0 * freq_index / head_width) * math.log(rope_base))
    rope_angle = position.astype(f32)[:, None] * inverse[None, :]
    rope_angle = jnp.concatenate([rope_angle, rope_angle], axis=-1)
    return (jnp.cos(rope_angle), jnp.sin(rope_angle))


def rotate(value_rows, cosine, rope_sine):
    half_width = value_rows.shape[-1] // 2
    turned = jnp.concatenate([-value_rows[..., half_width:], value_rows[..., :half_width]], axis=-1)
    return value_rows * cosine + turned * rope_sine


def rotate_back(gradient, cosine, rope_sine):
    shifted = gradient * rope_sine
    half_width = gradient.shape[-1] // 2
    return gradient * cosine + jnp.concatenate(
        [shifted[..., half_width:], -shifted[..., :half_width]], axis=-1
    )


def small_plane():
    return [lax.axis_size(a) for a in every] == [4, 4, 2]


def swap(v, axis, bit):
    return lax.ppermute(v, axis, [(i, i ^ bit) for i in range(lax.axis_size(axis))])


def core(v):
    return swap(v, "ctx", 1)


def over_x(v):
    return swap(v, "ctx", 2)


def over_y(v):
    return swap(v, "expert", 1)


def over_z(v):
    return swap(v, "dp", 1)


def after(v, *earlier):
    return lax.optimization_barrier((v, *earlier))[0]


class Places:
    def __init__(self):
        self.dp = lax.axis_index("dp")
        ctx = lax.axis_index("ctx")
        self.ctx = ctx
        self.z = lax.rem(self.dp, 2)
        self.x = lax.div(ctx, 2)
        self.c = lax.rem(ctx, 2)
        self.y = lax.axis_index("expert")
        self.to_x = {"ctx": (1 - self.x) * 2 + self.c}
        self.to_c = {"ctx": self.x * 2 + 1 - self.c}
        self.to_y = {"expert": 1 - self.y}
        self.to_z = {"dp": self.dp + 1 - 2 * self.z}

    def peers(self):
        found = []
        for r in range(1, 8):
            x, c, y = [
                1 - v if r & bit else v for v, bit in ((self.x, 4), (self.c, 2), (self.y, 1))
            ]
            found.append((x * 4 + c * 2 + y, {"ctx": x * 2 + c, "expert": y}))
        return found


def plane_slot(x, c, y):
    return x * 4 + y * 2 + c


def greet(targets):
    barrier = pltpu.get_barrier_semaphore()
    for target in targets:
        pl.semaphore_signal(barrier, inc=1, device_id=target, device_id_type=pl.DeviceIdType.MESH)
    pl.semaphore_wait(barrier, len(targets))


class Sender:
    def __init__(self, send_sem, recv_sem):
        self.send_sem = send_sem
        self.recv_sem = recv_sem
        self.copies = []

    def __call__(self, source, target_ref, device):
        i = len(self.copies)
        copy = pltpu.make_async_remote_copy(
            src_ref=source,
            dst_ref=target_ref,
            send_sem=self.send_sem.at[i],
            recv_sem=self.recv_sem.at[i],
            device_id=device,
            device_id_type=pl.DeviceIdType.MESH,
        )
        copy.start()
        self.copies.append(copy)
        return copy

    def finish(self):
        for copy in self.copies:
            copy.wait_send()


def half_fetch(here, send, sources, other, columns, rows, upper):
    def at(piece, part=None):
        first, size = piece * rows, rows
        if part == 0:
            size = upper
        elif part == 1:
            first, size = first + upper, rows - upper
        return other.at[pl.ds(pl.multiple_of(first, 16), size), columns]

    def piece(z, x, c):
        return z * 4 + x * 2 + c

    z, x, c = here.z, here.x, here.c
    got = {}

    def first():
        mine = piece(z, x, c)
        got["y"] = [
            send(
                source.at[pl.ds(pl.multiple_of(mine * rows, rows), rows), source_columns],
                other.at[pl.ds(pl.multiple_of(mine * rows, rows), rows), target_columns],
                here.to_y,
            )
            for source, source_columns, target_columns in sources
        ]

    def second():
        for copy in got["y"]:
            copy.wait_recv()
        mine = at(piece(z, x, c))
        got["x"] = send(mine, mine, here.to_x)
        got["z"] = send(mine, mine, here.to_z)
        got["c"] = send(mine, mine, here.to_c)

    def third():
        got["x"].wait_recv()
        from_x = piece(z, 1 - x, c)
        got["low"] = send(at(from_x, 1), at(from_x, 1), here.to_z)
        got["xc"] = send(at(from_x), at(from_x), here.to_c)
        got["z"].wait_recv()
        from_z = piece(1 - z, x, c)
        got["top"] = send(at(from_z, 0), at(from_z, 0), here.to_x)
        got["zc"] = send(at(from_z), at(from_z), here.to_c)

    def fourth():
        far = piece(1 - z, 1 - x, c)
        got["low"].wait_recv()
        got["lowc"] = send(at(far, 1), at(far, 1), here.to_c)
        got["top"].wait_recv()
        got["topc"] = send(at(far, 0), at(far, 0), here.to_c)

    def fifth():
        for name in ("c", "xc", "zc", "lowc", "topc"):
            got[name].wait_recv()

    return [first, second, third, fourth, fifth]


def block_gather(here, send, mine, local_sem, blocks, far_over_y=False, columns=None):
    rows = blocks.shape[0] // lax.axis_size(plane)
    half = rows // 2
    x, c, y = here.x, here.c, here.y
    got = {}

    def at(slot, part=None):
        first, size = slot * rows, rows
        if part is not None:
            first, size = first + part * half, half
        rows_of = pl.ds(pl.multiple_of(first, size), size)
        return blocks.at[rows_of] if columns is None else blocks.at[rows_of, columns]

    def first():
        slot = plane_slot(x, c, y)
        got["own"] = pltpu.make_async_copy(mine, at(slot), local_sem)
        got["own"].start()
        got["y"] = send(mine, at(slot), here.to_y)
        got["x"] = send(mine, at(slot), here.to_x)
        got["c"] = send(mine, at(slot), here.to_c)

    def second():
        got["y"].wait_recv()
        from_y = plane_slot(x, c, 1 - y)
        got["yc"] = send(at(from_y), at(from_y), here.to_c)
        if not far_over_y:
            got["top"] = send(at(from_y, 0), at(from_y, 0), here.to_x)
        got["x"].wait_recv()
        from_x = plane_slot(1 - x, c, y)
        got["xc"] = send(at(from_x), at(from_x), here.to_c)
        if far_over_y:
            got["top"] = send(at(from_x, 0), at(from_x, 0), here.to_y)
        got["low"] = send(at(from_x, 1), at(from_x, 1), here.to_y)

    def third():
        far = plane_slot(1 - x, c, 1 - y)
        got["top"].wait_recv()
        got["topc"] = send(at(far, 0), at(far, 0), here.to_c)
        got["low"].wait_recv()
        got["lowc"] = send(at(far, 1), at(far, 1), here.to_c)

    def fourth():
        for name in ("c", "yc", "xc", "topc", "lowc"):
            got[name].wait_recv()
        got["own"].wait()

    return [first, second, third, fourth], got


def turn_half(v):
    return pltpu.roll(v, v.shape[-1] // 2, axis=1)


def head_norm(v):
    return lax.rsqrt(jnp.mean(v * v, axis=-1, keepdims=True) + epsilon)


def fetch_kernel(
    hidden_ref,
    attn_gain_ref,
    query_gain_ref,
    key_gain_ref,
    ffn_gain_ref,
    cosine_ref,
    sine_ref,
    key_ref,
    value_ref,
    query_ref,
    output_ref,
    grad_ref,
    routes_across,
    kv_out,
    q_out,
    o_out,
    g_blocks,
    route_blocks,
    kv_all_out,
    normed_out,
    attended_out,
    query_pre_out,
    queries_out,
    key_pre_ref,
    residual_ref,
    ffn_ref,
    normed_owned,
    attended_owned,
    query_pre_ref,
    queries_ref,
    normed_ref,
    attended_ref,
    kv_own,
    kv_other,
    q_own,
    q_other,
    o_own,
    o_other,
    kv_pre,
    kv_low,
    kv_all,
    routes_ref,
    send_sem,
    recv_sem,
    local_sem,
):
    here = Places()
    greet([here.to_y, here.to_z, here.to_c, here.to_x])
    send = Sender(send_sem, recv_sem)
    count, width = hidden_ref.shape
    half = width // 2
    narrow = key_ref.shape[1]
    wide = query_ref.shape[1]
    prompt_all = kv_all.shape[0] - (count - PROMPT_DEV)
    spread, groups = lax.axis_size(plane), lax.axis_size("dp")
    tile = 512
    loads = [
        pltpu.make_async_copy(key_ref, kv_own.at[:, pl.ds(0, narrow)], local_sem.at[0]),
        pltpu.make_async_copy(value_ref, kv_own.at[:, pl.ds(narrow, narrow)], local_sem.at[1]),
        pltpu.make_async_copy(query_ref, q_own, local_sem.at[2]),
        pltpu.make_async_copy(output_ref, o_own, local_sem.at[3]),
    ]
    stores = [
        pltpu.make_async_copy(kv_other, kv_out, local_sem.at[4]),
        pltpu.make_async_copy(q_other, q_out, local_sem.at[5]),
        pltpu.make_async_copy(o_other, o_out, local_sem.at[6]),
        pltpu.make_async_copy(kv_all, kv_all_out, local_sem.at[7]),
        pltpu.make_async_copy(normed_owned, normed_out, local_sem.at[11]),
        pltpu.make_async_copy(attended_owned, attended_out, local_sem.at[12]),
        pltpu.make_async_copy(query_pre_ref, query_pre_out, local_sem.at[13]),
        pltpu.make_async_copy(queries_ref, queries_out, local_sem.at[14]),
    ]

    def part_of(size, which):
        first = here.y * size if which == 0 else size - here.y * size
        return pl.ds(pl.multiple_of(first, size), size)

    def project(source, weight, out, which, first, count_of_tiles, add):
        rows = part_of(weight.shape[0], which)

        @pl.loop(first, first + count_of_tiles)
        def _(i):
            cols = pl.ds(pl.multiple_of(i * tile, tile), tile)
            part = dot(source[:, rows], weight[:, cols])
            out[:, cols] = out[:, cols] + part if add else part

    def start():
        for load in loads:
            load.start()
        routes_ref[...] = routes_across[...].T
        inputs = hidden_ref[...].astype(f32)
        normed_ref[...] = (inputs * head_norm(inputs) * attn_gain_ref[...]).astype(bf16)

    def own_part():
        share = width // (spread * groups)
        for s in range(spread):
            normed_owned[s] = jnp.concatenate(
                [
                    normed_ref[:, (d * spread + s) * share : (d * spread + s + 1) * share]
                    for d in range(groups)
                ],
                axis=1,
            )
        stores[4].start()
        for load in loads[:3]:
            load.wait()
        project(normed_ref, kv_own, kv_pre, 0, 0, 2 * narrow // tile, False)
        project(normed_ref, q_own, query_pre_ref, 0, 0, wide // tile, False)

    exchange = {}

    def keys_part():
        project(normed_ref, kv_other, kv_pre, 1, 0, 2 * narrow // tile, True)
        stores[0].start()
        key_pre_ref[...] = kv_pre[:, :narrow]
        for h in range(narrow // HEAD_SIZE):
            cols = slice(h * HEAD_SIZE, (h + 1) * HEAD_SIZE)
            v = kv_pre[:, cols]
            v = v * head_norm(v) * key_gain_ref[...]
            kv_low[:, cols] = (v * cosine_ref[...] + turn_half(v) * sine_ref[...]).astype(bf16)
        kv_low[:, narrow:] = kv_pre[:, narrow:].astype(bf16)
        kv_all[prompt_all:, :] = kv_low[PROMPT_DEV:, :]
        source = kv_low.at[pl.ds(0, PROMPT_DEV)]
        slot = kv_all.at[pl.ds(pl.multiple_of(here.ctx * PROMPT_DEV, PROMPT_DEV), PROMPT_DEV)]
        exchange["own"] = pltpu.make_async_copy(source, slot, local_sem.at[8])
        exchange["own"].start()
        exchange["c"] = send(source, slot, here.to_c)
        exchange["x"] = send(source, slot, here.to_x)

    def keys_forward():
        exchange["x"].wait_recv()
        first = ((1 - here.x) * 2 + here.c) * PROMPT_DEV
        slot = kv_all.at[pl.ds(pl.multiple_of(first, PROMPT_DEV), PROMPT_DEV)]
        exchange["xc"] = send(slot, slot, here.to_c)

    def queries_first():
        project(normed_ref, q_other, query_pre_ref, 1, 0, wide // tile // 2, True)

    def queries_rest():
        stores[1].start()
        project(
            normed_ref, q_other, query_pre_ref, 1, wide // tile // 2, wide // tile // 2, True
        )
        for name in ("c", "xc"):
            exchange[name].wait_recv()
        exchange["own"].wait()
        stores[3].start()
        stores[6].start()

    group = 4
    pieces = 4

    def attend(part):
        visible = visible_keys(count, kv_all.shape[0])
        blocks = wide // HEAD_SIZE // group // pieces

        @pl.loop(part * blocks, (part + 1) * blocks)
        def _(i):
            first = lax.div(i * group, wide // narrow) * HEAD_SIZE
            keys = kv_all[:, pl.ds(pl.multiple_of(first, HEAD_SIZE), HEAD_SIZE)]
            values = kv_all[:, pl.ds(pl.multiple_of(narrow + first, HEAD_SIZE), HEAD_SIZE)]
            for h in range(group):
                cols = pl.ds(pl.multiple_of((i * group + h) * HEAD_SIZE, HEAD_SIZE), HEAD_SIZE)
                v = query_pre_ref[:, cols]
                v = v * head_norm(v) * query_gain_ref[...]
                queries = (v * cosine_ref[...] + turn_half(v) * sine_ref[...]).astype(bf16)
                queries_ref[:, cols] = queries
                probs = head_softmax(queries, keys, visible).astype(bf16)
                attended = dot(probs, values).astype(bf16)
                attended_ref[:, cols] = attended
                head = i * group + h
                at = pl.multiple_of(lax.div(head, spread) * HEAD_SIZE, HEAD_SIZE)
                attended_owned[lax.rem(head, spread), :, pl.ds(at, HEAD_SIZE)] = attended

    def output_own():
        stores[5].start()
        stores[7].start()
        loads[3].wait()
        project(attended_ref, o_own, residual_ref, 0, 0, width // tile, False)

    def finish_rows():
        stores[2].start()
        project(attended_ref, o_other, residual_ref, 1, 0, width // tile, True)
        residual = residual_ref[...] + hidden_ref[...].astype(f32)
        residual_ref[...] = residual
        ffn_ref[...] = (residual * head_norm(residual) * ffn_gain_ref[...]).astype(bf16)

    low, high = pl.ds(0, wide // 2), pl.ds(wide // 2, wide // 2)
    o_low, o_high = pl.ds(0, width // 2), pl.ds(width // 2, width // 2)
    rows, o_rows = half // 8, output_ref.shape[0] // 8
    kv, qa, qb, oa, ob, g, r = [
        half_fetch(
            here,
            send,
            [
                (key_ref, pl.ds(0, narrow), pl.ds(0, narrow)),
                (value_ref, pl.ds(0, narrow), pl.ds(narrow, narrow)),
            ],
            kv_other,
            pl.ds(0, 2 * narrow),
            rows,
            rows // 2,
        ),
        half_fetch(here, send, [(query_ref, low, low)], q_other, low, rows, rows // 2),
        half_fetch(here, send, [(query_ref, high, high)], q_other, high, rows, rows // 2),
        half_fetch(here, send, [(output_ref, o_low, o_low)], o_other, o_low, o_rows, o_rows // 4),
        half_fetch(
            here, send, [(output_ref, o_high, o_high)], o_other, o_high, o_rows, o_rows // 4
        ),
        block_gather(here, send, grad_ref, local_sem.at[9], g_blocks, True)[0],
        block_gather(here, send, routes_ref, local_sem.at[10], route_blocks)[0],
    ]
    steps = [
        kv[0], qa[0], qb[0], oa[0], ob[0], g[0], start, kv[1], kv[2], own_part, qa[1],
        kv[3], qa[2], qb[1], kv[4], keys_part, qa[3], qb[2], oa[1],
        keys_forward, qa[4], queries_first, qb[3], ob[1], qb[4], queries_rest,
        oa[2], r[0], lambda: attend(0), lambda: attend(1),
        oa[3], ob[2], g[1], r[1], lambda: attend(2), lambda: attend(3), oa[4], output_own,
        ob[3], g[2], r[2], ob[4], finish_rows, g[3], r[3],
    ]
    for step in steps:
        step()
    for store in stores:
        store.wait()
    send.finish()


def fetch_and_attend(
    hidden_in, attn_gain, query_gain, key_gain, ffn_gain, cosine, sine, key_matrix, value_matrix,
    query_weight, output_weight, out_grad, routes,
):
    rows, width = hidden_in.shape
    half, wide = query_weight.shape
    narrow = key_matrix.shape[1]
    spread = lax.axis_size(plane)
    keys = lax.axis_size("ctx") * PROMPT_DEV + rows - PROMPT_DEV
    vmem = pl.BlockSpec(memory_space=pltpu.VMEM)
    anywhere = pl.BlockSpec(memory_space=pl.ANY)
    copies = 5 * 10 + 1 + 2 * 9 + 3
    return pl.pallas_call(
        fetch_kernel,
        out_shape=[
            jax.ShapeDtypeStruct((half, 2 * narrow), bf16),
            jax.ShapeDtypeStruct((half, wide), bf16),
            jax.ShapeDtypeStruct(output_weight.shape, bf16),
            jax.ShapeDtypeStruct((spread * rows, width), bf16),
            jax.ShapeDtypeStruct((spread * rows, routes.shape[1]), jnp.int32),
            jax.ShapeDtypeStruct((keys, 2 * narrow), bf16),
            jax.ShapeDtypeStruct((spread, rows, width // spread), bf16),
            jax.ShapeDtypeStruct((spread, rows, wide // spread), bf16),
            jax.ShapeDtypeStruct((rows, wide), f32),
            jax.ShapeDtypeStruct((rows, wide), bf16),
            jax.ShapeDtypeStruct((rows, narrow), f32),
            jax.ShapeDtypeStruct((rows, width), f32),
            jax.ShapeDtypeStruct((rows, width), bf16),
        ],
        in_specs=[vmem] * 7 + [anywhere] * 5 + [vmem],
        out_specs=[anywhere] * 10 + [vmem] * 3,
        scratch_shapes=[
            pltpu.VMEM((spread, rows, width // spread), bf16),
            pltpu.VMEM((spread, rows, wide // spread), bf16),
            pltpu.VMEM((rows, wide), f32),
            pltpu.VMEM((rows, wide), bf16),
            pltpu.VMEM((rows, width), bf16),
            pltpu.VMEM((rows, wide), bf16),
            pltpu.VMEM((half, 2 * narrow), bf16),
            pltpu.VMEM((half, 2 * narrow), bf16),
            pltpu.VMEM((half, wide), bf16),
            pltpu.VMEM((half, wide), bf16),
            pltpu.VMEM(output_weight.shape, bf16),
            pltpu.VMEM(output_weight.shape, bf16),
            pltpu.VMEM((rows, 2 * narrow), f32),
            pltpu.VMEM((rows, 2 * narrow), bf16),
            pltpu.VMEM((keys, 2 * narrow), bf16),
            pltpu.VMEM(routes.shape, jnp.int32),
            pltpu.SemaphoreType.DMA((copies,)),
            pltpu.SemaphoreType.DMA((copies,)),
            pltpu.SemaphoreType.DMA((15,)),
        ],
        compiler_params=pltpu.CompilerParams(
            collective_id=1, has_side_effects=True, vmem_limit_bytes=60 * 2**20
        ),
        cost_estimate=pl.CostEstimate(
            flops=2 * rows * width * (2 * wide + 2 * narrow) * 2,
            bytes_accessed=60 * 2**20,
            transcendentals=0,
        ),
    )(
        hidden_in, attn_gain.reshape(1, width), query_gain.reshape(1, HEAD_SIZE),
        key_gain.reshape(1, HEAD_SIZE), ffn_gain.reshape(1, width), cosine, sine,
        key_matrix, value_matrix, query_weight, output_weight, out_grad, routes.T,
    )


def chip_rows(x, y, rows):
    first = plane_slot(x, 0, y) * rows
    return pl.ds(pl.multiple_of(first, rows), 2 * rows)


def across_down(rows, down_rows):
    return lax.dot_general(rows, down_rows, (((1,), (1,)), ((), ())), preferred_element_type=f32)


def expert_chunk(
    some, rows_v, g_v, gate_up_v, down_v, hidden_v, grad_v, total_v, gate, mark, q_v=None
):
    ff = down_v.shape[0]
    tile = 256

    @pl.loop(0, ff // tile, unroll=True)
    def _(f):
        at = pl.multiple_of(f * tile, tile)
        a = dot(rows_v[some, :], gate_up_v[:, pl.ds(at, tile)])
        b = dot(rows_v[some, :], gate_up_v[:, pl.ds(ff + at, tile)])
        if q_v is None:
            q = across_down(g_v[some, :], down_v[pl.ds(at, tile), :])
        else:
            q = q_v[some, pl.ds(at, tile)]
        s = 1.0 / (1.0 + jnp.exp(-a))
        raised_a = a * s
        hidden = raised_a * b
        total_v[...] = total_v[...] + jnp.where(
            mark, jnp.sum(hidden * q, axis=-1, keepdims=True), 0.0
        )
        back = gate * q
        hidden_v[some, pl.ds(at, tile)] = (gate * hidden).astype(bf16)
        grad_v[some, pl.ds(at, tile)] = (back * b * s * (1.0 + a * (1.0 - s))).astype(bf16)
        grad_v[some, pl.ds(ff + at, tile)] = (back * raised_a).astype(bf16)


def first_expert_kernel(
    ffn_ref,
    routes_ref,
    router_ref,
    g_hbm,
    gate_up_hbm,
    down_hbm,
    rows_out,
    hidden_out,
    grad_out,
    gates_ref,
    gate_grad_ref,
    down_grad_ref,
    rows_v,
    g_v,
    gate_up_v,
    down_v,
    hidden_v,
    grad_v,
    total_v,
    down_total,
    q_v,
    send_sem,
    recv_sem,
    local_sem,
):
    here = Places()
    greet([here.to_y, here.to_c, here.to_x])
    send = Sender(send_sem, recv_sem)
    count = ffn_ref.shape[0]
    experts = router_ref.shape[0]
    local_experts = down_hbm.shape[0]
    stages, got = block_gather(here, send, ffn_ref, local_sem.at[0], rows_v)
    stages[0]()
    loads = [
        pltpu.make_async_copy(down_hbm.at[0], down_v, local_sem.at[2]),
        pltpu.make_async_copy(g_hbm, g_v, local_sem.at[3]),
        pltpu.make_async_copy(gate_up_hbm.at[0], gate_up_v, local_sem.at[1]),
    ]
    for load in loads:
        load.start()
    first_expert = plane_index(here) * local_experts
    stores = []

    def chunk(x, y):
        some = chip_rows(x, y, count)
        logits = lax.dot_general(
            rows_v[some, :],
            router_ref[...],
            (((1,), (1,)), ((), ())),
            preferred_element_type=f32,
        )
        ids = lax.broadcasted_iota(jnp.int32, logits.shape, 1)
        routes = routes_ref[some, :]
        chosen = ids < 0
        for k in range(routes.shape[1]):
            chosen = chosen | (routes[:, k : k + 1] == ids)
        logits = jnp.where(chosen, logits, masked)
        raised = jnp.exp(logits - jnp.max(logits, axis=-1, keepdims=True))
        raised = jnp.where(chosen, raised, 0.0)
        gates = raised / jnp.sum(raised, axis=-1, keepdims=True)
        lane = lax.broadcasted_iota(jnp.int32, total_v.shape, 1)
        total_v[...] = jnp.zeros(total_v.shape, f32)
        columns = [
            jnp.sum(jnp.where(ids == first_expert + e, gates, 0.0), axis=-1, keepdims=True)
            for e in range(local_experts)
        ]
        spread = jnp.zeros(total_v.shape, f32)
        for e in range(local_experts):
            spread = jnp.where(lane == e, columns[e], spread)
        gates_ref[some, :] = spread
        mark = (lane == first_expert) | (lane == first_expert + experts)
        expert_chunk(
            some, rows_v, g_v, gate_up_v, down_v, hidden_v, grad_v, total_v, columns[0], mark, q_v
        )
        gate_grad_ref[some, :] = total_v[...]
        for source, target in ((hidden_v, hidden_out), (grad_v, grad_out), (rows_v, rows_out)):
            columns = pl.ds(0, source.shape[1])
            store = pltpu.make_async_copy(
                source.at[some, :], target.at[some, columns], local_sem.at[4 + len(stores)]
            )
            store.start()
            stores.append(store)
        add_down(some, len(stores) == 3, len(stores) == 12)

    def add_down(some, is_first, is_last):
        tile = 1024

        @pl.loop(0, down_total.shape[1] // tile)
        def _(i):
            cols = pl.ds(pl.multiple_of(i * tile, tile), tile)
            part = transposed_dot(hidden_v[some, :], g_v[some, cols])
            if not is_first:
                part = part + down_total[:, cols]
            if is_last:
                down_grad_ref[:, cols] = part.astype(bf16)
            else:
                down_total[:, cols] = part

    x, y = here.x, here.y
    for load in loads[:2]:
        load.wait()

    @pl.loop(0, rows_v.shape[0] // (2 * count))
    def _(i):
        some = pl.ds(pl.multiple_of(i * 2 * count, 2 * count), 2 * count)
        for at in range(0, down_v.shape[0], 256):
            q_v[some, at : at + 256] = across_down(g_v[some, :], down_v[at : at + 256, :])

    for name in ("c", "own"):
        arrive(got, name)
    loads[2].wait()
    chunk(x, y)
    stages[1]()
    arrive(got, "yc")
    chunk(x, 1 - y)
    stages[2]()
    arrive(got, "xc")
    chunk(1 - x, y)
    arrive(got, "topc")
    arrive(got, "lowc")
    chunk(1 - x, 1 - y)
    for store in stores:
        store.wait()
    send.finish()


def gather_first_expert(ffn_in, route_rows, router_weight, g_rows, gate_up, down_proj):
    experts, ff, width = down_proj.shape
    total = route_rows.shape[0]
    vmem = pl.BlockSpec(memory_space=pltpu.VMEM)
    anywhere = pl.BlockSpec(memory_space=pl.ANY)
    return pl.pallas_call(
        first_expert_kernel,
        out_shape=[
            jax.ShapeDtypeStruct((total, width), bf16),
            jax.ShapeDtypeStruct((total, ff), bf16),
            jax.ShapeDtypeStruct((total, 2 * experts * ff), bf16),
            jax.ShapeDtypeStruct((total, 128), f32),
            jax.ShapeDtypeStruct((total, 128), f32),
            jax.ShapeDtypeStruct((ff, width), bf16),
        ],
        in_specs=[anywhere] + [vmem] * 2 + [anywhere] * 3,
        out_specs=[anywhere] * 3 + [vmem] * 3,
        scratch_shapes=[
            pltpu.VMEM((total, width), bf16),
            pltpu.VMEM((total, width), bf16),
            pltpu.VMEM(gate_up.shape[1:], bf16),
            pltpu.VMEM(down_proj.shape[1:], bf16),
            pltpu.VMEM((total, ff), bf16),
            pltpu.VMEM((total, 2 * ff), bf16),
            pltpu.VMEM((2 * ffn_in.shape[0], 128), f32),
            pltpu.VMEM((ff, width), f32),
            pltpu.VMEM((total, ff), f32),
            pltpu.SemaphoreType.DMA((9,)),
            pltpu.SemaphoreType.DMA((9,)),
            pltpu.SemaphoreType.DMA((16,)),
        ],
        compiler_params=pltpu.CompilerParams(
            collective_id=2, has_side_effects=True, vmem_limit_bytes=56 * 2**20
        ),
        cost_estimate=pl.CostEstimate(
            flops=2 * total * width * 3 * ff,
            bytes_accessed=40 * 2**20,
            transcendentals=0,
        ),
    )(ffn_in, route_rows, router_weight.T, g_rows, gate_up, down_proj)


def next_expert_kernel(
    which, experts, rows_v, g_v, gates_ref, totals_ref, gate_up_v, down_v, _, hidden_v, grad_v,
    gate_grad_ref, total_v,
):
    lane = lax.broadcasted_iota(jnp.int32, total_v.shape, 1)
    expert = lax.axis_index(plane) * lax.div(experts, lax.axis_size(plane)) + which
    mark = (lane == expert) | (lane == expert + experts)
    total_v[...] = totals_ref[...]
    gate = jnp.sum(jnp.where(lane == which, gates_ref[...], 0.0), axis=-1, keepdims=True)
    some = pl.ds(0, rows_v.shape[0])
    expert_chunk(
        some, rows_v, g_v, gate_up_v.at[0], down_v.at[0], hidden_v, grad_v, total_v, gate, mark
    )
    total = total_v[...]
    high = total.astype(bf16).astype(f32)
    gate_grad_ref[...] = jnp.where(lane < experts, high, total - high).astype(bf16)


def last_expert(which, experts, rows, g_rows, gates, totals, gate_up, down_proj, grads):
    ff, width = down_proj.shape[1:]
    total = rows.shape[0]
    step = total // 4

    def block(columns):
        return pl.BlockSpec((step, columns), lambda i: (i, 0))

    def whole(shape):
        return pl.BlockSpec((1,) + shape[1:], lambda i: (which, 0, 0))

    def kernel(*refs):
        next_expert_kernel(which, experts, *refs)

    return pl.pallas_call(
        kernel,
        grid=(4,),
        out_shape=[
            jax.ShapeDtypeStruct((total, ff), bf16),
            jax.ShapeDtypeStruct(grads.shape, bf16),
            jax.ShapeDtypeStruct((total, 128), bf16),
        ],
        in_specs=[
            block(width), block(width), block(128), block(128),
            whole(gate_up.shape), whole(down_proj.shape), pl.BlockSpec(memory_space=pl.ANY),
        ],
        out_specs=[
            block(ff), pl.BlockSpec((step, 2 * ff), lambda i: (i, which)), block(128)
        ],
        input_output_aliases={6: 1},
        scratch_shapes=[pltpu.VMEM((step, 128), f32)],
        compiler_params=pltpu.CompilerParams(vmem_limit_bytes=56 * 2**20),
        cost_estimate=pl.CostEstimate(flops=10**6, bytes_accessed=10**6, transcendentals=0),
    )(rows, g_rows, gates, totals, gate_up, down_proj, grads)


def weight_grad_kernel(
    query_grad, kv_grad, branch, attended_owned, normed_owned, down_part, sums_ref,
    pre_v, branch_v, attended_v, normed_v, send_sem, recv_sem, local_sem,
):
    here = Places()
    greet([here.to_y, here.to_c, here.to_x])
    send = Sender(send_sem, recv_sem)
    count, wide = query_grad.shape
    narrow = kv_grad.shape[1]
    spread = lax.axis_size(plane)
    tile = sums_ref.shape[1]
    groups = lax.axis_size("dp")
    half = wide // 2
    low, high, last = pl.ds(0, half), pl.ds(half, half), pl.ds(wide, narrow)
    qa, _ = block_gather(
        here, send, query_grad.at[:, low], local_sem.at[1], pre_v, False, low
    )
    qb, _ = block_gather(
        here, send, query_grad.at[:, high], local_sem.at[2], pre_v, False, high
    )
    kv, _ = block_gather(here, send, kv_grad, local_sem.at[3], pre_v, False, last)
    loads = [pltpu.make_async_copy(branch, branch_v, local_sem.at[0])]
    for device in range(spread):
        slot = plane_slot(device // 4, device // 2 % 2, device % 2)
        rows = pl.ds(slot * count, count)
        for source, target in ((attended_owned, attended_v), (normed_owned, normed_v)):
            loads.append(
                pltpu.make_async_copy(
                    source.at[device], target.at[rows], local_sem.at[3 + len(loads)]
                )
            )

    output_rows = attended_v.shape[1] // groups * (branch.shape[1] // tile)
    pre_rows = normed_v.shape[1] // groups * ((wide + narrow) // tile)
    down_rows = down_part.shape[0] // groups
    kept = [
        pltpu.make_async_copy(
            down_part.at[pl.ds(d * down_rows, down_rows), pl.ds(i * tile, tile)],
            sums_ref.at[
                pl.ds(
                    d * (sums_ref.shape[0] // groups) + output_rows + pre_rows + i * down_rows,
                    down_rows,
                )
            ],
            local_sem.at[4 + 2 * spread + d * (down_part.shape[1] // tile) + i],
        )
        for d in range(groups)
        for i in range(down_part.shape[1] // tile)
    ]

    def start():
        for copy in loads + kept:
            copy.start()

    def product(left, right, base, first, tiles):
        rows = left.shape[1] // groups

        @pl.loop(first, first + tiles)
        def _(i):
            cols = pl.ds(pl.multiple_of(i * tile, tile), tile)
            part = transposed_dot(left[...], right[:, cols]).astype(bf16)
            for d in range(groups):
                at = d * (sums_ref.shape[0] // groups) + base + i * rows
                sums_ref[pl.ds(pl.multiple_of(at, 64), rows), :] = part[
                    d * rows : (d + 1) * rows
                ]

    def output_product():
        for load in loads:
            load.wait()
        product(attended_v, branch_v, 0, 0, branch.shape[1] // tile)

    steps = [
        qa[0], qb[0], kv[0], start, output_product, qa[1], qb[1], qa[2], kv[1], qb[2], qa[3],
        lambda: product(normed_v, pre_v, output_rows, 0, half // tile),
        kv[2], qb[3],
        lambda: product(normed_v, pre_v, output_rows, half // tile, half // tile),
        kv[3],
        lambda: product(normed_v, pre_v, output_rows, wide // tile, narrow // tile),
    ]
    for step in steps:
        step()
    for copy in kept:
        copy.wait()
    send.finish()


def weight_grads(query_grad, kv_grad, branch, attended_owned, normed_owned, down_part):
    count, wide = query_grad.shape
    narrow, width = kv_grad.shape[1], branch.shape[1]
    spread = lax.axis_size(plane)
    tile = narrow
    elements = attended_owned.shape[2] * width + normed_owned.shape[2] * (wide + narrow)
    elements += math.prod(down_part.shape)
    groups = lax.axis_size("dp")
    vmem = pl.BlockSpec(memory_space=pltpu.VMEM)
    anywhere = pl.BlockSpec(memory_space=pl.ANY)
    return pl.pallas_call(
        weight_grad_kernel,
        out_shape=jax.ShapeDtypeStruct((elements // tile, tile), bf16),
        in_specs=[anywhere] * 6,
        out_specs=vmem,
        scratch_shapes=[
            pltpu.VMEM((spread * count, wide + narrow), bf16),
            pltpu.VMEM((spread * count, width), bf16),
            pltpu.VMEM((spread * count, attended_owned.shape[2]), bf16),
            pltpu.VMEM((spread * count, normed_owned.shape[2]), bf16),
            pltpu.SemaphoreType.DMA((27,)),
            pltpu.SemaphoreType.DMA((27,)),
            pltpu.SemaphoreType.DMA((4 + 2 * spread + groups * (down_part.shape[1] // tile),)),
        ],
        compiler_params=pltpu.CompilerParams(
            collective_id=5, has_side_effects=True, vmem_limit_bytes=56 * 2**20
        ),
        cost_estimate=pl.CostEstimate(flops=10**6, bytes_accessed=10**6, transcendentals=0),
    )(query_grad, kv_grad, branch, attended_owned, normed_owned, down_part)


def untile_kernel(sums_ref, down_ref, output_ref, query_ref, key_ref, value_ref, downs_ref):
    tile = sums_ref.shape[1]
    at = 0

    def take(rows):
        nonlocal at
        part = sums_ref[at : at + rows, :].astype(f32)
        at = at + rows
        return part

    for out in (output_ref, query_ref):
        for first in range(0, out.shape[1], tile):
            out[:, first : first + tile] = take(out.shape[0])
    both = take(key_ref.shape[0])
    key_ref[...] = both[:, : key_ref.shape[1]]
    value_ref[...] = both[:, key_ref.shape[1] :]
    downs_ref[0] = down_ref[...].astype(f32)
    for first in range(0, downs_ref.shape[2], tile):
        downs_ref[1, :, first : first + tile] = take(downs_ref.shape[1])


def untile(sums, down, output_rows, wide, share, narrow):
    vmem = pl.BlockSpec(memory_space=pltpu.VMEM)
    rows, width = down.shape
    shapes = [
        (output_rows, width), (share, wide), (share, narrow), (share, narrow), (2, rows, width)
    ]
    return pl.pallas_call(
        untile_kernel,
        out_shape=[jax.ShapeDtypeStruct(shape, f32) for shape in shapes],
        in_specs=[vmem] * 2,
        out_specs=[vmem] * 5,
        compiler_params=pltpu.CompilerParams(vmem_limit_bytes=32 * 2**20),
    )(sums, down)


def arrive(got, name):
    copy = got[name]
    copy.wait() if name == "own" else copy.wait_recv()


def plane_index(here):
    return here.ctx * 2 + here.y


def plane_sum_kernel(across, parts, *refs):
    lefts, weight_hbm = refs[:parts], refs[parts]
    refs = refs[parts + 1 :]
    extra_ref, sources, targets = None, [], []
    if across:
        extra_ref, sources, targets = refs[0], refs[1:3], refs[4:6]
        refs = (refs[3],) + refs[6:]
    (
        out_ref, left_v, weight_v, part_v, core_v, edge_v, last_v, send_sem, recv_sem, local_sem,
    ) = refs
    here = Places()
    peers = here.peers() if across else []
    greet([device for _, device in peers] or [here.to_y, here.to_c, here.to_x])
    send = Sender(send_sem, recv_sem)
    count = out_ref.shape[0]
    half = count // 2
    experts = weight_hbm.shape[0]
    part_depth = lefts[0].shape[1]
    depth = part_depth * parts // experts
    width = weight_hbm.shape[1] if across else weight_hbm.shape[2]
    tile = 256
    x, y, c = here.x, here.y, here.c
    chips = [(1 - x, 1 - y), (1 - x, y), (x, 1 - y), (x, y)]
    weight_load = pltpu.make_async_copy(weight_hbm, weight_v, local_sem.at[0])
    weight_load.start()
    loads = []
    for k, (cx, cy) in enumerate(chips):
        some = chip_rows(cx, cy, count)
        loads.append(
            [
                pltpu.make_async_copy(
                    left.at[some, :],
                    left_v.at[k, :, pl.ds(e * part_depth, part_depth)],
                    local_sem.at[1 + parts * k + e],
                )
                for e, left in enumerate(lefts)
            ]
        )
        for load in loads[-1]:
            load.start()
    owned = []
    for index, device in peers:
        for source, target in zip(sources, targets):
            owned.append(send(source.at[index], target.at[plane_index(here)], device))
    kept = [
        pltpu.make_async_copy(
            source.at[plane_index(here)],
            target.at[plane_index(here)],
            local_sem.at[1 + 4 * parts + i],
        )
        for i, (source, target) in enumerate(zip(sources, targets))
    ]
    for copy in kept:
        copy.start()
    weight_load.wait()
    to_core = []

    def compute(k):
        for load in loads[k]:
            load.wait()

        @pl.loop(0, width // tile)
        def _(n):
            cols = pl.ds(pl.multiple_of(n * tile, tile), tile)
            total = None
            for e in range(experts):
                left = left_v[k, :, e * depth : (e + 1) * depth]
                if across:
                    part = lax.dot_general(
                        left,
                        weight_v[e, cols, :],
                        (((1,), (1,)), ((), ())),
                        preferred_element_type=f32,
                    )
                else:
                    part = dot(left, weight_v[e, :, cols])
                total = part if total is None else total + part
            part_v[k, :, cols] = total.astype(bf16)

        if extra_ref is not None:
            part_v[k, :, width:] = extra_ref[chip_rows(*chips[k], count), :]
        to_core.append(
            send(
                part_v.at[k, pl.ds(pl.multiple_of((1 - c) * count, count), count)],
                core_v.at[k],
                here.to_c,
            )
        )

    mine = pl.ds(pl.multiple_of(c * count, count), count)

    def chip_sum(k):
        to_core[k].wait_recv()
        return part_v[k, mine, :].astype(f32) + core_v[k].astype(f32)

    compute(0)
    compute(1)
    core_v[0] = chip_sum(0).astype(bf16)
    from_x = send(core_v.at[0, pl.ds(0, half)], edge_v.at[0], here.to_x)
    from_y = send(core_v.at[0, pl.ds(half, half)], edge_v.at[1], here.to_y)
    compute(2)
    over_x_sum = chip_sum(1)
    core_v[1, :half] = over_x_sum[:half].astype(bf16)
    from_y.wait_recv()
    core_v[1, half:] = (over_x_sum[half:] + edge_v[1].astype(f32)).astype(bf16)
    last_x = send(core_v.at[1], last_v.at[0], here.to_x)
    over_y_sum = chip_sum(2)
    core_v[2, half:] = over_y_sum[half:].astype(bf16)
    from_x.wait_recv()
    core_v[2, :half] = (over_y_sum[:half] + edge_v[0].astype(f32)).astype(bf16)
    last_y = send(core_v.at[2], last_v.at[1], here.to_y)
    compute(3)
    out_ref[...] = chip_sum(3)
    last_x.wait_recv()
    last_y.wait_recv()
    out_ref[...] = out_ref[...] + last_v[0].astype(f32) + last_v[1].astype(f32)
    for copy in owned:
        copy.wait_recv()
    for copy in kept:
        copy.wait()
    send.finish()


def plane_sum(lefts, weight, extra, owned, collective_id):
    across = extra is not None
    count = lefts[0].shape[0] // lax.axis_size(plane)
    width = weight.shape[1] if across else weight.shape[2]
    wide = width + (extra.shape[1] if across else 0)
    parts, depth = len(lefts), lefts[0].shape[1]
    vmem = pl.BlockSpec(memory_space=pltpu.VMEM)
    anywhere = pl.BlockSpec(memory_space=pl.ANY)

    def kernel(*refs):
        plane_sum_kernel(across, parts, *refs)

    return pl.pallas_call(
        kernel,
        out_shape=[jax.ShapeDtypeStruct((count, wide), f32)]
        + [jax.ShapeDtypeStruct(v.shape, v.dtype) for v in owned],
        in_specs=[anywhere] * (parts + 1) + [vmem] * across + [anywhere] * len(owned),
        out_specs=[vmem] + [anywhere] * len(owned),
        scratch_shapes=[
            pltpu.VMEM((4, 2 * count, parts * depth), bf16),
            pltpu.VMEM(weight.shape, bf16),
            pltpu.VMEM((4, 2 * count, wide), bf16),
            pltpu.VMEM((4, count, wide), bf16),
            pltpu.VMEM((2, count // 2, wide), bf16),
            pltpu.VMEM((2, count, wide), bf16),
            pltpu.SemaphoreType.DMA((8 + 7 * len(owned),)),
            pltpu.SemaphoreType.DMA((8 + 7 * len(owned),)),
            pltpu.SemaphoreType.DMA((1 + 4 * parts + len(owned),)),
        ],
        compiler_params=pltpu.CompilerParams(
            collective_id=collective_id, has_side_effects=True, vmem_limit_bytes=60 * 2**20
        ),
        cost_estimate=pl.CostEstimate(flops=10**6, bytes_accessed=10**6, transcendentals=0),
    )(*lefts, weight, *([extra] if across else []), *owned)


def head_softmax(queries, keys, visible):
    scores = lax.dot_general(
        queries, keys, (((1,), (1,)), ((), ())), preferred_element_type=f32
    ) * (HEAD_SIZE ** (-0.5))
    scores = jnp.where(visible, scores, masked)
    raised = jnp.exp(scores - jnp.max(scores, axis=-1, keepdims=True))
    return raised / jnp.sum(raised, axis=-1, keepdims=True)


def visible_keys(rows, keys):
    row = lax.broadcasted_iota(jnp.int32, (rows, keys), 0)
    key = lax.broadcasted_iota(jnp.int32, (rows, keys), 1)
    prompt_all = keys - (rows - PROMPT_DEV)
    own = lax.axis_index("ctx") * PROMPT_DEV + row
    position = jnp.where(row < PROMPT_DEV, own, prompt_all + row - PROMPT_DEV)
    return key <= position


def attention_kernel(
    query_pre_ref, gain_ref, cosine_ref, sine_ref, keys_ref, values_ref, queries_ref, attended_ref
):
    rows = query_pre_ref.shape[0]
    visible = visible_keys(rows, keys_ref.shape[0])
    keys = keys_ref[...]
    values = values_ref[...]
    for h in range(query_pre_ref.shape[1] // HEAD_SIZE):
        cols = slice(h * HEAD_SIZE, (h + 1) * HEAD_SIZE)
        v = query_pre_ref[:, cols]
        v = v * head_norm(v) * gain_ref[...]
        queries = (v * cosine_ref[...] + turn_half(v) * sine_ref[...]).astype(bf16)
        queries_ref[:, cols] = queries
        probs = head_softmax(queries, keys, visible).astype(bf16)
        attended_ref[:, cols] = dot(probs, values).astype(bf16)


def attention(query_pre, gain, cosine, sine, kv_all):
    rows, wide = query_pre.shape
    keys = kv_all.shape[0]
    group = wide // KEY_VALUE_HEADS
    small = pl.BlockSpec((rows, HEAD_SIZE), lambda i: (0, 0))
    block = pl.BlockSpec((rows, group), lambda i: (0, i))
    return pl.pallas_call(
        attention_kernel,
        grid=(KEY_VALUE_HEADS,),
        out_shape=[jax.ShapeDtypeStruct((rows, wide), bf16)] * 2,
        in_specs=[
            block,
            pl.BlockSpec((1, HEAD_SIZE), lambda i: (0, 0)),
            small,
            small,
            pl.BlockSpec((keys, HEAD_SIZE), lambda i: (0, i)),
            pl.BlockSpec((keys, HEAD_SIZE), lambda i: (0, KEY_VALUE_HEADS + i)),
        ],
        out_specs=[block, block],
        compiler_params=pltpu.CompilerParams(vmem_limit_bytes=48 * 2**20),
    )(query_pre, gain.reshape(1, HEAD_SIZE), cosine, sine, kv_all, kv_all)


def transposed_dot(a, b):
    return lax.dot_general(a, b, (((0,), (0,)), ((), ())), preferred_element_type=f32)


def back_heads(
    first,
    key_at,
    value_at,
    out_at,
    query_pre_ref,
    gain_ref,
    cosine_ref,
    sine_ref,
    keys_ref,
    values_ref,
    queries_ref,
    grad_ref,
    pre_grad_ref,
    key_grad_ref,
    value_grad_ref,
):
    rows = query_pre_ref.shape[0]
    visible = visible_keys(rows, keys_ref.shape[0])
    keys = keys_ref[:, pl.ds(key_at, HEAD_SIZE)]
    values = values_ref[:, pl.ds(value_at, HEAD_SIZE)]
    scale = HEAD_SIZE ** (-0.5)
    gain_grad = jnp.zeros((rows, HEAD_SIZE), f32)
    key_grad = jnp.zeros(keys.shape, f32)
    value_grad = jnp.zeros(keys.shape, f32)
    for h in range(QUERY_HEADS // KEY_VALUE_HEADS):
        cols = pl.ds(first + h * HEAD_SIZE, HEAD_SIZE)
        queries = queries_ref[:, cols]
        grad = grad_ref[:, cols]
        probs = head_softmax(queries, keys, visible)
        prob_grad = lax.dot_general(
            grad, values, (((1,), (1,)), ((), ())), preferred_element_type=f32
        )
        delta = jnp.sum(probs * prob_grad, axis=-1, keepdims=True)
        score_grad = (probs * (prob_grad - delta)).astype(bf16)
        key_grad = key_grad + transposed_dot(score_grad, queries)
        value_grad = value_grad + transposed_dot(probs.astype(bf16), grad)
        u = dot(score_grad, keys) * scale
        u = u * cosine_ref[...] + turn_half(u * sine_ref[...])
        v = query_pre_ref[:, cols]
        inv = head_norm(v)
        gain_grad = gain_grad + u * v * inv
        pre_grad_ref[:, cols] = norm_back(v, inv, gain_ref[...], u).astype(bf16)
    out = pl.ds(out_at, HEAD_SIZE)
    key_grad_ref[:, out] = (key_grad * scale).astype(key_grad_ref.dtype)
    value_grad_ref[:, out] = value_grad.astype(value_grad_ref.dtype)
    return jnp.sum(gain_grad, axis=0, keepdims=True)


def attention_back_kernel(*refs):
    refs[-1][0] = back_heads(0, 0, 0, 0, *refs[:-1])


def attention_back_gather_kernel(
    query_pre_ref, gain_ref, cosine_ref, sine_ref, kv_ref, queries_ref, grad_ref, branch,
    pre_grad_ref, key_grad_ref, value_grad_ref, gain_grad_ref, branch_rows,
    send_sem, recv_sem, local_sem,
):
    here = Places()
    greet([here.to_y, here.to_c, here.to_x])
    send = Sender(send_sem, recv_sem)
    stages, _ = block_gather(here, send, branch, local_sem.at[0], branch_rows)
    group = query_pre_ref.shape[1] // KEY_VALUE_HEADS
    narrow = kv_ref.shape[1] // 2

    def heads(first, count):
        @pl.loop(first, first + count)
        def _(i):
            at = pl.multiple_of(i * HEAD_SIZE, HEAD_SIZE)
            gain_grad_ref[i] = back_heads(
                pl.multiple_of(i * group, group),
                at,
                pl.multiple_of(narrow + i * HEAD_SIZE, HEAD_SIZE),
                at,
                query_pre_ref,
                gain_ref,
                cosine_ref,
                sine_ref,
                kv_ref,
                kv_ref,
                queries_ref,
                grad_ref,
                pre_grad_ref,
                key_grad_ref,
                value_grad_ref,
            )

    stages[0]()
    heads(0, KEY_VALUE_HEADS - 1)
    stages[1]()
    heads(KEY_VALUE_HEADS - 1, 1)
    stages[2]()
    stages[3]()
    send.finish()


def attention_back_gather(query_pre, gain, cosine, sine, kv_all, queries, attended_grad, branch):
    rows, wide = query_pre.shape
    keys, both = kv_all.shape
    vmem = pl.BlockSpec(memory_space=pltpu.VMEM)
    anywhere = pl.BlockSpec(memory_space=pl.ANY)
    return pl.pallas_call(
        attention_back_gather_kernel,
        out_shape=[
            jax.ShapeDtypeStruct((rows, wide), bf16),
            jax.ShapeDtypeStruct((keys, both // 2), f32),
            jax.ShapeDtypeStruct((keys, both // 2), f32),
            jax.ShapeDtypeStruct((KEY_VALUE_HEADS, 1, HEAD_SIZE), f32),
            jax.ShapeDtypeStruct((lax.axis_size(plane) * rows, branch.shape[1]), bf16),
        ],
        in_specs=[vmem] * 7 + [anywhere],
        out_specs=[vmem] * 4 + [anywhere],
        scratch_shapes=[
            pltpu.SemaphoreType.DMA((9,)),
            pltpu.SemaphoreType.DMA((9,)),
            pltpu.SemaphoreType.DMA((1,)),
        ],
        compiler_params=pltpu.CompilerParams(
            collective_id=6, has_side_effects=True, vmem_limit_bytes=48 * 2**20
        ),
        cost_estimate=pl.CostEstimate(flops=10**6, bytes_accessed=10**6, transcendentals=0),
    )(
        query_pre, gain.reshape(1, HEAD_SIZE), cosine, sine, kv_all, queries, attended_grad, branch
    )


def attention_back(query_pre, gain, cosine, sine, kv_all, queries, attended_grad):
    rows, wide = query_pre.shape
    keys, both = kv_all.shape
    group = wide // KEY_VALUE_HEADS
    small = pl.BlockSpec((rows, HEAD_SIZE), lambda i: (0, 0))
    block = pl.BlockSpec((rows, group), lambda i: (0, i))
    return pl.pallas_call(
        attention_back_kernel,
        grid=(KEY_VALUE_HEADS,),
        out_shape=[
            jax.ShapeDtypeStruct((rows, wide), bf16),
            jax.ShapeDtypeStruct((keys, both // 2), f32),
            jax.ShapeDtypeStruct((keys, both // 2), f32),
            jax.ShapeDtypeStruct((KEY_VALUE_HEADS, 1, HEAD_SIZE), f32),
        ],
        in_specs=[
            block,
            pl.BlockSpec((1, HEAD_SIZE), lambda i: (0, 0)),
            small,
            small,
            pl.BlockSpec((keys, HEAD_SIZE), lambda i: (0, i)),
            pl.BlockSpec((keys, HEAD_SIZE), lambda i: (0, KEY_VALUE_HEADS + i)),
            block,
            block,
        ],
        out_specs=[
            block,
            pl.BlockSpec((keys, HEAD_SIZE), lambda i: (0, i)),
            pl.BlockSpec((keys, HEAD_SIZE), lambda i: (0, i)),
            pl.BlockSpec((1, 1, HEAD_SIZE), lambda i: (i, 0, 0)),
        ],
        cost_estimate=pl.CostEstimate(flops=10**6, bytes_accessed=10**6, transcendentals=0),
        compiler_params=pltpu.CompilerParams(vmem_limit_bytes=48 * 2**20),
    )(
        query_pre, gain.reshape(1, HEAD_SIZE), cosine, sine, kv_all, kv_all, queries, attended_grad
    )


def join_halves(mine, other):
    lower = lax.axis_index("expert") == 0
    return jnp.concatenate(
        [jnp.where(lower, mine, other), jnp.where(lower, other, mine)], axis=1
    )


def dot(a, b):
    return jnp.dot(a, b, preferred_element_type=f32)


def ctx_sum(v):
    if not small_plane():
        return lax.psum_scatter(v, "ctx", scatter_dimension=1, tiled=True).astype(f32)
    member = lax.axis_index("ctx")

    def block(j):
        return lax.dynamic_slice_in_dim(v, (member ^ j) * PROMPT_DEV, PROMPT_DEV, axis=1)

    near = block(0).astype(f32) + core(block(1)).astype(f32)
    far = (block(2).astype(f32) + core(block(3)).astype(f32)).astype(bf16)
    return near + over_x(far).astype(f32)


def body(
    hidden_in,
    attn_gain,
    query_weight,
    key_matrix,
    value_matrix,
    query_gain,
    key_gain,
    output_weight,
    ffn_gain,
    router_weight,
    gate_up,
    down_proj,
    routes,
    out_grad,
):
    ctx_count = lax.axis_size("ctx")
    spread_count = lax.axis_size(plane)
    dp_count = lax.axis_size("dp")
    device_count = dp_count * spread_count
    local_experts = gate_up.shape[0]
    count_of_rows = hidden_in.shape[0]
    prompt_all = PROMPT_DEV * ctx_count
    hidden_ff = gate_up.shape[2] // 2
    member = lax.axis_index("ctx")
    offsets = jnp.arange(count_of_rows, dtype=jnp.int32)
    position = jnp.where(
        offsets < PROMPT_DEV, member * PROMPT_DEV + offsets, prompt_all + offsets - PROMPT_DEV
    )
    cosine, rope_sine = angles(position, HEAD_SIZE)
    narrow = KEY_VALUE_HEADS * HEAD_SIZE
    wide = QUERY_HEADS * HEAD_SIZE
    inputs = hidden_in.astype(f32)
    scale_in = rms_scale(inputs)

    def by_owner(v):
        v = v.reshape(count_of_rows, dp_count, spread_count, -1)
        return v.transpose(2, 0, 1, 3).reshape(spread_count, count_of_rows, -1)

    signed_sine = rope_sine * jnp.where(jnp.arange(HEAD_SIZE) < HEAD_SIZE // 2, -1.0, 1.0)
    if small_plane():
        (
            kv_other,
            q_other,
            o_other,
            g_rows,
            route_rows,
            kv_all,
            normed_owned,
            attended_owned,
            query_pre,
            queries,
            key_pre,
            residual,
            ffn_in,
        ) = fetch_and_attend(
            hidden_in, attn_gain, query_gain, key_gain, ffn_gain, cosine, signed_sine,
            key_matrix, value_matrix, query_weight, output_weight, out_grad, routes,
        )
        kv_weights = [jnp.concatenate([key_matrix, value_matrix], axis=1), kv_other]
        q_weights = [query_weight, q_other]
        o_weights = [output_weight, o_other]
    else:
        full = [
            lax.all_gather(w, "expert", axis=0, tiled=True)
            for w in (
                jnp.concatenate([key_matrix, value_matrix], axis=1),
                query_weight,
                output_weight,
            )
        ]
        kv_weights, q_weights, o_weights = [[w] for w in full]
        g_rows = lax.all_gather(out_grad, plane, axis=0, tiled=True)
        route_rows = lax.all_gather(routes, plane, axis=0, tiled=True)
        normalized_input = (inputs * scale_in * attn_gain).astype(bf16)
        query_pre = dot(normalized_input, q_weights[0])
        key_value_pre = dot(normalized_input, kv_weights[0])
        key_pre = key_value_pre[:, :narrow]
        key_heads = key_pre.reshape(count_of_rows, KEY_VALUE_HEADS, HEAD_SIZE)
        key_low = rotate(
            key_heads * rms_scale(key_heads) * key_gain, cosine[:, None, :], rope_sine[:, None, :]
        ).astype(bf16)
        kv_low = jnp.concatenate(
            [key_low.reshape(count_of_rows, narrow), key_value_pre[:, narrow:].astype(bf16)],
            axis=1,
        )
        kv_blocks = lax.all_gather(kv_low[:PROMPT_DEV], "ctx", axis=0, tiled=True)
        kv_all = jnp.concatenate([kv_blocks, kv_low[PROMPT_DEV:]], axis=0)
        queries, attended = attention(query_pre, query_gain, cosine, signed_sine, kv_all)
        residual = inputs + dot(attended, o_weights[0])
        ffn_in = (residual * rms_scale(residual) * ffn_gain).astype(bf16)
        normed_owned = by_owner(normalized_input)
        attended_owned = by_owner(attended)

    def owned(v):
        return lax.all_to_all(v, plane, split_axis=0, concat_axis=0, tiled=True)

    def backward_dot(v, weights):
        parts = [dot(v, w.T) for w in weights]
        return parts[0] if len(parts) == 1 else join_halves(*parts)

    key_before_norm = key_pre.reshape(count_of_rows, KEY_VALUE_HEADS, HEAD_SIZE)
    key_inv = rms_scale(key_before_norm)
    scale_ffn = rms_scale(residual)

    expert_count = local_experts * spread_count
    expert_ids = jnp.arange(expert_count, dtype=jnp.int32)

    def gates_of(some_rows, some_routes):
        logits = dot(some_rows, router_weight)
        chosen = jnp.any(some_routes[:, :, None] == expert_ids[None, None, :], axis=1)
        logits = jnp.where(chosen, logits, masked)
        raised = jnp.where(
            chosen, jnp.exp(logits - jnp.max(logits, axis=-1, keepdims=True)), 0.0
        )
        return raised / jnp.sum(raised, axis=-1, keepdims=True)

    gates = gates_of(ffn_in, routes)
    if small_plane():
        rows, hidden, grads, gates_mine, totals, down_part = gather_first_expert(
            ffn_in, route_rows, router_weight, g_rows, gate_up, down_proj
        )
        hiddens = [hidden]
        down_parts = [down_part]
        rows, grads = after((rows, grads), down_parts)
        hidden, grads, gate_grads = last_expert(
            1, expert_count, rows, g_rows, gates_mine, totals, gate_up, down_proj, grads
        )
        hiddens.append(hidden)
        projected_grads = [grads]
        gate_up_parts = [dot(rows.T, grads).astype(bf16)]
        down_late = dot(after(hidden, gate_up_parts).T, g_rows).astype(bf16)
    else:
        rows = lax.all_gather(ffn_in, plane, axis=0, tiled=True)
        first_expert = lax.axis_index(plane) * local_experts
        gates_mine = lax.dynamic_slice_in_dim(
            gates_of(rows, route_rows), first_expert, local_experts, axis=1
        )
        gate_grads, hiddens, projected_grads = [], [], []
        for which in range(local_experts):
            gate = gates_mine[:, which : which + 1]
            projected = dot(rows, gate_up[which])
            back = dot(g_rows, down_proj[which].T)
            gate_part = projected[:, :hidden_ff]
            up_part = projected[:, hidden_ff:]
            sigmoid_gate = jax.nn.sigmoid(gate_part)
            hidden = gate_part * sigmoid_gate * up_part
            gate_grads.append(jnp.sum(hidden * back, axis=-1))
            hiddens.append((gate * hidden).astype(bf16))
            back = gate * back
            gate_back = back * up_part * sigmoid_gate * (1.0 + gate_part * (1.0 - sigmoid_gate))
            up_back = back * gate_part * sigmoid_gate
            projected_grads.append(jnp.concatenate([gate_back, up_back], axis=-1).astype(bf16))
        attended_owned, normed_owned = owned(attended_owned), owned(normed_owned)
        down_parts = [dot(v.T, g_rows).astype(bf16) for v in hiddens]
        gate_up_parts = [dot(rows.T, v).astype(bf16) for v in projected_grads]
    down_low, gate_up_low = [
        [lax.psum_scatter(v, "dp", scatter_dimension=0, tiled=True) for v in parts]
        for parts in (down_parts, gate_up_parts)
    ]
    gate_up_grad = jnp.stack(
        [
            part.astype(f32)
            for v in gate_up_low
            for part in jnp.split(v, v.shape[1] // (2 * hidden_ff), axis=1)
        ]
    )
    projected_grads, hiddens = lax.optimization_barrier(
        ((projected_grads, hiddens), down_parts, gate_up_parts)
    )[0]
    if small_plane():
        back, attended_owned, normed_owned = plane_sum(
            projected_grads, gate_up, gate_grads, [attended_owned, normed_owned], 3
        )
        back_sum = back[:, :MODEL_WIDTH]
        gate_grad = (
            back[:, MODEL_WIDTH : MODEL_WIDTH + expert_count]
            + back[:, MODEL_WIDTH + expert_count : MODEL_WIDTH + 2 * expert_count]
        )
        moe_sum = None
    else:
        moe_part = 0.0
        row_part = 0.0
        for which in range(local_experts):
            row_part = row_part + dot(projected_grads[which], gate_up[which].T)
            moe_part = moe_part + dot(hiddens[which], down_proj[which])
        moe_sum, back_sum = [
            lax.psum_scatter(v.astype(bf16), plane, scatter_dimension=0, tiled=True).astype(f32)
            for v in (moe_part, row_part)
        ]
        gate_grad = lax.all_to_all(
            jnp.stack(gate_grads, axis=1).reshape(spread_count, count_of_rows, local_experts),
            plane,
            split_axis=0,
            concat_axis=0,
            tiled=True,
        )
        gate_grad = gate_grad.transpose(1, 0, 2).reshape(count_of_rows, expert_count)
    logit_grad = gates * (gate_grad - jnp.sum(gates * gate_grad, axis=-1, keepdims=True))

    grad_out = out_grad.astype(f32)
    router_local = jnp.dot(ffn_in.T, logit_grad, preferred_element_type=f32)
    ffn_in_grad = back_sum + jnp.dot(
        logit_grad, router_weight.astype(f32).T, precision=highest
    )
    residual_grad = grad_out + norm_back(residual, scale_ffn, ffn_gain, ffn_in_grad)
    ffn_gain_local = jnp.sum(ffn_in_grad * residual * scale_ffn, axis=0)
    branch_low = residual_grad.astype(bf16)
    attended_grad = backward_dot(branch_low, o_weights).astype(bf16)
    operands = (query_pre, query_gain, cosine, signed_sine, kv_all, queries, attended_grad)
    if small_plane():
        *attention_grads, branch_rows = attention_back_gather(*operands, branch_low)
    else:
        attention_grads = attention_back(*operands)
    query_pre_grad, key_grad_all, value_grad_all, query_gain_parts = attention_grads
    query_gain_local = jnp.sum(query_gain_parts, axis=(0, 1))
    pair_grads = jnp.stack([key_grad_all[:prompt_all], value_grad_all[:prompt_all]]).astype(bf16)
    prompt_grads = ctx_sum(pair_grads)
    key_grad = jnp.concatenate([prompt_grads[0], key_grad_all[prompt_all:]], axis=0).reshape(
        count_of_rows, KEY_VALUE_HEADS, HEAD_SIZE
    )
    value_gradient = jnp.concatenate([prompt_grads[1], value_grad_all[prompt_all:]], axis=0)
    key_rot_grad = rotate_back(key_grad, cosine[:, None, :], rope_sine[:, None, :])
    key_gain_local = jnp.sum(key_rot_grad * key_before_norm * key_inv, axis=(0, 1))
    key_pre_grad = (
        norm_back(key_before_norm, key_inv, key_gain, key_rot_grad)
        .astype(bf16)
        .reshape(count_of_rows, KEY_VALUE_HEADS * HEAD_SIZE)
    )
    key_value_grad = jnp.concatenate([key_pre_grad, value_gradient.astype(bf16)], axis=1)
    if small_plane():
        local = [
            weight_grads(
                query_pre_grad, key_value_grad, branch_rows, attended_owned, normed_owned, down_late
            )
        ]
    else:
        branch_rows = lax.all_gather(branch_low, plane, axis=0, tiled=True)
        pre_rows = lax.all_gather(
            jnp.concatenate([query_pre_grad, key_value_grad], axis=1), plane, axis=0, tiled=True
        )
        attended_owned, normed_owned = [
            v.reshape(spread_count * count_of_rows, -1) for v in (attended_owned, normed_owned)
        ]
        local = [
            dot(attended_owned.T, branch_rows).astype(bf16),
            dot(normed_owned.T, pre_rows).astype(bf16),
        ]
    query_pre_grad, key_value_grad = lax.optimization_barrier(
        ((query_pre_grad, key_value_grad), local)
    )[0]
    normed_grad = backward_dot(query_pre_grad, q_weights) + backward_dot(
        key_value_grad, kv_weights
    )
    attn_gain_local = jnp.sum(normed_grad * inputs * scale_in, axis=0)
    hidden_grad = residual_grad + norm_back(inputs, scale_in, attn_gain, normed_grad)
    if small_plane():
        moe_sum = plane_sum(after(hiddens, local), down_proj, None, [], 4)[0]
    block_out = (residual + moe_sum).astype(bf16)
    local = lax.optimization_barrier((local, gate_up_low, down_low))[0]
    summed = [lax.psum_scatter(v, "dp", scatter_dimension=0, tiled=True) for v in local]
    share = MODEL_WIDTH // device_count
    if small_plane():
        output_sum, query_sum, key_sum, value_sum, down_grad = untile(
            summed[0], down_low[0], wide // device_count, wide, share, narrow
        )
    else:
        output_sum, pre_sum = [v.astype(f32) for v in summed]
        query_sum = pre_sum[:, :wide]
        key_sum = pre_sum[:, wide : wide + narrow]
        value_sum = pre_sum[:, wide + narrow :]
        down_grad = jnp.stack([v.astype(f32) for v in down_low])

    small = jnp.concatenate(
        [
            v.reshape(device_count, -1)
            for v in (
                attn_gain_local,
                ffn_gain_local,
                query_gain_local,
                key_gain_local,
                router_local,
            )
        ],
        axis=1,
    )
    small = lax.all_to_all(small[:, None], every, split_axis=0, concat_axis=0, tiled=True)
    small = jnp.sum(small[:, 0], axis=0)
    head_share = HEAD_SIZE // device_count
    cuts = [share, share, head_share, head_share, share * expert_count]
    ends = [sum(cuts[: i + 1]) for i in range(5)]
    a_grad, f_grad, q_grad, k_grad, r_grad = [
        small[end - cut : end] for end, cut in zip(ends, cuts)
    ]
    return (
        block_out,
        hidden_grad,
        a_grad,
        query_sum,
        key_sum,
        value_sum,
        q_grad,
        k_grad,
        output_sum,
        f_grad,
        r_grad.reshape(share, expert_count),
        gate_up_grad,
        down_grad,
    )


def solution(mesh):
    placed = (
        P(("dp", "ctx", "expert"), None),
        P(),
        P("expert", None),
        P("expert", None),
        P("expert", None),
        P(),
        P(),
        P("expert", None),
        P(),
        P(),
        P(("ctx", "expert"), None, None),
        P(("ctx", "expert"), None, None),
        P(("dp", "ctx", "expert"), None),
        P(("dp", "ctx", "expert"), None),
    )
    return jax.shard_map(
        body,
        mesh=mesh,
        in_specs=placed,
        out_specs=(
            P(("dp", "ctx", "expert"), None),
            P(("dp", "ctx", "expert"), None),
            P(("dp", "ctx", "expert")),
            P(("dp", "ctx", "expert"), None),
            P(("dp", "ctx", "expert"), None),
            P(("dp", "ctx", "expert"), None),
            P(("dp", "ctx", "expert")),
            P(("dp", "ctx", "expert")),
            P(("dp", "ctx", "expert"), None),
            P(("dp", "ctx", "expert")),
            P(("dp", "ctx", "expert"), None),
            P(("ctx", "expert"), "dp", None),
            P(("ctx", "expert"), "dp", None),
        ),
        check_vma=False,
    )
```
